128 devices in a mesh: dp: 8 (over x_lo, y), head: 16 (over x_hi, z, core).
Axes of the slice: x: 4 (x_hi: 2, x_lo: 2; x = x_hi * 2 + x_lo), y: 4, z: 4, core: 2. Of those that a mesh axis runs over, the one named last changes fastest.
Arguments:
- block_input: bfloat16 [16384, 2048], P(('dp', 'head')), may hold values from -6 to 6
- cotangent: bfloat16 [16384, 2048], P(('dp', 'head')), may hold values from -6 to 6
- lengths: int32 [8, 3], P('dp'), may hold values from 1 to 1920, as said below
- gain_a: float32 [2048], replicated, may hold values from 0.5 to 1.5
- based_in: bfloat16 [2048, 2560], P(None, ('head', 'dp')), may hold values from -0.125 to 0.125
- based_out: bfloat16 [2048, 2048], P(('head', 'dp')), may hold values from -1.5 to 1.5
- gain_b: float32 [2048], replicated, may hold values from 0.5 to 1.5
- swa_in: bfloat16 [2048, 6144], P(None, ('head', 'dp')), may hold values from -0.125 to 0.125
- swa_out: bfloat16 [2048, 2048], P(('head', 'dp')), may hold values from -0.5 to 0.5
- gain_c: float32 [2048], replicated, may hold values from 0.5 to 1.5
- mlp_in: bfloat16 [2048, 2, 5632], P(None, None, ('head', 'dp')), may hold values from -0.125 to 0.125
- mlp_down: bfloat16 [5632, 2048], P(('head', 'dp')), may hold values from -0.078125 to 0.078125
Outputs:
- block_output: bfloat16 [16384, 2048], P(('dp', 'head'))
- input_grad: float32 [16384, 2048], P(('dp', 'head'))
- grad_gain_a: float32 [2048], replicated
- grad_based_in: float32 [2048, 2560], P(None, ('head', 'dp'))
- grad_based_out: float32 [2048, 2048], P(('head', 'dp'))
- grad_gain_b: float32 [2048], replicated
- grad_swa_in: float32 [2048, 6144], P(None, ('head', 'dp'))
- grad_swa_out: float32 [2048, 2048], P(('head', 'dp'))
- grad_gain_c: float32 [2048], replicated
- grad_mlp_in: float32 [2048, 2, 5632], P(None, None, ('head', 'dp'))
- grad_mlp_down: float32 [5632, 2048], P(('head', 'dp'))
The draws below stay inside these ranges and needn't reach their ends.
Inputs may be any that keep to these rules, and one draw needn't show every extreme that they name: `lengths`: in each group the 3 sequences take buckets of 64, 1920 and 64 consecutive slots, in this order; a sequence's tokens open its bucket and padding fills the rest. The middle sequence fills its bucket; each other one has 1 to 64 tokens.
All inputs are finite; a program needn't handle non-finite values.
Results may differ from the reference program's by a relative error of at most 0.033.
Values may be sent and summed in bfloat16 or wider, within the bound.
A program may use at most 192 MiB of HBM per device.

```python
import math
import jax
import jax.numpy as jnp
from jax import lax

D = 2048
HEADS = 16
FEAT = 16
HEAD_V = 128
WINDOW = 64
FF = 5632
TOK_DEV = 128
GROUP_TOK = 2048
GROUPS = 8
TOKENS = 16384
N_HEAD = 16


def draw_lengths(key, part):
    key = jax.random.fold_in(key, 11)
    half_len = TOK_DEV // 2
    short_lengths = jax.random.randint(key, (GROUPS, 2), 1, half_len + 1).astype(jnp.int32)
    long_lengths = jnp.full((GROUPS, 1), GROUP_TOK - 2 * half_len, dtype=jnp.int32)
    return jnp.concatenate([short_lengths[:, :1], long_lengths, short_lengths[:, 1:]], axis=1)


def block_levels(rng, extent, pieces, least, high):
    level = 1.0
    for dim, shards_of in pieces:
        draws = jax.random.uniform(jax.random.fold_in(jax.random.fold_in(rng, 6), dim), (shards_of,), jnp.float32, least / len(pieces), high / len(pieces))
        level = level * jnp.repeat(jnp.exp(draws), extent[dim] // shards_of).reshape((-1,) + (1,) * (len(extent) - 1 - dim))
    return level


def centred(stream_key, shape, spread, limit, shards=(), kind=jnp.bfloat16):
    result = spread * jax.random.normal(stream_key, shape, jnp.float32)
    if shards:
        result = result * block_levels(stream_key, shape, shards, -0.22, 0.18)
    return jnp.clip(result, -limit, limit).astype(kind)


def setup_inputs(seed: int = 0) -> dict:
    keys = jax.random.split(jax.random.key(seed), 13)
    return {
        "block_input": centred(keys[0], (TOKENS, D), 1.0, 6.0, ((0, 128),)),
        "cotangent": centred(keys[1], (TOKENS, D), 1.0, 6.0, ((0, 128),)),
        "lengths": draw_lengths(jax.random.fold_in(keys[12], 71), 0),
        "gain_a": jnp.clip(1.0 + 0.1 * jax.random.normal(keys[3], (D,), jnp.float32), 0.5, 1.5),
        "based_in": centred(keys[4], (D, HEADS * (2 * FEAT + HEAD_V)), D ** -0.5, 0.125, ((1, 128),)),
        "based_out": centred(keys[5], (HEADS * HEAD_V, D), (HEAD_V // 8) ** -0.5, 1.5, ((0, 128),)),
        "gain_b": jnp.clip(1.0 + 0.1 * jax.random.normal(keys[6], (D,), jnp.float32), 0.5, 1.5),
        "swa_in": centred(keys[7], (D, HEADS * 3 * HEAD_V), D ** -0.5, 0.125, ((1, 128),)),
        "swa_out": centred(keys[8], (HEADS * HEAD_V, D), HEAD_V ** -0.5, 0.5, ((0, 128),)),
        "gain_c": jnp.clip(1.0 + 0.1 * jax.random.normal(keys[9], (D,), jnp.float32), 0.5, 1.5),
        "mlp_in": centred(keys[10], (D, 2, FF), D ** -0.5, 0.125, ((2, 128),)),
        "mlp_down": centred(keys[11], (FF, D), FF ** -0.5, 0.078125, ((0, 128),)),
    }


EPSILON = 1e-05

@jax.custom_vjp
def low(v):
    return lax.optimization_barrier(v.astype(jnp.bfloat16)).astype(jnp.float32)

@jax.custom_vjp
def low_back(v):
    return v

def low_keep(v):
    return (low(v), None)

def low_pass(kept, grad):
    return (grad,)

def back_keep(v):
    return (v, None)

def back_low(kept, grad):
    return (low(grad),)
low.defvjp(low_keep, low_pass)
low_back.defvjp(back_keep, back_low)

def rms_norm(values, gain):
    scale = lax.rsqrt(lax.optimization_barrier(jnp.mean(values * values, axis=-1, keepdims=True)) + EPSILON)
    return values * scale * gain

def matmul(left_side, right_side):
    return jnp.dot(left_side, right_side, precision=lax.Precision.HIGHEST, preferred_element_type=jnp.float32)

def copies_of(normed):
    return low_back(jnp.broadcast_to(normed[None], (N_HEAD,) + normed.shape))

def grouped_in(copies, weight):
    parts = jnp.einsum('gtd,dgk->tgk', copies, weight.reshape(weight.shape[0], N_HEAD, -1), precision=lax.Precision.HIGHEST, preferred_element_type=jnp.float32)
    return parts.reshape(copies.shape[1], -1)

def grouped_out(mixed, weight):
    parts = jnp.einsum('tgk,gkd->gtd', mixed.reshape(mixed.shape[0], N_HEAD, -1), weight.reshape(N_HEAD, -1, weight.shape[1]), precision=lax.Precision.HIGHEST, preferred_element_type=jnp.float32)
    return lax.optimization_barrier(jnp.sum(low(parts), axis=0))

def layout(length_row):
    half_len = TOK_DEV // 2
    slot_ids = jnp.arange(GROUP_TOK, dtype=jnp.int32)
    segment = (slot_ids >= half_len).astype(jnp.int32) + (slot_ids >= GROUP_TOK - half_len).astype(jnp.int32)
    bucket_start = jnp.where(segment == 0, 0, jnp.where(segment == 1, half_len, GROUP_TOK - half_len)).astype(jnp.int32)
    position = slot_ids - bucket_start
    chosen = jnp.where(segment == 0, length_row[0], jnp.where(segment == 1, length_row[1], length_row[2]))
    return (segment, position, position < chosen)

def turning(position):
    half_width = HEAD_V // 2
    frequency = jnp.exp(-math.log(10000.0) * jnp.arange(half_width, dtype=jnp.float32) * 2.0 / HEAD_V)
    angles = position.astype(jnp.float32)[:, None] * frequency[None, :]
    angles = jnp.concatenate([angles, angles], axis=-1)[:, None, :]
    return (jnp.cos(angles), jnp.sin(angles))

def rotate_half(values):
    half_width = values.shape[-1] // 2
    return jnp.concatenate([-values[..., half_width:], values[..., :half_width]], axis=-1)

def rotary(values, cosine, sine_part):
    return values * cosine + rotate_half(values) * sine_part

def linear_head(queries, key_vecs, values, allowed):
    scores = low_back(matmul(queries, key_vecs.T) / math.sqrt(FEAT))
    kernel = jnp.where(allowed, 1.0 + scores + 0.5 * scores * scores, 0.0)
    totals = lax.optimization_barrier(jnp.sum(kernel, axis=1, keepdims=True))
    return matmul(low(kernel / totals), values)

def window_head(queries, key_vecs, values, allowed):
    scores = low_back(matmul(queries, key_vecs.T) / math.sqrt(HEAD_V))
    masked = jnp.where(allowed, scores, -1e+30)
    prob_weights = jax.nn.softmax(masked, axis=1)
    return matmul(low(prob_weights), values)

def by_heads(tensor):
    return jnp.transpose(tensor, (1, 0, 2))

def group_forward(inputs, length_row, params):
    gain_a, based_in, based_out, gain_b, swa_in, swa_out, gain_c, mlp_in, mlp_down = params
    segment, position, valid_mask = layout(length_row)
    slot_ids = jnp.arange(GROUP_TOK, dtype=jnp.int32)
    causal = (segment[:, None] == segment[None, :]) & (slot_ids[:, None] >= slot_ids[None, :])
    windowed = causal & (slot_ids[:, None] - slot_ids[None, :] < WINDOW)
    normed_first = low(rms_norm(inputs, gain_a))
    projected = low_back(grouped_in(copies_of(normed_first), based_in)).reshape(GROUP_TOK, HEADS, 2 * FEAT + HEAD_V)
    projected = low(projected)
    queries = by_heads(projected[:, :, :FEAT])
    key_vecs = by_heads(projected[:, :, FEAT:2 * FEAT])
    values = by_heads(projected[:, :, 2 * FEAT:])
    mixed_first = lax.map(jax.checkpoint(lambda item_set: linear_head(item_set[0], item_set[1], item_set[2], causal)), (queries, key_vecs, values))
    mixed_first = low_back(low(by_heads(mixed_first).reshape(GROUP_TOK, HEADS * HEAD_V)))
    middle = inputs + low_back(grouped_out(mixed_first, based_out))
    normed_second = low(rms_norm(middle, gain_b))
    projected = low_back(grouped_in(copies_of(normed_second), swa_in)).reshape(GROUP_TOK, HEADS, 3 * HEAD_V)
    cosine, sine_part = turning(position)
    queries = by_heads(low(rotary(projected[:, :, :HEAD_V], cosine, sine_part)))
    key_vecs = by_heads(low(rotary(projected[:, :, HEAD_V:2 * HEAD_V], cosine, sine_part)))
    values = by_heads(low(projected[:, :, 2 * HEAD_V:]))
    mixed_second = lax.map(jax.checkpoint(lambda item_set: window_head(item_set[0], item_set[1], item_set[2], windowed)), (queries, key_vecs, values))
    mixed_second = low_back(low(by_heads(mixed_second).reshape(GROUP_TOK, HEADS * HEAD_V)))
    late = middle + low_back(grouped_out(mixed_second, swa_out))
    normed_third = low(rms_norm(late, gain_c))
    third_copies = copies_of(normed_third)
    gate_part = low_back(grouped_in(third_copies, mlp_in[:, 0, :]))
    up_part = low_back(grouped_in(third_copies, mlp_in[:, 1, :]))
    activated = low(jax.nn.silu(gate_part) * up_part)
    return late + low_back(grouped_out(activated, mlp_down))

def reference(block_input, cotangent, lengths, gain_a, based_in, based_out, gain_b, swa_in, swa_out, gain_c, mlp_in, mlp_down):
    params = tuple((item.astype(jnp.float32) for item in (gain_a, based_in, based_out, gain_b, swa_in, swa_out, gain_c, mlp_in, mlp_down)))
    inputs = block_input.astype(jnp.float32).reshape(GROUPS, GROUP_TOK, D)

    def forward(params, inputs):
        group_step = jax.checkpoint(lambda rows, length_row: group_forward(rows, length_row, params))

        def scan_step(carried, group_pair):
            return (carried, group_step(group_pair[0], group_pair[1]))
        return lax.scan(scan_step, jnp.float32(0.0), (inputs, lengths))[1]
    outputs, pullback = jax.vjp(forward, params, inputs)
    valid_mask = jax.vmap(lambda length_row: layout(length_row)[2])(lengths)
    seed_grad = cotangent.astype(jnp.float32).reshape(GROUPS, GROUP_TOK, D) * valid_mask[:, :, None].astype(jnp.float32)
    param_grads, input_grads = pullback(seed_grad)
    return (outputs.reshape(TOKENS, D).astype(jnp.bfloat16), input_grads.reshape(TOKENS, D), param_grads[0], param_grads[1], param_grads[2], param_grads[3], param_grads[4], param_grads[5], param_grads[6], param_grads[7], param_grads[8])
```

```python
import functools
import math

import jax
import jax.numpy as jnp
import numpy as np
from jax import lax
from jax.experimental import pallas as pl
from jax.experimental.pallas import tpu as pltpu
from jax.sharding import Mesh
from jax.sharding import PartitionSpec as P

FEAT = 16
HEAD_V = 128
WINDOW = 64
EPSILON = 1e-05
D = 2048
TOK = 128
HALF_TOK = 1024
EDGE = 64
UNIT_PAD = 48
BIN_PAD = 32
STATE = 256
PLANE = ("xh", "xl", "y")
RING = ("z", "c")
ALL = ("xl", "y", "xh", "z", "c")
MESH = pl.DeviceIdType.MESH
BF = jnp.bfloat16
F32 = jnp.float32
VM = pl.BlockSpec(memory_space=pltpu.VMEM)
ANY = pl.BlockSpec(memory_space=pl.ANY)


def dnn(a, b):
    return lax.dot_general(a, b, (((1,), (0,)), ((), ())), preferred_element_type=F32)


def dnt(a, b):
    return lax.dot_general(a, b, (((1,), (1,)), ((), ())), preferred_element_type=F32)


def dtn(a, b):
    return lax.dot_general(a, b, (((0,), (0,)), ((), ())), preferred_element_type=F32)


def remote(src, dst, send_sem, recv_sem, device):
    copy = pltpu.make_async_remote_copy(
        src_ref=src,
        dst_ref=dst,
        send_sem=send_sem,
        recv_sem=recv_sem,
        device_id=device,
        device_id_type=MESH,
    )
    copy.start()
    return copy


def greet(devices):
    barrier = pltpu.get_barrier_semaphore()
    for device in devices:
        pl.semaphore_signal(barrier, inc=1, device_id=device, device_id_type=MESH)
    pl.semaphore_wait(barrier, len(devices))


class Ring:
    def __init__(self):
        self.z = lax.axis_index("z")
        self.c = lax.axis_index("c")
        self.oc = 1 - self.c
        self.zp = lax.rem(self.z + 1, 4)
        self.zm = lax.rem(self.z + 3, 4)
        self.zz = lax.rem(self.z + 2, 4)
        self.up = {"z": self.zp}
        self.dn = {"z": self.zm}
        self.sib = {"c": self.oc}

    def greet(self):
        greet((self.up, self.dn, self.sib))


def gather_rows(ring, buf, out_ref, ss, rs, ls, base=0):
    half = TOK // 2
    me = ring.z * 2 + ring.c
    below, above, far = ring.zm * 2 + ring.c, ring.zp * 2 + ring.c, ring.zz * 2 + ring.c

    def send(slot, part, device, index):
        piece = buf.at[slot, pl.ds(part * half, half), :]
        return remote(piece, piece, ss.at[base + index], rs.at[base + index], device)

    local = []

    def keep(slot):
        copy = pltpu.make_async_copy(
            buf.at[slot],
            out_ref.at[pl.ds(pl.multiple_of(slot * TOK, TOK), TOK), :],
            ls.at[len(local)],
        )
        copy.start()
        local.append(copy)

    up, dn, sib = ring.up, ring.dn, ring.sib
    cp = {}
    cp[0] = send(me, 0, up, 0)
    cp[1] = send(me, 1, dn, 1)
    cp[2] = send(me, 1, up, 2)
    cp[3] = send(me, 0, dn, 3)
    cp[4] = send(me, 0, sib, 4)
    cp[5] = send(me, 1, sib, 5)
    keep(me)
    cp[0].wait_recv()
    cp[6] = send(below, 0, up, 6)
    cp[8] = send(below, 0, sib, 8)
    cp[1].wait_recv()
    cp[7] = send(above, 1, dn, 7)
    cp[9] = send(above, 1, sib, 9)
    cp[2].wait_recv()
    cp[10] = send(below, 1, sib, 10)
    keep(below)
    cp[3].wait_recv()
    cp[11] = send(above, 0, sib, 11)
    keep(above)
    cp[4].wait_recv()
    cp[5].wait_recv()
    keep(ring.z * 2 + ring.oc)
    cp[8].wait_recv()
    cp[10].wait_recv()
    keep(ring.zm * 2 + ring.oc)
    cp[9].wait_recv()
    cp[11].wait_recv()
    keep(ring.zp * 2 + ring.oc)
    cp[6].wait_recv()
    cp[12] = send(far, 0, sib, 12)
    cp[7].wait_recv()
    cp[13] = send(far, 1, sib, 13)
    keep(far)
    cp[12].wait_recv()
    cp[13].wait_recv()
    keep(ring.zz * 2 + ring.oc)
    for index in range(14):
        cp[index].wait_send()
    for copy in local:
        copy.wait()


def scatter_sum(ring, a_ref, w_ref, part, sib_in, far_in, end_in, ss, rs, base=0):
    half = TOK // 2
    c, oc = ring.c, ring.oc
    up, dn, sib = ring.up, ring.dn, ring.sib
    order = (ring.zz, ring.zp, ring.zm, ring.z)
    step = 512

    def multiply(index):
        row = pl.multiple_of(order[index] * (2 * TOK), 2 * TOK)

        def one(n, carry):
            col = pl.ds(pl.multiple_of(n * step, step), step)
            res = dnn(a_ref[pl.ds(row, 2 * TOK), :], w_ref[:, col]).astype(BF)
            part[index, 0, :, col] = res[:TOK]
            part[index, 1, :, col] = res[TOK:]
            return carry

        lax.fori_loop(0, D // step, one, 0)
        return remote(
            part.at[index, oc], sib_in.at[index], ss.at[base + index], rs.at[base + index], sib
        )

    def add(index, rows_start, rows, other):
        def one(i, carry):
            at = pl.ds(pl.multiple_of(rows_start + i * 16, 16), 16)
            part[index, c, at, :] = (part[index, c, at, :].astype(F32) + other(i, at)).astype(BF)
            return carry

        lax.fori_loop(0, rows // 16, one, 0)

    def add_sib(index):
        add(index, 0, TOK, lambda i, at: sib_in[index, at, :].astype(F32))

    def send(src, dst, device, index):
        return remote(src, dst, ss.at[base + index], rs.at[base + index], device)

    low, high = pl.ds(0, half), pl.ds(half, half)
    cp = {}
    cp[0] = multiply(0)
    cp[1] = multiply(1)
    cp[0].wait_recv()
    add_sib(0)
    cp[4] = send(part.at[0, c, low, :], far_in.at[0], up, 4)
    cp[5] = send(part.at[0, c, high, :], far_in.at[1], dn, 5)
    cp[2] = multiply(2)
    cp[1].wait_recv()
    add_sib(1)
    cp[6] = send(part.at[1, c, high, :], end_in.at[0, high, :], up, 6)
    cp[3] = multiply(3)
    cp[2].wait_recv()
    add_sib(2)
    cp[7] = send(part.at[2, c, low, :], end_in.at[1, low, :], dn, 7)
    cp[4].wait_recv()
    add(1, 0, half, lambda i, at: far_in[0, pl.ds(pl.multiple_of(i * 16, 16), 16), :].astype(F32))
    cp[8] = send(part.at[1, c, low, :], end_in.at[0, low, :], up, 8)
    cp[5].wait_recv()
    add(2, half, half, lambda i, at: far_in[1, pl.ds(pl.multiple_of(i * 16, 16), 16), :].astype(F32))
    cp[9] = send(part.at[2, c, high, :], end_in.at[1, high, :], dn, 9)
    cp[3].wait_recv()
    add_sib(3)
    cp[6].wait_recv()
    cp[7].wait_recv()
    cp[8].wait_recv()
    cp[9].wait_recv()
    return cp


SCATTER_SCRATCH = [
    pltpu.VMEM((4, 2, TOK, D), BF),
    pltpu.VMEM((4, TOK, D), BF),
    pltpu.VMEM((2, TOK // 2, D), BF),
    pltpu.VMEM((2, TOK, D), BF),
]


def params(collective_id, limit=48):
    return pltpu.CompilerParams(
        collective_id=collective_id, has_side_effects=True, vmem_limit_bytes=limit << 20
    )


def scale_of(rows):
    return lax.rsqrt(jnp.mean(rows * rows, axis=-1, keepdims=True) + EPSILON)


def first_kernel(x_ref, gain_ref, out_ref, buf, ss, rs, ls):
    ring = Ring()
    me = ring.z * 2 + ring.c

    def one(i, carry):
        at = pl.ds(pl.multiple_of(i * 16, 16), 16)
        rows = x_ref[at, :].astype(F32)
        buf[me, at, :] = (rows * scale_of(rows) * gain_ref[...]).astype(BF)
        return carry

    lax.fori_loop(0, TOK // 16, one, 0)
    ring.greet()
    gather_rows(ring, buf, out_ref, ss, rs, ls)


def first_gather(x, gain):
    return pl.pallas_call(
        first_kernel,
        out_shape=jax.ShapeDtypeStruct((HALF_TOK, D), BF),
        in_specs=[VM, VM],
        out_specs=ANY,
        scratch_shapes=[
            pltpu.VMEM((8, TOK, D), BF),
            pltpu.SemaphoreType.DMA((14,)),
            pltpu.SemaphoreType.DMA((14,)),
            pltpu.SemaphoreType.DMA((8,)),
        ],
        compiler_params=params(1),
    )(x, gain)


def total_rows(part, end_in, c, at):
    return (
        part[3, c, at, :].astype(F32)
        + end_in[0, at, :].astype(F32)
        + end_in[1, at, :].astype(F32)
    )


def forward_kernel(
    a_ref, w_ref, x_ref, gain_ref, x_out, h_out, part, sib_in, far_in, end_in, buf, ss, rs, ls
):
    ring = Ring()
    me = ring.z * 2 + ring.c
    ring.greet()
    cp = scatter_sum(ring, a_ref, w_ref, part, sib_in, far_in, end_in, ss, rs)

    def one(i, carry):
        at = pl.ds(pl.multiple_of(i * 16, 16), 16)
        rows = x_ref[at, :].astype(F32) + total_rows(part, end_in, ring.c, at)
        x_out[at, :] = rows
        buf[me, at, :] = (rows * scale_of(rows) * gain_ref[...]).astype(BF)
        return carry

    lax.fori_loop(0, TOK // 16, one, 0)
    gather_rows(ring, buf, h_out, ss, rs, ls, base=10)
    for index in range(10):
        cp[index].wait_send()


def forward_step(a, w, x, gain, collective_id):
    return pl.pallas_call(
        forward_kernel,
        out_shape=(
            jax.ShapeDtypeStruct((TOK, D), F32),
            jax.ShapeDtypeStruct((HALF_TOK, D), BF),
        ),
        in_specs=[VM] * 4,
        out_specs=(VM, ANY),
        scratch_shapes=SCATTER_SCRATCH
        + [
            pltpu.VMEM((8, TOK, D), BF),
            pltpu.SemaphoreType.DMA((24,)),
            pltpu.SemaphoreType.DMA((24,)),
            pltpu.SemaphoreType.DMA((8,)),
        ],
        compiler_params=params(collective_id),
    )(a, w, x, gain)


def norm_back_rows(v_ref, gain_ref, grads, at, gain_acc):
    rows = v_ref[at, :].astype(F32)
    scale = scale_of(rows)
    unit = rows * scale
    gain_acc[...] += grads * unit
    scaled = grads * gain_ref[...]
    return scale * (scaled - unit * jnp.mean(scaled * unit, axis=-1, keepdims=True))


def backward_kernel(
    a_ref,
    w_ref,
    v_ref,
    gain_ref,
    d_ref,
    d_out,
    gain_out,
    e_out,
    part,
    sib_in,
    far_in,
    end_in,
    gain_acc,
    buf,
    ss,
    rs,
    ls,
):
    ring = Ring()
    me = ring.z * 2 + ring.c
    ring.greet()
    gain_acc[...] = jnp.zeros_like(gain_acc)
    cp = scatter_sum(ring, a_ref, w_ref, part, sib_in, far_in, end_in, ss, rs)

    def one(i, carry):
        at = pl.ds(pl.multiple_of(i * 16, 16), 16)
        grads = total_rows(part, end_in, ring.c, at)
        rows = d_ref[at, :] + norm_back_rows(v_ref, gain_ref, grads, at, gain_acc)
        d_out[at, :] = rows
        buf[me, at, :] = rows.astype(BF)
        return carry

    lax.fori_loop(0, TOK // 16, one, 0)
    gain_out[...] = jnp.sum(gain_acc[...], axis=0, keepdims=True)
    gather_rows(ring, buf, e_out, ss, rs, ls, base=10)
    for index in range(10):
        cp[index].wait_send()


def backward_step(a, w, v, gain, d, collective_id):
    return pl.pallas_call(
        backward_kernel,
        out_shape=(
            jax.ShapeDtypeStruct((TOK, D), F32),
            jax.ShapeDtypeStruct((1, D), F32),
            jax.ShapeDtypeStruct((HALF_TOK, D), BF),
        ),
        in_specs=[VM] * 5,
        out_specs=(VM, VM, ANY),
        scratch_shapes=SCATTER_SCRATCH
        + [
            pltpu.VMEM((16, D), F32),
            pltpu.VMEM((8, TOK, D), BF),
            pltpu.SemaphoreType.DMA((24,)),
            pltpu.SemaphoreType.DMA((24,)),
            pltpu.SemaphoreType.DMA((8,)),
        ],
        compiler_params=params(collective_id),
    )(a, w, v, gain, d)


def last_kernel(
    a_ref, w_ref, v_ref, gain_ref, d_ref, d_out, gain_out, part, sib_in, far_in, end_in, gain_acc, ss, rs
):
    ring = Ring()
    ring.greet()
    gain_acc[...] = jnp.zeros_like(gain_acc)
    cp = scatter_sum(ring, a_ref, w_ref, part, sib_in, far_in, end_in, ss, rs)

    def one(i, carry):
        at = pl.ds(pl.multiple_of(i * 16, 16), 16)
        grads = total_rows(part, end_in, ring.c, at)
        d_out[at, :] = d_ref[at, :] + norm_back_rows(v_ref, gain_ref, grads, at, gain_acc)
        return carry

    lax.fori_loop(0, TOK // 16, one, 0)
    gain_out[...] = jnp.sum(gain_acc[...], axis=0, keepdims=True)
    for index in range(10):
        cp[index].wait_send()


def last_step(a, w, v, gain, d):
    return pl.pallas_call(
        last_kernel,
        out_shape=(jax.ShapeDtypeStruct((TOK, D), F32), jax.ShapeDtypeStruct((1, D), F32)),
        in_specs=[VM] * 5,
        out_specs=(VM, VM),
        scratch_shapes=SCATTER_SCRATCH
        + [
            pltpu.VMEM((16, D), F32),
            pltpu.SemaphoreType.DMA((10,)),
            pltpu.SemaphoreType.DMA((10,)),
        ],
        compiler_params=params(6),
    )(a, w, v, gain, d)


def state_tables():
    first = np.zeros((128, STATE), np.float32)
    second = np.zeros((128, STATE), np.float32)
    bias = np.zeros((8, STATE), np.float32)
    coef = np.zeros((8, STATE), np.float32)
    bias[0, 0] = bias[1, 0] = 1.0
    coef[0, 0] = 1.0
    at = 1
    for i in range(FEAT):
        first[i, at] = 1.0
        bias[1, at] = 1.0
        coef[0, at] = 1.0 / math.sqrt(FEAT)
        at += 1
    for i in range(FEAT):
        for j in range(i, FEAT):
            first[i, at] = 1.0
            second[j, at] = 1.0
            coef[0, at] = (0.5 if i == j else 1.0) / FEAT
            at += 1
    picks = np.zeros((4, 128, 128), np.float32)
    for which in range(4):
        for i in range(FEAT):
            picks[which, which * FEAT + i, i] = 1.0
    return (
        np.stack([first, second]),
        np.concatenate([bias[:2], coef[:1], np.zeros((5, STATE), np.float32)]),
        picks,
    )


def causal_mask(row_start, col_start, rows, cols, edge):
    t = row_start + lax.broadcasted_iota(jnp.int32, (rows, cols), 0)
    u = col_start + lax.broadcasted_iota(jnp.int32, (rows, cols), 1)
    return (u <= t) & ((t >= edge) == (u >= edge))


BLK = 256
NBLK = HALF_TOK // BLK
INV_ROOT = 1.0 / math.sqrt(FEAT)


def linear_forward_kernel(
    p_ref, e_ref, t_ref, pick_ref, y_ref, sv_ref, sn_ref, qs, ks, num, den, sv_s, sn_s, sv_r, sn_r, ss, rs
):
    xh = lax.axis_index("xh")
    partner = {"xh": 1 - xh}
    edge = jnp.where(xh == 0, EDGE, HALF_TOK - EDGE)
    bias1, bias2, coef = t_ref[0:1, :], t_ref[1:2, :], t_ref[2:3, :]
    small = p_ref[:, 2 * HEAD_V :]
    for j in range(2):
        qs[j] = dnn(small, pick_ref[2 * j]).astype(BF)
        ks[j] = dnn(small, pick_ref[2 * j + 1]).astype(BF)

    def rows_of(r):
        return slice(r * BLK, (r + 1) * BLK)

    def phi_of(vecs):
        return (dnn(vecs, e_ref[0]) + bias1) * (dnn(vecs, e_ref[1]) + bias2)

    for j in range(2):
        sv = jnp.zeros((HEAD_V, STATE), F32)
        sn = jnp.zeros((1, STATE), F32)
        for r in range(NBLK):
            phi = phi_of(ks[j, rows_of(r), :])
            if r == 0:
                slot = lax.broadcasted_iota(jnp.int32, (BLK, STATE), 0)
                phi = jnp.where(slot >= EDGE, phi, 0.0)
            sv = sv + dtn(p_ref[rows_of(r), j * HEAD_V : (j + 1) * HEAD_V], phi.astype(BF))
            sn = sn + jnp.sum(phi, axis=0, keepdims=True)
        sv_s[j] = (sv * coef).astype(BF)
        sn_s[j] = jnp.broadcast_to(sn * coef, (8, STATE))
    greet((partner,))
    copies = (
        remote(sv_s, sv_r, ss.at[0], rs.at[0], partner),
        remote(sn_s, sn_r, ss.at[1], rs.at[1], partner),
    )
    for j in range(2):
        for r in range(NBLK):
            queries = qs[j, rows_of(r), :]
            rows_num = jnp.zeros((BLK, HEAD_V), F32)
            rows_den = jnp.zeros((BLK, 1), F32)
            for s in range(r + 1):
                scores = dnt(queries, ks[j, rows_of(s), :]) * INV_ROOT
                mask = causal_mask(r * BLK, s * BLK, BLK, BLK, edge)
                kernel = jnp.where(mask, 1.0 + scores + 0.5 * scores * scores, 0.0)
                rows_den = rows_den + jnp.sum(kernel, axis=-1, keepdims=True)
                rows_num = rows_num + dnn(
                    kernel.astype(BF), p_ref[rows_of(s), j * HEAD_V : (j + 1) * HEAD_V]
                )
            num[j, rows_of(r), :] = rows_num
            den[j, rows_of(r), :] = jnp.broadcast_to(rows_den, (BLK, HEAD_V))
    for copy in copies:
        copy.wait_recv()
    sv_ref[...] = sv_r[...]
    sn_ref[...] = sn_r[...]
    for j in range(2):
        for r in range(NBLK):
            phi = phi_of(qs[j, rows_of(r), :])
            cross_den = jnp.sum(phi * sn_r[j, 0:1, :], axis=-1, keepdims=True)
            cross_num = dnt(phi.astype(BF), sv_r[j])
            slot = r * BLK + lax.broadcasted_iota(jnp.int32, (BLK, HEAD_V), 0)
            seen = (slot < HALF_TOK - EDGE) & (xh == 1)
            top = num[j, rows_of(r), :] + jnp.where(seen, cross_num, 0.0)
            bottom = den[j, rows_of(r), :] + jnp.where(seen, cross_den, 0.0)
            y_ref[rows_of(r), j * HEAD_V : (j + 1) * HEAD_V] = (top / bottom).astype(BF)
    for copy in copies:
        copy.wait_send()


def linear_forward(p1, tables):
    return pl.pallas_call(
        linear_forward_kernel,
        out_shape=(
            jax.ShapeDtypeStruct((HALF_TOK, 2 * HEAD_V), BF),
            jax.ShapeDtypeStruct((2, HEAD_V, STATE), BF),
            jax.ShapeDtypeStruct((2, 8, STATE), F32),
        ),
        in_specs=[VM] * 4,
        out_specs=(VM, VM, VM),
        scratch_shapes=[
            pltpu.VMEM((2, HALF_TOK, 128), BF),
            pltpu.VMEM((2, HALF_TOK, 128), BF),
            pltpu.VMEM((2, HALF_TOK, HEAD_V), F32),
            pltpu.VMEM((2, HALF_TOK, HEAD_V), F32),
            pltpu.VMEM((2, HEAD_V, STATE), BF),
            pltpu.VMEM((2, 8, STATE), F32),
            pltpu.VMEM((2, HEAD_V, STATE), BF),
            pltpu.VMEM((2, 8, STATE), F32),
            pltpu.SemaphoreType.DMA((2,)),
            pltpu.SemaphoreType.DMA((2,)),
        ],
        compiler_params=params(7),
    )(p1, *tables)


def linear_backward_kernel(
    p_ref,
    dy_ref,
    sv_ref,
    sn_ref,
    e_ref,
    t_ref,
    pick_ref,
    dp_ref,
    qs,
    ks,
    dq,
    dk,
    dv,
    tv_s,
    tn_s,
    tv_r,
    tn_r,
    ss,
    rs,
):
    xh = lax.axis_index("xh")
    partner = {"xh": 1 - xh}
    edge = jnp.where(xh == 0, EDGE, HALF_TOK - EDGE)
    bias1, bias2, coef = t_ref[0:1, :], t_ref[1:2, :], t_ref[2:3, :]
    small = p_ref[:, 2 * HEAD_V :]
    for j in range(2):
        qs[j] = dnn(small, pick_ref[2 * j]).astype(BF)
        ks[j] = dnn(small, pick_ref[2 * j + 1]).astype(BF)
    dk[...] = jnp.zeros_like(dk)
    dv[...] = jnp.zeros_like(dv)

    def rows_of(r):
        return slice(r * BLK, (r + 1) * BLK)

    def factors_of(vecs):
        return (dnn(vecs, e_ref[0]) + bias1, dnn(vecs, e_ref[1]) + bias2)

    def factors_back(phi_grad, one, two):
        return dnt((phi_grad * two).astype(BF), e_ref[0]) + dnt(
            (phi_grad * one).astype(BF), e_ref[1]
        )

    for j in range(2):
        head = slice(j * HEAD_V, (j + 1) * HEAD_V)
        tv = jnp.zeros((HEAD_V, STATE), F32)
        tn = jnp.zeros((1, STATE), F32)
        for r in range(NBLK):
            queries = qs[j, rows_of(r), :]
            grads = dy_ref[rows_of(r), head]
            one, two = factors_of(queries)
            phi = one * two
            slot = r * BLK + lax.broadcasted_iota(jnp.int32, (BLK, 1), 0)
            seen = (slot < HALF_TOK - EDGE) & (xh == 1)
            cross_den = jnp.sum(phi * sn_ref[j, 0:1, :], axis=-1, keepdims=True)
            cross_num = dnt(phi.astype(BF), sv_ref[j])
            total = jnp.where(seen, cross_den, 0.0)
            dot = jnp.where(
                seen, jnp.sum(cross_num * grads.astype(F32), axis=-1, keepdims=True), 0.0
            )
            kept = []
            for s in range(r + 1):
                scores = dnt(queries, ks[j, rows_of(s), :]) * INV_ROOT
                mask = causal_mask(r * BLK, s * BLK, BLK, BLK, edge)
                kernel = jnp.where(mask, 1.0 + scores + 0.5 * scores * scores, 0.0)
                weight_grad = dnt(grads, p_ref[rows_of(s), head])
                total = total + jnp.sum(kernel, axis=-1, keepdims=True)
                dot = dot + jnp.sum(kernel * weight_grad, axis=-1, keepdims=True)
                kept.append((scores, mask, kernel, weight_grad))
            inverse = 1.0 / total
            mean = dot * inverse
            grads_n = (grads.astype(F32) * inverse).astype(BF)
            query_grad = jnp.zeros((BLK, 128), F32)
            for s in range(r + 1):
                scores, mask, kernel, weight_grad = kept[s]
                score_grad = jnp.where(
                    mask, (weight_grad - mean) * inverse * (1.0 + scores), 0.0
                ).astype(BF)
                query_grad = query_grad + dnn(score_grad, ks[j, rows_of(s), :])
                dk[j, rows_of(s), :] += dtn(score_grad, queries)
                dv[j, rows_of(s), :] += dtn(kernel.astype(BF), grads_n)
            shift = jnp.where(seen, -(mean * inverse), 0.0)
            cross_g = jnp.where(seen, grads_n, jnp.zeros_like(grads_n))
            phi_grad = dnn(cross_g, sv_ref[j]) + shift * sn_ref[j, 0:1, :]
            dq[j, rows_of(r), :] = query_grad * INV_ROOT + factors_back(phi_grad, one, two)
            tv = tv + dtn(cross_g, phi.astype(BF))
            tn = tn + jnp.sum(shift * phi, axis=0, keepdims=True)
        tv_s[j] = (tv * coef).astype(BF)
        tn_s[j] = jnp.broadcast_to(tn * coef, (8, STATE))
    greet((partner,))
    copies = (
        remote(tv_s, tv_r, ss.at[0], rs.at[0], partner),
        remote(tn_s, tn_r, ss.at[1], rs.at[1], partner),
    )
    for copy in copies:
        copy.wait_recv()
    for r in range(NBLK):
        placed = jnp.zeros((BLK, 128), F32)
        for j in range(2):
            head = slice(j * HEAD_V, (j + 1) * HEAD_V)
            one, two = factors_of(ks[j, rows_of(r), :])
            phi = one * two
            if r == 0:
                slot = lax.broadcasted_iota(jnp.int32, (BLK, STATE), 0)
                open_rows = slot >= EDGE
                phi = jnp.where(open_rows, phi, 0.0)
            phi_grad = dnn(p_ref[rows_of(r), head], tv_r[j]) + tn_r[j, 0:1, :]
            if r == 0:
                phi_grad = jnp.where(open_rows, phi_grad, 0.0)
            key_grad = dk[j, rows_of(r), :] * INV_ROOT + factors_back(phi_grad, one, two)
            value_grad = dv[j, rows_of(r), :] + dnt(phi.astype(BF), tv_r[j])
            dp_ref[rows_of(r), head] = value_grad.astype(BF)
            placed = placed + dnt(dq[j, rows_of(r), :].astype(BF), pick_ref[2 * j])
            placed = placed + dnt(key_grad.astype(BF), pick_ref[2 * j + 1])
        dp_ref[rows_of(r), 2 * HEAD_V :] = placed.astype(BF)
    for copy in copies:
        copy.wait_send()


def linear_backward(p1, dy, sv, sn, tables):
    return pl.pallas_call(
        linear_backward_kernel,
        out_shape=jax.ShapeDtypeStruct((HALF_TOK, 3 * HEAD_V), BF),
        in_specs=[VM] * 7,
        out_specs=VM,
        scratch_shapes=[
            pltpu.VMEM((2, HALF_TOK, 128), BF),
            pltpu.VMEM((2, HALF_TOK, 128), BF),
            pltpu.VMEM((2, HALF_TOK, 128), F32),
            pltpu.VMEM((2, HALF_TOK, 128), F32),
            pltpu.VMEM((2, HALF_TOK, HEAD_V), F32),
            pltpu.VMEM((2, HEAD_V, STATE), BF),
            pltpu.VMEM((2, 8, STATE), F32),
            pltpu.VMEM((2, HEAD_V, STATE), BF),
            pltpu.VMEM((2, 8, STATE), F32),
            pltpu.SemaphoreType.DMA((2,)),
            pltpu.SemaphoreType.DMA((2,)),
        ],
        compiler_params=params(8),
    )(p1, dy, sv, sn, *tables)


WBLK = 128
WKEYS = WBLK + WINDOW
INV_ROOT_V = 1.0 / math.sqrt(HEAD_V)


def window_mask(r, edge, lowest):
    t = r * WBLK + lax.broadcasted_iota(jnp.int32, (WBLK, WKEYS), 0)
    u = r * WBLK - WINDOW + lax.broadcasted_iota(jnp.int32, (WBLK, WKEYS), 1)
    return (u <= t) & (t - u < WINDOW) & ((t >= edge) == (u >= edge)) & (u >= lowest)


def window_forward_kernel(p_ref, cos_ref, sin_ref, y_ref, q_ref, kv_ref, ss, rs):
    xh = lax.axis_index("xh")
    partner = {"xh": 1 - xh}
    edge = jnp.where(xh == 0, EDGE, HALF_TOK - EDGE)
    lowest = jnp.where(xh == 0, 0, -WINDOW)

    def turned(r, part):
        rows = slice(r * WBLK, (r + 1) * WBLK)
        vecs = p_ref[rows, part * 128 : (part + 1) * 128]
        return (
            vecs * cos_ref[rows, :] + pltpu.roll(vecs, HEAD_V // 2, 1) * sin_ref[rows, :]
        ).astype(BF)

    blocks = HALF_TOK // WBLK
    for r in (blocks - 1,) + tuple(range(blocks - 1)):
        rows = slice(r * WBLK, (r + 1) * WBLK)
        shifted = slice(WINDOW + r * WBLK, WINDOW + (r + 1) * WBLK)
        for j in range(2):
            q_ref[rows, j * 128 : (j + 1) * 128] = turned(r, 3 * j)
            kv_ref[shifted, j * 128 : (j + 1) * 128] = turned(r, 3 * j + 1)
            kv_ref[shifted, (2 + j) * 128 : (3 + j) * 128] = p_ref[
                rows, (3 * j + 2) * 128 : (3 * j + 3) * 128
            ].astype(BF)
        if r == blocks - 1:
            greet((partner,))
            copy = remote(
                kv_ref.at[pl.ds(HALF_TOK, WINDOW), :],
                kv_ref.at[pl.ds(0, WINDOW), :],
                ss,
                rs,
                partner,
            )
    for r in tuple(range(1, blocks)) + (0,):
        if r == 0:
            copy.wait_recv()
        rows = slice(r * WBLK, (r + 1) * WBLK)
        keys = slice(r * WBLK, r * WBLK + WKEYS)
        mask = window_mask(r, edge, lowest)
        for j in range(2):
            head = slice(j * 128, (j + 1) * 128)
            scores = dnt(q_ref[rows, head], kv_ref[keys, head]) * INV_ROOT_V
            scores = jnp.where(mask, scores, -1e30)
            exps = jnp.exp(scores - jnp.max(scores, axis=-1, keepdims=True))
            probs = exps / jnp.sum(exps, axis=-1, keepdims=True)
            y_ref[rows, head] = dnn(
                probs.astype(BF), kv_ref[keys, (2 + j) * 128 : (3 + j) * 128]
            ).astype(BF)
    copy.wait_send()


def window_forward(p2, cosine, sine):
    return pl.pallas_call(
        window_forward_kernel,
        out_shape=(
            jax.ShapeDtypeStruct((HALF_TOK, 256), BF),
            jax.ShapeDtypeStruct((HALF_TOK, 256), BF),
            jax.ShapeDtypeStruct((HALF_TOK + WINDOW, 512), BF),
        ),
        in_specs=[VM] * 3,
        out_specs=(VM, VM, VM),
        scratch_shapes=[pltpu.SemaphoreType.DMA, pltpu.SemaphoreType.DMA],
        compiler_params=params(9),
    )(p2, cosine, sine)


def window_backward_kernel(
    q_ref, kv_ref, dy_ref, cos_ref, sin_ref, dp_ref, dkv, halo, ss, rs
):
    xh = lax.axis_index("xh")
    partner = {"xh": 1 - xh}
    edge = jnp.where(xh == 0, EDGE, HALF_TOK - EDGE)
    lowest = jnp.where(xh == 0, 0, -WINDOW)
    dkv[...] = jnp.zeros_like(dkv)
    blocks = HALF_TOK // WBLK

    def turned_back(r, grads):
        rows = slice(r * WBLK, (r + 1) * WBLK)
        return (
            grads * cos_ref[rows, :] + pltpu.roll(grads * sin_ref[rows, :], HEAD_V // 2, 1)
        ).astype(BF)

    for r in range(blocks):
        rows = slice(r * WBLK, (r + 1) * WBLK)
        keys = slice(r * WBLK, r * WBLK + WKEYS)
        mask = window_mask(r, edge, lowest)
        for j in range(2):
            head = slice(j * 128, (j + 1) * 128)
            vals = slice((2 + j) * 128, (3 + j) * 128)
            queries, grads = q_ref[rows, head], dy_ref[rows, head]
            scores = dnt(queries, kv_ref[keys, head]) * INV_ROOT_V
            scores = jnp.where(mask, scores, -1e30)
            exps = jnp.exp(scores - jnp.max(scores, axis=-1, keepdims=True))
            probs = exps / jnp.sum(exps, axis=-1, keepdims=True)
            prob_grad = dnt(grads, kv_ref[keys, vals])
            score_grad = (
                probs * (prob_grad - jnp.sum(prob_grad * probs, axis=-1, keepdims=True))
            ).astype(BF)
            dp_ref[rows, 3 * j * 128 : (3 * j + 1) * 128] = turned_back(
                r, dnn(score_grad, kv_ref[keys, head]) * INV_ROOT_V
            )
            dkv[keys, head] += dtn(score_grad, queries) * INV_ROOT_V
            dkv[keys, vals] += dtn(probs.astype(BF), grads)
        if r == 0:
            greet((partner,))
            copy = remote(dkv.at[pl.ds(0, WINDOW), :], halo, ss, rs, partner)
    for r in range(blocks):
        rows = slice(r * WBLK, (r + 1) * WBLK)
        shifted = slice(WINDOW + r * WBLK, WINDOW + (r + 1) * WBLK)
        if r == blocks - 1:
            copy.wait_recv()
            dkv[HALF_TOK : HALF_TOK + WINDOW, :] += halo[...]
        for j in range(2):
            dp_ref[rows, (3 * j + 1) * 128 : (3 * j + 2) * 128] = turned_back(
                r, dkv[shifted, j * 128 : (j + 1) * 128]
            )
            dp_ref[rows, (3 * j + 2) * 128 : (3 * j + 3) * 128] = dkv[
                shifted, (2 + j) * 128 : (3 + j) * 128
            ].astype(BF)
    copy.wait_send()


def window_backward(q, kv, dy, cosine, sine):
    return pl.pallas_call(
        window_backward_kernel,
        out_shape=jax.ShapeDtypeStruct((HALF_TOK, 768), BF),
        in_specs=[VM] * 5,
        out_specs=VM,
        scratch_shapes=[
            pltpu.VMEM((HALF_TOK + WINDOW, 512), F32),
            pltpu.VMEM((WINDOW, 512), F32),
            pltpu.SemaphoreType.DMA,
            pltpu.SemaphoreType.DMA,
        ],
        compiler_params=params(10),
    )(q, kv, dy, cosine, sine)


def plane_gather(rows):
    return lax.all_gather(rows, PLANE, axis=0, tiled=True)


def plane_reduce(rows):
    return lax.psum_scatter(rows.astype(BF), PLANE, scatter_dimension=0, tiled=True).astype(F32)


def padded(rows, count):
    return jnp.pad(rows, ((0, count - rows.shape[0]), (0, 0)))


def place():
    slot = lax.axis_index("xh") * HALF_TOK + jnp.arange(HALF_TOK, dtype=jnp.int32)
    last = 2 * HALF_TOK - EDGE
    segment = (slot >= EDGE).astype(jnp.int32) + (slot >= last).astype(jnp.int32)
    start = jnp.where(segment == 0, 0, jnp.where(segment == 1, EDGE, last)).astype(jnp.int32)
    return segment, slot - start


def body(
    block_input,
    cotangent,
    lengths,
    gain_a,
    based_in,
    based_out,
    gain_b,
    swa_in,
    swa_out,
    gain_c,
    mlp_in,
    mlp_down,
):
    gains = [gain.reshape(1, D) for gain in (gain_a, gain_b, gain_c)]
    units = mlp_down.shape[0]
    wide = based_in.shape[1]
    segment, position = place()
    first = (lax.axis_index("z") * 2 + lax.axis_index("c")) * TOK
    my_segment = lax.dynamic_slice_in_dim(segment, first, TOK)
    my_position = lax.dynamic_slice_in_dim(position, first, TOK)
    chosen = jnp.where(
        my_segment == 0,
        lengths[0, 0],
        jnp.where(my_segment == 1, lengths[0, 1], lengths[0, 2]),
    )
    valid = (my_position < chosen).astype(F32)
    cot_local = cotangent.astype(F32) * valid[:, None]
    frequency = jnp.exp(
        -math.log(10000.0) * jnp.arange(HEAD_V // 2, dtype=F32) * 2.0 / HEAD_V
    )
    angles = position.astype(F32)[:, None] * frequency[None, :]
    cosine, sine = jnp.cos(angles), jnp.sin(angles)
    cosine = jnp.concatenate([cosine, cosine], axis=1)
    sine = jnp.concatenate([-sine, sine], axis=1)

    lin_all = plane_gather(jnp.concatenate([padded(based_in.T, BIN_PAD), based_out], axis=0))
    win_all = plane_gather(jnp.concatenate([swa_in.T, swa_out], axis=0))
    ff_all = plane_gather(
        jnp.concatenate(
            [padded(part, UNIT_PAD) for part in (mlp_in[:, 0, :].T, mlp_in[:, 1, :].T, mlp_down)],
            axis=0,
        )
    )

    def pieces(rows, *counts):
        rows = rows.reshape(16, sum(counts), D)
        ends = np.cumsum((0,) + counts)
        return [
            rows[:, ends[i] : ends[i + 1]].reshape(16 * counts[i], D) for i in range(len(counts))
        ]

    lin_rows, lin_out = pieces(lin_all, BIN_PAD, 16)
    win_in, win_out = pieces(win_all, 48, 16)
    ff_gate, ff_up, ff_out = pieces(ff_all, UNIT_PAD, UNIT_PAD, UNIT_PAD)
    lin_heads = lin_rows.reshape(16, BIN_PAD, D)[:, :wide].reshape(2, 8 * wide, D)
    lin_in = jnp.concatenate(
        [
            lin_heads[:, 2 * FEAT :].reshape(2 * HEAD_V, D),
            lin_heads[:, : 2 * FEAT].reshape(4 * FEAT, D),
            jnp.zeros((128 - 4 * FEAT, D), BF),
        ],
        axis=0,
    )
    table_e, table_t, table_p = state_tables()
    tables = (jnp.asarray(table_e, BF), jnp.asarray(table_t, F32), jnp.asarray(table_p, BF))

    h1 = first_gather(block_input, gains[0])
    cot_all = lax.all_gather(cot_local.astype(BF), RING, axis=0, tiled=True)
    p1 = dnt(h1, lin_in).astype(BF)
    y1, state_v, state_n = linear_forward(p1, tables)
    x2, h2 = forward_step(y1, lin_out, block_input, gains[1], 2)
    p2 = dnt(h2, win_in)
    y2, queries, key_vals = window_forward(p2, cosine, sine)
    x3, h3 = forward_step(y2, win_out, x2, gains[2], 3)
    gate = dnt(h3, ff_gate)
    up = dnt(h3, ff_up)
    sig = jax.nn.sigmoid(gate)
    act = (gate * sig * up).astype(BF)
    out_sum = lax.psum_scatter(dnn(act, ff_out).astype(BF), RING, scatter_dimension=0, tiled=True)
    block_output = (x3 + out_sum.astype(F32)).astype(BF)

    d_act = dnt(cot_all, ff_out)
    d_gate = (d_act * up * sig * (1.0 + gate * (1.0 - sig))).astype(BF)
    d_up = (d_act * gate * sig).astype(BF)
    d_gu = jnp.concatenate([d_gate, d_up], axis=1)
    ff_in = jnp.concatenate([ff_gate, ff_up], axis=0)

    def reduce_together(*grads):
        rows = [grad.astype(BF).reshape(16, -1, D) for grad in grads]
        ends = np.cumsum([0] + [part.shape[1] for part in rows])
        total = plane_reduce(jnp.concatenate(rows, axis=1).reshape(-1, D))
        return [total[ends[i] : ends[i + 1]] for i in range(len(rows))]

    grad_down, grad_gate, grad_up = reduce_together(
        dtn(act, cot_all), dtn(d_gate, h3), dtn(d_up, h3)
    )
    dx3, grad_c, e3 = backward_step(d_gu, ff_in, x3, gains[2], cot_local, 4)
    d_y2 = dnt(e3, win_out).astype(BF)
    grad_win_out = dtn(y2, e3)
    d_p2 = window_backward(queries, key_vals, d_y2, cosine, sine)
    grad_win_in = dtn(d_p2, h2)
    dx2, grad_b, e2 = backward_step(d_p2, win_in, x2, gains[1], dx3, 5)
    d_y1 = dnt(e2, lin_out).astype(BF)
    grad_lin_out = dtn(y1, e2)
    d_p1 = linear_backward(p1, d_y1, state_v, state_n, tables)
    lin_grad = dtn(d_p1, h1).astype(BF)
    lin_grad = jnp.concatenate(
        [
            lin_grad[2 * HEAD_V : 2 * HEAD_V + 4 * FEAT].reshape(2, 2 * FEAT, D),
            lin_grad[: 2 * HEAD_V].reshape(2, HEAD_V, D),
        ],
        axis=1,
    ).reshape(16, wide, D)
    lin_grad = jnp.pad(lin_grad, ((0, 0), (0, BIN_PAD - wide), (0, 0))).reshape(16 * BIN_PAD, D)
    grad_win_in, grad_win_out, grad_lin_in, grad_lin_out = reduce_together(
        grad_win_in, grad_win_out, lin_grad, grad_lin_out
    )
    input_grad, grad_a = last_step(d_p1, lin_in, block_input, gains[0], dx2)
    gain_sums = lax.psum(jnp.concatenate([grad_a, grad_b, grad_c], axis=0), ALL)
    return (
        block_output,
        input_grad,
        gain_sums[0],
        grad_lin_in[:wide].T,
        grad_lin_out,
        gain_sums[1],
        grad_win_in.T,
        grad_win_out,
        gain_sums[2],
        jnp.stack([grad_gate[:units].T, grad_up[:units].T], axis=1),
        grad_down[:units],
    )


def solution(mesh):
    grid = Mesh(mesh.devices.reshape(2, 4, 2, 4, 2), ALL)
    tokens = P(ALL, None)
    weight = ("xh", "z", "c", "xl", "y")
    rows, cols = P(weight, None), P(None, weight)
    return jax.shard_map(
        body,
        mesh=grid,
        in_specs=(
            tokens,
            tokens,
            P(("xl", "y"), None),
            P(),
            cols,
            rows,
            P(),
            cols,
            rows,
            P(),
            P(None, None, weight),
            rows,
        ),
        out_specs=(
            tokens,
            tokens,
            P(),
            cols,
            rows,
            P(),
            cols,
            rows,
            P(),
            P(None, None, weight),
            rows,
        ),
        check_vma=False,
    )
```

```python
import functools
import math

import jax
import jax.numpy as jnp
import numpy as np
from jax import lax
from jax.experimental import pallas as pl
from jax.experimental.pallas import tpu as pltpu
from jax.sharding import Mesh
from jax.sharding import PartitionSpec as P

FEAT = 16
HEAD_V = 128
WINDOW = 64
EPSILON = 1e-05
D = 2048
TOK = 128
HALF_TOK = 1024
EDGE = 64
UNIT_PAD = 48
BIN_PAD = 32
STATE = 256
PLANE = ("xh", "xl", "y")
RING = ("z", "c")
ALL = ("xl", "y", "xh", "z", "c")
MESH = pl.DeviceIdType.MESH
BF = jnp.bfloat16
F32 = jnp.float32
VM = pl.BlockSpec(memory_space=pltpu.VMEM)
ANY = pl.BlockSpec(memory_space=pl.ANY)


def dnn(a, b):
    return lax.dot_general(a, b, (((1,), (0,)), ((), ())), preferred_element_type=F32)


def dnt(a, b):
    return lax.dot_general(a, b, (((1,), (1,)), ((), ())), preferred_element_type=F32)


def dtn(a, b):
    return lax.dot_general(a, b, (((0,), (0,)), ((), ())), preferred_element_type=F32)


def remote(src, dst, send_sem, recv_sem, device):
    copy = pltpu.make_async_remote_copy(
        src_ref=src,
        dst_ref=dst,
        send_sem=send_sem,
        recv_sem=recv_sem,
        device_id=device,
        device_id_type=MESH,
    )
    copy.start()
    return copy


def greet(devices):
    barrier = pltpu.get_barrier_semaphore()
    for device in devices:
        pl.semaphore_signal(barrier, inc=1, device_id=device, device_id_type=MESH)
    pl.semaphore_wait(barrier, len(devices))


class Ring:
    def __init__(self):
        self.z = lax.axis_index("z")
        self.c = lax.axis_index("c")
        self.oc = 1 - self.c
        self.zp = lax.rem(self.z + 1, 4)
        self.zm = lax.rem(self.z + 3, 4)
        self.zz = lax.rem(self.z + 2, 4)
        self.up = {"z": self.zp}
        self.dn = {"z": self.zm}
        self.sib = {"c": self.oc}

    def greet(self):
        greet((self.up, self.dn, self.sib))


class Plane:
    def __init__(self):
        self.x = lax.axis_index("xh") * 2 + lax.axis_index("xl")
        self.y = lax.axis_index("y")

    def at_x(self, x):
        return {"xh": lax.div(x, 2), "xl": lax.rem(x, 2)}

    def at_y(self, y):
        return {"y": y}

    def ring(self, along_x):
        me = self.x if along_x else self.y
        plus, minus, far = lax.rem(me + 1, 4), lax.rem(me + 3, 4), lax.rem(me + 2, 4)
        to = self.at_x if along_x else self.at_y
        return me, plus, minus, far, to(plus), to(minus)

    def neighbours(self):
        xs, ys = self.ring(True), self.ring(False)
        return (xs[4], xs[5], ys[4], ys[5])


def finish(steps):
    for _ in steps:
        pass


def advance(steps):
    next(steps, None)


def weave(main, *others):
    for _ in main:
        for other in others:
            advance(other)


def gather_steps(ring, buf, out_ref, ss, rs, ls, rows, base=0, ready=None):
    half = rows // 2
    me = ring.z * 2 + ring.c
    below, above, far = ring.zm * 2 + ring.c, ring.zp * 2 + ring.c, ring.zz * 2 + ring.c

    def send(slot, part, device, index):
        piece = buf.at[slot, pl.ds(part * half, half), :]
        return remote(piece, piece, ss.at[base + index], rs.at[base + index], device)

    local = []

    def keep(slot):
        copy = pltpu.make_async_copy(buf.at[slot], out_ref.at[slot], ls.at[len(local)])
        copy.start()
        local.append(copy)

    def done(chip):
        if ready is not None:
            ready(chip)

    up, dn, sib = ring.up, ring.dn, ring.sib
    cp = {}
    cp[0] = send(me, 0, up, 0)
    cp[1] = send(me, 1, dn, 1)
    cp[2] = send(me, 1, up, 2)
    cp[3] = send(me, 0, dn, 3)
    cp[4] = send(me, 0, sib, 4)
    cp[5] = send(me, 1, sib, 5)
    keep(me)
    yield
    cp[0].wait_recv()
    cp[6] = send(below, 0, up, 6)
    cp[8] = send(below, 0, sib, 8)
    yield
    cp[1].wait_recv()
    cp[7] = send(above, 1, dn, 7)
    cp[9] = send(above, 1, sib, 9)
    yield
    cp[2].wait_recv()
    cp[10] = send(below, 1, sib, 10)
    keep(below)
    cp[3].wait_recv()
    cp[11] = send(above, 0, sib, 11)
    keep(above)
    yield
    cp[4].wait_recv()
    cp[5].wait_recv()
    keep(ring.z * 2 + ring.oc)
    done(ring.z)
    yield
    cp[8].wait_recv()
    cp[10].wait_recv()
    keep(ring.zm * 2 + ring.oc)
    done(ring.zm)
    yield
    cp[6].wait_recv()
    cp[12] = send(far, 0, sib, 12)
    cp[7].wait_recv()
    cp[13] = send(far, 1, sib, 13)
    keep(far)
    yield
    cp[9].wait_recv()
    cp[11].wait_recv()
    keep(ring.zp * 2 + ring.oc)
    done(ring.zp)
    yield
    cp[12].wait_recv()
    cp[13].wait_recv()
    keep(ring.zz * 2 + ring.oc)
    done(ring.zz)
    for index in range(14):
        cp[index].wait_send()
    for copy in local:
        copy.wait()


def scatter_steps(ring, product, part, sib_in, far_in, end_in, ss, rs):
    half = TOK // 2
    c, oc = ring.c, ring.oc
    up, dn, sib = ring.up, ring.dn, ring.sib
    order = (ring.zz, ring.zp, ring.zm, ring.z)
    step = 512

    def multiply(index):
        row = pl.multiple_of(order[index] * (2 * TOK), 2 * TOK)

        def one(n, carry):
            col = pl.ds(pl.multiple_of(n * step, step), step)
            res = product(pl.ds(row, 2 * TOK), col).astype(BF)
            part[index, 0, :, col] = res[:TOK]
            part[index, 1, :, col] = res[TOK:]
            return carry

        lax.fori_loop(0, D // step, one, 0)
        return remote(part.at[index, oc], sib_in.at[index], ss.at[index], rs.at[index], sib)

    def add(index, rows_start, rows, other):
        def one(i, carry):
            at = pl.ds(pl.multiple_of(rows_start + i * 16, 16), 16)
            part[index, c, at, :] = (part[index, c, at, :].astype(F32) + other(i, at)).astype(BF)
            return carry

        lax.fori_loop(0, rows // 16, one, 0)

    def add_sib(index):
        add(index, 0, TOK, lambda i, at: sib_in[index, at, :].astype(F32))

    def add_far(index, which):
        add(
            index,
            which * half,
            half,
            lambda i, at: far_in[which, pl.ds(pl.multiple_of(i * 16, 16), 16), :].astype(F32),
        )

    def send(src, dst, device, index):
        return remote(src, dst, ss.at[index], rs.at[index], device)

    low, high = pl.ds(0, half), pl.ds(half, half)
    cp = {}
    cp[0] = multiply(0)
    cp[1] = multiply(1)
    cp[0].wait_recv()
    add_sib(0)
    cp[4] = send(part.at[0, c, low, :], far_in.at[0], up, 4)
    cp[5] = send(part.at[0, c, high, :], far_in.at[1], dn, 5)
    cp[2] = multiply(2)
    cp[1].wait_recv()
    add_sib(1)
    cp[6] = send(part.at[1, c, high, :], end_in.at[0, high, :], up, 6)
    cp[3] = multiply(3)
    cp[2].wait_recv()
    add_sib(2)
    cp[7] = send(part.at[2, c, low, :], end_in.at[1, low, :], dn, 7)
    yield
    cp[4].wait_recv()
    add_far(1, 0)
    cp[8] = send(part.at[1, c, low, :], end_in.at[0, low, :], up, 8)
    cp[5].wait_recv()
    add_far(2, 1)
    cp[9] = send(part.at[2, c, high, :], end_in.at[1, high, :], dn, 9)
    cp[3].wait_recv()
    add_sib(3)
    yield
    cp[6].wait_recv()
    cp[7].wait_recv()
    yield
    cp[8].wait_recv()
    cp[9].wait_recv()
    for index in range(10):
        cp[index].wait_send()


SCATTER_SCRATCH = [
    pltpu.VMEM((4, 2, TOK, D), BF),
    pltpu.VMEM((4, TOK, D), BF),
    pltpu.VMEM((2, TOK // 2, D), BF),
    pltpu.VMEM((2, TOK, D), BF),
    pltpu.SemaphoreType.DMA((10,)),
    pltpu.SemaphoreType.DMA((10,)),
]
GATHER_SCRATCH = [
    pltpu.VMEM((8, TOK, D), BF),
    pltpu.SemaphoreType.DMA((14,)),
    pltpu.SemaphoreType.DMA((14,)),
    pltpu.SemaphoreType.DMA((8,)),
]
HALF_SCRATCH = [pltpu.VMEM((8, TOK // 2, D), BF)] + GATHER_SCRATCH[1:]


def plane_view(plane, ref, half, stage, place, part):
    cols = pl.ds(half * (D // 2) + (part or 0) * (D // 4), D // 2 if part is None else D // 4)
    if stage == 0:
        return ref.at[place, plane.y, :, cols] if half == 0 else ref.at[plane.x, place, :, cols]
    return ref.at[:, place, :, cols] if half == 0 else ref.at[place, :, :, cols]


def plane_gather_steps(plane, buf, ss, rs):
    copies = []

    def send(view, device):
        copies.append(remote(view, view, ss.at[len(copies)], rs.at[len(copies)], device))
        return copies[-1]

    for stage in (0, 1):
        rings = [plane.ring(half == stage) for half in (0, 1)]
        near, far = [], []
        for half in (0, 1):
            me, plus, minus, _, to_plus, to_minus = rings[half]
            view = plane_view(plane, buf, half, stage, me, None)
            near.append((send(view, to_plus), send(view, to_minus)))
        yield
        for half in (0, 1):
            me, plus, minus, _, to_plus, to_minus = rings[half]
            near[half][0].wait_recv()
            far.append(send(plane_view(plane, buf, half, stage, minus, 0), to_plus))
            near[half][1].wait_recv()
            far.append(send(plane_view(plane, buf, half, stage, plus, 1), to_minus))
        yield
        for copy in far:
            copy.wait_recv()
    for copy in copies:
        copy.wait_send()


def plane_reduce_scratch(rows):
    return [
        pltpu.VMEM((4, 4, rows, D), BF),
        pltpu.VMEM((2, 2, 4, rows, D // 4), BF),
        pltpu.VMEM((2, 2, 4, rows, D // 2), BF),
        pltpu.VMEM((2, 2, rows, D // 4), BF),
        pltpu.VMEM((2, 2, rows, D // 2), BF),
        pltpu.SemaphoreType.DMA((24,)),
        pltpu.SemaphoreType.DMA((24,)),
    ]


def plane_reduce_steps(plane, grads, far_a, end_a, far_b, end_b, ss, rs, out_ref):
    copies = []
    rows = grads.shape[2]

    def send(src, dst, device):
        copies.append(remote(src, dst, ss.at[len(copies)], rs.at[len(copies)], device))
        return copies[-1]

    def add(view, other):
        def one(i, carry):
            at = pl.ds(pl.multiple_of(i * 16, 16), 16)
            piece = view.at[..., at, :]
            piece[...] = (piece[...].astype(F32) + other.at[..., at, :][...].astype(F32)).astype(BF)
            return carry

        lax.fori_loop(0, rows // 16, one, 0)

    for stage in (0, 1):
        rings = [plane.ring(half != stage) for half in (0, 1)]
        far_in, end_in = (far_a, end_a) if stage == 0 else (far_b, end_b)

        def view(half, place, part):
            return plane_view(plane, grads, half, 1 - stage, place, part)

        def ends(half, side, part):
            if part is None:
                return end_in.at[half, side]
            return end_in.at[half, side, ..., pl.ds(part * (D // 4), D // 4)]

        first, last = [], []
        for half in (0, 1):
            me, plus, minus, far, to_plus, to_minus = rings[half]
            first.append(
                (
                    send(view(half, far, 0), far_in.at[half, 0], to_plus),
                    send(view(half, far, 1), far_in.at[half, 1], to_minus),
                )
            )
            last.append(send(view(half, plus, 1), ends(half, 0, 1), to_plus))
            last.append(send(view(half, minus, 0), ends(half, 1, 0), to_minus))
        yield
        for half in (0, 1):
            me, plus, minus, far, to_plus, to_minus = rings[half]
            first[half][0].wait_recv()
            add(view(half, plus, 0), far_in.at[half, 0])
            last.append(send(view(half, plus, 0), ends(half, 0, 0), to_plus))
            first[half][1].wait_recv()
            add(view(half, minus, 1), far_in.at[half, 1])
            last.append(send(view(half, minus, 1), ends(half, 1, 1), to_minus))
        yield
        for copy in last:
            copy.wait_recv()
        for half in (0, 1):
            me = rings[half][0]
            if stage == 0:
                for side in (0, 1):
                    add(view(half, me, None), ends(half, side, None))
            else:
                cols = pl.ds(half * (D // 2), D // 2)
                out_ref[:, cols] = (
                    view(half, me, None)[...].astype(F32)
                    + end_in[half, 0].astype(F32)
                    + end_in[half, 1].astype(F32)
                )
        yield
    for copy in copies:
        copy.wait_send()


def load(src, dst, sem):
    copy = pltpu.make_async_copy(src, dst, sem)
    copy.start()
    return copy


def params(collective_id, limit=58):
    return pltpu.CompilerParams(
        collective_id=collective_id, has_side_effects=True, vmem_limit_bytes=limit << 20
    )


def sds(shape, dtype=BF):
    return jax.ShapeDtypeStruct(shape, dtype)


def scale_of(rows):
    return lax.rsqrt(jnp.mean(rows * rows, axis=-1, keepdims=True) + EPSILON)


def by_rows(one):
    def step(i, carry):
        one(pl.ds(pl.multiple_of(i * 16, 16), 16))
        return carry

    lax.fori_loop(0, TOK // 16, step, 0)


def total_rows(part, end_in, c, at):
    return (
        part[3, c, at, :].astype(F32)
        + end_in[0, at, :].astype(F32)
        + end_in[1, at, :].astype(F32)
    )


def chip_rows(chip):
    return pl.ds(pl.multiple_of(chip * (2 * TOK), 2 * TOK), 2 * TOK)


def first_kernel(
    x_ref, gain_ref, shard_ref, h_out, w_out, p_ref, wide, wss, wrs, buf, ss, rs, ls, wls
):
    ring, plane = Ring(), Plane()
    me = ring.z * 2 + ring.c
    barrier = pltpu.get_barrier_semaphore()
    partners = (ring.up, ring.dn, ring.sib) + plane.neighbours()
    for device in partners:
        pl.semaphore_signal(barrier, inc=1, device_id=device, device_id_type=MESH)
    wide[plane.x, plane.y] = shard_ref[...]

    def one(at):
        rows = x_ref[at, :].astype(F32)
        buf[me, at, :] = (rows * scale_of(rows) * gain_ref[...]).astype(BF)

    by_rows(one)
    pl.semaphore_wait(barrier, len(partners))
    weights = plane_gather_steps(plane, wide, wss, wrs)
    advance(weights)
    rows = gather_steps(ring, buf, h_out, ss, rs, ls, TOK)
    weave(rows, weights)
    finish(weights)
    keep = load(wide, w_out, wls)

    def project(i, carry):
        at = pl.ds(pl.multiple_of(i * 256, 256), 256)
        h = buf[pl.ds(2 * i, 2)].reshape(256, D)
        w = wide[:, :, :BIN_PAD, :].reshape(16 * BIN_PAD, D)
        p_ref[at, :] = dnt(h, w).astype(BF)
        return carry

    lax.fori_loop(0, 4, project, 0)
    keep.wait()


def first_step(x, gain, shard):
    return pl.pallas_call(
        first_kernel,
        out_shape=(
            sds((8, TOK, D)),
            sds((4, 4, BIN_PAD + 16, D)),
            sds((HALF_TOK, 16 * BIN_PAD)),
        ),
        in_specs=[VM] * 3,
        out_specs=(ANY, ANY, VM),
        scratch_shapes=[
            pltpu.VMEM((4, 4, BIN_PAD + 16, D), BF),
            pltpu.SemaphoreType.DMA((16,)),
            pltpu.SemaphoreType.DMA((16,)),
        ]
        + GATHER_SCRATCH
        + [pltpu.SemaphoreType.DMA],
        compiler_params=params(1),
    )(x, gain, shard)


def forward_kernel(
    off,
    a_ref,
    w_ref,
    x_ref,
    gain_ref,
    x_out,
    h_out,
    w,
    wls,
    part,
    sib_in,
    far_in,
    end_in,
    sss,
    srs,
    buf,
    ss,
    rs,
    ls,
):
    ring = Ring()
    me = ring.z * 2 + ring.c
    loading = load(w_ref.at[:, :, pl.ds(off, 16), :], w, wls)
    ring.greet()
    loading.wait()

    def product(rows, col):
        return dnn(a_ref[rows, :], w[:, :, :, col].reshape(256, -1))

    finish(scatter_steps(ring, product, part, sib_in, far_in, end_in, sss, srs))

    def one(at):
        rows = x_ref[at, :].astype(F32) + total_rows(part, end_in, ring.c, at)
        x_out[at, :] = rows
        buf[me, at, :] = (rows * scale_of(rows) * gain_ref[...]).astype(BF)

    by_rows(one)
    finish(gather_steps(ring, buf, h_out, ss, rs, ls, TOK))


def forward_step(a, w, off, x, gain, collective_id):
    return pl.pallas_call(
        functools.partial(forward_kernel, off),
        out_shape=(sds((TOK, D), F32), sds((8, TOK, D))),
        in_specs=[VM, ANY, VM, VM],
        out_specs=(VM, ANY),
        scratch_shapes=[pltpu.VMEM((4, 4, 16, D), BF), pltpu.SemaphoreType.DMA]
        + SCATTER_SCRATCH
        + GATHER_SCRATCH,
        compiler_params=params(collective_id),
    )(a, w, x, gain)


def norm_back_rows(v_ref, gain_ref, grads, at, gain_acc):
    rows = v_ref[at, :].astype(F32)
    scale = scale_of(rows)
    unit = rows * scale
    gain_acc[...] += grads * unit
    scaled = grads * gain_ref[...]
    return scale * (scaled - unit * jnp.mean(scaled * unit, axis=-1, keepdims=True))


CHUNK = 8 * UNIT_PAD


def mlp_kernel(
    h_ref, lo_ref, hi_ref, w_ref, act_ref, d_ref, down_ref, h, cot, gate_w, up_w, down_w, sems
):
    copies = {}
    copies["h"] = load(h_ref, h, sems.at[0])
    names = (("gate", gate_w), ("up", up_w), ("down", down_w))
    for n, (name, ref) in enumerate(names):
        for i in range(2):
            copies[name, i] = load(
                w_ref.at[pl.ds(8 * i, 8), pl.ds(n * UNIT_PAD, UNIT_PAD), :],
                ref.at[pl.ds(8 * i, 8)],
                sems.at[3 + 2 * n + i],
            )
        if n == 0:
            copies["lo"] = load(lo_ref, cot.at[:, pl.ds(0, TOK // 2), :], sems.at[1])
            copies["hi"] = load(hi_ref, cot.at[:, pl.ds(TOK // 2, TOK // 2), :], sems.at[2])
    copies["h"].wait()
    copies["lo"].wait()
    copies["hi"].wait()
    for i in range(2):
        for name, _ in names:
            copies[name, i].wait()
        units = slice(8 * i, 8 * i + 8)

        def one(n, carry):
            at = chip_rows(n)
            tokens = pl.ds(2 * n, 2)
            rows = h[tokens].reshape(2 * TOK, D)
            gate = dnt(rows, gate_w[units].reshape(CHUNK, D))
            up = dnt(rows, up_w[units].reshape(CHUNK, D))
            d_act = dnt(cot[tokens].reshape(2 * TOK, D), down_w[units].reshape(CHUNK, D))
            sig = 1.0 / (1.0 + jnp.exp(-gate))
            silu = gate * sig
            act_ref[at, i * CHUNK : (i + 1) * CHUNK] = (silu * up).astype(BF)
            d_ref[at, i * CHUNK : (i + 1) * CHUNK] = (
                d_act * up * (sig * (1.0 + gate * (1.0 - sig)))
            ).astype(BF)
            d_ref[at, (2 + i) * CHUNK : (3 + i) * CHUNK] = (d_act * silu).astype(BF)
            return carry

        lax.fori_loop(0, 4, one, 0)

    def last(n, carry):
        at = chip_rows(n)
        for col in range(0, D, 512):
            down_ref[at, col : col + 512] = dnn(
                act_ref[at, :], down_w[:, :, col : col + 512].reshape(2 * CHUNK, 512)
            ).astype(BF)
        return carry

    lax.fori_loop(0, 4, last, 0)


def mlp_step(h, lo, hi, w):
    return pl.pallas_call(
        mlp_kernel,
        out_shape=(
            sds((HALF_TOK, 2 * CHUNK)),
            sds((HALF_TOK, 4 * CHUNK)),
            sds((HALF_TOK, D)),
        ),
        in_specs=[ANY] * 4,
        out_specs=(VM, VM, VM),
        scratch_shapes=[
            pltpu.VMEM((8, TOK, D), BF),
            pltpu.VMEM((8, TOK, D), BF),
        ]
        + [pltpu.VMEM((16, UNIT_PAD, D), BF)] * 3
        + [pltpu.SemaphoreType.DMA((9,))],
        compiler_params=pltpu.CompilerParams(vmem_limit_bytes=58 << 20),
    )(h, lo, hi, w)


def mlp_grad_steps(jobs, stage, out_ref, sems):
    copies = []
    for n, (lhs, col, rhs, off, half) in enumerate(jobs):
        slot = n % 2
        if n >= 2:
            copies[n - 2].wait()

        def one(k, carry):
            cols = pl.ds(pl.multiple_of(k * 512, 512), 512)
            res = dtn(lhs[:, col : col + CHUNK], rhs[:, :, cols].reshape(HALF_TOK, 512))
            stage[slot, :, :, cols] = res.astype(BF).reshape(8, UNIT_PAD, 512)
            return carry

        lax.fori_loop(0, 4, one, 0)
        copies.append(
            load(
                stage.at[slot],
                out_ref.at[pl.ds(8 * half, 8), pl.ds(off, UNIT_PAD), :],
                sems.at[n],
            )
        )
        yield
    copies[-2].wait()
    copies[-1].wait()


def mlp_back_kernel(
    d_ref,
    act_ref,
    w_ref,
    wo_ref,
    h_ref,
    lo_ref,
    hi_ref,
    v_ref,
    gain_ref,
    res_ref,
    d_out,
    gain_out,
    e_out,
    dy_out,
    g_out,
    w,
    wo,
    h,
    cot,
    stage,
    sems,
    gsems,
    gain_acc,
    part,
    sib_in,
    far_in,
    end_in,
    sss,
    srs,
    buf,
    ss,
    rs,
    ls,
):
    ring = Ring()
    me = ring.z * 2 + ring.c
    loads = [
        load(w_ref.at[:, pl.ds(0, UNIT_PAD), :], w.at[0], sems.at[0]),
        load(w_ref.at[:, pl.ds(UNIT_PAD, UNIT_PAD), :], w.at[1], sems.at[1]),
    ]
    late = [
        load(h_ref, h, sems.at[2]),
        load(lo_ref, cot.at[:, pl.ds(0, TOK // 2), :], sems.at[3]),
        load(hi_ref, cot.at[:, pl.ds(TOK // 2, TOK // 2), :], sems.at[4]),
        load(wo_ref.at[:, :, pl.ds(48, 16), :], wo, sems.at[5]),
    ]
    ring.greet()
    gain_acc[...] = jnp.zeros_like(gain_acc)
    for copy in loads:
        copy.wait()

    def product(rows, col):
        return dnn(d_ref[rows, :], w[:, :, :, col].reshape(4 * CHUNK, -1))

    def grads():
        for copy in late:
            copy.wait()
        jobs = [(d_ref, n * CHUNK, h, (n // 2) * UNIT_PAD, n % 2) for n in range(4)]
        jobs += [(act_ref, n * CHUNK, cot, 2 * UNIT_PAD, n) for n in range(2)]
        yield from mlp_grad_steps(jobs, stage, g_out, gsems)

    weight_grads = grads()
    weave(
        scatter_steps(ring, product, part, sib_in, far_in, end_in, sss, srs),
        weight_grads,
    )

    def one(at):
        grad = total_rows(part, end_in, ring.c, at)
        rows = res_ref[at, :] + norm_back_rows(v_ref, gain_ref, grad, at, gain_acc)
        d_out[at, :] = rows
        buf[me, at, :] = rows.astype(BF)

    by_rows(one)

    def ready(chip):
        dy_out[chip_rows(chip), :] = dnt(
            buf[pl.ds(2 * chip, 2)].reshape(2 * TOK, D), wo[...].reshape(256, D)
        ).astype(BF)

    weave(gather_steps(ring, buf, e_out, ss, rs, ls, TOK, ready=ready), weight_grads)
    finish(weight_grads)
    gain_out[...] = jnp.sum(gain_acc[...], axis=0, keepdims=True)


def mlp_back_step(d, act, w, wo, h, lo, hi, v, gain, res):
    return pl.pallas_call(
        mlp_back_kernel,
        out_shape=(
            sds((TOK, D), F32),
            sds((1, D), F32),
            sds((8, TOK, D)),
            sds((HALF_TOK, 256)),
            sds((16, 3 * UNIT_PAD, D)),
        ),
        in_specs=[VM, VM, ANY, ANY, ANY, ANY, ANY, VM, VM, VM],
        out_specs=(VM, VM, ANY, VM, ANY),
        scratch_shapes=[
            pltpu.VMEM((2, 16, UNIT_PAD, D), BF),
            pltpu.VMEM((4, 4, 16, D), BF),
            pltpu.VMEM((8, TOK, D), BF),
            pltpu.VMEM((8, TOK, D), BF),
            pltpu.VMEM((2, 8, UNIT_PAD, D), BF),
            pltpu.SemaphoreType.DMA((6,)),
            pltpu.SemaphoreType.DMA((6,)),
            pltpu.VMEM((16, D), F32),
        ]
        + SCATTER_SCRATCH
        + GATHER_SCRATCH,
        compiler_params=params(4),
    )(d, act, w, wo, h, lo, hi, v, gain, res)


def window_back_out_kernel(
    d_ref,
    w_ref,
    wo_ref,
    h_ref,
    y_ref,
    e_ref,
    v_ref,
    gain_ref,
    res_ref,
    d_out,
    gain_out,
    e_out,
    dy_out,
    g_out,
    w,
    wo,
    h,
    e,
    sems,
    gain_acc,
    grads,
    far_a,
    end_a,
    far_b,
    end_b,
    gss,
    grs,
    part,
    sib_in,
    far_in,
    end_in,
    sss,
    srs,
    buf,
    ss,
    rs,
    ls,
):
    ring, plane = Ring(), Plane()
    me = ring.z * 2 + ring.c
    first = load(w_ref.at[:, :, pl.ds(0, 48), :], w, sems.at[0])
    late = [
        load(h_ref, h, sems.at[1]),
        load(e_ref, e, sems.at[2]),
        load(wo_ref.at[:, :, pl.ds(BIN_PAD, 16), :], wo, sems.at[3]),
    ]
    greet((ring.up, ring.dn, ring.sib) + plane.neighbours())
    gain_acc[...] = jnp.zeros_like(gain_acc)
    first.wait()

    def product(rows, col):
        return dnn(d_ref[rows, :], w[:, :, :, col].reshape(768, -1))

    def weights():
        for copy in late:
            copy.wait()

        def one(k, carry):
            cols = pl.ds(pl.multiple_of(k * 512, 512), 512)
            rows = h[:, :, cols].reshape(HALF_TOK, 512)
            for i in range(2):
                res = dtn(d_ref[:, i * 384 : (i + 1) * 384], rows).astype(BF)
                grads[2 * i : 2 * i + 2, :, :48, cols] = res.reshape(2, 4, 48, 512)
            res = dtn(y_ref[...], e[:, :, cols].reshape(HALF_TOK, 512)).astype(BF)
            grads[:, :, 48:, cols] = res.reshape(4, 4, 16, 512)
            return carry

        lax.fori_loop(0, 4, one, 0)
        yield from plane_reduce_steps(
            plane, grads, far_a, end_a, far_b, end_b, gss, grs, g_out
        )

    weight_grads = weights()
    weave(
        scatter_steps(ring, product, part, sib_in, far_in, end_in, sss, srs),
        weight_grads,
    )

    def one(at):
        grad = total_rows(part, end_in, ring.c, at)
        rows = res_ref[at, :] + norm_back_rows(v_ref, gain_ref, grad, at, gain_acc)
        d_out[at, :] = rows
        buf[me, at, :] = rows.astype(BF)

    by_rows(one)

    def ready(chip):
        dy_out[chip_rows(chip), :] = dnt(
            buf[pl.ds(2 * chip, 2)].reshape(2 * TOK, D), wo[...].reshape(256, D)
        ).astype(BF)

    weave(gather_steps(ring, buf, e_out, ss, rs, ls, TOK, ready=ready), weight_grads)
    finish(weight_grads)
    gain_out[...] = jnp.sum(gain_acc[...], axis=0, keepdims=True)


def window_back_out_step(d, w, wo, h, y, e, v, gain, res):
    return pl.pallas_call(
        window_back_out_kernel,
        out_shape=(
            sds((TOK, D), F32),
            sds((1, D), F32),
            sds((8, TOK, D)),
            sds((HALF_TOK, 256)),
            sds((64, D), F32),
        ),
        in_specs=[VM, ANY, ANY, ANY, VM, ANY, VM, VM, VM],
        out_specs=(VM, VM, ANY, VM, VM),
        scratch_shapes=[
            pltpu.VMEM((4, 4, 48, D), BF),
            pltpu.VMEM((4, 4, 16, D), BF),
            pltpu.VMEM((8, TOK, D), BF),
            pltpu.VMEM((8, TOK, D), BF),
            pltpu.SemaphoreType.DMA((4,)),
            pltpu.VMEM((16, D), F32),
        ]
        + plane_reduce_scratch(64)
        + SCATTER_SCRATCH
        + GATHER_SCRATCH,
        compiler_params=params(5),
    )(d, w, wo, h, y, e, v, gain, res)


def sum_everywhere(ring, plane, pack, ring_in, x_in, y_in, ss, rs):
    copies = []
    me = ring.z * 2 + ring.c

    def exchange(value, dst, own, count, device_of):
        pack[...] = value
        dst[own] = value
        sent = []
        for o in range(1, count):
            n = len(copies)
            sent.append(
                remote(
                    pack,
                    dst.at[own],
                    ss.at[n],
                    rs.at[n],
                    device_of(lax.rem(own + o, count)),
                )
            )
            copies.append(sent[-1])
        for copy in sent:
            copy.wait_recv()
        for copy in sent:
            copy.wait_send()
        total = dst[0]
        for k in range(1, count):
            total = total + dst[k]
        return total

    total = exchange(
        pack[...], ring_in, me, 8, lambda t: {"z": lax.div(t, 2), "c": lax.rem(t, 2)}
    )
    total = exchange(total, x_in, plane.x, 4, plane.at_x)
    return exchange(total, y_in, plane.y, 4, plane.at_y)


def last_kernel(
    d_ref,
    w_ref,
    h_ref,
    y_ref,
    e_ref,
    v_ref,
    gain_ref,
    res_ref,
    gb_ref,
    gc_ref,
    d_out,
    ga_out,
    gb_out,
    gc_out,
    g_out,
    w,
    h,
    e,
    sems,
    gain_acc,
    pack,
    ring_in,
    x_in,
    y_in,
    pss,
    prs,
    grads,
    far_a,
    end_a,
    far_b,
    end_b,
    gss,
    grs,
    part,
    sib_in,
    far_in,
    end_in,
    sss,
    srs,
):
    ring, plane = Ring(), Plane()
    first = load(w_ref.at[:, :, pl.ds(0, BIN_PAD), :], w, sems.at[0])
    late = [load(h_ref, h, sems.at[1]), load(e_ref, e, sems.at[2])]
    me = ring.z * 2 + ring.c
    partners = []
    for o in range(1, 8):
        to = lax.rem(me + o, 8)
        partners.append({"z": lax.div(to, 2), "c": lax.rem(to, 2)})
    for o in range(1, 4):
        partners.append(plane.at_x(lax.rem(plane.x + o, 4)))
        partners.append(plane.at_y(lax.rem(plane.y + o, 4)))
    greet(partners)
    gain_acc[...] = jnp.zeros_like(gain_acc)
    first.wait()

    def product(rows, col):
        return dnn(d_ref[rows, :], w[:, :, :, col].reshape(16 * BIN_PAD, -1))

    def weights():
        for copy in late:
            copy.wait()

        def one(k, carry):
            cols = pl.ds(pl.multiple_of(k * 512, 512), 512)
            res = dtn(d_ref[...], h[:, :, cols].reshape(HALF_TOK, 512)).astype(BF)
            grads[:, :, :BIN_PAD, cols] = res.reshape(4, 4, BIN_PAD, 512)
            res = dtn(y_ref[...], e[:, :, cols].reshape(HALF_TOK, 512)).astype(BF)
            grads[:, :, BIN_PAD:, cols] = res.reshape(4, 4, 16, 512)
            return carry

        lax.fori_loop(0, 4, one, 0)
        yield from plane_reduce_steps(
            plane, grads, far_a, end_a, far_b, end_b, gss, grs, g_out
        )

    weight_grads = weights()
    weave(
        scatter_steps(ring, product, part, sib_in, far_in, end_in, sss, srs),
        weight_grads,
    )

    def one(at):
        grad = total_rows(part, end_in, ring.c, at)
        d_out[at, :] = res_ref[at, :] + norm_back_rows(v_ref, gain_ref, grad, at, gain_acc)

    by_rows(one)
    wide = D // 8
    gains = (jnp.sum(gain_acc[...], axis=0, keepdims=True), gb_ref[...], gc_ref[...])
    for n, gain in enumerate(gains):
        for r in range(8):
            pack[r : r + 1, n * wide : (n + 1) * wide] = gain[:, r * wide : (r + 1) * wide]
    total = sum_everywhere(ring, plane, pack, ring_in, x_in, y_in, pss, prs)
    pack[...] = total
    for n, out in enumerate((ga_out, gb_out, gc_out)):
        for r in range(8):
            out[:, r * wide : (r + 1) * wide] = pack[r : r + 1, n * wide : (n + 1) * wide]
    finish(weight_grads)


def last_step(d, w, h, y, e, v, gain, res, grad_b, grad_c):
    small = (8, 3 * D // 8)
    return pl.pallas_call(
        last_kernel,
        out_shape=(
            sds((TOK, D), F32),
            sds((1, D), F32),
            sds((1, D), F32),
            sds((1, D), F32),
            sds((BIN_PAD + 16, D), F32),
        ),
        in_specs=[VM, ANY, ANY, VM, ANY, VM, VM, VM, VM, VM],
        out_specs=(VM,) * 5,
        scratch_shapes=[
            pltpu.VMEM((4, 4, BIN_PAD, D), BF),
            pltpu.VMEM((8, TOK, D), BF),
            pltpu.VMEM((8, TOK, D), BF),
            pltpu.SemaphoreType.DMA((3,)),
            pltpu.VMEM((16, D), F32),
            pltpu.VMEM(small, F32),
            pltpu.VMEM((8,) + small, F32),
            pltpu.VMEM((4,) + small, F32),
            pltpu.VMEM((4,) + small, F32),
            pltpu.SemaphoreType.DMA((13,)),
            pltpu.SemaphoreType.DMA((13,)),
        ]
        + plane_reduce_scratch(BIN_PAD + 16)
        + SCATTER_SCRATCH,
        compiler_params=params(6),
    )(d, w, h, y, e, v, gain, res, grad_b, grad_c)


def state_tables():
    first = np.zeros((128, STATE), np.float32)
    second = np.zeros((128, STATE), np.float32)
    bias = np.zeros((8, STATE), np.float32)
    coef = np.zeros((8, STATE), np.float32)
    bias[0, 0] = bias[1, 0] = 1.0
    coef[0, 0] = 1.0
    at = 1
    for i in range(FEAT):
        first[i, at] = 1.0
        bias[1, at] = 1.0
        coef[0, at] = 1.0 / math.sqrt(FEAT)
        at += 1
    for i in range(FEAT):
        for j in range(i, FEAT):
            first[i, at] = 1.0
            second[j, at] = 1.0
            coef[0, at] = (0.5 if i == j else 1.0) / FEAT
            at += 1
    picks = np.zeros((4, 128, 128), np.float32)
    for which in range(4):
        for i in range(FEAT):
            picks[which, which * FEAT + i, i] = 1.0
    return (
        np.stack([first, second]),
        np.concatenate([bias[:2], coef[:1], np.zeros((5, STATE), np.float32)]),
        picks,
    )


def causal_mask(row_start, col_start, rows, cols, edge):
    t = row_start + lax.broadcasted_iota(jnp.int32, (rows, cols), 0)
    u = col_start + lax.broadcasted_iota(jnp.int32, (rows, cols), 1)
    return (u <= t) & ((t >= edge) == (u >= edge))


BLK = 256
NBLK = HALF_TOK // BLK
INV_ROOT = 1.0 / math.sqrt(FEAT)


def select_table(width):
    table = np.zeros((16 * BIN_PAD, 3 * HEAD_V), np.float32)
    for shard in range(16):
        for i in range(width):
            head, col = shard // 8, (shard % 8) * width + i
            to = 2 * HEAD_V + 2 * FEAT * head + col if col < 2 * FEAT else head * HEAD_V + col - 2 * FEAT
            table[shard * BIN_PAD + i, to] = 1.0
    return table


def linear_forward_kernel(
    raw_ref,
    sel_ref,
    e_ref,
    t_ref,
    pick_ref,
    cot_ref,
    y_ref,
    p_ref,
    sv_ref,
    sn_ref,
    lo_ref,
    qs,
    ks,
    num,
    den,
    sv_s,
    sn_s,
    sv_r,
    sn_r,
    xss,
    xrs,
    buf,
    ss,
    rs,
    ls,
):
    ring = Ring()
    xh = lax.axis_index("xh")
    partner = {"xh": 1 - xh}
    edge = jnp.where(xh == 0, EDGE, HALF_TOK - EDGE)
    bias1, bias2, coef = t_ref[0:1, :], t_ref[1:2, :], t_ref[2:3, :]
    barrier = pltpu.get_barrier_semaphore()
    for device in (ring.up, ring.dn, ring.sib, partner):
        pl.semaphore_signal(barrier, inc=1, device_id=device, device_id_type=MESH)
    buf[ring.z * 2 + ring.c] = cot_ref[: TOK // 2, :]

    def rows_of(r):
        return slice(r * BLK, (r + 1) * BLK)

    for r in range(NBLK):
        p_ref[rows_of(r), :] = dnn(raw_ref[rows_of(r), :], sel_ref[...]).astype(BF)
    pl.semaphore_wait(barrier, 4)
    cots = gather_steps(ring, buf, lo_ref, ss, rs, ls, TOK // 2)
    advance(cots)
    small = p_ref[:, 2 * HEAD_V :]
    for j in range(2):
        qs[j] = dnn(small, pick_ref[2 * j]).astype(BF)
        ks[j] = dnn(small, pick_ref[2 * j + 1]).astype(BF)

    def phi_of(vecs):
        return (dnn(vecs, e_ref[0]) + bias1) * (dnn(vecs, e_ref[1]) + bias2)

    for j in range(2):
        sv = jnp.zeros((HEAD_V, STATE), F32)
        sn = jnp.zeros((1, STATE), F32)
        for r in range(NBLK):
            phi = phi_of(ks[j, rows_of(r), :])
            if r == 0:
                slot = lax.broadcasted_iota(jnp.int32, (BLK, STATE), 0)
                phi = jnp.where(slot >= EDGE, phi, 0.0)
            sv = sv + dtn(p_ref[rows_of(r), j * HEAD_V : (j + 1) * HEAD_V], phi.astype(BF))
            sn = sn + jnp.sum(phi, axis=0, keepdims=True)
        sv_s[j] = (sv * coef).astype(BF)
        sn_s[j] = jnp.broadcast_to(sn * coef, (8, STATE))
    copies = (
        remote(sv_s, sv_r, xss.at[0], xrs.at[0], partner),
        remote(sn_s, sn_r, xss.at[1], xrs.at[1], partner),
    )
    for j in range(2):
        for r in range(NBLK):
            advance(cots)
            queries = qs[j, rows_of(r), :]
            rows_num = jnp.zeros((BLK, HEAD_V), F32)
            rows_den = jnp.zeros((BLK, 1), F32)
            for s in range(r + 1):
                scores = dnt(queries, ks[j, rows_of(s), :]) * INV_ROOT
                mask = causal_mask(r * BLK, s * BLK, BLK, BLK, edge)
                kernel = jnp.where(mask, 1.0 + scores + 0.5 * scores * scores, 0.0)
                rows_den = rows_den + jnp.sum(kernel, axis=-1, keepdims=True)
                rows_num = rows_num + dnn(
                    kernel.astype(BF), p_ref[rows_of(s), j * HEAD_V : (j + 1) * HEAD_V]
                )
            num[j, rows_of(r), :] = rows_num
            den[j, rows_of(r), :] = jnp.broadcast_to(rows_den, (BLK, HEAD_V))
    for copy in copies:
        copy.wait_recv()
    sv_ref[...] = sv_r[...]
    sn_ref[...] = sn_r[...]
    for j in range(2):
        for r in range(NBLK):
            phi = phi_of(qs[j, rows_of(r), :])
            cross_den = jnp.sum(phi * sn_r[j, 0:1, :], axis=-1, keepdims=True)
            cross_num = dnt(phi.astype(BF), sv_r[j])
            slot = r * BLK + lax.broadcasted_iota(jnp.int32, (BLK, HEAD_V), 0)
            seen = (slot < HALF_TOK - EDGE) & (xh == 1)
            top = num[j, rows_of(r), :] + jnp.where(seen, cross_num, 0.0)
            bottom = den[j, rows_of(r), :] + jnp.where(seen, cross_den, 0.0)
            y_ref[rows_of(r), j * HEAD_V : (j + 1) * HEAD_V] = (top / bottom).astype(BF)
    for copy in copies:
        copy.wait_send()
    finish(cots)


def linear_forward(raw, select, tables, cot):
    return pl.pallas_call(
        linear_forward_kernel,
        out_shape=(
            sds((HALF_TOK, 2 * HEAD_V)),
            sds((HALF_TOK, 3 * HEAD_V)),
            sds((2, HEAD_V, STATE)),
            sds((2, 8, STATE), F32),
            sds((8, TOK // 2, D)),
        ),
        in_specs=[VM] * 6,
        out_specs=(VM, VM, VM, VM, ANY),
        scratch_shapes=[
            pltpu.VMEM((2, HALF_TOK, 128), BF),
            pltpu.VMEM((2, HALF_TOK, 128), BF),
            pltpu.VMEM((2, HALF_TOK, HEAD_V), F32),
            pltpu.VMEM((2, HALF_TOK, HEAD_V), F32),
            pltpu.VMEM((2, HEAD_V, STATE), BF),
            pltpu.VMEM((2, 8, STATE), F32),
            pltpu.VMEM((2, HEAD_V, STATE), BF),
            pltpu.VMEM((2, 8, STATE), F32),
            pltpu.SemaphoreType.DMA((2,)),
            pltpu.SemaphoreType.DMA((2,)),
        ]
        + HALF_SCRATCH,
        compiler_params=params(7),
    )(raw, select, *tables, cot)


def linear_backward_kernel(
    p_ref,
    dy_ref,
    sv_ref,
    sn_ref,
    sel_ref,
    e_ref,
    t_ref,
    pick_ref,
    raw_ref,
    dp_ref,
    qs,
    ks,
    dq,
    dk,
    dv,
    tv_s,
    tn_s,
    tv_r,
    tn_r,
    ss,
    rs,
):
    xh = lax.axis_index("xh")
    partner = {"xh": 1 - xh}
    edge = jnp.where(xh == 0, EDGE, HALF_TOK - EDGE)
    bias1, bias2, coef = t_ref[0:1, :], t_ref[1:2, :], t_ref[2:3, :]
    barrier = pltpu.get_barrier_semaphore()
    pl.semaphore_signal(barrier, inc=1, device_id=partner, device_id_type=MESH)
    small = p_ref[:, 2 * HEAD_V :]
    for j in range(2):
        qs[j] = dnn(small, pick_ref[2 * j]).astype(BF)
        ks[j] = dnn(small, pick_ref[2 * j + 1]).astype(BF)
    dk[...] = jnp.zeros_like(dk)
    dv[...] = jnp.zeros_like(dv)

    def rows_of(r):
        return slice(r * BLK, (r + 1) * BLK)

    def factors_of(vecs):
        return (dnn(vecs, e_ref[0]) + bias1, dnn(vecs, e_ref[1]) + bias2)

    def factors_back(phi_grad, one, two):
        return dnt((phi_grad * two).astype(BF), e_ref[0]) + dnt(
            (phi_grad * one).astype(BF), e_ref[1]
        )

    for j in range(2):
        head = slice(j * HEAD_V, (j + 1) * HEAD_V)
        tv = jnp.zeros((HEAD_V, STATE), F32)
        tn = jnp.zeros((1, STATE), F32)
        for r in range(NBLK):
            queries = qs[j, rows_of(r), :]
            grads = dy_ref[rows_of(r), head]
            one, two = factors_of(queries)
            phi = one * two
            slot = r * BLK + lax.broadcasted_iota(jnp.int32, (BLK, 1), 0)
            seen = (slot < HALF_TOK - EDGE) & (xh == 1)
            cross_den = jnp.sum(phi * sn_ref[j, 0:1, :], axis=-1, keepdims=True)
            cross_num = dnt(phi.astype(BF), sv_ref[j])
            total = jnp.where(seen, cross_den, 0.0)
            dot = jnp.where(
                seen, jnp.sum(cross_num * grads.astype(F32), axis=-1, keepdims=True), 0.0
            )
            kept = []
            for s in range(r + 1):
                scores = dnt(queries, ks[j, rows_of(s), :]) * INV_ROOT
                mask = causal_mask(r * BLK, s * BLK, BLK, BLK, edge)
                kernel = jnp.where(mask, 1.0 + scores + 0.5 * scores * scores, 0.0)
                weight_grad = dnt(grads, p_ref[rows_of(s), head])
                total = total + jnp.sum(kernel, axis=-1, keepdims=True)
                dot = dot + jnp.sum(kernel * weight_grad, axis=-1, keepdims=True)
                kept.append((scores, mask, kernel, weight_grad))
            inverse = 1.0 / total
            mean = dot * inverse
            grads_n = (grads.astype(F32) * inverse).astype(BF)
            query_grad = jnp.zeros((BLK, 128), F32)
            for s in range(r + 1):
                scores, mask, kernel, weight_grad = kept[s]
                score_grad = jnp.where(
                    mask, (weight_grad - mean) * inverse * (1.0 + scores), 0.0
                ).astype(BF)
                query_grad = query_grad + dnn(score_grad, ks[j, rows_of(s), :])
                dk[j, rows_of(s), :] += dtn(score_grad, queries)
                dv[j, rows_of(s), :] += dtn(kernel.astype(BF), grads_n)
            shift = jnp.where(seen, -(mean * inverse), 0.0)
            cross_g = jnp.where(seen, grads_n, jnp.zeros_like(grads_n))
            phi_grad = dnn(cross_g, sv_ref[j]) + shift * sn_ref[j, 0:1, :]
            dq[j, rows_of(r), :] = query_grad * INV_ROOT + factors_back(phi_grad, one, two)
            tv = tv + dtn(cross_g, phi.astype(BF))
            tn = tn + jnp.sum(shift * phi, axis=0, keepdims=True)
        tv_s[j] = (tv * coef).astype(BF)
        tn_s[j] = jnp.broadcast_to(tn * coef, (8, STATE))
    pl.semaphore_wait(barrier, 1)
    copies = (
        remote(tv_s, tv_r, ss.at[0], rs.at[0], partner),
        remote(tn_s, tn_r, ss.at[1], rs.at[1], partner),
    )
    for copy in copies:
        copy.wait_recv()
    for r in range(NBLK):
        placed = jnp.zeros((BLK, 128), F32)
        for j in range(2):
            head = slice(j * HEAD_V, (j + 1) * HEAD_V)
            one, two = factors_of(ks[j, rows_of(r), :])
            phi = one * two
            if r == 0:
                slot = lax.broadcasted_iota(jnp.int32, (BLK, STATE), 0)
                open_rows = slot >= EDGE
                phi = jnp.where(open_rows, phi, 0.0)
            phi_grad = dnn(p_ref[rows_of(r), head], tv_r[j]) + tn_r[j, 0:1, :]
            if r == 0:
                phi_grad = jnp.where(open_rows, phi_grad, 0.0)
            key_grad = dk[j, rows_of(r), :] * INV_ROOT + factors_back(phi_grad, one, two)
            value_grad = dv[j, rows_of(r), :] + dnt(phi.astype(BF), tv_r[j])
            dp_ref[rows_of(r), head] = value_grad.astype(BF)
            placed = placed + dnt(dq[j, rows_of(r), :].astype(BF), pick_ref[2 * j])
            placed = placed + dnt(key_grad.astype(BF), pick_ref[2 * j + 1])
        dp_ref[rows_of(r), 2 * HEAD_V :] = placed.astype(BF)
        raw_ref[rows_of(r), :] = dnt(dp_ref[rows_of(r), :], sel_ref[...]).astype(BF)
    for copy in copies:
        copy.wait_send()


def linear_backward(p1, dy, sv, sn, select, tables):
    return pl.pallas_call(
        linear_backward_kernel,
        out_shape=sds((HALF_TOK, 16 * BIN_PAD)),
        in_specs=[VM] * 8,
        out_specs=VM,
        scratch_shapes=[
            pltpu.VMEM((HALF_TOK, 3 * HEAD_V), BF),
            pltpu.VMEM((2, HALF_TOK, 128), BF),
            pltpu.VMEM((2, HALF_TOK, 128), BF),
            pltpu.VMEM((2, HALF_TOK, 128), F32),
            pltpu.VMEM((2, HALF_TOK, 128), F32),
            pltpu.VMEM((2, HALF_TOK, HEAD_V), F32),
            pltpu.VMEM((2, HEAD_V, STATE), BF),
            pltpu.VMEM((2, 8, STATE), F32),
            pltpu.VMEM((2, HEAD_V, STATE), BF),
            pltpu.VMEM((2, 8, STATE), F32),
            pltpu.SemaphoreType.DMA((2,)),
            pltpu.SemaphoreType.DMA((2,)),
        ],
        compiler_params=params(8),
    )(p1, dy, sv, sn, select, *tables)


WBLK = 128
WKEYS = WBLK + WINDOW
INV_ROOT_V = 1.0 / math.sqrt(HEAD_V)


def window_mask(r, edge, lowest):
    t = r * WBLK + lax.broadcasted_iota(jnp.int32, (WBLK, WKEYS), 0)
    u = r * WBLK - WINDOW + lax.broadcasted_iota(jnp.int32, (WBLK, WKEYS), 1)
    return (u <= t) & (t - u < WINDOW) & ((t >= edge) == (u >= edge)) & (u >= lowest)


def window_forward_kernel(
    h_ref,
    w_ref,
    cos_ref,
    sin_ref,
    cot_ref,
    y_ref,
    q_ref,
    kv_ref,
    hi_ref,
    h,
    w,
    sems,
    xss,
    xrs,
    buf,
    ss,
    rs,
    ls,
):
    ring = Ring()
    xh = lax.axis_index("xh")
    partner = {"xh": 1 - xh}
    edge = jnp.where(xh == 0, EDGE, HALF_TOK - EDGE)
    lowest = jnp.where(xh == 0, 0, -WINDOW)
    loads = (
        load(w_ref.at[:, :, pl.ds(0, 48), :], w, sems.at[0]),
        load(h_ref, h, sems.at[1]),
    )
    barrier = pltpu.get_barrier_semaphore()
    for device in (ring.up, ring.dn, ring.sib, partner):
        pl.semaphore_signal(barrier, inc=1, device_id=device, device_id_type=MESH)
    buf[ring.z * 2 + ring.c] = cot_ref[TOK // 2 :, :]
    pl.semaphore_wait(barrier, 4)
    cots = gather_steps(ring, buf, hi_ref, ss, rs, ls, TOK // 2)
    advance(cots)
    for copy in loads:
        copy.wait()
    size = 2 * TOK
    blocks = HALF_TOK // size

    def turned(vecs, rows):
        return (
            vecs * cos_ref[rows, :] + pltpu.roll(vecs, HEAD_V // 2, 1) * sin_ref[rows, :]
        ).astype(BF)

    for r in (blocks - 1,) + tuple(range(blocks - 1)):
        rows = slice(r * size, (r + 1) * size)
        shifted = slice(WINDOW + r * size, WINDOW + (r + 1) * size)
        tokens = h[2 * r : 2 * r + 2].reshape(size, D)
        for j in range(2):
            mat = w[2 * j : 2 * j + 2].reshape(384, D)
            proj = dnt(tokens, mat)
            q_ref[rows, j * 128 : (j + 1) * 128] = turned(proj[:, :128], rows)
            kv_ref[shifted, j * 128 : (j + 1) * 128] = turned(proj[:, 128:256], rows)
            kv_ref[shifted, (2 + j) * 128 : (3 + j) * 128] = proj[:, 256:].astype(BF)
        if r == blocks - 1:
            copy = remote(
                kv_ref.at[pl.ds(HALF_TOK, WINDOW), :],
                kv_ref.at[pl.ds(0, WINDOW), :],
                xss,
                xrs,
                partner,
            )
        advance(cots)
    for r in tuple(range(1, HALF_TOK // WBLK)) + (0,):
        if r == 0:
            copy.wait_recv()
        rows = slice(r * WBLK, (r + 1) * WBLK)
        keys = slice(r * WBLK, r * WBLK + WKEYS)
        mask = window_mask(r, edge, lowest)
        for j in range(2):
            head = slice(j * 128, (j + 1) * 128)
            scores = dnt(q_ref[rows, head], kv_ref[keys, head]) * INV_ROOT_V
            scores = jnp.where(mask, scores, -1e30)
            exps = jnp.exp(scores - jnp.max(scores, axis=-1, keepdims=True))
            probs = exps / jnp.sum(exps, axis=-1, keepdims=True)
            y_ref[rows, head] = dnn(
                probs.astype(BF), kv_ref[keys, (2 + j) * 128 : (3 + j) * 128]
            ).astype(BF)
        advance(cots)
    copy.wait_send()
    finish(cots)


def window_forward(h, w, cosine, sine, cot):
    return pl.pallas_call(
        window_forward_kernel,
        out_shape=(
            sds((HALF_TOK, 256)),
            sds((HALF_TOK, 256)),
            sds((HALF_TOK + WINDOW, 512)),
            sds((8, TOK // 2, D)),
        ),
        in_specs=[ANY, ANY, VM, VM, VM],
        out_specs=(VM, VM, VM, ANY),
        scratch_shapes=[
            pltpu.VMEM((8, TOK, D), BF),
            pltpu.VMEM((4, 4, 48, D), BF),
            pltpu.SemaphoreType.DMA((2,)),
            pltpu.SemaphoreType.DMA,
            pltpu.SemaphoreType.DMA,
        ]
        + HALF_SCRATCH,
        compiler_params=params(9),
    )(h, w, cosine, sine, cot)


def window_backward_kernel(
    q_ref, kv_ref, dy_ref, cos_ref, sin_ref, dp_ref, dkv, halo, ss, rs
):
    xh = lax.axis_index("xh")
    partner = {"xh": 1 - xh}
    edge = jnp.where(xh == 0, EDGE, HALF_TOK - EDGE)
    lowest = jnp.where(xh == 0, 0, -WINDOW)
    barrier = pltpu.get_barrier_semaphore()
    pl.semaphore_signal(barrier, inc=1, device_id=partner, device_id_type=MESH)
    dkv[...] = jnp.zeros_like(dkv)
    blocks = HALF_TOK // WBLK

    def turned_back(r, grads):
        rows = slice(r * WBLK, (r + 1) * WBLK)
        return (
            grads * cos_ref[rows, :] + pltpu.roll(grads * sin_ref[rows, :], HEAD_V // 2, 1)
        ).astype(BF)

    for r in range(blocks):
        rows = slice(r * WBLK, (r + 1) * WBLK)
        keys = slice(r * WBLK, r * WBLK + WKEYS)
        mask = window_mask(r, edge, lowest)
        for j in range(2):
            head = slice(j * 128, (j + 1) * 128)
            vals = slice((2 + j) * 128, (3 + j) * 128)
            queries, grads = q_ref[rows, head], dy_ref[rows, head]
            scores = dnt(queries, kv_ref[keys, head]) * INV_ROOT_V
            scores = jnp.where(mask, scores, -1e30)
            exps = jnp.exp(scores - jnp.max(scores, axis=-1, keepdims=True))
            probs = exps / jnp.sum(exps, axis=-1, keepdims=True)
            prob_grad = dnt(grads, kv_ref[keys, vals])
            score_grad = (
                probs * (prob_grad - jnp.sum(prob_grad * probs, axis=-1, keepdims=True))
            ).astype(BF)
            dp_ref[rows, 3 * j * 128 : (3 * j + 1) * 128] = turned_back(
                r, dnn(score_grad, kv_ref[keys, head]) * INV_ROOT_V
            )
            dkv[keys, head] += dtn(score_grad, queries) * INV_ROOT_V
            dkv[keys, vals] += dtn(probs.astype(BF), grads)
        if r == 0:
            pl.semaphore_wait(barrier, 1)
            copy = remote(dkv.at[pl.ds(0, WINDOW), :], halo, ss, rs, partner)
    for r in range(blocks):
        rows = slice(r * WBLK, (r + 1) * WBLK)
        shifted = slice(WINDOW + r * WBLK, WINDOW + (r + 1) * WBLK)
        if r == blocks - 1:
            copy.wait_recv()
            dkv[HALF_TOK : HALF_TOK + WINDOW, :] += halo[...]
        for j in range(2):
            dp_ref[rows, (3 * j + 1) * 128 : (3 * j + 2) * 128] = turned_back(
                r, dkv[shifted, j * 128 : (j + 1) * 128]
            )
            dp_ref[rows, (3 * j + 2) * 128 : (3 * j + 3) * 128] = dkv[
                shifted, (2 + j) * 128 : (3 + j) * 128
            ].astype(BF)
    copy.wait_send()


def window_backward(q, kv, dy, cosine, sine):
    return pl.pallas_call(
        window_backward_kernel,
        out_shape=jax.ShapeDtypeStruct((HALF_TOK, 768), BF),
        in_specs=[VM] * 5,
        out_specs=VM,
        scratch_shapes=[
            pltpu.VMEM((HALF_TOK + WINDOW, 512), F32),
            pltpu.VMEM((WINDOW, 512), F32),
            pltpu.SemaphoreType.DMA,
            pltpu.SemaphoreType.DMA,
        ],
        compiler_params=params(10),
    )(q, kv, dy, cosine, sine)


def padded(rows, count):
    return jnp.pad(rows, ((0, count - rows.shape[0]), (0, 0)))


def place():
    slot = lax.axis_index("xh") * HALF_TOK + jnp.arange(HALF_TOK, dtype=jnp.int32)
    last = 2 * HALF_TOK - EDGE
    segment = (slot >= EDGE).astype(jnp.int32) + (slot >= last).astype(jnp.int32)
    start = jnp.where(segment == 0, 0, jnp.where(segment == 1, EDGE, last)).astype(jnp.int32)
    return segment, slot - start


def body(
    block_input,
    cotangent,
    lengths,
    gain_a,
    based_in,
    based_out,
    gain_b,
    swa_in,
    swa_out,
    gain_c,
    mlp_in,
    mlp_down,
):
    gains = [gain.reshape(1, D) for gain in (gain_a, gain_b, gain_c)]
    units = mlp_down.shape[0]
    wide = based_in.shape[1]
    win_all = lax.all_gather(
        jnp.concatenate([swa_in.T, swa_out], axis=0), PLANE, axis=0, tiled=True
    ).reshape(4, 4, 64, D)
    ff_all = lax.all_gather(
        jnp.concatenate(
            [padded(part, UNIT_PAD) for part in (mlp_in[:, 0, :].T, mlp_in[:, 1, :].T, mlp_down)],
            axis=0,
        ),
        PLANE,
        axis=0,
        tiled=True,
    ).reshape(16, 3 * UNIT_PAD, D)
    segment, position = place()
    first = (lax.axis_index("z") * 2 + lax.axis_index("c")) * TOK
    my_segment = lax.dynamic_slice_in_dim(segment, first, TOK)
    my_position = lax.dynamic_slice_in_dim(position, first, TOK)
    chosen = jnp.where(
        my_segment == 0,
        lengths[0, 0],
        jnp.where(my_segment == 1, lengths[0, 1], lengths[0, 2]),
    )
    valid = (my_position < chosen)[:, None]
    cot_low = jnp.where(valid, cotangent, jnp.zeros_like(cotangent))
    cot_local = cot_low.astype(F32)
    frequency = jnp.exp(
        -math.log(10000.0) * jnp.arange(HEAD_V // 2, dtype=F32) * 2.0 / HEAD_V
    )
    angles = position.astype(F32)[:, None] * frequency[None, :]
    cosine, sine = jnp.cos(angles), jnp.sin(angles)
    cosine = jnp.concatenate([cosine, cosine], axis=1)
    sine = jnp.concatenate([-sine, sine], axis=1)
    tables = tuple(
        jnp.asarray(table, kind) for table, kind in zip(state_tables(), (BF, F32, BF))
    )
    select = jnp.asarray(select_table(wide), BF)

    shard = jnp.concatenate([padded(based_in.T, BIN_PAD), based_out], axis=0)
    h1, lin_all, raw = first_step(block_input, gains[0], shard)
    y1, p1, state_v, state_n, cot_lo = linear_forward(raw, select, tables, cot_low)
    x2, h2 = forward_step(y1, lin_all, BIN_PAD, block_input, gains[1], 2)
    y2, queries, key_vals, cot_hi = window_forward(h2, win_all, cosine, sine, cot_low)
    x3, h3 = forward_step(y2, win_all, 48, x2, gains[2], 3)
    act, d_gu, down = mlp_step(h3, cot_lo, cot_hi, ff_all)
    out_sum = lax.psum_scatter(down, RING, scatter_dimension=0, tiled=True)
    dx3, grad_c, e3, d_y2, ff_grads = mlp_back_step(
        d_gu, act, ff_all, win_all, h3, cot_lo, cot_hi, x3, gains[2], cot_local
    )
    ff_grads = lax.psum_scatter(
        ff_grads.reshape(-1, D), PLANE, scatter_dimension=0, tiled=True
    ).astype(F32)
    d_p2 = window_backward(queries, key_vals, d_y2, cosine, sine)
    dx2, grad_b, e2, d_y1, win_grads = window_back_out_step(
        d_p2, win_all, lin_all, h2, y2, e3, x2, gains[1], dx3
    )
    d_p1 = linear_backward(p1, d_y1, state_v, state_n, select, tables)
    input_grad, grad_a, grad_b, grad_c, lin_grads = last_step(
        d_p1, lin_all, h1, y1, e2, block_input, gains[0], dx2, grad_b, grad_c
    )
    block_output = (x3 + out_sum.astype(F32)).astype(BF)
    gate_grad = ff_grads[:units]
    up_grad = ff_grads[UNIT_PAD : UNIT_PAD + units]
    return (
        block_output,
        input_grad,
        grad_a.reshape(D),
        lin_grads[:wide].T,
        lin_grads[BIN_PAD:],
        grad_b.reshape(D),
        win_grads[:48].T,
        win_grads[48:],
        grad_c.reshape(D),
        jnp.stack([gate_grad.T, up_grad.T], axis=1),
        ff_grads[2 * UNIT_PAD : 2 * UNIT_PAD + units],
    )


def solution(mesh):
    grid = Mesh(mesh.devices.reshape(2, 4, 2, 4, 2), ALL)
    tokens = P(ALL, None)
    weight = ("xh", "z", "c", "xl", "y")
    rows, cols = P(weight, None), P(None, weight)
    return jax.shard_map(
        body,
        mesh=grid,
        in_specs=(
            tokens,
            tokens,
            P(("xl", "y"), None),
            P(),
            cols,
            rows,
            P(),
            cols,
            rows,
            P(),
            P(None, None, weight),
            rows,
        ),
        out_specs=(
            tokens,
            tokens,
            P(),
            cols,
            rows,
            P(),
            cols,
            rows,
            P(),
            P(None, None, weight),
            rows,
        ),
        check_vma=False,
    )
```

```python
import functools
import math

import jax
import jax.numpy as jnp
import numpy as np
from jax import lax
from jax.experimental import pallas as pl
from jax.experimental.pallas import tpu as pltpu
from jax.sharding import Mesh
from jax.sharding import PartitionSpec as P

FEAT = 16
HEAD_V = 128
WINDOW = 64
EPSILON = 1e-05
D = 2048
TOK = 128
HALF_TOK = 1024
EDGE = 64
UNIT_PAD = 48
BIN_PAD = 32
STATE = 256
PLANE = ("xh", "xl", "y")
RING = ("z", "c")
ALL = ("xl", "y", "xh", "z", "c")
MESH = pl.DeviceIdType.MESH
BF = jnp.bfloat16
F32 = jnp.float32
VM = pl.BlockSpec(memory_space=pltpu.VMEM)
ANY = pl.BlockSpec(memory_space=pl.ANY)


def dnn(a, b):
    return lax.dot_general(a, b, (((1,), (0,)), ((), ())), preferred_element_type=F32)


def dnt(a, b):
    return lax.dot_general(a, b, (((1,), (1,)), ((), ())), preferred_element_type=F32)


def dtn(a, b):
    return lax.dot_general(a, b, (((0,), (0,)), ((), ())), preferred_element_type=F32)


def remote(src, dst, send_sem, recv_sem, device):
    copy = pltpu.make_async_remote_copy(
        src_ref=src,
        dst_ref=dst,
        send_sem=send_sem,
        recv_sem=recv_sem,
        device_id=device,
        device_id_type=MESH,
    )
    copy.start()
    return copy


def greet(devices):
    barrier = pltpu.get_barrier_semaphore()
    for device in devices:
        pl.semaphore_signal(barrier, inc=1, device_id=device, device_id_type=MESH)
    pl.semaphore_wait(barrier, len(devices))


class Ring:
    def __init__(self):
        self.z = lax.axis_index("z")
        self.c = lax.axis_index("c")
        self.oc = 1 - self.c
        self.zp = lax.rem(self.z + 1, 4)
        self.zm = lax.rem(self.z + 3, 4)
        self.zz = lax.rem(self.z + 2, 4)
        self.up = {"z": self.zp}
        self.dn = {"z": self.zm}
        self.sib = {"c": self.oc}

    def greet(self):
        greet((self.up, self.dn, self.sib))


class Plane:
    def __init__(self):
        self.x = lax.axis_index("xh") * 2 + lax.axis_index("xl")
        self.y = lax.axis_index("y")

    def at_x(self, x):
        return {"xh": lax.div(x, 2), "xl": lax.rem(x, 2)}

    def at_y(self, y):
        return {"y": y}

    def ring(self, along_x):
        me = self.x if along_x else self.y
        plus, minus, far = lax.rem(me + 1, 4), lax.rem(me + 3, 4), lax.rem(me + 2, 4)
        to = self.at_x if along_x else self.at_y
        return me, plus, minus, far, to(plus), to(minus)

    def neighbours(self):
        xs, ys = self.ring(True), self.ring(False)
        return (xs[4], xs[5], ys[4], ys[5])


def finish(steps):
    for _ in steps:
        pass


def advance(steps):
    next(steps, None)


def weave(main, *others):
    for _ in main:
        for other in others:
            advance(other)


CHUNKS = 2


def gather_steps(ring, buf, out_ref, ss, rs, ls, rows, start=0, base=0, keep=True, ready=None):
    half = rows // 2
    me = ring.z * 2 + ring.c
    below, above, far = ring.zm * 2 + ring.c, ring.zp * 2 + ring.c, ring.zz * 2 + ring.c

    def send(slot, part, device, index):
        piece = buf.at[slot, pl.ds(start + part * half, half), :]
        return remote(piece, piece, ss.at[base + index], rs.at[base + index], device)

    local = []

    def save(slot):
        if keep:
            copy = pltpu.make_async_copy(buf.at[slot], out_ref.at[slot], ls.at[len(local)])
            copy.start()
            local.append(copy)

    def done(chip):
        if ready is not None:
            ready(chip)

    up, dn, sib = ring.up, ring.dn, ring.sib
    cp = {}
    cp[0] = send(me, 0, up, 0)
    cp[1] = send(me, 1, dn, 1)
    cp[2] = send(me, 1, up, 2)
    cp[3] = send(me, 0, dn, 3)
    cp[4] = send(me, 0, sib, 4)
    cp[5] = send(me, 1, sib, 5)
    save(me)
    yield
    cp[0].wait_recv()
    cp[6] = send(below, 0, up, 6)
    cp[8] = send(below, 0, sib, 8)
    cp[1].wait_recv()
    cp[7] = send(above, 1, dn, 7)
    cp[9] = send(above, 1, sib, 9)
    yield
    cp[2].wait_recv()
    cp[10] = send(below, 1, sib, 10)
    save(below)
    cp[3].wait_recv()
    cp[11] = send(above, 0, sib, 11)
    save(above)
    yield
    cp[4].wait_recv()
    cp[5].wait_recv()
    save(ring.z * 2 + ring.oc)
    done(ring.z)
    cp[8].wait_recv()
    cp[10].wait_recv()
    save(ring.zm * 2 + ring.oc)
    done(ring.zm)
    yield
    cp[6].wait_recv()
    cp[12] = send(far, 0, sib, 12)
    cp[7].wait_recv()
    cp[13] = send(far, 1, sib, 13)
    save(far)
    cp[9].wait_recv()
    cp[11].wait_recv()
    save(ring.zp * 2 + ring.oc)
    done(ring.zp)
    yield
    cp[12].wait_recv()
    cp[13].wait_recv()
    save(ring.zz * 2 + ring.oc)
    done(ring.zz)
    for index in range(14):
        cp[index].wait_send()
    for copy in local:
        copy.wait()


def scatter_steps(ring, product, part, sib_in, far_in, end_in, ss, rs, ready):
    rows = TOK // CHUNKS
    half = rows // 2
    c, oc = ring.c, ring.oc
    up, dn, sib = ring.up, ring.dn, ring.sib
    order = (ring.zz, ring.zp, ring.zm, ring.z)
    step = 512
    cp = {}

    def send(q, index, src, dst, device):
        n = q * 10 + index
        cp[q, index] = remote(src, dst, ss.at[n], rs.at[n], device)

    def multiply(index):
        row = pl.multiple_of(order[index] * (2 * TOK), 2 * TOK)

        def one(n, carry):
            col = pl.ds(pl.multiple_of(n * step, step), step)
            res = product(pl.ds(row, 2 * TOK), col).astype(BF)
            part[index, 0, :, col] = res[:TOK]
            part[index, 1, :, col] = res[TOK:]
            return carry

        lax.fori_loop(0, D // step, one, 0)
        for q in range(CHUNKS):
            at = pl.ds(q * rows, rows)
            send(q, index, part.at[index, oc, at, :], sib_in.at[index, at, :], sib)

    def add(index, first, count, other):
        def one(i, carry):
            at = pl.ds(pl.multiple_of(first + i * 16, 16), 16)
            part[index, c, at, :] = (part[index, c, at, :].astype(F32) + other(at)).astype(BF)
            return carry

        lax.fori_loop(0, count // 16, one, 0)

    def add_sib(q, index):
        cp[q, index].wait_recv()
        add(index, q * rows, rows, lambda at: sib_in[index, at, :].astype(F32))

    def piece(q, which):
        return pl.ds(q * rows + which * half, half)

    def far(q):
        add_sib(q, 0)
        send(q, 4, part.at[0, c, piece(q, 0), :], far_in.at[piece(q, 0), :], up)
        send(q, 5, part.at[0, c, piece(q, 1), :], far_in.at[piece(q, 1), :], dn)

    def near(q):
        add_sib(q, 1)
        send(q, 6, part.at[1, c, piece(q, 1), :], end_in.at[0, piece(q, 1), :], up)
        add_sib(q, 2)
        send(q, 7, part.at[2, c, piece(q, 0), :], end_in.at[1, piece(q, 0), :], dn)

    def passed(q):
        for which, device in ((0, up), (1, dn)):
            cp[q, 4 + which].wait_recv()
            at = piece(q, which)
            add(1 + which, q * rows + which * half, half, lambda at: far_in[at, :].astype(F32))
            send(q, 8 + which, part.at[1 + which, c, at, :], end_in.at[which, at, :], device)

    multiply(0)
    multiply(1)
    far(0)
    for q in range(1, CHUNKS):
        far(q)
    yield
    multiply(2)
    near(0)
    multiply(3)
    yield
    passed(0)
    for q in range(1, CHUNKS):
        near(q)
    yield
    for q in range(1, CHUNKS):
        passed(q)
    for q in range(CHUNKS):
        add_sib(q, 3)
        for index in range(6, 10):
            cp[q, index].wait_recv()
        ready(q)
        yield
    for copy in cp.values():
        copy.wait_send()


def rows_reduce_steps(ring, src_ref, q, part, sib_in, far_in, end_in, ss, rs, ls, ready):
    rows = TOK // CHUNKS
    half = rows // 2
    order = (ring.zz, ring.zp, ring.zm, ring.z)
    up, dn, sib = ring.up, ring.dn, ring.sib
    cp, loads = {}, []

    def send(index, src, dst, device):
        cp[index] = remote(src, dst, ss.at[index], rs.at[index], device)

    def source(index, core):
        start = order[index] * (2 * TOK) + core * TOK + q * rows
        return src_ref.at[pl.ds(pl.multiple_of(start, 16), rows), :]

    def add(index, first, count, other):
        def one(i, carry):
            at = pl.ds(pl.multiple_of(first + i * 16, 16), 16)
            part[index, at, :] = (part[index, at, :].astype(F32) + other(at)).astype(BF)
            return carry

        lax.fori_loop(0, count // 16, one, 0)

    def add_sib(index):
        loads[index].wait()
        cp[index].wait_recv()
        add(index, 0, rows, lambda at: sib_in[index, at, :].astype(F32))

    low, high = pl.ds(0, half), pl.ds(half, half)
    for index in range(4):
        send(index, source(index, ring.oc), sib_in.at[index], sib)
        loads.append(load(source(index, ring.c), part.at[index], ls.at[index]))
    yield
    add_sib(0)
    send(4, part.at[0, low, :], far_in.at[low, :], up)
    send(5, part.at[0, high, :], far_in.at[high, :], dn)
    add_sib(1)
    send(6, part.at[1, high, :], end_in.at[0, high, :], up)
    add_sib(2)
    send(7, part.at[2, low, :], end_in.at[1, low, :], dn)
    add_sib(3)
    yield
    for which, device in ((0, up), (1, dn)):
        cp[4 + which].wait_recv()
        at = (low, high)[which]
        add(1 + which, which * half, half, lambda at: far_in[at, :].astype(F32))
        send(8 + which, part.at[1 + which, at, :], end_in.at[which, at, :], device)
    yield
    for index in range(6, 10):
        cp[index].wait_recv()

    def total(i, carry):
        at = pl.ds(pl.multiple_of(i * 16, 16), 16)
        ready(
            at,
            pl.ds(pl.multiple_of(q * rows + i * 16, 16), 16),
            part[3, at, :].astype(F32)
            + end_in[0, at, :].astype(F32)
            + end_in[1, at, :].astype(F32),
        )
        return carry

    lax.fori_loop(0, rows // 16, total, 0)
    for copy in cp.values():
        copy.wait_send()


ROWS_SCRATCH = [
    pltpu.VMEM((4, TOK // CHUNKS, D), BF),
    pltpu.VMEM((4, TOK // CHUNKS, D), BF),
    pltpu.VMEM((TOK // CHUNKS, D), BF),
    pltpu.VMEM((2, TOK // CHUNKS, D), BF),
    pltpu.SemaphoreType.DMA((10,)),
    pltpu.SemaphoreType.DMA((10,)),
    pltpu.SemaphoreType.DMA((4,)),
]
SCATTER_SCRATCH = [
    pltpu.VMEM((4, 2, TOK, D), BF),
    pltpu.VMEM((4, TOK, D), BF),
    pltpu.VMEM((TOK, D), BF),
    pltpu.VMEM((2, TOK, D), BF),
    pltpu.SemaphoreType.DMA((10 * CHUNKS,)),
    pltpu.SemaphoreType.DMA((10 * CHUNKS,)),
]
GATHER_SCRATCH = [
    pltpu.VMEM((8, TOK, D), BF),
    pltpu.SemaphoreType.DMA((14 * CHUNKS,)),
    pltpu.SemaphoreType.DMA((14 * CHUNKS,)),
    pltpu.SemaphoreType.DMA((8,)),
]
HALF_SCRATCH = [pltpu.VMEM((8, TOK // 2, D), BF)] + GATHER_SCRATCH[1:]


def plane_view(plane, ref, half, stage, place, part):
    cols = pl.ds(half * (D // 2) + (part or 0) * (D // 4), D // 2 if part is None else D // 4)
    if stage == 0:
        return ref.at[place, plane.y, :, cols] if half == 0 else ref.at[plane.x, place, :, cols]
    return ref.at[:, place, :, cols] if half == 0 else ref.at[place, :, :, cols]


def plane_gather_steps(plane, buf, ss, rs):
    copies = []

    def send(view, device):
        copies.append(remote(view, view, ss.at[len(copies)], rs.at[len(copies)], device))
        return copies[-1]

    for stage in (0, 1):
        rings = [plane.ring(half == stage) for half in (0, 1)]
        near, far = [], []
        for half in (0, 1):
            me, plus, minus, _, to_plus, to_minus = rings[half]
            view = plane_view(plane, buf, half, stage, me, None)
            near.append((send(view, to_plus), send(view, to_minus)))
        yield
        for half in (0, 1):
            me, plus, minus, _, to_plus, to_minus = rings[half]
            near[half][0].wait_recv()
            far.append(send(plane_view(plane, buf, half, stage, minus, 0), to_plus))
            near[half][1].wait_recv()
            far.append(send(plane_view(plane, buf, half, stage, plus, 1), to_minus))
        yield
        for copy in far:
            copy.wait_recv()
    for copy in copies:
        copy.wait_send()


def plane_reduce_scratch(rows):
    return [
        pltpu.VMEM((4, 4, rows, D), BF),
        pltpu.VMEM((2, 2, 4, rows, D // 4), BF),
        pltpu.VMEM((2, 2, 4, rows, D // 2), BF),
        pltpu.VMEM((2, 2, rows, D // 4), BF),
        pltpu.VMEM((2, 2, rows, D // 2), BF),
        pltpu.SemaphoreType.DMA((24,)),
        pltpu.SemaphoreType.DMA((24,)),
    ]


def plane_reduce_steps(plane, grads, far_a, end_a, far_b, end_b, ss, rs, outs):
    copies = []
    rows = grads.shape[2]

    def send(src, dst, device):
        copies.append(remote(src, dst, ss.at[len(copies)], rs.at[len(copies)], device))
        return copies[-1]

    def add(view, other):
        def one(i, carry):
            at = pl.ds(pl.multiple_of(i * 16, 16), 16)
            piece = view.at[..., at, :]
            piece[...] = (piece[...].astype(F32) + other.at[..., at, :][...].astype(F32)).astype(BF)
            return carry

        lax.fori_loop(0, rows // 16, one, 0)

    for stage in (0, 1):
        rings = [plane.ring(half != stage) for half in (0, 1)]
        far_in, end_in = (far_a, end_a) if stage == 0 else (far_b, end_b)

        def view(half, place, part):
            return plane_view(plane, grads, half, 1 - stage, place, part)

        def ends(half, side, part):
            if part is None:
                return end_in.at[half, side]
            return end_in.at[half, side, ..., pl.ds(part * (D // 4), D // 4)]

        first, last = [], []
        for half in (0, 1):
            me, plus, minus, far, to_plus, to_minus = rings[half]
            first.append(
                (
                    send(view(half, far, 0), far_in.at[half, 0], to_plus),
                    send(view(half, far, 1), far_in.at[half, 1], to_minus),
                )
            )
            last.append(send(view(half, plus, 1), ends(half, 0, 1), to_plus))
            last.append(send(view(half, minus, 0), ends(half, 1, 0), to_minus))
        yield
        for half in (0, 1):
            me, plus, minus, far, to_plus, to_minus = rings[half]
            first[half][0].wait_recv()
            add(view(half, plus, 0), far_in.at[half, 0])
            last.append(send(view(half, plus, 0), ends(half, 0, 0), to_plus))
            first[half][1].wait_recv()
            add(view(half, minus, 1), far_in.at[half, 1])
            last.append(send(view(half, minus, 1), ends(half, 1, 1), to_minus))
        yield
        for copy in last:
            copy.wait_recv()
        for half in (0, 1):
            me = rings[half][0]
            if stage == 0:
                for side in (0, 1):
                    add(view(half, me, None), ends(half, side, None))
            else:
                cols = pl.ds(half * (D // 2), D // 2)
                total = (
                    view(half, me, None)[...].astype(F32)
                    + end_in[half, 0].astype(F32)
                    + end_in[half, 1].astype(F32)
                )
                for start, out_ref in outs:
                    out_ref[:, cols] = total[start : start + out_ref.shape[0]]
        yield
    for copy in copies:
        copy.wait_send()


def load(src, dst, sem):
    copy = pltpu.make_async_copy(src, dst, sem)
    copy.start()
    return copy


def params(collective_id, limit=58):
    return pltpu.CompilerParams(
        collective_id=collective_id, has_side_effects=True, vmem_limit_bytes=limit << 20
    )


def sds(shape, dtype=BF):
    return jax.ShapeDtypeStruct(shape, dtype)


def scale_of(rows):
    return lax.rsqrt(jnp.mean(rows * rows, axis=-1, keepdims=True) + EPSILON)


def by_rows(one, start=0, rows=TOK):
    def step(i, carry):
        one(pl.ds(pl.multiple_of(start + i * 16, 16), 16))
        return carry

    lax.fori_loop(0, rows // 16, step, 0)


def scatter_gather(ring, product, one, scatter, gather, out_ref, done=None, others=()):
    part, sib_in, far_in, end_in, sss, srs = scatter
    buf, ss, rs, ls = gather
    rows = TOK // CHUNKS
    gathers = []

    def ready(q):
        by_rows(one, q * rows, rows)
        last = q == CHUNKS - 1
        steps = gather_steps(
            ring,
            buf,
            out_ref,
            ss,
            rs,
            ls,
            rows,
            start=q * rows,
            base=14 * q,
            keep=last,
            ready=done if last else None,
        )
        advance(steps)
        gathers.append(steps)

    weave(scatter_steps(ring, product, part, sib_in, far_in, end_in, sss, srs, ready), *others)
    for _ in range(5):
        for steps in gathers:
            advance(steps)
        for other in others:
            advance(other)
    for steps in gathers:
        finish(steps)


def total_rows(part, end_in, c, at):
    return (
        part[3, c, at, :].astype(F32)
        + end_in[0, at, :].astype(F32)
        + end_in[1, at, :].astype(F32)
    )


def chip_rows(chip):
    return pl.ds(pl.multiple_of(chip * (2 * TOK), 2 * TOK), 2 * TOK)


def first_kernel(
    x_ref, gain_ref, in_ref, out_ref, h_out, w_out, p_ref, wide, wss, wrs, buf, ss, rs, ls, wls
):
    ring, plane = Ring(), Plane()
    me = ring.z * 2 + ring.c
    barrier = pltpu.get_barrier_semaphore()
    partners = (ring.up, ring.dn, ring.sib) + plane.neighbours()
    for device in partners:
        pl.semaphore_signal(barrier, inc=1, device_id=device, device_id_type=MESH)
    wide[plane.x, plane.y, BIN_PAD // 2 : BIN_PAD, :] = jnp.zeros((BIN_PAD // 2, D), BF)
    wide[plane.x, plane.y, : in_ref.shape[0], :] = in_ref[...]
    wide[plane.x, plane.y, BIN_PAD:, :] = out_ref[...]

    def one(at):
        rows = x_ref[at, :].astype(F32)
        buf[me, at, :] = (rows * scale_of(rows) * gain_ref[...]).astype(BF)

    by_rows(one)
    pl.semaphore_wait(barrier, len(partners))
    weights = plane_gather_steps(plane, wide, wss, wrs)
    rows = gather_steps(ring, buf, h_out, ss, rs, ls, TOK)
    advance(weights)
    advance(rows)
    advance(weights)
    advance(weights)
    advance(rows)
    advance(rows)
    advance(weights)
    finish(rows)
    finish(weights)
    keep = load(wide, w_out, wls)

    def project(i, carry):
        at = pl.ds(pl.multiple_of(i * 256, 256), 256)
        h = buf[pl.ds(2 * i, 2)].reshape(256, D)
        w = wide[:, :, :BIN_PAD, :].reshape(16 * BIN_PAD, D)
        p_ref[at, :] = dnt(h, w).astype(BF)
        return carry

    lax.fori_loop(0, 4, project, 0)
    keep.wait()


def first_step(x, gain, rows_in, rows_out):
    return pl.pallas_call(
        first_kernel,
        out_shape=(
            sds((8, TOK, D)),
            sds((4, 4, BIN_PAD + 16, D)),
            sds((HALF_TOK, 16 * BIN_PAD)),
        ),
        in_specs=[VM] * 4,
        out_specs=(ANY, ANY, VM),
        scratch_shapes=[
            pltpu.VMEM((4, 4, BIN_PAD + 16, D), BF),
            pltpu.SemaphoreType.DMA((16,)),
            pltpu.SemaphoreType.DMA((16,)),
        ]
        + GATHER_SCRATCH
        + [pltpu.SemaphoreType.DMA],
        compiler_params=params(1),
    )(x, gain, rows_in, rows_out)


def forward_kernel(
    off,
    a_ref,
    w_ref,
    x_ref,
    gain_ref,
    x_out,
    h_out,
    w,
    wls,
    part,
    sib_in,
    far_in,
    end_in,
    sss,
    srs,
    buf,
    ss,
    rs,
    ls,
):
    ring = Ring()
    me = ring.z * 2 + ring.c
    loading = load(w_ref.at[:, :, pl.ds(off, 16), :], w, wls)
    ring.greet()
    loading.wait()

    def product(rows, col):
        return dnn(a_ref[rows, :], w[:, :, :, col].reshape(256, -1))

    def one(at):
        rows = x_ref[at, :].astype(F32) + total_rows(part, end_in, ring.c, at)
        x_out[at, :] = rows
        buf[me, at, :] = (rows * scale_of(rows) * gain_ref[...]).astype(BF)

    scatter = (part, sib_in, far_in, end_in, sss, srs)
    scatter_gather(ring, product, one, scatter, (buf, ss, rs, ls), h_out)


def forward_step(a, w, off, x, gain, collective_id):
    return pl.pallas_call(
        functools.partial(forward_kernel, off),
        out_shape=(sds((TOK, D), F32), sds((8, TOK, D))),
        in_specs=[VM, ANY, VM, VM],
        out_specs=(VM, ANY),
        scratch_shapes=[pltpu.VMEM((4, 4, 16, D), BF), pltpu.SemaphoreType.DMA]
        + SCATTER_SCRATCH
        + GATHER_SCRATCH,
        compiler_params=params(collective_id),
    )(a, w, x, gain)


def norm_back_rows(v_ref, gain_ref, grads, at):
    rows = v_ref[at, :].astype(F32)
    scale = scale_of(rows)
    unit = rows * scale
    scaled = grads * gain_ref[...]
    return scale * (scaled - unit * jnp.mean(scaled * unit, axis=-1, keepdims=True))


CHUNK = 8 * UNIT_PAD


def mlp_kernel(
    h_ref, lo_ref, hi_ref, w_ref, act_ref, d_ref, down_ref, h, cot, gate_w, up_w, down_w, sems
):
    copies = {}
    copies["h"] = load(h_ref, h, sems.at[0])
    names = (("gate", gate_w), ("up", up_w), ("down", down_w))
    for n, (name, ref) in enumerate(names):
        for i in range(2):
            copies[name, i] = load(
                w_ref.at[pl.ds(8 * i, 8), pl.ds(n * UNIT_PAD, UNIT_PAD), :],
                ref.at[pl.ds(8 * i, 8)],
                sems.at[3 + 2 * n + i],
            )
        if n == 0:
            copies["lo"] = load(lo_ref, cot.at[:, pl.ds(0, TOK // 2), :], sems.at[1])
            copies["hi"] = load(hi_ref, cot.at[:, pl.ds(TOK // 2, TOK // 2), :], sems.at[2])
    copies["h"].wait()
    copies["lo"].wait()
    copies["hi"].wait()
    for i in range(2):
        for name, _ in names:
            copies[name, i].wait()
        units = slice(8 * i, 8 * i + 8)

        def one(n, carry):
            at = chip_rows(n)
            tokens = pl.ds(2 * n, 2)
            rows = h[tokens].reshape(2 * TOK, D)
            gate = dnt(rows, gate_w[units].reshape(CHUNK, D))
            up = dnt(rows, up_w[units].reshape(CHUNK, D))
            d_act = dnt(cot[tokens].reshape(2 * TOK, D), down_w[units].reshape(CHUNK, D))
            sig = 1.0 / (1.0 + jnp.exp(-gate))
            silu = gate * sig
            act_ref[at, i * CHUNK : (i + 1) * CHUNK] = (silu * up).astype(BF)
            d_ref[at, i * CHUNK : (i + 1) * CHUNK] = (
                d_act * up * (sig * (1.0 + gate * (1.0 - sig)))
            ).astype(BF)
            d_ref[at, (2 + i) * CHUNK : (3 + i) * CHUNK] = (d_act * silu).astype(BF)
            return carry

        lax.fori_loop(0, 4, one, 0)

    def last(n, carry):
        at = chip_rows(n)
        for col in range(0, D, 512):
            down_ref[at, col : col + 512] = dnn(
                act_ref[at, :], down_w[:, :, col : col + 512].reshape(2 * CHUNK, 512)
            ).astype(BF)
        return carry

    lax.fori_loop(0, 4, last, 0)


def mlp_step(h, lo, hi, w):
    return pl.pallas_call(
        mlp_kernel,
        out_shape=(
            sds((HALF_TOK, 2 * CHUNK)),
            sds((HALF_TOK, 4 * CHUNK)),
            sds((HALF_TOK, D)),
        ),
        in_specs=[ANY] * 4,
        out_specs=(VM, VM, VM),
        scratch_shapes=[
            pltpu.VMEM((8, TOK, D), BF),
            pltpu.VMEM((8, TOK, D), BF),
        ]
        + [pltpu.VMEM((16, UNIT_PAD, D), BF)] * 3
        + [pltpu.SemaphoreType.DMA((9,))],
        compiler_params=pltpu.CompilerParams(vmem_limit_bytes=58 << 20),
    )(h, lo, hi, w)


def mlp_grad_steps(jobs, stage, out_ref, sems, gain_acc):
    copies = []
    for n, (lhs, col, rhs, off, half, w) in enumerate(jobs):
        slot = n % 2
        if n >= 2:
            copies[n - 2].wait()

        def one(k, carry):
            cols = pl.ds(pl.multiple_of(k * 512, 512), 512)
            res = dtn(lhs[:, col : col + CHUNK], rhs[:, :, cols].reshape(HALF_TOK, 512))
            stage[slot, :, :, cols] = res.astype(BF).reshape(8, UNIT_PAD, 512)
            if w is not None:
                own = w[8 * half : 8 * half + 8, :, cols].reshape(CHUNK, 512).astype(F32)
                gain_acc[:, cols] += jnp.sum(res * own, axis=0, keepdims=True)
            return carry

        lax.fori_loop(0, 4, one, 0)
        copies.append(
            load(
                stage.at[slot],
                out_ref.at[pl.ds(8 * half, 8), pl.ds(off, UNIT_PAD), :],
                sems.at[n],
            )
        )
        yield
    copies[-2].wait()
    copies[-1].wait()


def mlp_back_kernel(
    d_ref,
    act_ref,
    w_ref,
    wo_ref,
    h_ref,
    lo_ref,
    hi_ref,
    v_ref,
    gain_ref,
    res_ref,
    d_out,
    gain_out,
    e_out,
    dy_out,
    g_out,
    w,
    wo,
    h,
    cot,
    stage,
    sems,
    gsems,
    gain_acc,
    part,
    sib_in,
    far_in,
    end_in,
    sss,
    srs,
    buf,
    ss,
    rs,
    ls,
):
    ring = Ring()
    me = ring.z * 2 + ring.c
    loads = [
        load(w_ref.at[:, pl.ds(0, UNIT_PAD), :], w.at[0], sems.at[0]),
        load(w_ref.at[:, pl.ds(UNIT_PAD, UNIT_PAD), :], w.at[1], sems.at[1]),
    ]
    late = [
        load(h_ref, h, sems.at[2]),
        load(lo_ref, cot.at[:, pl.ds(0, TOK // 2), :], sems.at[3]),
        load(hi_ref, cot.at[:, pl.ds(TOK // 2, TOK // 2), :], sems.at[4]),
        load(wo_ref.at[:, :, pl.ds(48, 16), :], wo, sems.at[5]),
    ]
    ring.greet()
    gain_acc[...] = jnp.zeros_like(gain_acc)
    for copy in loads:
        copy.wait()

    def product(rows, col):
        return dnn(d_ref[rows, :], w[:, :, :, col].reshape(4 * CHUNK, -1))

    def grads():
        for copy in late:
            copy.wait()
        jobs = [
            (d_ref, n * CHUNK, h, (n // 2) * UNIT_PAD, n % 2, w.at[n // 2]) for n in range(4)
        ]
        jobs += [(act_ref, n * CHUNK, cot, 2 * UNIT_PAD, n, None) for n in range(2)]
        yield from mlp_grad_steps(jobs, stage, g_out, gsems, gain_acc)

    weight_grads = grads()

    def one(at):
        grad = total_rows(part, end_in, ring.c, at)
        rows = res_ref[at, :].astype(F32) + norm_back_rows(v_ref, gain_ref, grad, at)
        d_out[at, :] = rows
        buf[me, at, :] = rows.astype(BF)

    def done(chip):
        dy_out[chip_rows(chip), :] = dnt(
            buf[pl.ds(2 * chip, 2)].reshape(2 * TOK, D), wo[...].reshape(256, D)
        ).astype(BF)

    scatter = (part, sib_in, far_in, end_in, sss, srs)
    scatter_gather(
        ring, product, one, scatter, (buf, ss, rs, ls), e_out, done, (weight_grads,)
    )
    finish(weight_grads)
    gain_out[...] = gain_acc[...] / gain_ref[...]


def mlp_back_step(d, act, w, wo, h, lo, hi, v, gain, res):
    return pl.pallas_call(
        mlp_back_kernel,
        out_shape=(
            sds((TOK, D), F32),
            sds((1, D), F32),
            sds((8, TOK, D)),
            sds((HALF_TOK, 256)),
            sds((16, 3 * UNIT_PAD, D)),
        ),
        in_specs=[VM, VM, ANY, ANY, ANY, ANY, ANY, VM, VM, VM],
        out_specs=(VM, VM, ANY, VM, ANY),
        scratch_shapes=[
            pltpu.VMEM((2, 16, UNIT_PAD, D), BF),
            pltpu.VMEM((4, 4, 16, D), BF),
            pltpu.VMEM((8, TOK, D), BF),
            pltpu.VMEM((8, TOK, D), BF),
            pltpu.VMEM((2, 8, UNIT_PAD, D), BF),
            pltpu.SemaphoreType.DMA((6,)),
            pltpu.SemaphoreType.DMA((6,)),
            pltpu.VMEM((1, D), F32),
        ]
        + SCATTER_SCRATCH
        + GATHER_SCRATCH,
        compiler_params=params(4),
    )(d, act, w, wo, h, lo, hi, v, gain, res)


def window_back_out_kernel(
    d_ref,
    w_ref,
    wo_ref,
    h_ref,
    y_ref,
    e_ref,
    v_ref,
    gain_ref,
    res_ref,
    d_out,
    gain_out,
    e_out,
    dy_out,
    g_out,
    w,
    wo,
    h,
    e,
    sems,
    gain_acc,
    grads,
    part,
    sib_in,
    far_in,
    end_in,
    sss,
    srs,
    buf,
    ss,
    rs,
    ls,
):
    ring = Ring()
    me = ring.z * 2 + ring.c
    first = load(w_ref.at[:, :, pl.ds(0, 48), :], w, sems.at[0])
    late = [
        load(h_ref, h, sems.at[1]),
        load(e_ref, e, sems.at[2]),
        load(wo_ref.at[:, :, pl.ds(BIN_PAD, 16), :], wo, sems.at[3]),
    ]
    ring.greet()
    gain_acc[...] = jnp.zeros_like(gain_acc)
    first.wait()

    def product(rows, col):
        return dnn(d_ref[rows, :], w[:, :, :, col].reshape(768, -1))

    def weights():
        for copy in late:
            copy.wait()

        for k in range(4):
            cols = slice(k * 512, (k + 1) * 512)
            rows = h[:, :, cols].reshape(HALF_TOK, 512)
            for i in range(2):
                res = dtn(d_ref[:, i * 384 : (i + 1) * 384], rows)
                own = w[2 * i : 2 * i + 2, :, :, cols].reshape(384, 512).astype(F32)
                gain_acc[:, cols] += jnp.sum(res * own, axis=0, keepdims=True)
                grads[2 * i : 2 * i + 2, :, :48, cols] = res.astype(BF).reshape(2, 4, 48, 512)
            res = dtn(y_ref[...], e[:, :, cols].reshape(HALF_TOK, 512)).astype(BF)
            grads[:, :, 48:, cols] = res.reshape(4, 4, 16, 512)
            yield
        copy = load(grads, g_out, sems.at[4])
        yield
        copy.wait()

    weight_grads = weights()

    def one(at):
        grad = total_rows(part, end_in, ring.c, at)
        rows = res_ref[at, :].astype(F32) + norm_back_rows(v_ref, gain_ref, grad, at)
        d_out[at, :] = rows
        buf[me, at, :] = rows.astype(BF)

    def done(chip):
        dy_out[chip_rows(chip), :] = dnt(
            buf[pl.ds(2 * chip, 2)].reshape(2 * TOK, D), wo[...].reshape(256, D)
        ).astype(BF)

    scatter = (part, sib_in, far_in, end_in, sss, srs)
    scatter_gather(
        ring, product, one, scatter, (buf, ss, rs, ls), e_out, done, (weight_grads,)
    )
    finish(weight_grads)
    gain_out[...] = gain_acc[...] / gain_ref[...]


def window_back_out_step(d, w, wo, h, y, e, v, gain, res):
    return pl.pallas_call(
        window_back_out_kernel,
        out_shape=(
            sds((TOK, D), F32),
            sds((1, D), F32),
            sds((8, TOK, D)),
            sds((HALF_TOK, 256)),
            sds((4, 4, 64, D)),
        ),
        in_specs=[VM, ANY, ANY, ANY, VM, ANY, VM, VM, VM],
        out_specs=(VM, VM, ANY, VM, ANY),
        scratch_shapes=[
            pltpu.VMEM((4, 4, 48, D), BF),
            pltpu.VMEM((4, 4, 16, D), BF),
            pltpu.VMEM((8, TOK, D), BF),
            pltpu.VMEM((8, TOK, D), BF),
            pltpu.SemaphoreType.DMA((5,)),
            pltpu.VMEM((1, D), F32),
            pltpu.VMEM((4, 4, 64, D), BF),
        ]
        + SCATTER_SCRATCH
        + GATHER_SCRATCH,
        compiler_params=params(5),
    )(d, w, wo, h, y, e, v, gain, res)


def sum_steps(ring, plane, pack, ring_in, x_in, y_in, ss, rs):
    copies = []
    stages = (
        (ring_in, ring.z * 2 + ring.c, 8, lambda t: {"z": lax.div(t, 2), "c": lax.rem(t, 2)}),
        (x_in, plane.x, 4, plane.at_x),
        (y_in, plane.y, 4, plane.at_y),
    )
    for dst, own, count, device_of in stages:
        dst[own] = pack[...]
        sent = []
        for o in range(1, count):
            n = len(copies) + len(sent)
            device = device_of(lax.rem(own + o, count))
            sent.append(remote(pack, dst.at[own], ss.at[n], rs.at[n], device))
        yield
        for copy in sent:
            copy.wait_recv()
        for copy in sent:
            copy.wait_send()
        copies += sent
        total = dst[0]
        for k in range(1, count):
            total = total + dst[k]
        pack[...] = total


def last_kernel(
    d_ref,
    w_ref,
    h_ref,
    y_ref,
    e_ref,
    v_ref,
    gain_ref,
    res_ref,
    gb_ref,
    gc_ref,
    d_out,
    ga_out,
    gb_out,
    gc_out,
    in_out,
    out_out,
    w,
    h,
    e,
    sems,
    gain_acc,
    pack,
    ring_in,
    x_in,
    y_in,
    pss,
    prs,
    grads,
    far_a,
    end_a,
    far_b,
    end_b,
    gss,
    grs,
    part,
    sib_in,
    far_in,
    end_in,
    sss,
    srs,
):
    ring, plane = Ring(), Plane()
    first = load(w_ref.at[:, :, pl.ds(0, BIN_PAD), :], w, sems.at[0])
    late = [load(h_ref, h, sems.at[1]), load(e_ref, e, sems.at[2])]
    me = ring.z * 2 + ring.c
    partners = []
    for o in range(1, 8):
        to = lax.rem(me + o, 8)
        partners.append({"z": lax.div(to, 2), "c": lax.rem(to, 2)})
    for o in range(1, 4):
        partners.append(plane.at_x(lax.rem(plane.x + o, 4)))
        partners.append(plane.at_y(lax.rem(plane.y + o, 4)))
    greet(partners)
    first.wait()

    def product(rows, col):
        return dnn(d_ref[rows, :], w[:, :, :, col].reshape(16 * BIN_PAD, -1))

    wide = D // 8

    def weights():
        for copy in late:
            copy.wait()
        for k in range(4):
            cols = slice(k * 512, (k + 1) * 512)
            res = dtn(d_ref[...], h[:, :, cols].reshape(HALF_TOK, 512))
            own = w[:, :, :, cols].reshape(16 * BIN_PAD, 512).astype(F32)
            gain_acc[:, cols] = jnp.sum(res * own, axis=0, keepdims=True)
            grads[:, :, :BIN_PAD, cols] = res.astype(BF).reshape(4, 4, BIN_PAD, 512)
            res = dtn(y_ref[...], e[:, :, cols].reshape(HALF_TOK, 512)).astype(BF)
            grads[:, :, BIN_PAD:, cols] = res.reshape(4, 4, 16, 512)
        reduce = plane_reduce_steps(
            plane,
            grads,
            far_a,
            end_a,
            far_b,
            end_b,
            gss,
            grs,
            ((0, in_out), (BIN_PAD, out_out)),
        )
        advance(reduce)
        gains = (gain_acc[...] / gain_ref[...], gb_ref[...], gc_ref[...])
        for n, gain in enumerate(gains):
            for r in range(8):
                pack[r : r + 1, n * wide : (n + 1) * wide] = gain[:, r * wide : (r + 1) * wide]
        sums = sum_steps(ring, plane, pack, ring_in, x_in, y_in, pss, prs)
        advance(sums)
        yield
        for _ in range(4):
            advance(reduce)
            advance(sums)
            yield
        finish(sums)
        finish(reduce)

    weight_grads = weights()

    def one(at):
        grad = total_rows(part, end_in, ring.c, at)
        d_out[at, :] = res_ref[at, :] + norm_back_rows(v_ref, gain_ref, grad, at)

    def ready(q):
        by_rows(one, q * (TOK // CHUNKS), TOK // CHUNKS)

    weave(
        scatter_steps(ring, product, part, sib_in, far_in, end_in, sss, srs, ready),
        weight_grads,
    )
    finish(weight_grads)
    for n, out in enumerate((ga_out, gb_out, gc_out)):
        for r in range(8):
            out[:, r * wide : (r + 1) * wide] = pack[r : r + 1, n * wide : (n + 1) * wide]


def last_step(d, w, h, y, e, v, gain, res, grad_b, grad_c, width):
    small = (8, 3 * D // 8)
    return pl.pallas_call(
        last_kernel,
        out_shape=(
            sds((TOK, D), F32),
            sds((1, D), F32),
            sds((1, D), F32),
            sds((1, D), F32),
            sds((width, D), F32),
            sds((16, D), F32),
        ),
        in_specs=[VM, ANY, ANY, VM, ANY, VM, VM, VM, VM, VM],
        out_specs=(VM,) * 6,
        scratch_shapes=[
            pltpu.VMEM((4, 4, BIN_PAD, D), BF),
            pltpu.VMEM((8, TOK, D), BF),
            pltpu.VMEM((8, TOK, D), BF),
            pltpu.SemaphoreType.DMA((3,)),
            pltpu.VMEM((1, D), F32),
            pltpu.VMEM(small, F32),
            pltpu.VMEM((8,) + small, F32),
            pltpu.VMEM((4,) + small, F32),
            pltpu.VMEM((4,) + small, F32),
            pltpu.SemaphoreType.DMA((13,)),
            pltpu.SemaphoreType.DMA((13,)),
        ]
        + plane_reduce_scratch(BIN_PAD + 16)
        + SCATTER_SCRATCH,
        compiler_params=params(6),
    )(d, w, h, y, e, v, gain, res, grad_b, grad_c)


def state_tables():
    first = np.zeros((128, STATE), np.float32)
    second = np.zeros((128, STATE), np.float32)
    bias = np.zeros((8, STATE), np.float32)
    coef = np.zeros((8, STATE), np.float32)
    bias[0, 0] = bias[1, 0] = 1.0
    coef[0, 0] = 1.0
    at = 1
    for i in range(FEAT):
        first[i, at] = 1.0
        bias[1, at] = 1.0
        coef[0, at] = 1.0 / math.sqrt(FEAT)
        at += 1
    for i in range(FEAT):
        for j in range(i, FEAT):
            first[i, at] = 1.0
            second[j, at] = 1.0
            coef[0, at] = (0.5 if i == j else 1.0) / FEAT
            at += 1
    picks = np.zeros((4, 128, 128), np.float32)
    for which in range(4):
        for i in range(FEAT):
            picks[which, which * FEAT + i, i] = 1.0
    return (
        np.stack([first, second]),
        np.concatenate([bias[:2], coef[:1], np.zeros((5, STATE), np.float32)]),
        picks,
    )


def causal_mask(row_start, col_start, rows, cols, edge):
    t = row_start + lax.broadcasted_iota(jnp.int32, (rows, cols), 0)
    u = col_start + lax.broadcasted_iota(jnp.int32, (rows, cols), 1)
    return (u <= t) & ((t >= edge) == (u >= edge))


BLK = 256
NBLK = HALF_TOK // BLK
INV_ROOT = 1.0 / math.sqrt(FEAT)


def select_table(width):
    table = np.zeros((16 * BIN_PAD, 3 * HEAD_V), np.float32)
    for shard in range(16):
        for i in range(width):
            head, col = shard // 8, (shard % 8) * width + i
            to = 2 * HEAD_V + 2 * FEAT * head + col if col < 2 * FEAT else head * HEAD_V + col - 2 * FEAT
            table[shard * BIN_PAD + i, to] = 1.0
    return table


def linear_forward_kernel(
    raw_ref,
    sel_ref,
    e_ref,
    t_ref,
    pick_ref,
    cot_ref,
    y_ref,
    p_ref,
    sv_ref,
    sn_ref,
    lo_ref,
    qs,
    ks,
    num,
    den,
    sv_s,
    sn_s,
    sv_r,
    sn_r,
    xss,
    xrs,
    buf,
    ss,
    rs,
    ls,
):
    ring = Ring()
    xh = lax.axis_index("xh")
    partner = {"xh": 1 - xh}
    edge = jnp.where(xh == 0, EDGE, HALF_TOK - EDGE)
    bias1, bias2, coef = t_ref[0:1, :], t_ref[1:2, :], t_ref[2:3, :]
    barrier = pltpu.get_barrier_semaphore()
    for device in (ring.up, ring.dn, ring.sib, partner):
        pl.semaphore_signal(barrier, inc=1, device_id=device, device_id_type=MESH)
    buf[ring.z * 2 + ring.c] = cot_ref[: TOK // 2, :]

    def rows_of(r):
        return slice(r * BLK, (r + 1) * BLK)

    for r in range(NBLK):
        p_ref[rows_of(r), :] = dnn(raw_ref[rows_of(r), :], sel_ref[...]).astype(BF)
    pl.semaphore_wait(barrier, 4)
    cots = gather_steps(ring, buf, lo_ref, ss, rs, ls, TOK // 2)
    advance(cots)
    small = p_ref[:, 2 * HEAD_V :]
    for j in range(2):
        qs[j] = dnn(small, pick_ref[2 * j]).astype(BF)
        ks[j] = dnn(small, pick_ref[2 * j + 1]).astype(BF)

    def phi_of(vecs):
        return (dnn(vecs, e_ref[0]) + bias1) * (dnn(vecs, e_ref[1]) + bias2)

    for j in range(2):
        sv = jnp.zeros((HEAD_V, STATE), F32)
        sn = jnp.zeros((1, STATE), F32)
        for r in range(NBLK):
            phi = phi_of(ks[j, rows_of(r), :])
            if r == 0:
                slot = lax.broadcasted_iota(jnp.int32, (BLK, STATE), 0)
                phi = jnp.where(slot >= EDGE, phi, 0.0)
            sv = sv + dtn(p_ref[rows_of(r), j * HEAD_V : (j + 1) * HEAD_V], phi.astype(BF))
            sn = sn + jnp.sum(phi, axis=0, keepdims=True)
        sv_s[j] = (sv * coef).astype(BF)
        sn_s[j] = jnp.broadcast_to(sn * coef, (8, STATE))
    copies = (
        remote(sv_s, sv_r, xss.at[0], xrs.at[0], partner),
        remote(sn_s, sn_r, xss.at[1], xrs.at[1], partner),
    )
    for j in range(2):
        for r in range(NBLK):
            queries = qs[j, rows_of(r), :]
            rows_num = jnp.zeros((BLK, HEAD_V), F32)
            rows_den = jnp.zeros((BLK, 1), F32)
            for s in range(r + 1):
                scores = dnt(queries, ks[j, rows_of(s), :]) * INV_ROOT
                mask = causal_mask(r * BLK, s * BLK, BLK, BLK, edge)
                kernel = jnp.where(mask, 1.0 + scores + 0.5 * scores * scores, 0.0)
                rows_den = rows_den + jnp.sum(kernel, axis=-1, keepdims=True)
                rows_num = rows_num + dnn(
                    kernel.astype(BF), p_ref[rows_of(s), j * HEAD_V : (j + 1) * HEAD_V]
                )
            num[j, rows_of(r), :] = rows_num
            den[j, rows_of(r), :] = jnp.broadcast_to(rows_den, (BLK, HEAD_V))
    advance(cots)
    advance(cots)
    for copy in copies:
        copy.wait_recv()
    sv_ref[...] = sv_r[...]
    sn_ref[...] = sn_r[...]
    for j in range(2):
        for r in range(NBLK):
            phi = phi_of(qs[j, rows_of(r), :])
            cross_den = jnp.sum(phi * sn_r[j, 0:1, :], axis=-1, keepdims=True)
            cross_num = dnt(phi.astype(BF), sv_r[j])
            slot = r * BLK + lax.broadcasted_iota(jnp.int32, (BLK, HEAD_V), 0)
            seen = (slot < HALF_TOK - EDGE) & (xh == 1)
            top = num[j, rows_of(r), :] + jnp.where(seen, cross_num, 0.0)
            bottom = den[j, rows_of(r), :] + jnp.where(seen, cross_den, 0.0)
            y_ref[rows_of(r), j * HEAD_V : (j + 1) * HEAD_V] = (top / bottom).astype(BF)
    for copy in copies:
        copy.wait_send()
    finish(cots)


def linear_forward(raw, select, tables, cot):
    return pl.pallas_call(
        linear_forward_kernel,
        out_shape=(
            sds((HALF_TOK, 2 * HEAD_V)),
            sds((HALF_TOK, 3 * HEAD_V)),
            sds((2, HEAD_V, STATE)),
            sds((2, 8, STATE), F32),
            sds((8, TOK // 2, D)),
        ),
        in_specs=[VM] * 6,
        out_specs=(VM, VM, VM, VM, ANY),
        scratch_shapes=[
            pltpu.VMEM((2, HALF_TOK, 128), BF),
            pltpu.VMEM((2, HALF_TOK, 128), BF),
            pltpu.VMEM((2, HALF_TOK, HEAD_V), F32),
            pltpu.VMEM((2, HALF_TOK, HEAD_V), F32),
            pltpu.VMEM((2, HEAD_V, STATE), BF),
            pltpu.VMEM((2, 8, STATE), F32),
            pltpu.VMEM((2, HEAD_V, STATE), BF),
            pltpu.VMEM((2, 8, STATE), F32),
            pltpu.SemaphoreType.DMA((2,)),
            pltpu.SemaphoreType.DMA((2,)),
        ]
        + HALF_SCRATCH,
        compiler_params=params(7),
    )(raw, select, *tables, cot)


def linear_backward_kernel(
    p_ref,
    dy_ref,
    sv_ref,
    sn_ref,
    sel_ref,
    e_ref,
    t_ref,
    pick_ref,
    down_ref,
    x_ref,
    low_ref,
    g_ref,
    raw_ref,
    out_ref,
    gin_ref,
    gout_ref,
    dp_ref,
    qs,
    ks,
    dq,
    dk,
    dv,
    tv_s,
    tn_s,
    tv_r,
    tn_r,
    ss,
    rs,
    part,
    sib_in,
    far_in,
    end_in,
    bss,
    brs,
    bls,
    gls,
    grads,
    far_a,
    end_a,
    far_b,
    end_b,
    gss,
    grs,
):
    ring, plane = Ring(), Plane()
    loading = load(g_ref, grads, gls)
    xh = lax.axis_index("xh")
    partner = {"xh": 1 - xh}
    edge = jnp.where(xh == 0, EDGE, HALF_TOK - EDGE)
    bias1, bias2, coef = t_ref[0:1, :], t_ref[1:2, :], t_ref[2:3, :]
    barrier = pltpu.get_barrier_semaphore()
    partners = (ring.up, ring.dn, ring.sib, partner) + plane.neighbours()
    for device in partners:
        pl.semaphore_signal(barrier, inc=1, device_id=device, device_id_type=MESH)
    out_ref[: TOK // 2, :] = low_ref[...]

    def write(at, rows, total):
        out_ref[rows, :] = (x_ref[rows, :] + total).astype(BF)

    sums = rows_reduce_steps(
        ring, down_ref, 1, part, sib_in, far_in, end_in, bss, brs, bls, write
    )
    reduce = plane_reduce_steps(
        plane, grads, far_a, end_a, far_b, end_b, gss, grs, ((0, gin_ref), (48, gout_ref))
    )
    pl.semaphore_wait(barrier, len(partners))
    advance(sums)
    loading.wait()
    advance(reduce)
    small = p_ref[:, 2 * HEAD_V :]
    for j in range(2):
        qs[j] = dnn(small, pick_ref[2 * j]).astype(BF)
        ks[j] = dnn(small, pick_ref[2 * j + 1]).astype(BF)
    dk[...] = jnp.zeros_like(dk)
    dv[...] = jnp.zeros_like(dv)

    def rows_of(r):
        return slice(r * BLK, (r + 1) * BLK)

    def factors_of(vecs):
        return (dnn(vecs, e_ref[0]) + bias1, dnn(vecs, e_ref[1]) + bias2)

    def factors_back(phi_grad, one, two):
        return dnt((phi_grad * two).astype(BF), e_ref[0]) + dnt(
            (phi_grad * one).astype(BF), e_ref[1]
        )

    for j in range(2):
        head = slice(j * HEAD_V, (j + 1) * HEAD_V)
        tv = jnp.zeros((HEAD_V, STATE), F32)
        tn = jnp.zeros((1, STATE), F32)
        for r in range(NBLK):
            if r == 2:
                advance(sums)
                advance(reduce)
            queries = qs[j, rows_of(r), :]
            grads_y = dy_ref[rows_of(r), head]
            one, two = factors_of(queries)
            phi = one * two
            slot = r * BLK + lax.broadcasted_iota(jnp.int32, (BLK, 1), 0)
            seen = (slot < HALF_TOK - EDGE) & (xh == 1)
            cross_den = jnp.sum(phi * sn_ref[j, 0:1, :], axis=-1, keepdims=True)
            cross_num = dnt(phi.astype(BF), sv_ref[j])
            total = jnp.where(seen, cross_den, 0.0)
            dot = jnp.where(
                seen, jnp.sum(cross_num * grads_y.astype(F32), axis=-1, keepdims=True), 0.0
            )
            kept = []
            for s in range(r + 1):
                scores = dnt(queries, ks[j, rows_of(s), :]) * INV_ROOT
                mask = causal_mask(r * BLK, s * BLK, BLK, BLK, edge)
                kernel = jnp.where(mask, 1.0 + scores + 0.5 * scores * scores, 0.0)
                weight_grad = dnt(grads_y, p_ref[rows_of(s), head])
                total = total + jnp.sum(kernel, axis=-1, keepdims=True)
                dot = dot + jnp.sum(kernel * weight_grad, axis=-1, keepdims=True)
                kept.append((scores, mask, kernel, weight_grad))
            inverse = 1.0 / total
            mean = dot * inverse
            grads_n = (grads_y.astype(F32) * inverse).astype(BF)
            query_grad = jnp.zeros((BLK, 128), F32)
            for s in range(r + 1):
                scores, mask, kernel, weight_grad = kept[s]
                score_grad = jnp.where(
                    mask, (weight_grad - mean) * inverse * (1.0 + scores), 0.0
                ).astype(BF)
                query_grad = query_grad + dnn(score_grad, ks[j, rows_of(s), :])
                dk[j, rows_of(s), :] += dtn(score_grad, queries)
                dv[j, rows_of(s), :] += dtn(kernel.astype(BF), grads_n)
            shift = jnp.where(seen, -(mean * inverse), 0.0)
            cross_g = jnp.where(seen, grads_n, jnp.zeros_like(grads_n))
            phi_grad = dnn(cross_g, sv_ref[j]) + shift * sn_ref[j, 0:1, :]
            dq[j, rows_of(r), :] = query_grad * INV_ROOT + factors_back(phi_grad, one, two)
            tv = tv + dtn(cross_g, phi.astype(BF))
            tn = tn + jnp.sum(shift * phi, axis=0, keepdims=True)
        tv_s[j] = (tv * coef).astype(BF)
        tn_s[j] = jnp.broadcast_to(tn * coef, (8, STATE))
    copies = (
        remote(tv_s, tv_r, ss.at[0], rs.at[0], partner),
        remote(tn_s, tn_r, ss.at[1], rs.at[1], partner),
    )
    advance(sums)
    advance(reduce)
    for copy in copies:
        copy.wait_recv()
    for r in range(NBLK):
        if r == 2:
            advance(reduce)
        placed = jnp.zeros((BLK, 128), F32)
        for j in range(2):
            head = slice(j * HEAD_V, (j + 1) * HEAD_V)
            one, two = factors_of(ks[j, rows_of(r), :])
            phi = one * two
            if r == 0:
                slot = lax.broadcasted_iota(jnp.int32, (BLK, STATE), 0)
                open_rows = slot >= EDGE
                phi = jnp.where(open_rows, phi, 0.0)
            phi_grad = dnn(p_ref[rows_of(r), head], tv_r[j]) + tn_r[j, 0:1, :]
            if r == 0:
                phi_grad = jnp.where(open_rows, phi_grad, 0.0)
            key_grad = dk[j, rows_of(r), :] * INV_ROOT + factors_back(phi_grad, one, two)
            value_grad = dv[j, rows_of(r), :] + dnt(phi.astype(BF), tv_r[j])
            dp_ref[rows_of(r), head] = value_grad.astype(BF)
            placed = placed + dnt(dq[j, rows_of(r), :].astype(BF), pick_ref[2 * j])
            placed = placed + dnt(key_grad.astype(BF), pick_ref[2 * j + 1])
        dp_ref[rows_of(r), 2 * HEAD_V :] = placed.astype(BF)
        raw_ref[rows_of(r), :] = dnt(dp_ref[rows_of(r), :], sel_ref[...]).astype(BF)
    for copy in copies:
        copy.wait_send()
    finish(sums)
    finish(reduce)


def linear_backward(p1, dy, sv, sn, select, tables, down, x, low, grads):
    return pl.pallas_call(
        linear_backward_kernel,
        out_shape=(
            sds((HALF_TOK, 16 * BIN_PAD)),
            sds((TOK, D)),
            sds((48, D), F32),
            sds((16, D), F32),
        ),
        in_specs=[VM] * 8 + [ANY, VM, VM, ANY],
        out_specs=(VM,) * 4,
        scratch_shapes=[
            pltpu.VMEM((HALF_TOK, 3 * HEAD_V), BF),
            pltpu.VMEM((2, HALF_TOK, 128), BF),
            pltpu.VMEM((2, HALF_TOK, 128), BF),
            pltpu.VMEM((2, HALF_TOK, 128), F32),
            pltpu.VMEM((2, HALF_TOK, 128), F32),
            pltpu.VMEM((2, HALF_TOK, HEAD_V), F32),
            pltpu.VMEM((2, HEAD_V, STATE), BF),
            pltpu.VMEM((2, 8, STATE), F32),
            pltpu.VMEM((2, HEAD_V, STATE), BF),
            pltpu.VMEM((2, 8, STATE), F32),
            pltpu.SemaphoreType.DMA((2,)),
            pltpu.SemaphoreType.DMA((2,)),
        ]
        + ROWS_SCRATCH
        + [pltpu.SemaphoreType.DMA]
        + plane_reduce_scratch(64),
        compiler_params=params(8),
    )(p1, dy, sv, sn, select, *tables, down, x, low, grads)


WBLK = 128
WKEYS = WBLK + WINDOW
INV_ROOT_V = 1.0 / math.sqrt(HEAD_V)


def turn_tables():
    slot = np.arange(2 * HALF_TOK)
    last = 2 * HALF_TOK - EDGE
    position = slot - np.where(slot < EDGE, 0, np.where(slot < last, EDGE, last))
    frequency = np.exp(-math.log(10000.0) * np.arange(HEAD_V // 2) * 2.0 / HEAD_V)
    angles = position[:, None] * frequency[None, :]
    cosine, sine = np.cos(angles), np.sin(angles)
    pair = np.stack(
        [np.concatenate([cosine, cosine], axis=1), np.concatenate([-sine, sine], axis=1)]
    )
    return pair.reshape(2, 2, HALF_TOK, HEAD_V).transpose(1, 0, 2, 3).astype(np.float32)


def window_mask(r, edge, lowest):
    t = r * WBLK + lax.broadcasted_iota(jnp.int32, (WBLK, WKEYS), 0)
    u = r * WBLK - WINDOW + lax.broadcasted_iota(jnp.int32, (WBLK, WKEYS), 1)
    return (u <= t) & (t - u < WINDOW) & ((t >= edge) == (u >= edge)) & (u >= lowest)


def window_forward_kernel(
    h_ref,
    w_ref,
    turn_ref,
    cot_ref,
    y_ref,
    q_ref,
    kv_ref,
    hi_ref,
    h,
    w,
    turn,
    sems,
    xss,
    xrs,
    buf,
    ss,
    rs,
    ls,
):
    ring = Ring()
    xh = lax.axis_index("xh")
    partner = {"xh": 1 - xh}
    edge = jnp.where(xh == 0, EDGE, HALF_TOK - EDGE)
    lowest = jnp.where(xh == 0, 0, -WINDOW)
    loads = (
        load(w_ref.at[:, :, pl.ds(0, 48), :], w, sems.at[0]),
        load(h_ref, h, sems.at[1]),
        load(turn_ref.at[xh], turn, sems.at[2]),
    )
    barrier = pltpu.get_barrier_semaphore()
    for device in (ring.up, ring.dn, ring.sib, partner):
        pl.semaphore_signal(barrier, inc=1, device_id=device, device_id_type=MESH)
    buf[ring.z * 2 + ring.c] = cot_ref[TOK // 2 :, :]
    pl.semaphore_wait(barrier, 4)
    cots = gather_steps(ring, buf, hi_ref, ss, rs, ls, TOK // 2)
    advance(cots)
    for copy in loads:
        copy.wait()
    size = 2 * TOK
    blocks = HALF_TOK // size

    def turned(vecs, rows):
        return (
            vecs * turn[0, rows, :] + pltpu.roll(vecs, HEAD_V // 2, 1) * turn[1, rows, :]
        ).astype(BF)

    for r in (blocks - 1,) + tuple(range(blocks - 1)):
        rows = slice(r * size, (r + 1) * size)
        shifted = slice(WINDOW + r * size, WINDOW + (r + 1) * size)
        tokens = h[2 * r : 2 * r + 2].reshape(size, D)
        for j in range(2):
            mat = w[2 * j : 2 * j + 2].reshape(384, D)
            proj = dnt(tokens, mat)
            q_ref[rows, j * 128 : (j + 1) * 128] = turned(proj[:, :128], rows)
            kv_ref[shifted, j * 128 : (j + 1) * 128] = turned(proj[:, 128:256], rows)
            kv_ref[shifted, (2 + j) * 128 : (3 + j) * 128] = proj[:, 256:].astype(BF)
        if r == blocks - 1:
            copy = remote(
                kv_ref.at[pl.ds(HALF_TOK, WINDOW), :],
                kv_ref.at[pl.ds(0, WINDOW), :],
                xss,
                xrs,
                partner,
            )
    advance(cots)
    advance(cots)
    for r in tuple(range(1, HALF_TOK // WBLK)) + (0,):
        if r == 0:
            copy.wait_recv()
        rows = slice(r * WBLK, (r + 1) * WBLK)
        keys = slice(r * WBLK, r * WBLK + WKEYS)
        mask = window_mask(r, edge, lowest)
        for j in range(2):
            head = slice(j * 128, (j + 1) * 128)
            scores = dnt(q_ref[rows, head], kv_ref[keys, head]) * INV_ROOT_V
            scores = jnp.where(mask, scores, -1e30)
            exps = jnp.exp(scores - jnp.max(scores, axis=-1, keepdims=True))
            probs = exps / jnp.sum(exps, axis=-1, keepdims=True)
            y_ref[rows, head] = dnn(
                probs.astype(BF), kv_ref[keys, (2 + j) * 128 : (3 + j) * 128]
            ).astype(BF)
    copy.wait_send()
    finish(cots)


def window_forward(h, w, turns, cot):
    return pl.pallas_call(
        window_forward_kernel,
        out_shape=(
            sds((HALF_TOK, 256)),
            sds((HALF_TOK, 256)),
            sds((HALF_TOK + WINDOW, 512)),
            sds((8, TOK // 2, D)),
        ),
        in_specs=[ANY, ANY, ANY, VM],
        out_specs=(VM, VM, VM, ANY),
        scratch_shapes=[
            pltpu.VMEM((8, TOK, D), BF),
            pltpu.VMEM((4, 4, 48, D), BF),
            pltpu.VMEM((2, HALF_TOK, HEAD_V), F32),
            pltpu.SemaphoreType.DMA((3,)),
            pltpu.SemaphoreType.DMA,
            pltpu.SemaphoreType.DMA,
        ]
        + HALF_SCRATCH,
        compiler_params=params(9),
    )(h, w, turns, cot)


def window_backward_kernel(
    q_ref,
    kv_ref,
    dy_ref,
    turn_ref,
    down_ref,
    x_ref,
    dp_ref,
    low_ref,
    dkv,
    halo,
    turn,
    tls,
    ss,
    rs,
    part,
    sib_in,
    far_in,
    end_in,
    bss,
    brs,
    bls,
):
    ring = Ring()
    xh = lax.axis_index("xh")
    partner = {"xh": 1 - xh}
    turning = load(turn_ref.at[xh], turn, tls)
    edge = jnp.where(xh == 0, EDGE, HALF_TOK - EDGE)
    lowest = jnp.where(xh == 0, 0, -WINDOW)
    barrier = pltpu.get_barrier_semaphore()
    for device in (ring.up, ring.dn, ring.sib, partner):
        pl.semaphore_signal(barrier, inc=1, device_id=device, device_id_type=MESH)
    dkv[...] = jnp.zeros_like(dkv)
    blocks = HALF_TOK // WBLK

    def write(at, rows, total):
        low_ref[at, :] = (x_ref[rows, :] + total).astype(BF)

    sums = rows_reduce_steps(
        ring, down_ref, 0, part, sib_in, far_in, end_in, bss, brs, bls, write
    )
    pl.semaphore_wait(barrier, 4)
    advance(sums)
    turning.wait()

    def turned_back(r, grads):
        rows = slice(r * WBLK, (r + 1) * WBLK)
        return (
            grads * turn[0, rows, :] + pltpu.roll(grads * turn[1, rows, :], HEAD_V // 2, 1)
        ).astype(BF)

    for r in range(blocks):
        rows = slice(r * WBLK, (r + 1) * WBLK)
        keys = slice(r * WBLK, r * WBLK + WKEYS)
        mask = window_mask(r, edge, lowest)
        for j in range(2):
            head = slice(j * 128, (j + 1) * 128)
            vals = slice((2 + j) * 128, (3 + j) * 128)
            queries, grads = q_ref[rows, head], dy_ref[rows, head]
            scores = dnt(queries, kv_ref[keys, head]) * INV_ROOT_V
            scores = jnp.where(mask, scores, -1e30)
            exps = jnp.exp(scores - jnp.max(scores, axis=-1, keepdims=True))
            probs = exps / jnp.sum(exps, axis=-1, keepdims=True)
            prob_grad = dnt(grads, kv_ref[keys, vals])
            score_grad = (
                probs * (prob_grad - jnp.sum(prob_grad * probs, axis=-1, keepdims=True))
            ).astype(BF)
            dp_ref[rows, 3 * j * 128 : (3 * j + 1) * 128] = turned_back(
                r, dnn(score_grad, kv_ref[keys, head]) * INV_ROOT_V
            )
            dkv[keys, head] += dtn(score_grad, queries) * INV_ROOT_V
            dkv[keys, vals] += dtn(probs.astype(BF), grads)
        if r == 0:
            copy = remote(dkv.at[pl.ds(0, WINDOW), :], halo, ss, rs, partner)
        if r in (1, 5, blocks - 1):
            advance(sums)
    for r in range(blocks):
        rows = slice(r * WBLK, (r + 1) * WBLK)
        shifted = slice(WINDOW + r * WBLK, WINDOW + (r + 1) * WBLK)
        if r == blocks - 1:
            copy.wait_recv()
            dkv[HALF_TOK : HALF_TOK + WINDOW, :] += halo[...]
        for j in range(2):
            dp_ref[rows, (3 * j + 1) * 128 : (3 * j + 2) * 128] = turned_back(
                r, dkv[shifted, j * 128 : (j + 1) * 128]
            )
            dp_ref[rows, (3 * j + 2) * 128 : (3 * j + 3) * 128] = dkv[
                shifted, (2 + j) * 128 : (3 + j) * 128
            ].astype(BF)
    copy.wait_send()
    finish(sums)


def window_backward(q, kv, dy, turns, down, x):
    return pl.pallas_call(
        window_backward_kernel,
        out_shape=(sds((HALF_TOK, 768)), sds((TOK // 2, D))),
        in_specs=[VM, VM, VM, ANY, ANY, VM],
        out_specs=(VM, VM),
        scratch_shapes=[
            pltpu.VMEM((HALF_TOK + WINDOW, 512), F32),
            pltpu.VMEM((WINDOW, 512), F32),
            pltpu.VMEM((2, HALF_TOK, HEAD_V), F32),
            pltpu.SemaphoreType.DMA,
            pltpu.SemaphoreType.DMA,
            pltpu.SemaphoreType.DMA,
        ]
        + ROWS_SCRATCH,
        compiler_params=params(10),
    )(q, kv, dy, turns, down, x)


def padded(rows, count):
    return jnp.pad(rows, ((0, count - rows.shape[0]), (0, 0)))


def place():
    slot = lax.axis_index("xh") * HALF_TOK + jnp.arange(HALF_TOK, dtype=jnp.int32)
    last = 2 * HALF_TOK - EDGE
    segment = (slot >= EDGE).astype(jnp.int32) + (slot >= last).astype(jnp.int32)
    start = jnp.where(segment == 0, 0, jnp.where(segment == 1, EDGE, last)).astype(jnp.int32)
    return segment, slot - start


def body(
    block_input,
    cotangent,
    lengths,
    gain_a,
    based_in,
    based_out,
    gain_b,
    swa_in,
    swa_out,
    gain_c,
    mlp_in,
    mlp_down,
):
    gains = [gain.reshape(1, D) for gain in (gain_a, gain_b, gain_c)]
    units = mlp_down.shape[0]
    wide = based_in.shape[1]
    win_all = lax.all_gather(
        jnp.concatenate([swa_in.T, swa_out], axis=0), PLANE, axis=0, tiled=True
    ).reshape(4, 4, 64, D)
    ff_all = lax.all_gather(
        jnp.concatenate(
            [padded(part, UNIT_PAD) for part in (mlp_in[:, 0, :].T, mlp_in[:, 1, :].T, mlp_down)],
            axis=0,
        ),
        PLANE,
        axis=0,
        tiled=True,
    ).reshape(16, 3 * UNIT_PAD, D)
    segment, position = place()
    first = (lax.axis_index("z") * 2 + lax.axis_index("c")) * TOK
    my_segment = lax.dynamic_slice_in_dim(segment, first, TOK)
    my_position = lax.dynamic_slice_in_dim(position, first, TOK)
    chosen = jnp.where(
        my_segment == 0,
        lengths[0, 0],
        jnp.where(my_segment == 1, lengths[0, 1], lengths[0, 2]),
    )
    valid = (my_position < chosen)[:, None]
    cot_low = jnp.where(valid, cotangent, jnp.zeros_like(cotangent))
    tables = tuple(
        jnp.asarray(table, kind) for table, kind in zip(state_tables(), (BF, F32, BF))
    )
    select = jnp.asarray(select_table(wide), BF)

    turns = jnp.asarray(turn_tables())

    h1, lin_all, raw = first_step(block_input, gains[0], based_in.T, based_out)
    y1, p1, state_v, state_n, cot_lo = linear_forward(raw, select, tables, cot_low)
    x2, h2 = forward_step(y1, lin_all, BIN_PAD, block_input, gains[1], 2)
    y2, queries, key_vals, cot_hi = window_forward(h2, win_all, turns, cot_low)
    x3, h3 = forward_step(y2, win_all, 48, x2, gains[2], 3)
    act, d_gu, down = mlp_step(h3, cot_lo, cot_hi, ff_all)
    dx3, grad_c, e3, d_y2, ff_grads = mlp_back_step(
        d_gu, act, ff_all, win_all, h3, cot_lo, cot_hi, x3, gains[2], cot_low
    )
    ff_grads = lax.psum_scatter(
        ff_grads.reshape(-1, D), PLANE, scatter_dimension=0, tiled=True
    ).astype(F32)
    d_p2, out_low = window_backward(queries, key_vals, d_y2, turns, down, x3)
    dx2, grad_b, e2, d_y1, win_grads = window_back_out_step(
        d_p2, win_all, lin_all, h2, y2, e3, x2, gains[1], dx3
    )
    d_p1, block_output, grad_win_in, grad_win_out = linear_backward(
        p1, d_y1, state_v, state_n, select, tables, down, x3, out_low, win_grads
    )
    input_grad, grad_a, grad_b, grad_c, grad_lin_in, grad_lin_out = last_step(
        d_p1, lin_all, h1, y1, e2, block_input, gains[0], dx2, grad_b, grad_c, wide
    )
    gate_grad = ff_grads[:units]
    up_grad = ff_grads[UNIT_PAD : UNIT_PAD + units]
    return (
        block_output,
        input_grad,
        grad_a.reshape(D),
        grad_lin_in.T,
        grad_lin_out,
        grad_b.reshape(D),
        grad_win_in.T,
        grad_win_out,
        grad_c.reshape(D),
        jnp.stack([gate_grad.T, up_grad.T], axis=1),
        ff_grads[2 * UNIT_PAD : 2 * UNIT_PAD + units],
    )


def solution(mesh):
    grid = Mesh(mesh.devices.reshape(2, 4, 2, 4, 2), ALL)
    tokens = P(ALL, None)
    weight = ("xh", "z", "c", "xl", "y")
    rows, cols = P(weight, None), P(None, weight)
    return jax.shard_map(
        body,
        mesh=grid,
        in_specs=(
            tokens,
            tokens,
            P(("xl", "y"), None),
            P(),
            cols,
            rows,
            P(),
            cols,
            rows,
            P(),
            P(None, None, weight),
            rows,
        ),
        out_specs=(
            tokens,
            tokens,
            P(),
            cols,
            rows,
            P(),
            cols,
            rows,
            P(),
            P(None, None, weight),
            rows,
        ),
        check_vma=False,
    )
```

```python
import functools
import math
import types

import jax
import jax.numpy as jnp
import numpy as np
from jax import lax
from jax.experimental import pallas as pl
from jax.experimental.pallas import tpu as pltpu
from jax.sharding import Mesh
from jax.sharding import PartitionSpec as P

FEAT = 16
HEAD_V = 128
WINDOW = 64
EPSILON = 1e-05
D = 2048
TOK = 128
HALF_TOK = 1024
EDGE = 64
UNIT_PAD = 48
BIN_PAD = 32
STATE = 256
PLANE = ("xh", "xl", "y")
RING = ("z", "c")
ALL = ("xl", "y", "xh", "z", "c")
MESH = pl.DeviceIdType.MESH
BF = jnp.bfloat16
F32 = jnp.float32
VM = pl.BlockSpec(memory_space=pltpu.VMEM)
ANY = pl.BlockSpec(memory_space=pl.ANY)


def dnn(a, b):
    return lax.dot_general(a, b, (((1,), (0,)), ((), ())), preferred_element_type=F32)


def dnt(a, b):
    return lax.dot_general(a, b, (((1,), (1,)), ((), ())), preferred_element_type=F32)


def dtn(a, b):
    return lax.dot_general(a, b, (((0,), (0,)), ((), ())), preferred_element_type=F32)


def remote(src, dst, send_sem, recv_sem, device):
    copy = pltpu.make_async_remote_copy(
        src_ref=src,
        dst_ref=dst,
        send_sem=send_sem,
        recv_sem=recv_sem,
        device_id=device,
        device_id_type=MESH,
    )
    copy.start()
    return copy


def greet(devices):
    barrier = pltpu.get_barrier_semaphore()
    for device in devices:
        pl.semaphore_signal(barrier, inc=1, device_id=device, device_id_type=MESH)
    pl.semaphore_wait(barrier, len(devices))


class Ring:
    def __init__(self):
        self.z = lax.axis_index("z")
        self.c = lax.axis_index("c")
        self.oc = 1 - self.c
        self.zp = lax.rem(self.z + 1, 4)
        self.zm = lax.rem(self.z + 3, 4)
        self.zz = lax.rem(self.z + 2, 4)
        self.up = {"z": self.zp}
        self.dn = {"z": self.zm}
        self.sib = {"c": self.oc}

    def greet(self):
        greet((self.up, self.dn, self.sib))


class Plane:
    def __init__(self):
        self.x = lax.axis_index("xh") * 2 + lax.axis_index("xl")
        self.y = lax.axis_index("y")

    def at_x(self, x):
        return {"xh": lax.div(x, 2), "xl": lax.rem(x, 2)}

    def at_y(self, y):
        return {"y": y}

    def ring(self, along_x):
        me = self.x if along_x else self.y
        plus, minus, far = lax.rem(me + 1, 4), lax.rem(me + 3, 4), lax.rem(me + 2, 4)
        to = self.at_x if along_x else self.at_y
        return me, plus, minus, far, to(plus), to(minus)

    def neighbours(self):
        xs, ys = self.ring(True), self.ring(False)
        return (xs[4], xs[5], ys[4], ys[5])


def finish(steps):
    for _ in steps:
        pass


def advance(steps):
    next(steps, None)


def weave(main, *others):
    for _ in main:
        for other in others:
            advance(other)


CHUNKS = 2


def gather_steps(ring, buf, out_ref, ss, rs, ls, rows, start=0, base=0, keep=True, ready=None):
    half = rows // 2
    me = ring.z * 2 + ring.c
    below, above, far = ring.zm * 2 + ring.c, ring.zp * 2 + ring.c, ring.zz * 2 + ring.c

    def send(slot, part, device, index):
        piece = buf.at[slot, pl.ds(start + part * half, half), :]
        return remote(piece, piece, ss.at[base + index], rs.at[base + index], device)

    local = []

    def save(slot):
        if keep:
            copy = pltpu.make_async_copy(buf.at[slot], out_ref.at[slot], ls.at[len(local)])
            copy.start()
            local.append(copy)

    def done(chip):
        if ready is not None:
            ready(chip)

    up, dn, sib = ring.up, ring.dn, ring.sib
    cp = {}
    cp[0] = send(me, 0, up, 0)
    cp[1] = send(me, 1, dn, 1)
    cp[2] = send(me, 1, up, 2)
    cp[3] = send(me, 0, dn, 3)
    cp[4] = send(me, 0, sib, 4)
    cp[5] = send(me, 1, sib, 5)
    save(me)
    yield
    cp[0].wait_recv()
    cp[6] = send(below, 0, up, 6)
    cp[8] = send(below, 0, sib, 8)
    cp[1].wait_recv()
    cp[7] = send(above, 1, dn, 7)
    cp[9] = send(above, 1, sib, 9)
    yield
    cp[2].wait_recv()
    cp[10] = send(below, 1, sib, 10)
    save(below)
    cp[3].wait_recv()
    cp[11] = send(above, 0, sib, 11)
    save(above)
    yield
    cp[4].wait_recv()
    cp[5].wait_recv()
    save(ring.z * 2 + ring.oc)
    done(ring.z)
    cp[8].wait_recv()
    cp[10].wait_recv()
    save(ring.zm * 2 + ring.oc)
    done(ring.zm)
    yield
    cp[6].wait_recv()
    cp[12] = send(far, 0, sib, 12)
    cp[7].wait_recv()
    cp[13] = send(far, 1, sib, 13)
    save(far)
    cp[9].wait_recv()
    cp[11].wait_recv()
    save(ring.zp * 2 + ring.oc)
    done(ring.zp)
    yield
    cp[12].wait_recv()
    cp[13].wait_recv()
    save(ring.zz * 2 + ring.oc)
    done(ring.zz)
    for index in range(14):
        cp[index].wait_send()
    for copy in local:
        copy.wait()


def scatter_steps(ring, product, part, sib_in, far_in, end_in, ss, rs, ready):
    rows = TOK // CHUNKS
    half = rows // 2
    c, oc = ring.c, ring.oc
    up, dn, sib = ring.up, ring.dn, ring.sib
    order = (ring.zz, ring.zp, ring.zm, ring.z)
    step = 512
    cp = {}

    def send(q, index, src, dst, device):
        n = q * 10 + index
        cp[q, index] = remote(src, dst, ss.at[n], rs.at[n], device)

    def multiply(index):
        row = pl.multiple_of(order[index] * (2 * TOK), 2 * TOK)

        def one(n, carry):
            col = pl.ds(pl.multiple_of(n * step, step), step)
            res = product(pl.ds(row, 2 * TOK), col).astype(BF)
            part[index, 0, :, col] = res[:TOK]
            part[index, 1, :, col] = res[TOK:]
            return carry

        lax.fori_loop(0, D // step, one, 0)
        for q in range(CHUNKS):
            at = pl.ds(q * rows, rows)
            send(q, index, part.at[index, oc, at, :], sib_in.at[index, at, :], sib)

    def add(index, first, count, other):
        def one(i, carry):
            at = pl.ds(pl.multiple_of(first + i * 16, 16), 16)
            part[index, c, at, :] = (part[index, c, at, :].astype(F32) + other(at)).astype(BF)
            return carry

        lax.fori_loop(0, count // 16, one, 0)

    def add_sib(q, index):
        cp[q, index].wait_recv()
        add(index, q * rows, rows, lambda at: sib_in[index, at, :].astype(F32))

    def piece(q, which):
        return pl.ds(q * rows + which * half, half)

    def far(q):
        add_sib(q, 0)
        send(q, 4, part.at[0, c, piece(q, 0), :], far_in.at[piece(q, 0), :], up)
        send(q, 5, part.at[0, c, piece(q, 1), :], far_in.at[piece(q, 1), :], dn)

    def near(q):
        add_sib(q, 1)
        send(q, 6, part.at[1, c, piece(q, 1), :], end_in.at[0, piece(q, 1), :], up)
        add_sib(q, 2)
        send(q, 7, part.at[2, c, piece(q, 0), :], end_in.at[1, piece(q, 0), :], dn)

    def passed(q):
        for which, device in ((0, up), (1, dn)):
            cp[q, 4 + which].wait_recv()
            at = piece(q, which)
            add(1 + which, q * rows + which * half, half, lambda at: far_in[at, :].astype(F32))
            send(q, 8 + which, part.at[1 + which, c, at, :], end_in.at[which, at, :], device)

    multiply(0)
    multiply(1)
    far(0)
    for q in range(1, CHUNKS):
        far(q)
    yield
    multiply(2)
    near(0)
    multiply(3)
    yield
    passed(0)
    for q in range(1, CHUNKS):
        near(q)
    yield
    for q in range(1, CHUNKS):
        passed(q)
    for q in range(CHUNKS):
        add_sib(q, 3)
        for index in range(6, 10):
            cp[q, index].wait_recv()
        ready(q)
        yield
    for copy in cp.values():
        copy.wait_send()


def rows_reduce_steps(ring, src_ref, q, part, sib_in, far_in, end_in, ss, rs, ls, ready):
    rows = TOK // CHUNKS
    half = rows // 2
    order = (ring.zz, ring.zp, ring.zm, ring.z)
    up, dn, sib = ring.up, ring.dn, ring.sib
    cp, loads = {}, []

    def send(index, src, dst, device):
        cp[index] = remote(src, dst, ss.at[index], rs.at[index], device)

    def source(index, core):
        start = order[index] * (2 * TOK) + core * TOK + q * rows
        return src_ref.at[pl.ds(pl.multiple_of(start, 16), rows), :]

    def add(index, first, count, other):
        def one(i, carry):
            at = pl.ds(pl.multiple_of(first + i * 16, 16), 16)
            part[index, at, :] = (part[index, at, :].astype(F32) + other(at)).astype(BF)
            return carry

        lax.fori_loop(0, count // 16, one, 0)

    def add_sib(index):
        loads[index].wait()
        cp[index].wait_recv()
        add(index, 0, rows, lambda at: sib_in[index, at, :].astype(F32))

    low, high = pl.ds(0, half), pl.ds(half, half)
    for index in range(4):
        send(index, source(index, ring.oc), sib_in.at[index], sib)
        loads.append(load(source(index, ring.c), part.at[index], ls.at[index]))
    yield
    add_sib(0)
    send(4, part.at[0, low, :], far_in.at[low, :], up)
    send(5, part.at[0, high, :], far_in.at[high, :], dn)
    add_sib(1)
    send(6, part.at[1, high, :], end_in.at[0, high, :], up)
    add_sib(2)
    send(7, part.at[2, low, :], end_in.at[1, low, :], dn)
    add_sib(3)
    yield
    for which, device in ((0, up), (1, dn)):
        cp[4 + which].wait_recv()
        at = (low, high)[which]
        add(1 + which, which * half, half, lambda at: far_in[at, :].astype(F32))
        send(8 + which, part.at[1 + which, at, :], end_in.at[which, at, :], device)
    yield
    for index in range(6, 10):
        cp[index].wait_recv()

    def total(i, carry):
        at = pl.ds(pl.multiple_of(i * 16, 16), 16)
        ready(
            at,
            pl.ds(pl.multiple_of(q * rows + i * 16, 16), 16),
            part[3, at, :].astype(F32)
            + end_in[0, at, :].astype(F32)
            + end_in[1, at, :].astype(F32),
        )
        return carry

    lax.fori_loop(0, rows // 16, total, 0)
    for copy in cp.values():
        copy.wait_send()


ROWS_SCRATCH = {
    "bpart": pltpu.VMEM((4, TOK // CHUNKS, D), BF),
    "bsib": pltpu.VMEM((4, TOK // CHUNKS, D), BF),
    "bfar": pltpu.VMEM((TOK // CHUNKS, D), BF),
    "bend": pltpu.VMEM((2, TOK // CHUNKS, D), BF),
    "bss": pltpu.SemaphoreType.DMA((10,)),
    "brs": pltpu.SemaphoreType.DMA((10,)),
    "bls": pltpu.SemaphoreType.DMA((4,)),
}
SCATTER_SCRATCH = {
    "part": pltpu.VMEM((4, 2, TOK, D), BF),
    "sib_in": pltpu.VMEM((4, TOK, D), BF),
    "far_in": pltpu.VMEM((TOK, D), BF),
    "end_in": pltpu.VMEM((2, TOK, D), BF),
    "sss": pltpu.SemaphoreType.DMA((10 * CHUNKS,)),
    "srs": pltpu.SemaphoreType.DMA((10 * CHUNKS,)),
}
GATHER_SCRATCH = {
    "buf": pltpu.VMEM((8, TOK, D), BF),
    "ss": pltpu.SemaphoreType.DMA((14 * CHUNKS,)),
    "rs": pltpu.SemaphoreType.DMA((14 * CHUNKS,)),
    "ls": pltpu.SemaphoreType.DMA((8,)),
}
HALF_SCRATCH = {
    "cbuf": pltpu.VMEM((8, TOK // 2, D), BF),
    "css": pltpu.SemaphoreType.DMA((14,)),
    "crs": pltpu.SemaphoreType.DMA((14,)),
    "cls": pltpu.SemaphoreType.DMA((8,)),
}


def plane_view(plane, ref, half, stage, place, part):
    cols = pl.ds(half * (D // 2) + (part or 0) * (D // 4), D // 2 if part is None else D // 4)
    if stage == 0:
        return ref.at[place, plane.y, :, cols] if half == 0 else ref.at[plane.x, place, :, cols]
    return ref.at[:, place, :, cols] if half == 0 else ref.at[place, :, :, cols]


def plane_gather_steps(plane, buf, ss, rs):
    copies = []
    quarter = D // 4

    def view(half, first, second, part):
        x, y = (first, second) if half == 0 else (second, first)
        cols = pl.ds(half * 2 * quarter + (part or 0) * quarter, quarter if part is not None else 2 * quarter)
        return buf.at[x, y, :, cols]

    def send(ref, device):
        copies.append(remote(ref, ref, ss.at[len(copies)], rs.at[len(copies)], device))
        return copies[-1]

    firsts = [plane.ring(half == 0) for half in (0, 1)]
    seconds = [plane.ring(half == 1) for half in (0, 1)]
    near, passed, spread = {}, {}, {}

    def go_on(half, place):
        me, plus, minus, far, to_plus, to_minus = seconds[half]
        piece = view(half, place, me, None)
        spread[half, len(spread)] = (place, send(piece, to_plus), send(piece, to_minus))

    def pass_on(entry):
        half, (place, up, dn) = entry
        me, plus, minus, far, to_plus, to_minus = seconds[half]
        up.wait_recv()
        send(view(half, place, minus, 0), to_plus)
        dn.wait_recv()
        send(view(half, place, plus, 1), to_minus)

    for half in (0, 1):
        me, plus, minus, far, to_plus, to_minus = firsts[half]
        piece = view(half, me, seconds[half][0], None)
        near[half] = (send(piece, to_plus), send(piece, to_minus))
    for half in (0, 1):
        go_on(half, firsts[half][0])
    yield
    for half in (0, 1):
        me, plus, minus, far, to_plus, to_minus = firsts[half]
        other = seconds[half][0]
        near[half][0].wait_recv()
        up = send(view(half, minus, other, 0), to_plus)
        near[half][1].wait_recv()
        passed[half] = (up, send(view(half, plus, other, 1), to_minus))
    for half in (0, 1):
        go_on(half, firsts[half][2])
        go_on(half, firsts[half][1])
    yield
    for half in (0, 1):
        passed[half][0].wait_recv()
        passed[half][1].wait_recv()
        go_on(half, firsts[half][3])
    entries = [(key[0], value) for key, value in spread.items()]
    for entry in entries[:2]:
        pass_on(entry)
    yield
    for entry in entries[2:]:
        pass_on(entry)
    yield
    for copy in copies[-2 * len(entries) :]:
        copy.wait_recv()
    for copy in copies:
        copy.wait_send()


GATHER_COPIES = 40


def plane_reduce_scratch(name, rows):
    return {
        name: pltpu.VMEM((4, 4, rows, D), BF),
        name + "_far": pltpu.VMEM((2, 2, 4, rows, D // 4), BF),
        name + "_end": pltpu.VMEM((2, 2, 4, rows, D // 2), BF),
        name + "_far2": pltpu.VMEM((2, 2, rows, D // 4), BF),
        name + "_end2": pltpu.VMEM((2, 2, rows, D // 2), BF),
        name + "_ss": pltpu.SemaphoreType.DMA((24,)),
        name + "_rs": pltpu.SemaphoreType.DMA((24,)),
    }


def plane_reduce(plane, r, name, outs):
    refs = [getattr(r, name + end) for end in ("", "_far", "_end", "_far2", "_end2", "_ss", "_rs")]
    return plane_reduce_steps(plane, *refs, outs)


def plane_reduce_steps(plane, grads, far_a, end_a, far_b, end_b, ss, rs, outs):
    copies = []
    rows = grads.shape[2]

    def send(src, dst, device):
        copies.append(remote(src, dst, ss.at[len(copies)], rs.at[len(copies)], device))
        return copies[-1]

    def add(view, *others):
        def one(i, carry):
            at = pl.ds(pl.multiple_of(i * 16, 16), 16)
            piece = view.at[..., at, :]
            total = piece[...].astype(F32)
            for other in others:
                total = total + other.at[..., at, :][...].astype(F32)
            piece[...] = total.astype(BF)
            return carry

        lax.fori_loop(0, rows // 16, one, 0)

    for stage in (0, 1):
        rings = [plane.ring(half != stage) for half in (0, 1)]
        far_in, end_in = (far_a, end_a) if stage == 0 else (far_b, end_b)

        def view(half, place, part):
            return plane_view(plane, grads, half, 1 - stage, place, part)

        def ends(half, side, part):
            if part is None:
                return end_in.at[half, side]
            return end_in.at[half, side, ..., pl.ds(part * (D // 4), D // 4)]

        first, last = [], []
        for half in (0, 1):
            me, plus, minus, far, to_plus, to_minus = rings[half]
            first.append(
                (
                    send(view(half, far, 0), far_in.at[half, 0], to_plus),
                    send(view(half, far, 1), far_in.at[half, 1], to_minus),
                )
            )
            last.append(send(view(half, plus, 1), ends(half, 0, 1), to_plus))
            last.append(send(view(half, minus, 0), ends(half, 1, 0), to_minus))
        yield
        for half in (0, 1):
            me, plus, minus, far, to_plus, to_minus = rings[half]
            first[half][0].wait_recv()
            add(view(half, plus, 0), far_in.at[half, 0])
            last.append(send(view(half, plus, 0), ends(half, 0, 0), to_plus))
            first[half][1].wait_recv()
            add(view(half, minus, 1), far_in.at[half, 1])
            last.append(send(view(half, minus, 1), ends(half, 1, 1), to_minus))
        yield
        for copy in last:
            copy.wait_recv()
        for half in (0, 1):
            me = rings[half][0]
            if stage == 0:
                add(view(half, me, None), ends(half, 0, None), ends(half, 1, None))
            else:
                cols = pl.ds(half * (D // 2), D // 2)
                total = (
                    view(half, me, None)[...].astype(F32)
                    + end_in[half, 0].astype(F32)
                    + end_in[half, 1].astype(F32)
                )
                for start, out_ref in outs:
                    out_ref[:, cols] = total[start : start + out_ref.shape[0]]
        yield
    for copy in copies:
        copy.wait_send()


def load(src, dst, sem):
    copy = pltpu.make_async_copy(src, dst, sem)
    copy.start()
    return copy


def params(collective_id, limit=58):
    return pltpu.CompilerParams(
        collective_id=collective_id, has_side_effects=True, vmem_limit_bytes=limit << 20
    )


def sds(shape, dtype=BF):
    return jax.ShapeDtypeStruct(shape, dtype)


def scale_of(rows):
    return lax.rsqrt(jnp.mean(rows * rows, axis=-1, keepdims=True) + EPSILON)


def by_rows(one, start=0, rows=TOK):
    def step(i, carry):
        one(pl.ds(pl.multiple_of(start + i * 16, 16), 16))
        return carry

    lax.fori_loop(0, rows // 16, step, 0)


def total_rows(part, end_in, c, at):
    return (
        part[3, c, at, :].astype(F32)
        + end_in[0, at, :].astype(F32)
        + end_in[1, at, :].astype(F32)
    )


def chip_rows(chip):
    return pl.ds(pl.multiple_of(chip * (2 * TOK), 2 * TOK), 2 * TOK)


def build(body, inputs, outputs, scratch, collective_id):
    names = list(inputs) + list(outputs) + list(scratch)

    def kernel(*refs):
        body(types.SimpleNamespace(**dict(zip(names, refs))))

    results = pl.pallas_call(
        kernel,
        out_shape=tuple(shape for shape, _ in outputs.values()),
        in_specs=[spec for _, spec in inputs.values()],
        out_specs=tuple(spec for _, spec in outputs.values()),
        scratch_shapes=list(scratch.values()),
        compiler_params=params(collective_id),
    )(*[array for array, _ in inputs.values()])
    return types.SimpleNamespace(**dict(zip(outputs, results)))


def vm(array):
    return (array, VM)


def hbm(array):
    return (array, ANY)


def signal(partners):
    barrier = pltpu.get_barrier_semaphore()
    for device in partners:
        pl.semaphore_signal(barrier, inc=1, device_id=device, device_id_type=MESH)


def arrive(partners):
    pl.semaphore_wait(pltpu.get_barrier_semaphore(), len(partners))


def scatter(ring, r, product, ready):
    return scatter_steps(
        ring, product, r.part, r.sib_in, r.far_in, r.end_in, r.sss, r.srs, ready
    )


def scatter_gather(ring, r, product, one, out_ref, done=None, others=()):
    rows = TOK // CHUNKS
    gathers = []

    def ready(q):
        by_rows(one, q * rows, rows)
        last = q == CHUNKS - 1
        steps = gather_steps(
            ring,
            r.buf,
            out_ref,
            r.ss,
            r.rs,
            r.ls,
            rows,
            start=q * rows,
            base=14 * q,
            keep=last,
            ready=done if last else None,
        )
        advance(steps)
        gathers.append(steps)

    weave(scatter(ring, r, product, ready), *others)
    for _ in range(5):
        for steps in gathers:
            advance(steps)
        for other in others:
            advance(other)
    for steps in gathers:
        finish(steps)


def sums_of(r, ring, at):
    return total_rows(r.part, r.end_in, ring.c, at)


def half_gather(ring, r, out_ref):
    return gather_steps(ring, r.cbuf, out_ref, r.css, r.crs, r.cls, TOK // 2)


def rows_reduce(ring, r, q, ready):
    return rows_reduce_steps(
        ring, r.down, q, r.bpart, r.bsib, r.bfar, r.bend, r.bss, r.brs, r.bls, ready
    )


def norm_into(r, ring, x_ref, gain_ref, at, rows):
    r.buf[ring.z * 2 + ring.c, at, :] = (rows * scale_of(rows) * gain_ref[...]).astype(BF)


def first_body(r):
    ring, plane = Ring(), Plane()
    partners = (ring.up, ring.dn, ring.sib) + plane.neighbours()
    signal(partners)
    r.wide[plane.x, plane.y, BIN_PAD // 2 : BIN_PAD, :] = jnp.zeros((BIN_PAD // 2, D), BF)
    r.wide[plane.x, plane.y, : r.rows_in.shape[0], :] = r.rows_in[...]
    r.wide[plane.x, plane.y, BIN_PAD:, :] = r.rows_out[...]

    def one(at):
        rows = r.x[at, :].astype(F32)
        norm_into(r, ring, r.x, r.gain, at, rows)

    by_rows(one)
    arrive(partners)
    weights = plane_gather_steps(plane, r.wide, r.wss, r.wrs)
    rows = gather_steps(ring, r.buf, r.h, r.ss, r.rs, r.ls, TOK)
    advance(weights)
    advance(rows)
    advance(weights)
    advance(weights)
    advance(rows)
    advance(rows)
    advance(weights)
    finish(rows)
    finish(weights)
    keep = load(r.wide, r.w, r.wls)

    def project(i, carry):
        at = pl.ds(pl.multiple_of(i * 256, 256), 256)
        h = r.buf[pl.ds(2 * i, 2)].reshape(256, D)
        w = r.wide[:, :, :BIN_PAD, :].reshape(16 * BIN_PAD, D)
        r.raw[at, :] = dnt(h, w).astype(BF)
        return carry

    lax.fori_loop(0, 4, project, 0)
    keep.wait()


def first_step(x, gain, rows_in, rows_out):
    return build(
        first_body,
        {"x": vm(x), "gain": vm(gain), "rows_in": vm(rows_in), "rows_out": vm(rows_out)},
        {
            "h": (sds((8, TOK, D)), ANY),
            "w": (sds((4, 4, BIN_PAD + 16, D)), ANY),
            "raw": (sds((HALF_TOK, 16 * BIN_PAD)), VM),
        },
        {
            "wide": pltpu.VMEM((4, 4, BIN_PAD + 16, D), BF),
            "wss": pltpu.SemaphoreType.DMA((GATHER_COPIES,)),
            "wrs": pltpu.SemaphoreType.DMA((GATHER_COPIES,)),
            "wls": pltpu.SemaphoreType.DMA,
        }
        | GATHER_SCRATCH,
        1,
    )


def ring_forward(r, ring, y_ref, w_ref, others=()):
    def product(rows, col):
        return dnn(y_ref[rows, :], w_ref[:, :, :, col].reshape(256, -1))

    def one(at):
        rows = r.x[at, :].astype(F32) + sums_of(r, ring, at)
        r.x_out[at, :] = rows
        norm_into(r, ring, r.x, r.gain, at, rows)

    scatter_gather(ring, r, product, one, r.h_out, others=others)


def norm_back_rows(v_ref, gain_ref, grads, at):
    rows = v_ref[at, :].astype(F32)
    scale = scale_of(rows)
    unit = rows * scale
    scaled = grads * gain_ref[...]
    return scale * (scaled - unit * jnp.mean(scaled * unit, axis=-1, keepdims=True))


def ring_backward(r, ring, product, wo_ref, others):
    def one(at):
        grad = sums_of(r, ring, at)
        rows = r.res[at, :].astype(F32) + norm_back_rows(r.v, r.gain, grad, at)
        r.d_out[at, :] = rows
        r.buf[ring.z * 2 + ring.c, at, :] = rows.astype(BF)

    def done(chip):
        r.dy_out[chip_rows(chip), :] = dnt(
            r.buf[pl.ds(2 * chip, 2)].reshape(2 * TOK, D), wo_ref[...].reshape(256, D)
        ).astype(BF)

    scatter_gather(ring, r, product, one, r.e_out, done, others)


CHUNK = 8 * UNIT_PAD


def mlp_forward(r, copies):
    copies["h"].wait()
    copies["lo"].wait()
    copies["hi"].wait()
    for i in range(2):
        for name in ("gate", "up", "down"):
            copies[name, i].wait()
        units = slice(8 * i, 8 * i + 8)

        def one(n, carry):
            at = chip_rows(n)
            tokens = pl.ds(2 * n, 2)
            rows = r.hv[tokens].reshape(2 * TOK, D)
            gate = dnt(rows, r.wv[0, units].reshape(CHUNK, D))
            up = dnt(rows, r.wv[1, units].reshape(CHUNK, D))
            d_act = dnt(r.cotv[tokens].reshape(2 * TOK, D), r.downv[units].reshape(CHUNK, D))
            sig = 1.0 / (1.0 + jnp.exp(-gate))
            silu = gate * sig
            r.act[at, i * CHUNK : (i + 1) * CHUNK] = (silu * up).astype(BF)
            r.d_gu[at, i * CHUNK : (i + 1) * CHUNK] = (
                d_act * up * (sig * (1.0 + gate * (1.0 - sig)))
            ).astype(BF)
            r.d_gu[at, (2 + i) * CHUNK : (3 + i) * CHUNK] = (d_act * silu).astype(BF)
            return carry

        lax.fori_loop(0, 4, one, 0)


def mlp_down_steps(r):
    for n in range(4):
        at = slice(2 * TOK * n, 2 * TOK * (n + 1))
        for col in range(0, D, 512):
            r.outv[at, col : col + 512] = dnn(
                r.act[at, :], r.downv[:, :, col : col + 512].reshape(2 * CHUNK, 512)
            ).astype(BF)
        if n == 1:
            yield
    copy = load(r.outv, r.down, r.msem.at[9])
    yield
    copy.wait()


def mlp_grad_steps(r, jobs):
    copies = []
    for n, (lhs, col, rhs, off, half, w) in enumerate(jobs):
        slot = n % 2
        if n >= 2:
            copies[n - 2].wait()

        def one(k, carry):
            cols = pl.ds(pl.multiple_of(k * 512, 512), 512)
            res = dtn(lhs[:, col : col + CHUNK], rhs[:, :, cols].reshape(HALF_TOK, 512))
            r.stage[slot, :, :, cols] = res.astype(BF).reshape(8, UNIT_PAD, 512)
            if w is not None:
                own = w[8 * half : 8 * half + 8, :, cols].reshape(CHUNK, 512).astype(F32)
                r.gacc[:, cols] += jnp.sum(res * own, axis=0, keepdims=True)
            return carry

        lax.fori_loop(0, 4, one, 0)
        copies.append(
            load(
                r.stage.at[slot],
                r.grads.at[pl.ds(8 * half, 8), pl.ds(off, UNIT_PAD), :],
                r.gsem.at[n],
            )
        )
        yield
    copies[-2].wait()
    copies[-1].wait()


def mlp_body(r):
    ring = Ring()
    partners = (ring.up, ring.dn, ring.sib)
    copies = {"h": load(r.h, r.hv, r.msem.at[0])}
    for n, (name, ref) in enumerate((("gate", r.wv.at[0]), ("up", r.wv.at[1]), ("down", r.downv))):
        for i in range(2):
            copies[name, i] = load(
                r.w.at[pl.ds(8 * i, 8), pl.ds(n * UNIT_PAD, UNIT_PAD), :],
                ref.at[pl.ds(8 * i, 8)],
                r.msem.at[3 + 2 * n + i],
            )
        if n == 0:
            copies["lo"] = load(r.lo, r.cotv.at[:, pl.ds(0, TOK // 2), :], r.msem.at[1])
            copies["hi"] = load(r.hi, r.cotv.at[:, pl.ds(TOK // 2, TOK // 2), :], r.msem.at[2])
    late = load(r.wo.at[:, :, pl.ds(48, 16), :], r.wov, r.msem.at[10])
    signal(partners)
    r.gacc[...] = jnp.zeros_like(r.gacc)
    mlp_forward(r, copies)
    late.wait()
    arrive(partners)

    def product(rows, col):
        return dnn(r.d_gu[rows, :], r.wv[:, :, :, col].reshape(4 * CHUNK, -1))

    def weights():
        yield from mlp_down_steps(r)
        jobs = [
            (r.d_gu, n * CHUNK, r.hv, (n // 2) * UNIT_PAD, n % 2, r.wv.at[n // 2])
            for n in range(4)
        ]
        jobs += [(r.act, n * CHUNK, r.cotv, 2 * UNIT_PAD, n, None) for n in range(2)]
        yield from mlp_grad_steps(r, jobs)

    weight_grads = weights()
    ring_backward(r, ring, product, r.wov, (weight_grads,))
    finish(weight_grads)
    r.gain_out[...] = r.gacc[...] / r.gain[...]


def mlp_step(h, lo, hi, w, wo, v, gain, cot):
    return build(
        mlp_body,
        {
            "h": hbm(h),
            "lo": hbm(lo),
            "hi": hbm(hi),
            "w": hbm(w),
            "wo": hbm(wo),
            "v": vm(v),
            "gain": vm(gain),
            "res": vm(cot),
        },
        {
            "down": (sds((HALF_TOK, D)), ANY),
            "d_out": (sds((TOK, D), F32), VM),
            "gain_out": (sds((1, D), F32), VM),
            "e_out": (sds((8, TOK, D)), ANY),
            "dy_out": (sds((HALF_TOK, 256)), VM),
            "grads": (sds((16, 3 * UNIT_PAD, D)), ANY),
        },
        {
            "hv": pltpu.VMEM((8, TOK, D), BF),
            "cotv": pltpu.VMEM((8, TOK, D), BF),
            "wv": pltpu.VMEM((2, 16, UNIT_PAD, D), BF),
            "downv": pltpu.VMEM((16, UNIT_PAD, D), BF),
            "wov": pltpu.VMEM((4, 4, 16, D), BF),
            "act": pltpu.VMEM((HALF_TOK, 2 * CHUNK), BF),
            "d_gu": pltpu.VMEM((HALF_TOK, 4 * CHUNK), BF),
            "outv": pltpu.VMEM((HALF_TOK, D), BF),
            "stage": pltpu.VMEM((2, 8, UNIT_PAD, D), BF),
            "gacc": pltpu.VMEM((1, D), F32),
            "msem": pltpu.SemaphoreType.DMA((11,)),
            "gsem": pltpu.SemaphoreType.DMA((6,)),
        }
        | SCATTER_SCRATCH
        | GATHER_SCRATCH,
        4,
    )


def state_tables():
    first = np.zeros((128, STATE), np.float32)
    second = np.zeros((128, STATE), np.float32)
    bias = np.zeros((8, STATE), np.float32)
    coef = np.zeros((8, STATE), np.float32)
    bias[0, 0] = bias[1, 0] = 1.0
    coef[0, 0] = 1.0
    at = 1
    for i in range(FEAT):
        first[i, at] = 1.0
        bias[1, at] = 1.0
        coef[0, at] = 1.0 / math.sqrt(FEAT)
        at += 1
    for i in range(FEAT):
        for j in range(i, FEAT):
            first[i, at] = 1.0
            second[j, at] = 1.0
            coef[0, at] = (0.5 if i == j else 1.0) / FEAT
            at += 1
    picks = np.zeros((4, 128, 128), np.float32)
    for which in range(4):
        for i in range(FEAT):
            picks[which, which * FEAT + i, i] = 1.0
    return (
        np.stack([first, second]),
        np.concatenate([bias[:2], coef[:1], np.zeros((5, STATE), np.float32)]),
        picks,
    )


def select_table(width):
    table = np.zeros((16 * BIN_PAD, 3 * HEAD_V), np.float32)
    for shard in range(16):
        for i in range(width):
            head, col = shard // 8, (shard % 8) * width + i
            to = 2 * HEAD_V + 2 * FEAT * head + col if col < 2 * FEAT else head * HEAD_V + col - 2 * FEAT
            table[shard * BIN_PAD + i, to] = 1.0
    return table


BLK = 256
NBLK = HALF_TOK // BLK
INV_ROOT = 1.0 / math.sqrt(FEAT)


def rows_of(b):
    return slice(b * BLK, (b + 1) * BLK)


def head_of(j):
    return slice(j * HEAD_V, (j + 1) * HEAD_V)


def causal_mask(start, edge):
    t = start + lax.broadcasted_iota(jnp.int32, (BLK, BLK), 0)
    u = start + lax.broadcasted_iota(jnp.int32, (BLK, BLK), 1)
    return (u <= t) & ((t >= edge) == (u >= edge))


class Linear:
    def __init__(self, r):
        self.r = r
        self.xh = lax.axis_index("xh")
        self.partner = {"xh": 1 - self.xh}
        self.edge = jnp.where(self.xh == 0, EDGE, HALF_TOK - EDGE)
        self.second = jnp.where(self.xh == 1, 1.0, 0.0)
        self.coef = r.t[2:3, :]

    def vectors(self):
        r = self.r
        small = r.p[:, 2 * HEAD_V :]
        for j in range(2):
            r.qs[j] = dnn(small, r.pick[2 * j]).astype(BF)
            r.ks[j] = dnn(small, r.pick[2 * j + 1]).astype(BF)

    def factors(self, vecs):
        r = self.r
        return dnn(vecs, r.e[0]) + r.t[0:1, :], dnn(vecs, r.e[1]) + r.t[1:2, :]

    def factors_back(self, grad, one, two):
        r = self.r
        return dnt((grad * two).astype(BF), r.e[0]) + dnt((grad * one).astype(BF), r.e[1])

    def key_open(self, width):
        slot = lax.broadcasted_iota(jnp.int32, (BLK, width), 0)
        return (slot >= EDGE) | (self.xh == 1)

    def sees_state(self, b, width):
        slot = b * BLK + lax.broadcasted_iota(jnp.int32, (BLK, width), 0)
        return (slot < HALF_TOK - EDGE) | (self.xh == 0)

    def scores(self, j, b):
        r = self.r
        scores = dnt(r.qs[j, rows_of(b), :], r.ks[j, rows_of(b), :]) * INV_ROOT
        mask = causal_mask(b * BLK, self.edge)
        return scores, mask, jnp.where(mask, 1.0 + scores + 0.5 * scores * scores, 0.0)


def linear_forward_part(r, ring, cots):
    lin = Linear(r)
    for b in range(NBLK):
        r.p[rows_of(b), :] = dnn(r.raw[rows_of(b), :], r.sel[...]).astype(BF)
    lin.vectors()
    for j in range(2):
        sv = jnp.zeros((HEAD_V, STATE), F32)
        sn = jnp.zeros((1, STATE), F32)
        for b in range(NBLK):
            r.pre_v[j, b] = sv
            r.pre_n[j, b] = jnp.broadcast_to(sn, (8, STATE))
            one, two = lin.factors(r.ks[j, rows_of(b), :])
            phi = one * two
            if b == 0:
                phi = jnp.where(lin.key_open(STATE), phi, 0.0)
            sv = sv + dtn(r.p[rows_of(b), head_of(j)], phi.astype(BF)) * lin.coef
            sn = sn + jnp.sum(phi, axis=0, keepdims=True) * lin.coef
        r.sv_s[j] = sv.astype(BF)
        r.sn_s[j] = jnp.broadcast_to(sn, (8, STATE))
    copies = (
        remote(r.sv_s, r.sv_r, r.xss.at[0], r.xrs.at[0], lin.partner),
        remote(r.sn_s, r.sn_r, r.xss.at[1], r.xrs.at[1], lin.partner),
    )
    for j in range(2):
        for b in range(NBLK):
            _, _, kernel = lin.scores(j, b)
            r.num[j, rows_of(b), :] = dnn(kernel.astype(BF), r.p[rows_of(b), head_of(j)])
            r.den[j, rows_of(b), :] = jnp.broadcast_to(
                jnp.sum(kernel, axis=-1, keepdims=True), (BLK, HEAD_V)
            )
    advance(cots)
    for copy in copies:
        copy.wait_recv()
    for j in range(2):
        if j == 1:
            advance(cots)
        got_v = r.sv_r[j].astype(F32) * lin.second
        got_n = r.sn_r[j] * lin.second
        for b in range(NBLK):
            state_v = (r.pre_v[j, b] + got_v).astype(BF)
            state_n = r.pre_n[j, b] + got_n
            r.sv[j, b] = state_v
            r.sn[j, b] = state_n
            one, two = lin.factors(r.qs[j, rows_of(b), :])
            phi = one * two
            den = jnp.sum(phi * state_n[0:1, :], axis=-1, keepdims=True)
            num = dnt(phi.astype(BF), state_v)
            seen = lin.sees_state(b, HEAD_V)
            top = r.num[j, rows_of(b), :] + jnp.where(seen, num, 0.0)
            bottom = r.den[j, rows_of(b), :] + jnp.where(seen, den, 0.0)
            r.y[rows_of(b), head_of(j)] = (top / bottom).astype(BF)
    for copy in copies:
        copy.wait_send()


STATE_SCRATCH = {
    "qs": pltpu.VMEM((2, HALF_TOK, 128), BF),
    "ks": pltpu.VMEM((2, HALF_TOK, 128), BF),
    "sv_s": pltpu.VMEM((2, HEAD_V, STATE), BF),
    "sn_s": pltpu.VMEM((2, 8, STATE), F32),
    "sv_r": pltpu.VMEM((2, HEAD_V, STATE), BF),
    "sn_r": pltpu.VMEM((2, 8, STATE), F32),
    "pre_v": pltpu.VMEM((2, NBLK, HEAD_V, STATE), F32),
    "pre_n": pltpu.VMEM((2, NBLK, 8, STATE), F32),
    "xss": pltpu.SemaphoreType.DMA((2,)),
    "xrs": pltpu.SemaphoreType.DMA((2,)),
}


def linear_body(r):
    ring = Ring()
    partners = (ring.up, ring.dn, ring.sib, {"xh": 1 - lax.axis_index("xh")})
    signal(partners)
    loading = load(r.w.at[:, :, pl.ds(BIN_PAD, 16), :], r.wv, r.wls)
    r.cbuf[ring.z * 2 + ring.c] = r.cot[: TOK // 2, :]
    arrive(partners)
    cots = half_gather(ring, r, r.lo)
    advance(cots)
    linear_forward_part(r, ring, cots)
    loading.wait()
    ring_forward(r, ring, r.y, r.wv, (cots,))
    finish(cots)


def linear_step(raw, select, tables, cot, w, x, gain):
    return build(
        linear_body,
        {
            "raw": vm(raw),
            "sel": vm(select),
            "e": vm(tables[0]),
            "t": vm(tables[1]),
            "pick": vm(tables[2]),
            "cot": vm(cot),
            "w": hbm(w),
            "x": vm(x),
            "gain": vm(gain),
        },
        {
            "y": (sds((HALF_TOK, 2 * HEAD_V)), VM),
            "p": (sds((HALF_TOK, 3 * HEAD_V)), VM),
            "sv": (sds((2, NBLK, HEAD_V, STATE)), VM),
            "sn": (sds((2, NBLK, 8, STATE), F32), VM),
            "lo": (sds((8, TOK // 2, D)), ANY),
            "x_out": (sds((TOK, D), F32), VM),
            "h_out": (sds((8, TOK, D)), ANY),
        },
        {
            "num": pltpu.VMEM((2, HALF_TOK, HEAD_V), F32),
            "den": pltpu.VMEM((2, HALF_TOK, HEAD_V), F32),
            "wv": pltpu.VMEM((4, 4, 16, D), BF),
            "wls": pltpu.SemaphoreType.DMA,
        }
        | STATE_SCRATCH
        | HALF_SCRATCH
        | SCATTER_SCRATCH
        | GATHER_SCRATCH,
        2,
    )


def linear_backward_part(r, others):
    lin = Linear(r)
    lin.vectors()
    for j in range(2):
        tv = jnp.zeros((HEAD_V, STATE), F32)
        tn = jnp.zeros((1, STATE), F32)
        for b in range(NBLK):
            queries = r.qs[j, rows_of(b), :]
            grads = r.dy[rows_of(b), head_of(j)]
            one, two = lin.factors(queries)
            phi = one * two
            phi_low = phi.astype(BF)
            seen = lin.sees_state(b, 1)
            state_v, state_n = r.sv[j, b], r.sn[j, b, 0:1, :]
            scores, mask, kernel = lin.scores(j, b)
            weight_grad = dnt(grads, r.p[rows_of(b), head_of(j)])
            den = jnp.sum(phi * state_n, axis=-1, keepdims=True)
            num = dnt(phi_low, state_v)
            dot = jnp.sum(num * grads.astype(F32), axis=-1, keepdims=True)
            total = jnp.where(seen, den, 0.0) + jnp.sum(kernel, axis=-1, keepdims=True)
            dot = jnp.where(seen, dot, 0.0) + jnp.sum(kernel * weight_grad, axis=-1, keepdims=True)
            inverse = 1.0 / total
            mean = dot * inverse
            grads_n = (grads.astype(F32) * inverse).astype(BF)
            score_grad = jnp.where(
                mask, (weight_grad - mean) * inverse * (1.0 + scores), 0.0
            ).astype(BF)
            r.dk[j, rows_of(b), :] = dtn(score_grad, queries)
            r.dv[j, rows_of(b), :] = dtn(kernel.astype(BF), grads_n)
            shift = jnp.where(seen, -(mean * inverse), 0.0)
            grads_s = jnp.where(seen, grads_n, jnp.zeros_like(grads_n))
            phi_grad = dnn(grads_s, state_v) + shift * state_n
            r.dq[j, rows_of(b), :] = dnn(
                score_grad, r.ks[j, rows_of(b), :]
            ) * INV_ROOT + lin.factors_back(phi_grad, one, two)
            own_v = dtn(grads_s, phi_low) * lin.coef
            own_n = jnp.sum(shift * phi, axis=0, keepdims=True) * lin.coef
            r.pre_v[j, b] = own_v
            r.pre_n[j, b] = jnp.broadcast_to(own_n, (8, STATE))
            tv, tn = tv + own_v, tn + own_n
            if (j, b) in ((0, 2), (1, 1)):
                for other in others:
                    advance(other)
        r.sv_s[j] = tv.astype(BF)
        r.sn_s[j] = jnp.broadcast_to(tn, (8, STATE))
    copies = (
        remote(r.sv_s, r.sv_r, r.xss.at[0], r.xrs.at[0], lin.partner),
        remote(r.sn_s, r.sn_r, r.xss.at[1], r.xrs.at[1], lin.partner),
    )
    for other in others:
        advance(other)
    for copy in copies:
        copy.wait_recv()
    after_v = [r.sv_r[j].astype(F32) * (1.0 - lin.second) for j in range(2)]
    after_n = [r.sn_r[j, 0:1, :] * (1.0 - lin.second) for j in range(2)]
    for b in reversed(range(NBLK)):
        placed = jnp.zeros((BLK, 128), F32)
        for j in range(2):
            one, two = lin.factors(r.ks[j, rows_of(b), :])
            phi = one * two
            state = after_v[j].astype(BF)
            phi_grad = dnn(r.p[rows_of(b), head_of(j)], state) + after_n[j]
            if b == 0:
                visible = lin.key_open(STATE)
                phi = jnp.where(visible, phi, 0.0)
                phi_grad = jnp.where(visible, phi_grad, 0.0)
            key_grad = r.dk[j, rows_of(b), :] * INV_ROOT + lin.factors_back(phi_grad, one, two)
            value_grad = r.dv[j, rows_of(b), :] + dnt(phi.astype(BF), state)
            r.dp[rows_of(b), head_of(j)] = value_grad.astype(BF)
            placed = placed + dnt(r.dq[j, rows_of(b), :].astype(BF), r.pick[2 * j])
            placed = placed + dnt(key_grad.astype(BF), r.pick[2 * j + 1])
            after_v[j] = after_v[j] + r.pre_v[j, b]
            after_n[j] = after_n[j] + r.pre_n[j, b, 0:1, :]
        r.dp[rows_of(b), 2 * HEAD_V :] = placed.astype(BF)
        r.draw[rows_of(b), :] = dnt(r.dp[rows_of(b), :], r.sel[...]).astype(BF)
    for copy in copies:
        copy.wait_send()


def sum_steps(ring, plane, r):
    copies = []
    stages = (
        (r.ring_in, ring.z * 2 + ring.c, 8, lambda t: {"z": lax.div(t, 2), "c": lax.rem(t, 2)}),
        (r.x_in, plane.x, 4, plane.at_x),
        (r.y_in, plane.y, 4, plane.at_y),
    )
    for dst, own, count, device_of in stages:
        dst[own] = r.pack[...]
        sent = []
        for o in range(1, count):
            n = len(copies) + len(sent)
            device = device_of(lax.rem(own + o, count))
            sent.append(remote(r.pack, dst.at[own], r.pss.at[n], r.prs.at[n], device))
        yield
        for copy in sent:
            copy.wait_recv()
        for copy in sent:
            copy.wait_send()
        copies += sent
        total = dst[0]
        for k in range(1, count):
            total = total + dst[k]
        r.pack[...] = total


def last_body(r):
    ring, plane = Ring(), Plane()
    me = ring.z * 2 + ring.c
    partners = []
    for o in range(1, 8):
        to = lax.rem(me + o, 8)
        partners.append({"z": lax.div(to, 2), "c": lax.rem(to, 2)})
    for o in range(1, 4):
        partners.append(plane.at_x(lax.rem(plane.x + o, 4)))
        partners.append(plane.at_y(lax.rem(plane.y + o, 4)))
    signal(partners)
    loads = [
        load(r.g, r.win, r.lsem.at[0]),
        load(r.w.at[:, :, pl.ds(0, BIN_PAD), :], r.wv, r.lsem.at[1]),
        load(r.h, r.hv, r.lsem.at[2]),
        load(r.e2, r.ev, r.lsem.at[3]),
    ]
    r.out[: TOK // 2, :] = r.low[...]

    def write(at, rows, total):
        r.out[rows, :] = (r.x3[rows, :] + total).astype(BF)

    sums = rows_reduce(ring, r, 1, write)
    win = plane_reduce(plane, r, "win", ((0, r.win_in), (48, r.win_out)))
    arrive(partners)
    advance(sums)
    loads[0].wait()
    advance(win)
    linear_backward_part(r, (sums, win))
    finish(sums)
    for copy in loads[1:]:
        copy.wait()
    wide = D // 8

    def product(rows, col):
        return dnn(r.draw[rows, :], r.wv[:, :, :, col].reshape(16 * BIN_PAD, -1))

    def weights():
        for k in range(4):
            cols = slice(k * 512, (k + 1) * 512)
            res = dtn(r.draw[...], r.hv[:, :, cols].reshape(HALF_TOK, 512))
            own = r.wv[:, :, :, cols].reshape(16 * BIN_PAD, 512).astype(F32)
            r.gacc[:, cols] = jnp.sum(res * own, axis=0, keepdims=True)
            r.lin[:, :, :BIN_PAD, cols] = res.astype(BF).reshape(4, 4, BIN_PAD, 512)
            res = dtn(r.y[...], r.ev[:, :, cols].reshape(HALF_TOK, 512)).astype(BF)
            r.lin[:, :, BIN_PAD:, cols] = res.reshape(4, 4, 16, 512)
        reduce = plane_reduce(plane, r, "lin", ((0, r.lin_in), (BIN_PAD, r.lin_out)))
        advance(reduce)
        gains = (r.gacc[...] / r.gain[...], r.gain_b[...], r.gain_c[...])
        for n, gain in enumerate(gains):
            for i in range(8):
                r.pack[i : i + 1, n * wide : (n + 1) * wide] = gain[:, i * wide : (i + 1) * wide]
        gain_sums = sum_steps(ring, plane, r)
        advance(gain_sums)
        yield
        for _ in range(4):
            advance(win)
            advance(reduce)
            advance(gain_sums)
            yield
        finish(win)
        finish(gain_sums)
        finish(reduce)

    weight_grads = weights()

    def one(at):
        r.d_out[at, :] = r.res[at, :] + norm_back_rows(r.v, r.gain, sums_of(r, ring, at), at)

    def ready(q):
        by_rows(one, q * (TOK // CHUNKS), TOK // CHUNKS)

    weave(scatter(ring, r, product, ready), weight_grads)
    finish(weight_grads)
    for n, out in enumerate((r.ga, r.gb, r.gc)):
        for i in range(8):
            out[:, i * wide : (i + 1) * wide] = r.pack[i : i + 1, n * wide : (n + 1) * wide]


def last_step(lin, dy, select, tables, down, x3, low, g, w, h, e2, v, gain, res, gain_b, gain_c, width):
    small = (8, 3 * D // 8)
    return build(
        last_body,
        {
            "p": vm(lin.p),
            "dy": vm(dy),
            "sv": vm(lin.sv),
            "sn": vm(lin.sn),
            "sel": vm(select),
            "e": vm(tables[0]),
            "t": vm(tables[1]),
            "pick": vm(tables[2]),
            "down": hbm(down),
            "x3": vm(x3),
            "low": vm(low),
            "g": hbm(g),
            "w": hbm(w),
            "h": hbm(h),
            "e2": hbm(e2),
            "y": vm(lin.y),
            "v": vm(v),
            "gain": vm(gain),
            "res": vm(res),
            "gain_b": vm(gain_b),
            "gain_c": vm(gain_c),
        },
        {
            "out": (sds((TOK, D)), VM),
            "d_out": (sds((TOK, D), F32), VM),
            "ga": (sds((1, D), F32), VM),
            "gb": (sds((1, D), F32), VM),
            "gc": (sds((1, D), F32), VM),
            "win_in": (sds((48, D), F32), VM),
            "win_out": (sds((16, D), F32), VM),
            "lin_in": (sds((width, D), F32), VM),
            "lin_out": (sds((16, D), F32), VM),
        },
        {
            "dp": pltpu.VMEM((HALF_TOK, 3 * HEAD_V), BF),
            "draw": pltpu.VMEM((HALF_TOK, 16 * BIN_PAD), BF),
            "dq": pltpu.VMEM((2, HALF_TOK, 128), F32),
            "dk": pltpu.VMEM((2, HALF_TOK, 128), F32),
            "dv": pltpu.VMEM((2, HALF_TOK, HEAD_V), F32),
            "wv": pltpu.VMEM((4, 4, BIN_PAD, D), BF),
            "hv": pltpu.VMEM((8, TOK, D), BF),
            "ev": pltpu.VMEM((8, TOK, D), BF),
            "gacc": pltpu.VMEM((1, D), F32),
            "pack": pltpu.VMEM(small, F32),
            "ring_in": pltpu.VMEM((8,) + small, F32),
            "x_in": pltpu.VMEM((4,) + small, F32),
            "y_in": pltpu.VMEM((4,) + small, F32),
            "pss": pltpu.SemaphoreType.DMA((13,)),
            "prs": pltpu.SemaphoreType.DMA((13,)),
            "lsem": pltpu.SemaphoreType.DMA((4,)),
        }
        | STATE_SCRATCH
        | ROWS_SCRATCH
        | plane_reduce_scratch("win", 64)
        | plane_reduce_scratch("lin", BIN_PAD + 16)
        | SCATTER_SCRATCH,
        6,
    )


WBLK = 128
WKEYS = WBLK + WINDOW
INV_ROOT_V = 1.0 / math.sqrt(HEAD_V)


def turn_tables():
    slot = np.arange(2 * HALF_TOK)
    last = 2 * HALF_TOK - EDGE
    position = slot - np.where(slot < EDGE, 0, np.where(slot < last, EDGE, last))
    frequency = np.exp(-math.log(10000.0) * np.arange(HEAD_V // 2) * 2.0 / HEAD_V)
    angles = position[:, None] * frequency[None, :]
    cosine, sine = np.cos(angles), np.sin(angles)
    pair = np.stack(
        [np.concatenate([cosine, cosine], axis=1), np.concatenate([-sine, sine], axis=1)]
    )
    return pair.reshape(2, 2, HALF_TOK, HEAD_V).transpose(1, 0, 2, 3).astype(np.float32)


class Window:
    def __init__(self):
        self.xh = lax.axis_index("xh")
        self.partner = {"xh": 1 - self.xh}
        self.edge = jnp.where(self.xh == 0, EDGE, HALF_TOK - EDGE)
        self.lowest = jnp.where(self.xh == 0, 0, -WINDOW)

    def mask(self, b):
        t = b * WBLK + lax.broadcasted_iota(jnp.int32, (WBLK, WKEYS), 0)
        u = b * WBLK - WINDOW + lax.broadcasted_iota(jnp.int32, (WBLK, WKEYS), 1)
        same = (t >= self.edge) == (u >= self.edge)
        return (u <= t) & (t - u < WINDOW) & same & (u >= self.lowest)

    def probs(self, r, b, j):
        rows, keys, head = window_rows(b), window_keys(b), head_of(j)
        scores = dnt(r.q[rows, head], r.kv[keys, head]) * INV_ROOT_V
        scores = jnp.where(self.mask(b), scores, -1e30)
        exps = jnp.exp(scores - jnp.max(scores, axis=-1, keepdims=True))
        return exps / jnp.sum(exps, axis=-1, keepdims=True)


def window_rows(b):
    return slice(b * WBLK, (b + 1) * WBLK)


def window_keys(b):
    return slice(b * WBLK, b * WBLK + WKEYS)


def window_forward_part(r, cots):
    win = Window()
    size = 2 * TOK
    blocks = HALF_TOK // size

    def turned(vecs, rows):
        return (
            vecs * r.turn[0, rows, :] + pltpu.roll(vecs, HEAD_V // 2, 1) * r.turn[1, rows, :]
        ).astype(BF)

    for b in (blocks - 1,) + tuple(range(blocks - 1)):
        rows = slice(b * size, (b + 1) * size)
        shifted = slice(WINDOW + b * size, WINDOW + (b + 1) * size)
        tokens = r.hv[2 * b : 2 * b + 2].reshape(size, D)
        for j in range(2):
            proj = dnt(tokens, r.wiv[2 * j : 2 * j + 2].reshape(384, D))
            r.q[rows, head_of(j)] = turned(proj[:, :128], rows)
            r.kv[shifted, head_of(j)] = turned(proj[:, 128:256], rows)
            r.kv[shifted, head_of(2 + j)] = proj[:, 256:].astype(BF)
        if b == blocks - 1:
            copy = remote(
                r.kv.at[pl.ds(HALF_TOK, WINDOW), :],
                r.kv.at[pl.ds(0, WINDOW), :],
                r.xss,
                r.xrs,
                win.partner,
            )
    advance(cots)
    for b in tuple(range(1, HALF_TOK // WBLK)) + (0,):
        if b == 0:
            copy.wait_recv()
        for j in range(2):
            r.y[window_rows(b), head_of(j)] = dnn(
                win.probs(r, b, j).astype(BF), r.kv[window_keys(b), head_of(2 + j)]
            ).astype(BF)
        if b == 4:
            advance(cots)
    copy.wait_send()


def window_body(r):
    ring = Ring()
    partners = (ring.up, ring.dn, ring.sib, {"xh": 1 - lax.axis_index("xh")})
    signal(partners)
    loads = (
        load(r.w.at[:, :, pl.ds(0, 48), :], r.wiv, r.lsem.at[0]),
        load(r.h, r.hv, r.lsem.at[1]),
        load(r.turns.at[lax.axis_index("xh")], r.turn, r.lsem.at[2]),
        load(r.w.at[:, :, pl.ds(48, 16), :], r.wov, r.lsem.at[3]),
    )
    r.cbuf[ring.z * 2 + ring.c] = r.cot[TOK // 2 :, :]
    arrive(partners)
    cots = half_gather(ring, r, r.hi)
    advance(cots)
    for copy in loads:
        copy.wait()
    window_forward_part(r, cots)
    ring_forward(r, ring, r.y, r.wov, (cots,))
    finish(cots)


def window_step(h, w, turns, cot, x, gain):
    return build(
        window_body,
        {
            "h": hbm(h),
            "w": hbm(w),
            "turns": hbm(turns),
            "cot": vm(cot),
            "x": vm(x),
            "gain": vm(gain),
        },
        {
            "y": (sds((HALF_TOK, 256)), VM),
            "q": (sds((HALF_TOK, 256)), VM),
            "kv": (sds((HALF_TOK + WINDOW, 512)), VM),
            "hi": (sds((8, TOK // 2, D)), ANY),
            "x_out": (sds((TOK, D), F32), VM),
            "h_out": (sds((8, TOK, D)), ANY),
        },
        {
            "hv": pltpu.VMEM((8, TOK, D), BF),
            "wiv": pltpu.VMEM((4, 4, 48, D), BF),
            "wov": pltpu.VMEM((4, 4, 16, D), BF),
            "turn": pltpu.VMEM((2, HALF_TOK, HEAD_V), F32),
            "lsem": pltpu.SemaphoreType.DMA((4,)),
            "xss": pltpu.SemaphoreType.DMA,
            "xrs": pltpu.SemaphoreType.DMA,
        }
        | HALF_SCRATCH
        | SCATTER_SCRATCH
        | GATHER_SCRATCH,
        3,
    )


def window_backward_part(r, sums):
    win = Window()
    blocks = HALF_TOK // WBLK

    def turned_back(b, grads):
        rows = window_rows(b)
        return (
            grads * r.turn[0, rows, :] + pltpu.roll(grads * r.turn[1, rows, :], HEAD_V // 2, 1)
        ).astype(BF)

    for b in range(blocks):
        rows, keys = window_rows(b), window_keys(b)
        for j in range(2):
            head, vals = head_of(j), head_of(2 + j)
            queries, grads = r.q[rows, head], r.dy[rows, head]
            probs = win.probs(r, b, j)
            prob_grad = dnt(grads, r.kv[keys, vals])
            score_grad = (
                probs * (prob_grad - jnp.sum(prob_grad * probs, axis=-1, keepdims=True))
            ).astype(BF)
            r.dp[rows, head_of(3 * j)] = turned_back(
                b, dnn(score_grad, r.kv[keys, head]) * INV_ROOT_V
            )
            r.dkv[keys, head] += dtn(score_grad, queries) * INV_ROOT_V
            r.dkv[keys, vals] += dtn(probs.astype(BF), grads)
        if b == 0:
            copy = remote(r.dkv.at[pl.ds(0, WINDOW), :], r.halo, r.xss, r.xrs, win.partner)
        if b in (2, 6):
            advance(sums)
    for b in range(blocks):
        shifted = slice(WINDOW + b * WBLK, WINDOW + (b + 1) * WBLK)
        if b == blocks - 1:
            copy.wait_recv()
            r.dkv[HALF_TOK : HALF_TOK + WINDOW, :] += r.halo[...]
        for j in range(2):
            r.dp[window_rows(b), head_of(3 * j + 1)] = turned_back(b, r.dkv[shifted, head_of(j)])
            r.dp[window_rows(b), head_of(3 * j + 2)] = r.dkv[shifted, head_of(2 + j)].astype(BF)
    copy.wait_send()


def window_back_body(r):
    ring = Ring()
    partners = (ring.up, ring.dn, ring.sib, {"xh": 1 - lax.axis_index("xh")})
    signal(partners)
    turning = load(r.turns.at[lax.axis_index("xh")], r.turn, r.lsem.at[0])
    loads = [
        load(r.w.at[:, :, pl.ds(0, 48), :], r.wiv, r.lsem.at[1]),
        load(r.h, r.hv, r.lsem.at[2]),
        load(r.e, r.ev, r.lsem.at[3]),
        load(r.wo.at[:, :, pl.ds(BIN_PAD, 16), :], r.wov, r.lsem.at[4]),
    ]
    r.dkv[...] = jnp.zeros_like(r.dkv)
    r.gacc[...] = jnp.zeros_like(r.gacc)

    def write(at, rows, total):
        r.low[at, :] = (r.x3[rows, :] + total).astype(BF)

    sums = rows_reduce(ring, r, 0, write)
    arrive(partners)
    advance(sums)
    turning.wait()
    window_backward_part(r, sums)
    finish(sums)
    for copy in loads:
        copy.wait()

    def product(rows, col):
        return dnn(r.dp[rows, :], r.wiv[:, :, :, col].reshape(768, -1))

    def weights():
        for k in range(4):
            cols = slice(k * 512, (k + 1) * 512)
            rows = r.hv[:, :, cols].reshape(HALF_TOK, 512)
            for i in range(2):
                res = dtn(r.dp[:, i * 384 : (i + 1) * 384], rows)
                own = r.wiv[2 * i : 2 * i + 2, :, :, cols].reshape(384, 512).astype(F32)
                r.gacc[:, cols] += jnp.sum(res * own, axis=0, keepdims=True)
                r.gstage[2 * i : 2 * i + 2, :, :48, cols] = res.astype(BF).reshape(2, 4, 48, 512)
            res = dtn(r.y[...], r.ev[:, :, cols].reshape(HALF_TOK, 512)).astype(BF)
            r.gstage[:, :, 48:, cols] = res.reshape(4, 4, 16, 512)
            yield
        copy = load(r.gstage, r.grads, r.lsem.at[5])
        yield
        copy.wait()

    weight_grads = weights()
    ring_backward(r, ring, product, r.wov, (weight_grads,))
    finish(weight_grads)
    r.gain_out[...] = r.gacc[...] / r.gain[...]


def window_back_step(win, dy, turns, down, x3, w, wo, h, e, v, gain, res):
    return build(
        window_back_body,
        {
            "q": vm(win.q),
            "kv": vm(win.kv),
            "dy": vm(dy),
            "turns": hbm(turns),
            "down": hbm(down),
            "x3": vm(x3),
            "w": hbm(w),
            "wo": hbm(wo),
            "h": hbm(h),
            "e": hbm(e),
            "y": vm(win.y),
            "v": vm(v),
            "gain": vm(gain),
            "res": vm(res),
        },
        {
            "low": (sds((TOK // 2, D)), VM),
            "d_out": (sds((TOK, D), F32), VM),
            "gain_out": (sds((1, D), F32), VM),
            "e_out": (sds((8, TOK, D)), ANY),
            "dy_out": (sds((HALF_TOK, 256)), VM),
            "grads": (sds((4, 4, 64, D)), ANY),
        },
        {
            "dkv": pltpu.VMEM((HALF_TOK + WINDOW, 512), F32),
            "halo": pltpu.VMEM((WINDOW, 512), F32),
            "turn": pltpu.VMEM((2, HALF_TOK, HEAD_V), F32),
            "dp": pltpu.VMEM((HALF_TOK, 768), BF),
            "wiv": pltpu.VMEM((4, 4, 48, D), BF),
            "wov": pltpu.VMEM((4, 4, 16, D), BF),
            "hv": pltpu.VMEM((8, TOK, D), BF),
            "ev": pltpu.VMEM((8, TOK, D), BF),
            "gstage": pltpu.VMEM((4, 4, 64, D), BF),
            "gacc": pltpu.VMEM((1, D), F32),
            "lsem": pltpu.SemaphoreType.DMA((6,)),
            "xss": pltpu.SemaphoreType.DMA,
            "xrs": pltpu.SemaphoreType.DMA,
        }
        | ROWS_SCRATCH
        | SCATTER_SCRATCH
        | GATHER_SCRATCH,
        5,
    )


def padded(rows, count):
    return jnp.pad(rows, ((0, count - rows.shape[0]), (0, 0)))


def place():
    slot = lax.axis_index("xh") * HALF_TOK + jnp.arange(HALF_TOK, dtype=jnp.int32)
    last = 2 * HALF_TOK - EDGE
    segment = (slot >= EDGE).astype(jnp.int32) + (slot >= last).astype(jnp.int32)
    start = jnp.where(segment == 0, 0, jnp.where(segment == 1, EDGE, last)).astype(jnp.int32)
    return segment, slot - start


def body(
    block_input,
    cotangent,
    lengths,
    gain_a,
    based_in,
    based_out,
    gain_b,
    swa_in,
    swa_out,
    gain_c,
    mlp_in,
    mlp_down,
):
    gains = [gain.reshape(1, D) for gain in (gain_a, gain_b, gain_c)]
    units = mlp_down.shape[0]
    wide = based_in.shape[1]
    win_all = lax.all_gather(
        jnp.concatenate([swa_in.T, swa_out], axis=0), PLANE, axis=0, tiled=True
    ).reshape(4, 4, 64, D)
    ff_all = lax.all_gather(
        jnp.concatenate(
            [padded(part, UNIT_PAD) for part in (mlp_in[:, 0, :].T, mlp_in[:, 1, :].T, mlp_down)],
            axis=0,
        ),
        PLANE,
        axis=0,
        tiled=True,
    ).reshape(16, 3 * UNIT_PAD, D)
    segment, position = place()
    first = (lax.axis_index("z") * 2 + lax.axis_index("c")) * TOK
    my_segment = lax.dynamic_slice_in_dim(segment, first, TOK)
    my_position = lax.dynamic_slice_in_dim(position, first, TOK)
    chosen = jnp.where(
        my_segment == 0,
        lengths[0, 0],
        jnp.where(my_segment == 1, lengths[0, 1], lengths[0, 2]),
    )
    valid = (my_position < chosen)[:, None]
    cot_low = jnp.where(valid, cotangent, jnp.zeros_like(cotangent))
    tables = tuple(
        jnp.asarray(table, kind) for table, kind in zip(state_tables(), (BF, F32, BF))
    )
    select = jnp.asarray(select_table(wide), BF)

    turns = jnp.asarray(turn_tables())

    start = first_step(block_input, gains[0], based_in.T, based_out)
    lin = linear_step(start.raw, select, tables, cot_low, start.w, block_input, gains[1])
    win = window_step(lin.h_out, win_all, turns, cot_low, lin.x_out, gains[2])
    mlp = mlp_step(win.h_out, lin.lo, win.hi, ff_all, win_all, win.x_out, gains[2], cot_low)
    ff_grads = lax.psum_scatter(
        mlp.grads.reshape(-1, D), PLANE, scatter_dimension=0, tiled=True
    ).astype(F32)
    back = window_back_step(
        win,
        mlp.dy_out,
        turns,
        mlp.down,
        win.x_out,
        win_all,
        start.w,
        lin.h_out,
        mlp.e_out,
        lin.x_out,
        gains[1],
        mlp.d_out,
    )
    end = last_step(
        lin,
        back.dy_out,
        select,
        tables,
        mlp.down,
        win.x_out,
        back.low,
        back.grads,
        start.w,
        start.h,
        back.e_out,
        block_input,
        gains[0],
        back.d_out,
        back.gain_out,
        mlp.gain_out,
        wide,
    )
    gate_grad = ff_grads[:units]
    up_grad = ff_grads[UNIT_PAD : UNIT_PAD + units]
    return (
        end.out,
        end.d_out,
        end.ga.reshape(D),
        end.lin_in.T,
        end.lin_out,
        end.gb.reshape(D),
        end.win_in.T,
        end.win_out,
        end.gc.reshape(D),
        jnp.stack([gate_grad.T, up_grad.T], axis=1),
        ff_grads[2 * UNIT_PAD : 2 * UNIT_PAD + units],
    )


def solution(mesh):
    grid = Mesh(mesh.devices.reshape(2, 4, 2, 4, 2), ALL)
    tokens = P(ALL, None)
    weight = ("xh", "z", "c", "xl", "y")
    rows, cols = P(weight, None), P(None, weight)
    return jax.shard_map(
        body,
        mesh=grid,
        in_specs=(
            tokens,
            tokens,
            P(("xl", "y"), None),
            P(),
            cols,
            rows,
            P(),
            cols,
            rows,
            P(),
            P(None, None, weight),
            rows,
        ),
        out_specs=(
            tokens,
            tokens,
            P(),
            cols,
            rows,
            P(),
            cols,
            rows,
            P(),
            P(None, None, weight),
            rows,
        ),
        check_vma=False,
    )
```

```python
import functools
import math
import types

import jax
import jax.numpy as jnp
import numpy as np
from jax import lax
from jax.experimental import pallas as pl
from jax.experimental.pallas import tpu as pltpu
from jax.sharding import Mesh
from jax.sharding import PartitionSpec as P

FEAT = 16
HEAD_V = 128
WINDOW = 64
EPSILON = 1e-05
D = 2048
TOK = 128
HALF_TOK = 1024
EDGE = 64
UNIT_PAD = 48
BIN_PAD = 32
STATE = 256
PLANE = ("xh", "xl", "y")
RING = ("z", "c")
ALL = ("xl", "y", "xh", "z", "c")
MESH = pl.DeviceIdType.MESH
BF = jnp.bfloat16
F32 = jnp.float32
VM = pl.BlockSpec(memory_space=pltpu.VMEM)
ANY = pl.BlockSpec(memory_space=pl.ANY)


def dnn(a, b):
    return lax.dot_general(a, b, (((1,), (0,)), ((), ())), preferred_element_type=F32)


def dnt(a, b):
    return lax.dot_general(a, b, (((1,), (1,)), ((), ())), preferred_element_type=F32)


def dtn(a, b):
    return lax.dot_general(a, b, (((0,), (0,)), ((), ())), preferred_element_type=F32)


def remote(src, dst, send_sem, recv_sem, device):
    copy = pltpu.make_async_remote_copy(
        src_ref=src,
        dst_ref=dst,
        send_sem=send_sem,
        recv_sem=recv_sem,
        device_id=device,
        device_id_type=MESH,
    )
    copy.start()
    return copy


def greet(devices):
    barrier = pltpu.get_barrier_semaphore()
    for device in devices:
        pl.semaphore_signal(barrier, inc=1, device_id=device, device_id_type=MESH)
    pl.semaphore_wait(barrier, len(devices))


class Ring:
    def __init__(self):
        self.z = lax.axis_index("z")
        self.c = lax.axis_index("c")
        self.oc = 1 - self.c
        self.zp = lax.rem(self.z + 1, 4)
        self.zm = lax.rem(self.z + 3, 4)
        self.zz = lax.rem(self.z + 2, 4)
        self.up = {"z": self.zp}
        self.dn = {"z": self.zm}
        self.sib = {"c": self.oc}

    def greet(self):
        greet((self.up, self.dn, self.sib))


class Plane:
    def __init__(self):
        self.x = lax.axis_index("xh") * 2 + lax.axis_index("xl")
        self.y = lax.axis_index("y")

    def at_x(self, x):
        return {"xh": lax.div(x, 2), "xl": lax.rem(x, 2)}

    def at_y(self, y):
        return {"y": y}

    def ring(self, along_x):
        me = self.x if along_x else self.y
        plus, minus, far = lax.rem(me + 1, 4), lax.rem(me + 3, 4), lax.rem(me + 2, 4)
        to = self.at_x if along_x else self.at_y
        return me, plus, minus, far, to(plus), to(minus)

    def neighbours(self):
        xs, ys = self.ring(True), self.ring(False)
        return (xs[4], xs[5], ys[4], ys[5])


def finish(steps):
    for _ in steps:
        pass


def advance(steps):
    next(steps, None)


def weave(main, *others):
    for _ in main:
        for other in others:
            advance(other)


CHUNKS = 2


def gather_steps(ring, buf, out_ref, ss, rs, ls, rows, start=0, base=0, keep=True, ready=None):
    half = rows // 2
    me = ring.z * 2 + ring.c
    below, above, far = ring.zm * 2 + ring.c, ring.zp * 2 + ring.c, ring.zz * 2 + ring.c

    def send(slot, part, device, index):
        piece = buf.at[slot, pl.ds(start + part * half, half), :]
        return remote(piece, piece, ss.at[base + index], rs.at[base + index], device)

    local = []

    def save(slot):
        if keep:
            copy = pltpu.make_async_copy(buf.at[slot], out_ref.at[slot], ls.at[len(local)])
            copy.start()
            local.append(copy)

    def done(chip):
        if ready is not None:
            ready(chip)

    up, dn, sib = ring.up, ring.dn, ring.sib
    cp = {}
    cp[0] = send(me, 0, up, 0)
    cp[1] = send(me, 1, dn, 1)
    cp[2] = send(me, 1, up, 2)
    cp[3] = send(me, 0, dn, 3)
    cp[4] = send(me, 0, sib, 4)
    cp[5] = send(me, 1, sib, 5)
    save(me)
    yield
    cp[0].wait_recv()
    cp[6] = send(below, 0, up, 6)
    cp[8] = send(below, 0, sib, 8)
    cp[1].wait_recv()
    cp[7] = send(above, 1, dn, 7)
    cp[9] = send(above, 1, sib, 9)
    yield
    cp[2].wait_recv()
    cp[10] = send(below, 1, sib, 10)
    save(below)
    cp[3].wait_recv()
    cp[11] = send(above, 0, sib, 11)
    save(above)
    yield
    cp[4].wait_recv()
    cp[5].wait_recv()
    save(ring.z * 2 + ring.oc)
    done(ring.z)
    cp[8].wait_recv()
    cp[10].wait_recv()
    save(ring.zm * 2 + ring.oc)
    done(ring.zm)
    yield
    cp[6].wait_recv()
    cp[12] = send(far, 0, sib, 12)
    cp[7].wait_recv()
    cp[13] = send(far, 1, sib, 13)
    save(far)
    cp[9].wait_recv()
    cp[11].wait_recv()
    save(ring.zp * 2 + ring.oc)
    done(ring.zp)
    yield
    cp[12].wait_recv()
    cp[13].wait_recv()
    save(ring.zz * 2 + ring.oc)
    done(ring.zz)
    for index in range(14):
        cp[index].wait_send()
    for copy in local:
        copy.wait()


def scatter_steps(ring, product, part, sib_in, far_in, end_in, ss, rs, ready, before=None):
    rows = TOK // CHUNKS
    half = rows // 2
    c, oc = ring.c, ring.oc
    up, dn, sib = ring.up, ring.dn, ring.sib
    order = (ring.zz, ring.zp, ring.zm, ring.z)
    step = 512
    cp = {}

    def send(q, index, src, dst, device):
        n = q * 10 + index
        cp[q, index] = remote(src, dst, ss.at[n], rs.at[n], device)

    def multiply(index):
        row = pl.multiple_of(order[index] * (2 * TOK), 2 * TOK)

        def one(n, carry):
            col = pl.ds(pl.multiple_of(n * step, step), step)
            res = product(pl.ds(row, 2 * TOK), col).astype(BF)
            part[index, 0, :, col] = res[:TOK]
            part[index, 1, :, col] = res[TOK:]
            return carry

        lax.fori_loop(0, D // step, one, 0)
        for q in range(CHUNKS):
            at = pl.ds(q * rows, rows)
            send(q, index, part.at[index, oc, at, :], sib_in.at[index, at, :], sib)

    def add(index, first, count, other):
        def one(i, carry):
            at = pl.ds(pl.multiple_of(first + i * 16, 16), 16)
            part[index, c, at, :] = (part[index, c, at, :].astype(F32) + other(at)).astype(BF)
            return carry

        lax.fori_loop(0, count // 16, one, 0)

    def add_sib(q, index):
        cp[q, index].wait_recv()
        add(index, q * rows, rows, lambda at: sib_in[index, at, :].astype(F32))

    def piece(q, which):
        return pl.ds(q * rows + which * half, half)

    def far(q):
        add_sib(q, 0)
        send(q, 4, part.at[0, c, piece(q, 0), :], far_in.at[piece(q, 0), :], up)
        send(q, 5, part.at[0, c, piece(q, 1), :], far_in.at[piece(q, 1), :], dn)

    def near_up(q):
        add_sib(q, 1)
        send(q, 6, part.at[1, c, piece(q, 1), :], end_in.at[0, piece(q, 1), :], up)

    def near_dn(q):
        add_sib(q, 2)
        send(q, 7, part.at[2, c, piece(q, 0), :], end_in.at[1, piece(q, 0), :], dn)

    def passed(q):
        for which, device in ((0, up), (1, dn)):
            cp[q, 4 + which].wait_recv()
            at = piece(q, which)
            add(1 + which, q * rows + which * half, half, lambda at: far_in[at, :].astype(F32))
            send(q, 8 + which, part.at[1 + which, c, at, :], end_in.at[which, at, :], device)

    def make(index):
        if before is not None:
            before(index, order[index])

    def each(one):
        for q in range(CHUNKS):
            one(q)

    make(0)
    multiply(0)
    if before is None:
        multiply(1)
        each(far)
    else:
        make(1)
        each(far)
        multiply(1)
    make(2)
    each(near_up)
    multiply(2)
    make(3)
    each(near_dn)
    multiply(3)
    yield
    each(passed)
    yield
    each(lambda q: add_sib(q, 3))
    yield
    for q in range(CHUNKS):
        for index in range(6, 10):
            cp[q, index].wait_recv()
        ready(q)
        yield
    for copy in cp.values():
        copy.wait_send()


def rows_reduce_steps(ring, src_ref, q, part, sib_in, far_in, end_in, ss, rs, ls, ready):
    rows = TOK // CHUNKS
    half = rows // 2
    order = (ring.zz, ring.zp, ring.zm, ring.z)
    up, dn, sib = ring.up, ring.dn, ring.sib
    cp, loads = {}, []

    def send(index, src, dst, device):
        cp[index] = remote(src, dst, ss.at[index], rs.at[index], device)

    def source(index, core):
        start = order[index] * (2 * TOK) + core * TOK + q * rows
        return src_ref.at[pl.ds(pl.multiple_of(start, 16), rows), :]

    def add(index, first, count, other):
        def one(i, carry):
            at = pl.ds(pl.multiple_of(first + i * 16, 16), 16)
            part[index, at, :] = (part[index, at, :].astype(F32) + other(at)).astype(BF)
            return carry

        lax.fori_loop(0, count // 16, one, 0)

    def add_sib(index):
        loads[index].wait()
        cp[index].wait_recv()
        add(index, 0, rows, lambda at: sib_in[index, at, :].astype(F32))

    low, high = pl.ds(0, half), pl.ds(half, half)
    for index in range(4):
        send(index, source(index, ring.oc), sib_in.at[index], sib)
        loads.append(load(source(index, ring.c), part.at[index], ls.at[index]))
    yield
    add_sib(0)
    send(4, part.at[0, low, :], far_in.at[low, :], up)
    send(5, part.at[0, high, :], far_in.at[high, :], dn)
    add_sib(1)
    send(6, part.at[1, high, :], end_in.at[0, high, :], up)
    add_sib(2)
    send(7, part.at[2, low, :], end_in.at[1, low, :], dn)
    add_sib(3)
    yield
    for which, device in ((0, up), (1, dn)):
        cp[4 + which].wait_recv()
        at = (low, high)[which]
        add(1 + which, which * half, half, lambda at: far_in[at, :].astype(F32))
        send(8 + which, part.at[1 + which, at, :], end_in.at[which, at, :], device)
    yield
    for index in range(6, 10):
        cp[index].wait_recv()

    def total(i, carry):
        at = pl.ds(pl.multiple_of(i * 16, 16), 16)
        ready(
            at,
            pl.ds(pl.multiple_of(q * rows + i * 16, 16), 16),
            part[3, at, :].astype(F32)
            + end_in[0, at, :].astype(F32)
            + end_in[1, at, :].astype(F32),
        )
        return carry

    lax.fori_loop(0, rows // 16, total, 0)
    for copy in cp.values():
        copy.wait_send()


ROWS_SCRATCH = {
    "bpart": pltpu.VMEM((4, TOK // CHUNKS, D), BF),
    "bsib": pltpu.VMEM((4, TOK // CHUNKS, D), BF),
    "bfar": pltpu.VMEM((TOK // CHUNKS, D), BF),
    "bend": pltpu.VMEM((2, TOK // CHUNKS, D), BF),
    "bss": pltpu.SemaphoreType.DMA((10,)),
    "brs": pltpu.SemaphoreType.DMA((10,)),
    "bls": pltpu.SemaphoreType.DMA((4,)),
}
SCATTER_SCRATCH = {
    "part": pltpu.VMEM((4, 2, TOK, D), BF),
    "sib_in": pltpu.VMEM((4, TOK, D), BF),
    "far_in": pltpu.VMEM((TOK, D), BF),
    "end_in": pltpu.VMEM((2, TOK, D), BF),
    "sss": pltpu.SemaphoreType.DMA((10 * CHUNKS,)),
    "srs": pltpu.SemaphoreType.DMA((10 * CHUNKS,)),
}
GATHER_SCRATCH = {
    "buf": pltpu.VMEM((8, TOK, D), BF),
    "ss": pltpu.SemaphoreType.DMA((14 * CHUNKS,)),
    "rs": pltpu.SemaphoreType.DMA((14 * CHUNKS,)),
    "ls": pltpu.SemaphoreType.DMA((8,)),
}
HALF_SCRATCH = {
    "cbuf": pltpu.VMEM((8, TOK // 2, D), BF),
    "css": pltpu.SemaphoreType.DMA((14,)),
    "crs": pltpu.SemaphoreType.DMA((14,)),
    "cls": pltpu.SemaphoreType.DMA((8,)),
}


def plane_view(plane, ref, half, stage, place, part):
    cols = pl.ds(half * (D // 2) + (part or 0) * (D // 4), D // 2 if part is None else D // 4)
    if stage == 0:
        return ref.at[place, plane.y, :, cols] if half == 0 else ref.at[plane.x, place, :, cols]
    return ref.at[:, place, :, cols] if half == 0 else ref.at[place, :, :, cols]


def plane_gather_steps(plane, buf, ss, rs):
    copies = []
    quarter = D // 4

    def view(half, first, second, part):
        x, y = (first, second) if half == 0 else (second, first)
        cols = pl.ds(half * 2 * quarter + (part or 0) * quarter, quarter if part is not None else 2 * quarter)
        return buf.at[x, y, :, cols]

    def send(ref, device):
        copies.append(remote(ref, ref, ss.at[len(copies)], rs.at[len(copies)], device))
        return copies[-1]

    firsts = [plane.ring(half == 0) for half in (0, 1)]
    seconds = [plane.ring(half == 1) for half in (0, 1)]
    near, passed, spread = {}, {}, {}

    def go_on(half, place):
        me, plus, minus, far, to_plus, to_minus = seconds[half]
        piece = view(half, place, me, None)
        spread[half, len(spread)] = (place, send(piece, to_plus), send(piece, to_minus))

    def pass_on(entry):
        half, (place, up, dn) = entry
        me, plus, minus, far, to_plus, to_minus = seconds[half]
        up.wait_recv()
        send(view(half, place, minus, 0), to_plus)
        dn.wait_recv()
        send(view(half, place, plus, 1), to_minus)

    for half in (0, 1):
        me, plus, minus, far, to_plus, to_minus = firsts[half]
        piece = view(half, me, seconds[half][0], None)
        near[half] = (send(piece, to_plus), send(piece, to_minus))
    for half in (0, 1):
        go_on(half, firsts[half][0])
    yield
    for half in (0, 1):
        me, plus, minus, far, to_plus, to_minus = firsts[half]
        other = seconds[half][0]
        near[half][0].wait_recv()
        up = send(view(half, minus, other, 0), to_plus)
        near[half][1].wait_recv()
        passed[half] = (up, send(view(half, plus, other, 1), to_minus))
    for half in (0, 1):
        go_on(half, firsts[half][2])
        go_on(half, firsts[half][1])
    yield
    for half in (0, 1):
        passed[half][0].wait_recv()
        passed[half][1].wait_recv()
        go_on(half, firsts[half][3])
    entries = [(key[0], value) for key, value in spread.items()]
    for entry in entries[:2]:
        pass_on(entry)
    yield
    for entry in entries[2:]:
        pass_on(entry)
    yield
    for copy in copies[-2 * len(entries) :]:
        copy.wait_recv()
    for copy in copies:
        copy.wait_send()


GATHER_COPIES = 40


def plane_reduce_scratch(name, rows):
    return {
        name: pltpu.VMEM((4, 4, rows, D), BF),
        name + "_far": pltpu.VMEM((2, 2, 4, rows, D // 4), BF),
        name + "_end": pltpu.VMEM((2, 2, 4, rows, D // 2), BF),
        name + "_far2": pltpu.VMEM((2, 2, rows, D // 4), BF),
        name + "_end2": pltpu.VMEM((2, 2, rows, D // 2), BF),
        name + "_ss": pltpu.SemaphoreType.DMA((24,)),
        name + "_rs": pltpu.SemaphoreType.DMA((24,)),
    }


def plane_reduce(plane, r, name, outs):
    refs = [getattr(r, name + end) for end in ("", "_far", "_end", "_far2", "_end2", "_ss", "_rs")]
    return plane_reduce_steps(plane, *refs, outs)


def plane_reduce_steps(plane, grads, far_a, end_a, far_b, end_b, ss, rs, outs):
    copies = []
    rows = grads.shape[2]

    def send(src, dst, device):
        copies.append(remote(src, dst, ss.at[len(copies)], rs.at[len(copies)], device))
        return copies[-1]

    def add(view, *others):
        def one(i, carry):
            at = pl.ds(pl.multiple_of(i * 16, 16), 16)
            piece = view.at[..., at, :]
            total = piece[...].astype(F32)
            for other in others:
                total = total + other.at[..., at, :][...].astype(F32)
            piece[...] = total.astype(BF)
            return carry

        lax.fori_loop(0, rows // 16, one, 0)

    for stage in (0, 1):
        rings = [plane.ring(half != stage) for half in (0, 1)]
        far_in, end_in = (far_a, end_a) if stage == 0 else (far_b, end_b)

        def view(half, place, part):
            return plane_view(plane, grads, half, 1 - stage, place, part)

        def ends(half, side, part):
            if part is None:
                return end_in.at[half, side]
            return end_in.at[half, side, ..., pl.ds(part * (D // 4), D // 4)]

        first, last = [], []
        for half in (0, 1):
            me, plus, minus, far, to_plus, to_minus = rings[half]
            first.append(
                (
                    send(view(half, far, 0), far_in.at[half, 0], to_plus),
                    send(view(half, far, 1), far_in.at[half, 1], to_minus),
                )
            )
            last.append(send(view(half, plus, 1), ends(half, 0, 1), to_plus))
            last.append(send(view(half, minus, 0), ends(half, 1, 0), to_minus))
        yield
        for half in (0, 1):
            me, plus, minus, far, to_plus, to_minus = rings[half]
            first[half][0].wait_recv()
            add(view(half, plus, 0), far_in.at[half, 0])
            last.append(send(view(half, plus, 0), ends(half, 0, 0), to_plus))
            first[half][1].wait_recv()
            add(view(half, minus, 1), far_in.at[half, 1])
            last.append(send(view(half, minus, 1), ends(half, 1, 1), to_minus))
        yield
        for copy in last:
            copy.wait_recv()
        for half in (0, 1):
            me = rings[half][0]
            if stage == 0:
                add(view(half, me, None), ends(half, 0, None), ends(half, 1, None))
            else:
                cols = pl.ds(half * (D // 2), D // 2)
                total = (
                    view(half, me, None)[...].astype(F32)
                    + end_in[half, 0].astype(F32)
                    + end_in[half, 1].astype(F32)
                )
                for start, out_ref in outs:
                    out_ref[:, cols] = total[start : start + out_ref.shape[0]]
    for copy in copies:
        copy.wait_send()


def load(src, dst, sem):
    copy = pltpu.make_async_copy(src, dst, sem)
    copy.start()
    return copy


def params(collective_id, limit=58):
    return pltpu.CompilerParams(
        collective_id=collective_id, has_side_effects=True, vmem_limit_bytes=limit << 20
    )


def sds(shape, dtype=BF):
    return jax.ShapeDtypeStruct(shape, dtype)


def scale_of(rows):
    return lax.rsqrt(jnp.mean(rows * rows, axis=-1, keepdims=True) + EPSILON)


def by_rows(one, start=0, rows=TOK):
    def step(i, carry):
        one(pl.ds(pl.multiple_of(start + i * 16, 16), 16))
        return carry

    lax.fori_loop(0, rows // 16, step, 0)


def total_rows(part, end_in, c, at):
    return (
        part[3, c, at, :].astype(F32)
        + end_in[0, at, :].astype(F32)
        + end_in[1, at, :].astype(F32)
    )


def chip_rows(chip):
    return pl.ds(pl.multiple_of(chip * (2 * TOK), 2 * TOK), 2 * TOK)


def build(body, inputs, outputs, scratch, collective_id):
    names = list(inputs) + list(outputs) + list(scratch)

    def kernel(*refs):
        body(types.SimpleNamespace(**dict(zip(names, refs))))

    results = pl.pallas_call(
        kernel,
        out_shape=tuple(shape for shape, _ in outputs.values()),
        in_specs=[spec for _, spec in inputs.values()],
        out_specs=tuple(spec for _, spec in outputs.values()),
        scratch_shapes=list(scratch.values()),
        compiler_params=params(collective_id),
    )(*[array for array, _ in inputs.values()])
    return types.SimpleNamespace(**dict(zip(outputs, results)))


def vm(array):
    return (array, VM)


def hbm(array):
    return (array, ANY)


def signal(partners):
    barrier = pltpu.get_barrier_semaphore()
    for device in partners:
        pl.semaphore_signal(barrier, inc=1, device_id=device, device_id_type=MESH)


def arrive(partners):
    pl.semaphore_wait(pltpu.get_barrier_semaphore(), len(partners))


def scatter(ring, r, product, ready, before=None):
    return scatter_steps(
        ring, product, r.part, r.sib_in, r.far_in, r.end_in, r.sss, r.srs, ready, before
    )


def scatter_gather(ring, r, product, one, out_ref, done=None, others=(), before=None):
    rows = TOK // CHUNKS
    gathers = []

    def ready(q):
        by_rows(one, q * rows, rows)
        last = q == CHUNKS - 1
        steps = gather_steps(
            ring,
            r.buf,
            out_ref,
            r.ss,
            r.rs,
            r.ls,
            rows,
            start=q * rows,
            base=14 * q,
            keep=last,
            ready=done if last else None,
        )
        advance(steps)
        gathers.append(steps)

    weave(scatter(ring, r, product, ready, before), *others)
    for _ in range(5):
        for steps in gathers:
            advance(steps)
        for other in others:
            advance(other)
    for steps in gathers:
        finish(steps)


def sums_of(r, ring, at):
    return total_rows(r.part, r.end_in, ring.c, at)


def half_gather(ring, r, out_ref):
    return gather_steps(ring, r.cbuf, out_ref, r.css, r.crs, r.cls, TOK // 2)


def rows_reduce(ring, r, q, ready):
    return rows_reduce_steps(
        ring, r.down, q, r.bpart, r.bsib, r.bfar, r.bend, r.bss, r.brs, r.bls, ready
    )


def norm_into(r, ring, gain_ref, at, rows):
    r.buf[ring.z * 2 + ring.c, at, :] = (rows * scale_of(rows) * gain_ref[...]).astype(BF)


def first_part(r, ring, plane):
    def one(at):
        norm_into(r, ring, r.gain_a, at, r.x[at, :].astype(F32))

    by_rows(one)
    arrive(r.partners)
    weights = plane_gather_steps(plane, r.wide, r.wss, r.wrs)

    def project(chip):
        h = r.buf[pl.ds(2 * chip, 2)].reshape(2 * TOK, D)
        r.raw[chip_rows(chip), :] = dnt(h, r.wide[...].reshape(16 * BIN_PAD, D)).astype(BF)

    rows = gather_steps(ring, r.buf, r.h, r.fss, r.frs, r.fls, TOK, ready=project)
    outs = plane_gather_steps(plane, r.wout, r.oss, r.ors)
    advance(weights)
    advance(rows)
    advance(weights)
    advance(outs)
    advance(weights)
    advance(outs)
    advance(rows)
    advance(weights)
    advance(rows)
    finish(weights)
    advance(outs)
    keep = load(r.wide, r.w_in, r.wls.at[0])
    finish(rows)
    return outs, keep


def ring_forward(r, ring, y_ref, w_ref, gain_ref, others=(), before=None):
    def product(rows, col):
        return dnn(y_ref[rows, :], w_ref[:, :, :, col].reshape(256, -1))

    def one(at):
        rows = r.x[at, :].astype(F32) + sums_of(r, ring, at)
        r.x_out[at, :] = rows
        norm_into(r, ring, gain_ref, at, rows)

    scatter_gather(ring, r, product, one, r.h_out, others=others, before=before)


def norm_back_rows(v_ref, gain_ref, grads, at):
    rows = v_ref[at, :].astype(F32)
    scale = scale_of(rows)
    unit = rows * scale
    scaled = grads * gain_ref[...]
    return scale * (scaled - unit * jnp.mean(scaled * unit, axis=-1, keepdims=True))


def ring_backward(r, ring, product, wo_ref, others, before=None, also=None):
    def one(at):
        grad = sums_of(r, ring, at)
        rows = r.res[at, :].astype(F32) + norm_back_rows(r.v, r.gain, grad, at)
        r.d_out[at, :] = rows
        r.buf[ring.z * 2 + ring.c, at, :] = rows.astype(BF)

    def done(chip):
        rows = r.buf[pl.ds(2 * chip, 2)].reshape(2 * TOK, D)
        r.dy_out[chip_rows(chip), :] = dnt(rows, wo_ref[...].reshape(256, D)).astype(BF)
        if also is not None:
            also(chip, rows)

    scatter_gather(ring, r, product, one, r.e_out, done, others, before)


CHUNK = 8 * UNIT_PAD


def mlp_chip(r, chip, i):
    at = chip_rows(chip)
    tokens = pl.ds(2 * chip, 2)
    units = slice(8 * i, 8 * i + 8)
    rows = r.hv[tokens].reshape(2 * TOK, D)
    gate = dnt(rows, r.wv[0, units].reshape(CHUNK, D))
    up = dnt(rows, r.wv[1, units].reshape(CHUNK, D))
    d_act = dnt(r.cotv[tokens].reshape(2 * TOK, D), r.downv[units].reshape(CHUNK, D))
    sig = 1.0 / (1.0 + jnp.exp(-gate))
    silu = gate * sig
    first = i * CHUNK
    r.act[at, first : first + CHUNK] = (silu * up).astype(BF)
    r.d_gu[at, first : first + CHUNK] = (
        d_act * up * (sig * (1.0 + gate * (1.0 - sig)))
    ).astype(BF)
    r.d_gu[at, first + 2 * CHUNK : first + 3 * CHUNK] = (d_act * silu).astype(BF)


def mlp_down_steps(r):
    for n in range(4):
        at = slice(2 * TOK * n, 2 * TOK * (n + 1))
        for col in range(0, D, 512):
            r.outv[at, col : col + 512] = dnn(
                r.act[at, :], r.downv[:, :, col : col + 512].reshape(2 * CHUNK, 512)
            ).astype(BF)
        if n == 1:
            yield
    copy = load(r.outv, r.down, r.msem.at[9])
    yield
    copy.wait()


def mlp_grad_steps(r, jobs):
    copies = []
    for n, (lhs, col, rhs, off, half, w) in enumerate(jobs):
        slot = n % 2
        if n >= 2:
            copies[n - 2].wait()

        res = dtn(lhs[:, col : col + CHUNK], rhs[...].reshape(HALF_TOK, D))
        r.stage[slot] = res.astype(BF).reshape(8, UNIT_PAD, D)
        if w is not None:
            own = w[8 * half : 8 * half + 8].reshape(CHUNK, D).astype(F32)
            r.gacc[...] += jnp.sum(res * own, axis=0, keepdims=True)
        copies.append(
            load(
                r.stage.at[slot],
                r.grads.at[pl.ds(8 * half, 8), pl.ds(off, UNIT_PAD), :],
                r.gsem.at[n],
            )
        )
        yield
    copies[-2].wait()
    copies[-1].wait()


def mlp_body(r):
    ring = Ring()
    partners = (ring.up, ring.dn, ring.sib)
    half = TOK // 2
    weights_in, tokens_in = {}, {}

    def fetch(index, chip):
        at = pl.ds(2 * chip, 2)
        pairs = (
            (r.h.at[at], r.hv.at[at]),
            (r.lo.at[at], r.cotv.at[at, pl.ds(0, half), :]),
            (r.hi.at[at], r.cotv.at[at, pl.ds(half, half), :]),
        )
        tokens_in[index] = [
            load(src, dst, r.tsem.at[3 * index + n]) for n, (src, dst) in enumerate(pairs)
        ]

    fetch(0, ring.zz)
    for i in range(2):
        for n, ref in enumerate((r.wv.at[0], r.wv.at[1], r.downv)):
            weights_in[i, n] = load(
                r.w.at[pl.ds(8 * i, 8), pl.ds(n * UNIT_PAD, UNIT_PAD), :],
                ref.at[pl.ds(8 * i, 8)],
                r.msem.at[3 * i + n],
            )
    for index, chip in ((1, ring.zp), (2, ring.zm), (3, ring.z)):
        fetch(index, chip)
    late = load(r.wo.at[:, :, pl.ds(48, 16), :], r.wov, r.msem.at[10])
    signal(partners)
    r.gacc[...] = jnp.zeros_like(r.gacc)
    arrive(partners)

    def before(index, chip):
        for copy in tokens_in[index]:
            copy.wait()
        for i in range(2):
            if index == 0:
                for n in range(3):
                    weights_in[i, n].wait()
            mlp_chip(r, chip, i)

    def product(rows, col):
        return dnn(r.d_gu[rows, :], r.wv[:, :, :, col].reshape(4 * CHUNK, -1))

    def weights():
        yield from mlp_down_steps(r)
        jobs = [
            (r.d_gu, n * CHUNK, r.hv, (n // 2) * UNIT_PAD, n % 2, r.wv.at[n // 2])
            for n in range(4)
        ]
        jobs += [(r.act, n * CHUNK, r.cotv, 2 * UNIT_PAD, n, None) for n in range(2)]
        yield from mlp_grad_steps(r, jobs)

    weight_grads = weights()
    late.wait()
    ring_backward(r, ring, product, r.wov, (weight_grads,), before)
    finish(weight_grads)
    r.gain_out[...] = r.gacc[...] / r.gain[...]


def mlp_step(h, lo, hi, w, wo, v, gain, cot):
    return build(
        mlp_body,
        {
            "h": hbm(h),
            "lo": hbm(lo),
            "hi": hbm(hi),
            "w": hbm(w),
            "wo": hbm(wo),
            "v": vm(v),
            "gain": vm(gain),
            "res": vm(cot),
        },
        {
            "down": (sds((HALF_TOK, D)), ANY),
            "d_out": (sds((TOK, D), F32), VM),
            "gain_out": (sds((1, D), F32), VM),
            "e_out": (sds((8, TOK, D)), ANY),
            "dy_out": (sds((HALF_TOK, 256)), VM),
            "grads": (sds((16, 3 * UNIT_PAD, D)), ANY),
        },
        {
            "hv": pltpu.VMEM((8, TOK, D), BF),
            "cotv": pltpu.VMEM((8, TOK, D), BF),
            "wv": pltpu.VMEM((2, 16, UNIT_PAD, D), BF),
            "downv": pltpu.VMEM((16, UNIT_PAD, D), BF),
            "wov": pltpu.VMEM((4, 4, 16, D), BF),
            "act": pltpu.VMEM((HALF_TOK, 2 * CHUNK), BF),
            "d_gu": pltpu.VMEM((HALF_TOK, 4 * CHUNK), BF),
            "outv": pltpu.VMEM((HALF_TOK, D), BF),
            "stage": pltpu.VMEM((2, 8, UNIT_PAD, D), BF),
            "gacc": pltpu.VMEM((1, D), F32),
            "msem": pltpu.SemaphoreType.DMA((11,)),
            "tsem": pltpu.SemaphoreType.DMA((12,)),
            "gsem": pltpu.SemaphoreType.DMA((6,)),
        }
        | SCATTER_SCRATCH
        | GATHER_SCRATCH,
        4,
    )


def state_tables():
    first = np.zeros((128, STATE), np.float32)
    second = np.zeros((128, STATE), np.float32)
    bias = np.zeros((8, STATE), np.float32)
    coef = np.zeros((8, STATE), np.float32)
    bias[0, 0] = bias[1, 0] = 1.0
    coef[0, 0] = 1.0
    at = 1
    for i in range(FEAT):
        first[i, at] = 1.0
        bias[1, at] = 1.0
        coef[0, at] = 1.0 / math.sqrt(FEAT)
        at += 1
    for i in range(FEAT):
        for j in range(i, FEAT):
            first[i, at] = 1.0
            second[j, at] = 1.0
            coef[0, at] = (0.5 if i == j else 1.0) / FEAT
            at += 1
    picks = np.zeros((4, 128, 128), np.float32)
    for which in range(4):
        for i in range(FEAT):
            picks[which, which * FEAT + i, i] = 1.0
    return (
        np.stack([first, second]),
        np.concatenate([bias[:2], coef[:1], np.zeros((5, STATE), np.float32)]),
        picks,
    )


def select_table(width):
    table = np.zeros((16 * BIN_PAD, 3 * HEAD_V), np.float32)
    for shard in range(16):
        for i in range(width):
            head, col = shard // 8, (shard % 8) * width + i
            to = 2 * HEAD_V + 2 * FEAT * head + col if col < 2 * FEAT else head * HEAD_V + col - 2 * FEAT
            table[shard * BIN_PAD + i, to] = 1.0
    return table


BLK = 256
NBLK = HALF_TOK // BLK
INV_ROOT = 1.0 / math.sqrt(FEAT)


def rows_of(b):
    return slice(b * BLK, (b + 1) * BLK)


def head_of(j):
    return slice(j * HEAD_V, (j + 1) * HEAD_V)


def chip_block(b):
    return pl.ds(pl.multiple_of(b * BLK, BLK), BLK) if not isinstance(b, int) else rows_of(b)


def causal_mask(start, edge):
    t = start + lax.broadcasted_iota(jnp.int32, (BLK, BLK), 0)
    u = start + lax.broadcasted_iota(jnp.int32, (BLK, BLK), 1)
    return (u <= t) & ((t >= edge) == (u >= edge))


class Linear:
    def __init__(self, r):
        self.r = r
        self.xh = lax.axis_index("xh")
        self.partner = {"xh": 1 - self.xh}
        self.edge = jnp.where(self.xh == 0, EDGE, HALF_TOK - EDGE)
        self.second = jnp.where(self.xh == 1, 1.0, 0.0)
        self.coef = r.t[2:3, :]

    def vectors(self):
        r = self.r
        small = r.p[:, 2 * HEAD_V :]
        for j in range(2):
            r.qs[j] = dnn(small, r.pick[2 * j]).astype(BF)
            r.ks[j] = dnn(small, r.pick[2 * j + 1]).astype(BF)

    def factors(self, vecs):
        r = self.r
        return dnn(vecs, r.e[0]) + r.t[0:1, :], dnn(vecs, r.e[1]) + r.t[1:2, :]

    def factors_back(self, grad, one, two):
        r = self.r
        return dnt((grad * two).astype(BF), r.e[0]) + dnt((grad * one).astype(BF), r.e[1])

    def key_open(self, width):
        slot = lax.broadcasted_iota(jnp.int32, (BLK, width), 0)
        return (slot >= EDGE) | (self.xh == 1)

    def sees_state(self, b, width):
        slot = b * BLK + lax.broadcasted_iota(jnp.int32, (BLK, width), 0)
        return (slot < HALF_TOK - EDGE) | (self.xh == 0)

    def scores(self, j, b):
        r = self.r
        scores = dnt(r.qs[j, chip_block(b), :], r.ks[j, chip_block(b), :]) * INV_ROOT
        mask = causal_mask(b * BLK, self.edge)
        return scores, mask, jnp.where(mask, 1.0 + scores + 0.5 * scores * scores, 0.0)


def linear_states(r, lin):
    for b in range(NBLK):
        r.p[rows_of(b), :] = dnn(r.raw[rows_of(b), :], r.sel[...]).astype(BF)
    lin.vectors()
    for j in range(2):
        sv = jnp.zeros((HEAD_V, STATE), F32)
        sn = jnp.zeros((1, STATE), F32)
        for b in range(NBLK):
            r.pre_v[j, b] = sv
            r.pre_n[j, b] = jnp.broadcast_to(sn, (8, STATE))
            one, two = lin.factors(r.ks[j, rows_of(b), :])
            phi = one * two
            if b == 0:
                phi = jnp.where(lin.key_open(STATE), phi, 0.0)
            sv = sv + dtn(r.p[rows_of(b), head_of(j)], phi.astype(BF)) * lin.coef
            sn = sn + jnp.sum(phi, axis=0, keepdims=True) * lin.coef
        r.sv_s[j] = sv.astype(BF)
        r.sn_s[j] = jnp.broadcast_to(sn, (8, STATE))
    return (
        remote(r.sv_s, r.sv_r, r.xss.at[0], r.xrs.at[0], lin.partner),
        remote(r.sn_s, r.sn_r, r.xss.at[1], r.xrs.at[1], lin.partner),
    )


def linear_own(r, lin, b):
    rows = chip_block(b)
    for j in range(2):
        _, _, kernel = lin.scores(j, b)
        r.num[j, rows, :] = dnn(kernel.astype(BF), r.p[rows, head_of(j)])
        r.den[j, rows, :] = jnp.broadcast_to(
            jnp.sum(kernel, axis=-1, keepdims=True), (BLK, HEAD_V)
        )


def linear_rest(r, lin, b):
    rows = chip_block(b)
    for j in range(2):
        state_v = (r.pre_v[j, b] + r.sv_r[j].astype(F32) * lin.second).astype(BF)
        state_n = r.pre_n[j, b] + r.sn_r[j] * lin.second
        r.sv[j, b] = state_v
        r.sn[j, b] = state_n
        one, two = lin.factors(r.qs[j, rows, :])
        phi = one * two
        den = jnp.sum(phi * state_n[0:1, :], axis=-1, keepdims=True)
        num = dnt(phi.astype(BF), state_v)
        seen = lin.sees_state(b, HEAD_V)
        top = r.num[j, rows, :] + jnp.where(seen, num, 0.0)
        bottom = r.den[j, rows, :] + jnp.where(seen, den, 0.0)
        r.y[rows, head_of(j)] = (top / bottom).astype(BF)


STATE_SCRATCH = {
    "qs": pltpu.VMEM((2, HALF_TOK, 128), BF),
    "ks": pltpu.VMEM((2, HALF_TOK, 128), BF),
    "sv_s": pltpu.VMEM((2, HEAD_V, STATE), BF),
    "sn_s": pltpu.VMEM((2, 8, STATE), F32),
    "sv_r": pltpu.VMEM((2, HEAD_V, STATE), BF),
    "sn_r": pltpu.VMEM((2, 8, STATE), F32),
    "pre_v": pltpu.VMEM((2, NBLK, HEAD_V, STATE), F32),
    "pre_n": pltpu.VMEM((2, NBLK, 8, STATE), F32),
    "xss": pltpu.SemaphoreType.DMA((2,)),
    "xrs": pltpu.SemaphoreType.DMA((2,)),
}


def linear_body(r):
    ring, plane = Ring(), Plane()
    r.partners = (ring.up, ring.dn, ring.sib, {"xh": 1 - lax.axis_index("xh")})
    r.partners += plane.neighbours()
    signal(r.partners)
    own = r.wide.at[plane.x, plane.y]
    own[BIN_PAD // 2 :, :] = jnp.zeros((BIN_PAD // 2, D), BF)
    own[: r.rows_in.shape[0], :] = r.rows_in[...]
    r.wout[plane.x, plane.y] = r.rows_out[...]
    r.cbuf[ring.z * 2 + ring.c] = r.cot[: TOK // 2, :]
    outs, keep = first_part(r, ring, plane)
    cots = half_gather(ring, r, r.lo)
    advance(cots)
    lin = Linear(r)
    states = linear_states(r, lin)
    advance(outs)
    linear_own(r, lin, ring.zz)
    advance(outs)
    linear_own(r, lin, ring.zp)
    advance(cots)
    advance(cots)
    finish(outs)
    keep_out = load(r.wout, r.w_out, r.wls.at[1])

    def before(index, chip):
        if index == 0:
            for copy in states:
                copy.wait_recv()
        if index >= 2:
            linear_own(r, lin, chip)
        linear_rest(r, lin, chip)

    ring_forward(r, ring, r.y, r.wout, r.gain_b, (cots,), before)
    finish(cots)
    keep.wait()
    keep_out.wait()
    for copy in states:
        copy.wait_send()


def linear_step(select, tables, cot, x, gain_a, gain_b, rows_in, rows_out):
    return build(
        linear_body,
        {
            "sel": vm(select),
            "e": vm(tables[0]),
            "t": vm(tables[1]),
            "pick": vm(tables[2]),
            "cot": vm(cot),
            "x": vm(x),
            "gain_a": vm(gain_a),
            "gain_b": vm(gain_b),
            "rows_in": vm(rows_in),
            "rows_out": vm(rows_out),
        },
        {
            "h": (sds((8, TOK, D)), ANY),
            "w_in": (sds((4, 4, BIN_PAD, D)), ANY),
            "w_out": (sds((4, 4, 16, D)), ANY),
            "y": (sds((HALF_TOK, 2 * HEAD_V)), VM),
            "p": (sds((HALF_TOK, 3 * HEAD_V)), VM),
            "sv": (sds((2, NBLK, HEAD_V, STATE)), VM),
            "sn": (sds((2, NBLK, 8, STATE), F32), VM),
            "lo": (sds((8, TOK // 2, D)), ANY),
            "x_out": (sds((TOK, D), F32), VM),
            "h_out": (sds((8, TOK, D)), ANY),
        },
        {
            "raw": pltpu.VMEM((HALF_TOK, 16 * BIN_PAD), BF),
            "num": pltpu.VMEM((2, HALF_TOK, HEAD_V), F32),
            "den": pltpu.VMEM((2, HALF_TOK, HEAD_V), F32),
            "wide": pltpu.VMEM((4, 4, BIN_PAD, D), BF),
            "wout": pltpu.VMEM((4, 4, 16, D), BF),
            "wss": pltpu.SemaphoreType.DMA((GATHER_COPIES,)),
            "wrs": pltpu.SemaphoreType.DMA((GATHER_COPIES,)),
            "oss": pltpu.SemaphoreType.DMA((GATHER_COPIES,)),
            "ors": pltpu.SemaphoreType.DMA((GATHER_COPIES,)),
            "wls": pltpu.SemaphoreType.DMA((2,)),
            "fss": pltpu.SemaphoreType.DMA((14,)),
            "frs": pltpu.SemaphoreType.DMA((14,)),
            "fls": pltpu.SemaphoreType.DMA((8,)),
        }
        | STATE_SCRATCH
        | HALF_SCRATCH
        | SCATTER_SCRATCH
        | GATHER_SCRATCH,
        2,
    )


def linear_backward_own(r, lin, sums, win):
    lin.vectors()
    for j in range(2):
        tv = jnp.zeros((HEAD_V, STATE), F32)
        tn = jnp.zeros((1, STATE), F32)
        for b in range(NBLK):
            queries = r.qs[j, rows_of(b), :]
            grads = r.dy[rows_of(b), head_of(j)]
            one, two = lin.factors(queries)
            phi = one * two
            phi_low = phi.astype(BF)
            seen = lin.sees_state(b, 1)
            state_v, state_n = r.sv[j, b], r.sn[j, b, 0:1, :]
            scores, mask, kernel = lin.scores(j, b)
            weight_grad = dnt(grads, r.p[rows_of(b), head_of(j)])
            den = jnp.sum(phi * state_n, axis=-1, keepdims=True)
            num = dnt(phi_low, state_v)
            dot = jnp.sum(num * grads.astype(F32), axis=-1, keepdims=True)
            total = jnp.where(seen, den, 0.0) + jnp.sum(kernel, axis=-1, keepdims=True)
            dot = jnp.where(seen, dot, 0.0) + jnp.sum(kernel * weight_grad, axis=-1, keepdims=True)
            inverse = 1.0 / total
            mean = dot * inverse
            grads_n = (grads.astype(F32) * inverse).astype(BF)
            score_grad = jnp.where(
                mask, (weight_grad - mean) * inverse * (1.0 + scores), 0.0
            ).astype(BF)
            r.dk[j, rows_of(b), :] = dtn(score_grad, queries)
            r.dv[j, rows_of(b), :] = dtn(kernel.astype(BF), grads_n)
            shift = jnp.where(seen, -(mean * inverse), 0.0)
            grads_s = jnp.where(seen, grads_n, jnp.zeros_like(grads_n))
            phi_grad = dnn(grads_s, state_v) + shift * state_n
            r.dq[j, rows_of(b), :] = dnn(
                score_grad, r.ks[j, rows_of(b), :]
            ) * INV_ROOT + lin.factors_back(phi_grad, one, two)
            own_v = dtn(grads_s, phi_low) * lin.coef
            own_n = jnp.sum(shift * phi, axis=0, keepdims=True) * lin.coef
            r.pre_v[j, b] = own_v
            r.pre_n[j, b] = jnp.broadcast_to(own_n, (8, STATE))
            tv, tn = tv + own_v, tn + own_n
            if (j, b) in ((0, 0), (0, 3)):
                advance(sums)
            if (j, b) == (1, 2):
                advance(win)
        r.sv_s[j] = tv.astype(BF)
        r.sn_s[j] = jnp.broadcast_to(tn, (8, STATE))
    copies = (
        remote(r.sv_s, r.sv_r, r.xss.at[0], r.xrs.at[0], lin.partner),
        remote(r.sn_s, r.sn_r, r.xss.at[1], r.xrs.at[1], lin.partner),
    )
    for j in range(2):
        tv = jnp.zeros((HEAD_V, STATE), F32)
        tn = jnp.zeros((8, STATE), F32)
        for b in reversed(range(NBLK)):
            own_v, own_n = r.pre_v[j, b], r.pre_n[j, b]
            r.pre_v[j, b] = tv
            r.pre_n[j, b] = tn
            tv, tn = tv + own_v, tn + own_n
    return copies


def linear_backward_rest(r, lin, b):
    rows = chip_block(b)
    first = 1.0 - lin.second
    visible = lin.key_open(STATE) | (b > 0)
    placed = jnp.zeros((BLK, 128), F32)
    for j in range(2):
        one, two = lin.factors(r.ks[j, rows, :])
        phi = jnp.where(visible, one * two, 0.0)
        state = (r.pre_v[j, b] + r.sv_r[j].astype(F32) * first).astype(BF)
        state_n = r.pre_n[j, b, 0:1, :] + r.sn_r[j, 0:1, :] * first
        phi_grad = jnp.where(visible, dnn(r.p[rows, head_of(j)], state) + state_n, 0.0)
        key_grad = r.dk[j, rows, :] * INV_ROOT + lin.factors_back(phi_grad, one, two)
        value_grad = r.dv[j, rows, :] + dnt(phi.astype(BF), state)
        r.dp[rows, head_of(j)] = value_grad.astype(BF)
        placed = placed + dnt(r.dq[j, rows, :].astype(BF), r.pick[2 * j])
        placed = placed + dnt(key_grad.astype(BF), r.pick[2 * j + 1])
    r.dp[rows, 2 * HEAD_V :] = placed.astype(BF)
    r.draw[rows, :] = dnt(r.dp[rows, :], r.sel[...]).astype(BF)


def sum_steps(ring, plane, r):
    copies = []
    stages = (
        (r.ring_in, ring.z * 2 + ring.c, 8, lambda t: {"z": lax.div(t, 2), "c": lax.rem(t, 2)}),
        (r.x_in, plane.x, 4, plane.at_x),
        (r.y_in, plane.y, 4, plane.at_y),
    )
    for dst, own, count, device_of in stages:
        dst[own] = r.pack[...]
        sent = []
        for o in range(1, count):
            n = len(copies) + len(sent)
            device = device_of(lax.rem(own + o, count))
            sent.append(remote(r.pack, dst.at[own], r.pss.at[n], r.prs.at[n], device))
        yield
        for copy in sent:
            copy.wait_recv()
        for copy in sent:
            copy.wait_send()
        copies += sent
        total = dst[0]
        for k in range(1, count):
            total = total + dst[k]
        r.pack[...] = total


def last_body(r):
    ring, plane = Ring(), Plane()
    me = ring.z * 2 + ring.c
    partners = []
    for o in range(1, 8):
        to = lax.rem(me + o, 8)
        partners.append({"z": lax.div(to, 2), "c": lax.rem(to, 2)})
    for o in range(1, 4):
        partners.append(plane.at_x(lax.rem(plane.x + o, 4)))
        partners.append(plane.at_y(lax.rem(plane.y + o, 4)))
    signal(partners)
    loads = [
        load(r.g, r.win, r.lsem.at[0]),
        load(r.w, r.wv, r.lsem.at[1]),
        load(r.h, r.hv, r.lsem.at[2]),
    ]
    r.out[: TOK // 2, :] = r.low[...]

    def write(at, rows, total):
        r.out[rows, :] = (r.x3[rows, :] + total).astype(BF)

    sums = rows_reduce(ring, r, 1, write)
    win = plane_reduce(plane, r, "win", ((0, r.win_in), (48, r.win_out), (64, r.lin_out)))
    arrive(partners)
    advance(sums)
    loads[0].wait()
    advance(win)
    lin = Linear(r)
    states = linear_backward_own(r, lin, sums, win)
    finish(sums)
    for copy in loads[1:]:
        copy.wait()

    def before(index, chip):
        if index == 0:
            for copy in states:
                copy.wait_recv()
        linear_backward_rest(r, lin, chip)

    wide = D // 8

    def product(rows, col):
        return dnn(r.draw[rows, :], r.wv[:, :, :, col].reshape(16 * BIN_PAD, -1))

    def weights():
        for k in range(4):
            cols = slice(k * 512, (k + 1) * 512)
            res = dtn(r.draw[...], r.hv[:, :, cols].reshape(HALF_TOK, 512))
            own = r.wv[:, :, :, cols].reshape(16 * BIN_PAD, 512).astype(F32)
            r.gacc[:, cols] = jnp.sum(res * own, axis=0, keepdims=True)
            r.lin[:, :, :, cols] = res.astype(BF).reshape(4, 4, BIN_PAD, 512)
        reduce = plane_reduce(plane, r, "lin", ((0, r.lin_in),))
        advance(reduce)
        gains = (r.gacc[...] / r.gain[...], r.gain_b[...], r.gain_c[...])
        for n, gain in enumerate(gains):
            for i in range(8):
                r.pack[i : i + 1, n * wide : (n + 1) * wide] = gain[:, i * wide : (i + 1) * wide]
        gain_sums = sum_steps(ring, plane, r)
        advance(gain_sums)
        yield
        advance(reduce)
        advance(gain_sums)
        yield
        advance(win)
        advance(reduce)
        advance(gain_sums)
        yield
        advance(win)
        yield
        advance(reduce)
        finish(gain_sums)
        yield
        finish(win)
        finish(reduce)

    weight_grads = weights()

    def one(at):
        r.d_out[at, :] = r.res[at, :] + norm_back_rows(r.v, r.gain, sums_of(r, ring, at), at)

    def ready(q):
        by_rows(one, q * (TOK // CHUNKS), TOK // CHUNKS)

    weave(scatter(ring, r, product, ready, before), weight_grads)
    for copy in states:
        copy.wait_send()
    finish(weight_grads)
    for n, out in enumerate((r.ga, r.gb, r.gc)):
        for i in range(8):
            out[:, i * wide : (i + 1) * wide] = r.pack[i : i + 1, n * wide : (n + 1) * wide]


def last_step(lin, dy, select, tables, down, x3, low, g, w, h, v, gain, res, gain_b, gain_c, width):
    small = (8, 3 * D // 8)
    return build(
        last_body,
        {
            "p": vm(lin.p),
            "dy": vm(dy),
            "sv": vm(lin.sv),
            "sn": vm(lin.sn),
            "sel": vm(select),
            "e": vm(tables[0]),
            "t": vm(tables[1]),
            "pick": vm(tables[2]),
            "down": hbm(down),
            "x3": vm(x3),
            "low": vm(low),
            "g": hbm(g),
            "w": hbm(w),
            "h": hbm(h),
            "v": vm(v),
            "gain": vm(gain),
            "res": vm(res),
            "gain_b": vm(gain_b),
            "gain_c": vm(gain_c),
        },
        {
            "out": (sds((TOK, D)), VM),
            "d_out": (sds((TOK, D), F32), VM),
            "ga": (sds((1, D), F32), VM),
            "gb": (sds((1, D), F32), VM),
            "gc": (sds((1, D), F32), VM),
            "win_in": (sds((48, D), F32), VM),
            "win_out": (sds((16, D), F32), VM),
            "lin_in": (sds((width, D), F32), VM),
            "lin_out": (sds((16, D), F32), VM),
        },
        {
            "dp": pltpu.VMEM((HALF_TOK, 3 * HEAD_V), BF),
            "draw": pltpu.VMEM((HALF_TOK, 16 * BIN_PAD), BF),
            "dq": pltpu.VMEM((2, HALF_TOK, 128), F32),
            "dk": pltpu.VMEM((2, HALF_TOK, 128), F32),
            "dv": pltpu.VMEM((2, HALF_TOK, HEAD_V), F32),
            "wv": pltpu.VMEM((4, 4, BIN_PAD, D), BF),
            "hv": pltpu.VMEM((8, TOK, D), BF),
            "gacc": pltpu.VMEM((1, D), F32),
            "pack": pltpu.VMEM(small, F32),
            "ring_in": pltpu.VMEM((8,) + small, F32),
            "x_in": pltpu.VMEM((4,) + small, F32),
            "y_in": pltpu.VMEM((4,) + small, F32),
            "pss": pltpu.SemaphoreType.DMA((13,)),
            "prs": pltpu.SemaphoreType.DMA((13,)),
            "lsem": pltpu.SemaphoreType.DMA((3,)),
        }
        | STATE_SCRATCH
        | ROWS_SCRATCH
        | plane_reduce_scratch("win", 80)
        | plane_reduce_scratch("lin", BIN_PAD)
        | SCATTER_SCRATCH,
        6,
    )


WBLK = 128
WKEYS = WBLK + WINDOW
INV_ROOT_V = 1.0 / math.sqrt(HEAD_V)


def turn_tables():
    slot = np.arange(2 * HALF_TOK)
    last = 2 * HALF_TOK - EDGE
    position = slot - np.where(slot < EDGE, 0, np.where(slot < last, EDGE, last))
    frequency = np.exp(-math.log(10000.0) * np.arange(HEAD_V // 2) * 2.0 / HEAD_V)
    angles = position[:, None] * frequency[None, :]
    cosine, sine = np.cos(angles), np.sin(angles)
    pair = np.stack(
        [np.concatenate([cosine, cosine], axis=1), np.concatenate([-sine, sine], axis=1)]
    )
    return pair.reshape(2, 2, HALF_TOK, HEAD_V).transpose(1, 0, 2, 3).astype(np.float32)


class Window:
    def __init__(self):
        self.xh = lax.axis_index("xh")
        self.partner = {"xh": 1 - self.xh}
        self.edge = jnp.where(self.xh == 0, EDGE, HALF_TOK - EDGE)
        self.lowest = jnp.where(self.xh == 0, 0, -WINDOW)

    def mask(self, b):
        t = b * WBLK + lax.broadcasted_iota(jnp.int32, (WBLK, WKEYS), 0)
        u = b * WBLK - WINDOW + lax.broadcasted_iota(jnp.int32, (WBLK, WKEYS), 1)
        same = (t >= self.edge) == (u >= self.edge)
        return (u <= t) & (t - u < WINDOW) & same & (u >= self.lowest)

    def probs(self, r, b, j):
        rows, keys, head = window_rows(b), window_keys(b), head_of(j)
        scores = dnt(r.q[rows, head], r.kv[keys, head]) * INV_ROOT_V
        scores = jnp.where(self.mask(b), scores, -1e30)
        exps = jnp.exp(scores - jnp.max(scores, axis=-1, keepdims=True))
        return exps / jnp.sum(exps, axis=-1, keepdims=True)


def window_rows(b):
    return pl.ds(b * WBLK if isinstance(b, int) else pl.multiple_of(b * WBLK, WBLK), WBLK)


def window_keys(b):
    return pl.ds(b * WBLK if isinstance(b, int) else pl.multiple_of(b * WBLK, WBLK), WKEYS)


def window_vectors(r, win, cots):
    size = 2 * TOK
    blocks = HALF_TOK // size

    def turned(vecs, rows):
        return (
            vecs * r.turn[0, rows, :] + pltpu.roll(vecs, HEAD_V // 2, 1) * r.turn[1, rows, :]
        ).astype(BF)

    for b in (blocks - 1,) + tuple(range(blocks - 1)):
        rows = slice(b * size, (b + 1) * size)
        shifted = slice(WINDOW + b * size, WINDOW + (b + 1) * size)
        tokens = r.hv[2 * b : 2 * b + 2].reshape(size, D)
        for j in range(2):
            proj = dnt(tokens, r.wiv[2 * j : 2 * j + 2].reshape(384, D))
            r.q[rows, head_of(j)] = turned(proj[:, :128], rows)
            r.kv[shifted, head_of(j)] = turned(proj[:, 128:256], rows)
            r.kv[shifted, head_of(2 + j)] = proj[:, 256:].astype(BF)
        if b == blocks - 1:
            copy = remote(
                r.kv.at[pl.ds(HALF_TOK, WINDOW), :],
                r.kv.at[pl.ds(0, WINDOW), :],
                r.xss,
                r.xrs,
                win.partner,
            )
    advance(cots)
    return copy


def window_chip(r, win, chip):
    for i in range(2 * TOK // WBLK):
        b = chip * (2 * TOK // WBLK) + i
        for j in range(2):
            r.y[window_rows(b), head_of(j)] = dnn(
                win.probs(r, b, j).astype(BF), r.kv[window_keys(b), head_of(2 + j)]
            ).astype(BF)


def window_body(r):
    ring = Ring()
    partners = (ring.up, ring.dn, ring.sib, {"xh": 1 - lax.axis_index("xh")})
    signal(partners)
    loads = (
        load(r.w.at[:, :, pl.ds(0, 48), :], r.wiv, r.lsem.at[0]),
        load(r.h, r.hv, r.lsem.at[1]),
        load(r.turns.at[lax.axis_index("xh")], r.turn, r.lsem.at[2]),
        load(r.w.at[:, :, pl.ds(48, 16), :], r.wov, r.lsem.at[3]),
    )
    r.cbuf[ring.z * 2 + ring.c] = r.cot[TOK // 2 :, :]
    arrive(partners)
    cots = half_gather(ring, r, r.hi)
    advance(cots)
    for copy in loads:
        copy.wait()
    win = Window()
    halo = window_vectors(r, win, cots)

    def before(index, chip):
        if index == 0:
            halo.wait_recv()
        window_chip(r, win, chip)

    ring_forward(r, ring, r.y, r.wov, r.gain, (cots,), before)
    finish(cots)
    halo.wait_send()


def window_step(h, w, turns, cot, x, gain):
    return build(
        window_body,
        {
            "h": hbm(h),
            "w": hbm(w),
            "turns": hbm(turns),
            "cot": vm(cot),
            "x": vm(x),
            "gain": vm(gain),
        },
        {
            "y": (sds((HALF_TOK, 256)), VM),
            "q": (sds((HALF_TOK, 256)), VM),
            "kv": (sds((HALF_TOK + WINDOW, 512)), VM),
            "hi": (sds((8, TOK // 2, D)), ANY),
            "x_out": (sds((TOK, D), F32), VM),
            "h_out": (sds((8, TOK, D)), ANY),
        },
        {
            "hv": pltpu.VMEM((8, TOK, D), BF),
            "wiv": pltpu.VMEM((4, 4, 48, D), BF),
            "wov": pltpu.VMEM((4, 4, 16, D), BF),
            "turn": pltpu.VMEM((2, HALF_TOK, HEAD_V), F32),
            "lsem": pltpu.SemaphoreType.DMA((4,)),
            "xss": pltpu.SemaphoreType.DMA,
            "xrs": pltpu.SemaphoreType.DMA,
        }
        | HALF_SCRATCH
        | SCATTER_SCRATCH
        | GATHER_SCRATCH,
        3,
    )


def window_back_halo(r, win):
    rows, keys = window_rows(0), window_keys(0)
    for j in range(2):
        head, vals = head_of(j), head_of(2 + j)
        probs = win.probs(r, 0, j)
        prob_grad = dnt(r.dy[rows, head], r.kv[keys, vals])
        score_grad = (
            probs * (prob_grad - jnp.sum(prob_grad * probs, axis=-1, keepdims=True))
        ).astype(BF)
        r.halo_s[:, head] = dtn(score_grad, r.q[rows, head])[:WINDOW] * INV_ROOT_V
        r.halo_s[:, vals] = dtn(probs.astype(BF), r.dy[rows, head])[:WINDOW]
    return remote(r.halo_s, r.halo, r.xss, r.xrs, win.partner)


def turned_back(r, rows, grads):
    return (
        grads * r.turn[0, rows, :] + pltpu.roll(grads * r.turn[1, rows, :], HEAD_V // 2, 1)
    ).astype(BF)


def window_back_block(r, win, b):
    rows, keys = window_rows(b), window_keys(b)
    for j in range(2):
        head, vals = head_of(j), head_of(2 + j)
        queries, grads = r.q[rows, head], r.dy[rows, head]
        probs = win.probs(r, b, j)
        prob_grad = dnt(grads, r.kv[keys, vals])
        score_grad = (
            probs * (prob_grad - jnp.sum(prob_grad * probs, axis=-1, keepdims=True))
        ).astype(BF)
        r.dp[rows, head_of(3 * j)] = turned_back(
            r, rows, dnn(score_grad, r.kv[keys, head]) * INV_ROOT_V
        )
        r.dkv[keys, head] += dtn(score_grad, queries) * INV_ROOT_V
        r.dkv[keys, vals] += dtn(probs.astype(BF), grads)


def window_back_chip(r, chip):
    last = pl.ds(pl.multiple_of((chip + 1) * (2 * TOK), WINDOW), WINDOW)
    r.dkv[last, :] += jnp.where(chip == HALF_TOK // (2 * TOK) - 1, r.halo[...], 0.0)
    shifted = pl.ds(pl.multiple_of(chip * (2 * TOK) + WINDOW, WINDOW), 2 * TOK)
    rows = chip_rows(chip)
    for j in range(2):
        r.dp[rows, head_of(3 * j + 1)] = turned_back(r, rows, r.dkv[shifted, head_of(j)])
        r.dp[rows, head_of(3 * j + 2)] = r.dkv[shifted, head_of(2 + j)].astype(BF)


def window_back_body(r):
    ring = Ring()
    partners = (ring.up, ring.dn, ring.sib, {"xh": 1 - lax.axis_index("xh")})
    signal(partners)
    turning = load(r.turns.at[lax.axis_index("xh")], r.turn, r.lsem.at[0])
    loads = [
        load(r.w.at[:, :, pl.ds(0, 48), :], r.wiv, r.lsem.at[1]),
        load(r.h, r.hv, r.lsem.at[2]),
        load(r.e, r.ev, r.lsem.at[3]),
        load(r.wo, r.wov, r.lsem.at[4]),
    ]
    r.dkv[...] = jnp.zeros_like(r.dkv)
    r.oacc[...] = jnp.zeros_like(r.oacc)
    r.gacc[...] = jnp.zeros_like(r.gacc)

    def write(at, rows, total):
        r.low[at, :] = (r.x3[rows, :] + total).astype(BF)

    sums = rows_reduce(ring, r, 0, write)
    arrive(partners)
    advance(sums)
    turning.wait()
    win = Window()
    halo = window_back_halo(r, win)
    for copy in loads:
        copy.wait()
    blocks = HALF_TOK // WBLK

    def before(index, chip):
        turns = ((0, 1, 2), (0, 1), (1, 2), (1,))[index]
        for n in turns:
            window_back_block(r, win, lax.rem(2 * chip + n, blocks))
        if index == 0:
            advance(sums)
            halo.wait_recv()
        window_back_chip(r, chip)
        if index in (1, 3):
            advance(sums)

    def product(rows, col):
        return dnn(r.dp[rows, :], r.wiv[:, :, :, col].reshape(768, -1))

    def weights():
        for k in range(4):
            cols = slice(k * 512, (k + 1) * 512)
            rows = r.hv[:, :, cols].reshape(HALF_TOK, 512)
            for i in range(2):
                res = dtn(r.dp[:, i * 384 : (i + 1) * 384], rows)
                own = r.wiv[2 * i : 2 * i + 2, :, :, cols].reshape(384, 512).astype(F32)
                r.gacc[:, cols] += jnp.sum(res * own, axis=0, keepdims=True)
                r.gstage[2 * i : 2 * i + 2, :, :48, cols] = res.astype(BF).reshape(2, 4, 48, 512)
            res = dtn(r.y[...], r.ev[:, :, cols].reshape(HALF_TOK, 512)).astype(BF)
            r.gstage[:, :, 48:, cols] = res.reshape(4, 4, 16, 512)
            yield
        copy = load(r.gstage, r.grads.at[:, :, pl.ds(0, 64), :], r.lsem.at[5])
        yield
        copy.wait()

    def also(chip, rows):
        r.oacc[...] += dtn(r.y1[chip_rows(chip), :], rows)

    weight_grads = weights()
    ring_backward(r, ring, product, r.wov, (weight_grads,), before, also)
    finish(sums)
    halo.wait_send()
    r.ostage[...] = r.oacc[...].astype(BF).reshape(4, 4, 16, D)
    copy = load(r.ostage, r.grads.at[:, :, pl.ds(64, 16), :], r.lsem.at[6])
    finish(weight_grads)
    copy.wait()
    r.gain_out[...] = r.gacc[...] / r.gain[...]


def window_back_step(win, y1, dy, turns, down, x3, w, wo, h, e, v, gain, res):
    return build(
        window_back_body,
        {
            "q": vm(win.q),
            "kv": vm(win.kv),
            "dy": vm(dy),
            "turns": hbm(turns),
            "down": hbm(down),
            "x3": vm(x3),
            "w": hbm(w),
            "wo": hbm(wo),
            "h": hbm(h),
            "e": hbm(e),
            "y": vm(win.y),
            "y1": vm(y1),
            "v": vm(v),
            "gain": vm(gain),
            "res": vm(res),
        },
        {
            "low": (sds((TOK // 2, D)), VM),
            "d_out": (sds((TOK, D), F32), VM),
            "gain_out": (sds((1, D), F32), VM),
            "e_out": (sds((8, TOK, D)), ANY),
            "dy_out": (sds((HALF_TOK, 256)), VM),
            "grads": (sds((4, 4, 80, D)), ANY),
        },
        {
            "dkv": pltpu.VMEM((HALF_TOK + WINDOW, 512), F32),
            "halo": pltpu.VMEM((WINDOW, 512), F32),
            "halo_s": pltpu.VMEM((WINDOW, 512), F32),
            "turn": pltpu.VMEM((2, HALF_TOK, HEAD_V), F32),
            "dp": pltpu.VMEM((HALF_TOK, 768), BF),
            "wiv": pltpu.VMEM((4, 4, 48, D), BF),
            "wov": pltpu.VMEM((4, 4, 16, D), BF),
            "hv": pltpu.VMEM((8, TOK, D), BF),
            "ev": pltpu.VMEM((8, TOK, D), BF),
            "gstage": pltpu.VMEM((4, 4, 64, D), BF),
            "oacc": pltpu.VMEM((256, D), F32),
            "ostage": pltpu.VMEM((4, 4, 16, D), BF),
            "gacc": pltpu.VMEM((1, D), F32),
            "lsem": pltpu.SemaphoreType.DMA((7,)),
            "xss": pltpu.SemaphoreType.DMA,
            "xrs": pltpu.SemaphoreType.DMA,
        }
        | ROWS_SCRATCH
        | SCATTER_SCRATCH
        | GATHER_SCRATCH,
        5,
    )


def padded(rows, count):
    return jnp.pad(rows, ((0, count - rows.shape[0]), (0, 0)))


def place():
    slot = lax.axis_index("xh") * HALF_TOK + jnp.arange(HALF_TOK, dtype=jnp.int32)
    last = 2 * HALF_TOK - EDGE
    segment = (slot >= EDGE).astype(jnp.int32) + (slot >= last).astype(jnp.int32)
    start = jnp.where(segment == 0, 0, jnp.where(segment == 1, EDGE, last)).astype(jnp.int32)
    return segment, slot - start


def body(
    block_input,
    cotangent,
    lengths,
    gain_a,
    based_in,
    based_out,
    gain_b,
    swa_in,
    swa_out,
    gain_c,
    mlp_in,
    mlp_down,
):
    gains = [gain.reshape(1, D) for gain in (gain_a, gain_b, gain_c)]
    units = mlp_down.shape[0]
    wide = based_in.shape[1]
    win_all = lax.all_gather(
        jnp.concatenate([swa_in.T, swa_out], axis=0), PLANE, axis=0, tiled=True
    ).reshape(4, 4, 64, D)
    ff_all = lax.all_gather(
        jnp.concatenate(
            [padded(part, UNIT_PAD) for part in (mlp_in[:, 0, :].T, mlp_in[:, 1, :].T, mlp_down)],
            axis=0,
        ),
        PLANE,
        axis=0,
        tiled=True,
    ).reshape(16, 3 * UNIT_PAD, D)
    segment, position = place()
    first = (lax.axis_index("z") * 2 + lax.axis_index("c")) * TOK
    my_segment = lax.dynamic_slice_in_dim(segment, first, TOK)
    my_position = lax.dynamic_slice_in_dim(position, first, TOK)
    chosen = jnp.where(
        my_segment == 0,
        lengths[0, 0],
        jnp.where(my_segment == 1, lengths[0, 1], lengths[0, 2]),
    )
    valid = (my_position < chosen)[:, None]
    cot_low = jnp.where(valid, cotangent, jnp.zeros_like(cotangent))
    tables = tuple(
        jnp.asarray(table, kind) for table, kind in zip(state_tables(), (BF, F32, BF))
    )
    select = jnp.asarray(select_table(wide), BF)

    turns = jnp.asarray(turn_tables())

    lin = linear_step(
        select, tables, cot_low, block_input, gains[0], gains[1], based_in.T, based_out
    )
    win = window_step(lin.h_out, win_all, turns, cot_low, lin.x_out, gains[2])
    mlp = mlp_step(win.h_out, lin.lo, win.hi, ff_all, win_all, win.x_out, gains[2], cot_low)
    ff_grads = lax.psum_scatter(
        mlp.grads.reshape(-1, D), PLANE, scatter_dimension=0, tiled=True
    ).astype(F32)
    back = window_back_step(
        win,
        lin.y,
        mlp.dy_out,
        turns,
        mlp.down,
        win.x_out,
        win_all,
        lin.w_out,
        lin.h_out,
        mlp.e_out,
        lin.x_out,
        gains[1],
        mlp.d_out,
    )
    end = last_step(
        lin,
        back.dy_out,
        select,
        tables,
        mlp.down,
        win.x_out,
        back.low,
        back.grads,
        lin.w_in,
        lin.h,
        block_input,
        gains[0],
        back.d_out,
        back.gain_out,
        mlp.gain_out,
        wide,
    )
    gate_grad = ff_grads[:units]
    up_grad = ff_grads[UNIT_PAD : UNIT_PAD + units]
    return (
        end.out,
        end.d_out,
        end.ga.reshape(D),
        end.lin_in.T,
        end.lin_out,
        end.gb.reshape(D),
        end.win_in.T,
        end.win_out,
        end.gc.reshape(D),
        jnp.stack([gate_grad.T, up_grad.T], axis=1),
        ff_grads[2 * UNIT_PAD : 2 * UNIT_PAD + units],
    )


def solution(mesh):
    grid = Mesh(mesh.devices.reshape(2, 4, 2, 4, 2), ALL)
    tokens = P(ALL, None)
    weight = ("xh", "z", "c", "xl", "y")
    rows, cols = P(weight, None), P(None, weight)
    return jax.shard_map(
        body,
        mesh=grid,
        in_specs=(
            tokens,
            tokens,
            P(("xl", "y"), None),
            P(),
            cols,
            rows,
            P(),
            cols,
            rows,
            P(),
            P(None, None, weight),
            rows,
        ),
        out_specs=(
            tokens,
            tokens,
            P(),
            cols,
            rows,
            P(),
            cols,
            rows,
            P(),
            P(None, None, weight),
            rows,
        ),
        check_vma=False,
    )
```

```python
import functools
import math
import types

import jax
import jax.numpy as jnp
import numpy as np
from jax import lax
from jax.experimental import pallas as pl
from jax.experimental.pallas import tpu as pltpu
from jax.sharding import Mesh
from jax.sharding import PartitionSpec as P

FEAT = 16
HEAD_V = 128
WINDOW = 64
EPSILON = 1e-05
D = 2048
TOK = 128
HALF_TOK = 1024
EDGE = 64
UNIT_PAD = 48
BIN_PAD = 32
STATE = 256
PLANE = ("xh", "xl", "y")
RING = ("z", "c")
ALL = ("xl", "y", "xh", "z", "c")
MESH = pl.DeviceIdType.MESH
BF = jnp.bfloat16
F32 = jnp.float32
VM = pl.BlockSpec(memory_space=pltpu.VMEM)
ANY = pl.BlockSpec(memory_space=pl.ANY)
SM = pl.BlockSpec(memory_space=pltpu.SMEM)


def dnn(a, b):
    return lax.dot_general(a, b, (((1,), (0,)), ((), ())), preferred_element_type=F32)


def dnt(a, b):
    return lax.dot_general(a, b, (((1,), (1,)), ((), ())), preferred_element_type=F32)


def dtn(a, b):
    return lax.dot_general(a, b, (((0,), (0,)), ((), ())), preferred_element_type=F32)


def remote(src, dst, send_sem, recv_sem, device):
    copy = pltpu.make_async_remote_copy(
        src_ref=src,
        dst_ref=dst,
        send_sem=send_sem,
        recv_sem=recv_sem,
        device_id=device,
        device_id_type=MESH,
    )
    copy.start()
    return copy


def greet(devices):
    barrier = pltpu.get_barrier_semaphore()
    for device in devices:
        pl.semaphore_signal(barrier, inc=1, device_id=device, device_id_type=MESH)
    pl.semaphore_wait(barrier, len(devices))


class Ring:
    def __init__(self):
        self.z = lax.axis_index("z")
        self.c = lax.axis_index("c")
        self.oc = 1 - self.c
        self.zp = lax.rem(self.z + 1, 4)
        self.zm = lax.rem(self.z + 3, 4)
        self.zz = lax.rem(self.z + 2, 4)
        self.up = {"z": self.zp}
        self.dn = {"z": self.zm}
        self.sib = {"c": self.oc}

    def greet(self):
        greet((self.up, self.dn, self.sib))


class Plane:
    def __init__(self):
        self.x = lax.axis_index("xh") * 2 + lax.axis_index("xl")
        self.y = lax.axis_index("y")

    def at_x(self, x):
        return {"xh": lax.div(x, 2), "xl": lax.rem(x, 2)}

    def at_y(self, y):
        return {"y": y}

    def ring(self, along_x):
        me = self.x if along_x else self.y
        plus, minus, far = lax.rem(me + 1, 4), lax.rem(me + 3, 4), lax.rem(me + 2, 4)
        to = self.at_x if along_x else self.at_y
        return me, plus, minus, far, to(plus), to(minus)

    def neighbours(self):
        xs, ys = self.ring(True), self.ring(False)
        return (xs[4], xs[5], ys[4], ys[5])


def finish(steps):
    for _ in steps:
        pass


def advance(steps):
    next(steps, None)


def weave(main, *others):
    for _ in main:
        for other in others:
            advance(other)


CHUNKS = 2


def gather_steps(ring, buf, out_ref, ss, rs, ls, rows, start=0, base=0, keep=True, ready=None):
    half = rows // 2
    me = ring.z * 2 + ring.c
    below, above, far = ring.zm * 2 + ring.c, ring.zp * 2 + ring.c, ring.zz * 2 + ring.c

    def send(slot, part, device, index):
        piece = buf.at[slot, pl.ds(start + part * half, half), :]
        return remote(piece, piece, ss.at[base + index], rs.at[base + index], device)

    local = []

    def save(slot):
        if keep:
            copy = pltpu.make_async_copy(buf.at[slot], out_ref.at[slot], ls.at[len(local)])
            copy.start()
            local.append(copy)

    def done(chip):
        if ready is not None:
            ready(chip)

    up, dn, sib = ring.up, ring.dn, ring.sib
    cp = {}
    cp[0] = send(me, 0, up, 0)
    cp[1] = send(me, 1, dn, 1)
    cp[2] = send(me, 1, up, 2)
    cp[3] = send(me, 0, dn, 3)
    cp[4] = send(me, 0, sib, 4)
    cp[5] = send(me, 1, sib, 5)
    save(me)
    yield
    cp[0].wait_recv()
    cp[6] = send(below, 0, up, 6)
    cp[8] = send(below, 0, sib, 8)
    cp[1].wait_recv()
    cp[7] = send(above, 1, dn, 7)
    cp[9] = send(above, 1, sib, 9)
    yield
    cp[2].wait_recv()
    cp[10] = send(below, 1, sib, 10)
    save(below)
    cp[3].wait_recv()
    cp[11] = send(above, 0, sib, 11)
    save(above)
    yield
    cp[4].wait_recv()
    cp[5].wait_recv()
    save(ring.z * 2 + ring.oc)
    done(ring.z)
    cp[8].wait_recv()
    cp[10].wait_recv()
    save(ring.zm * 2 + ring.oc)
    done(ring.zm)
    yield
    cp[6].wait_recv()
    cp[12] = send(far, 0, sib, 12)
    cp[7].wait_recv()
    cp[13] = send(far, 1, sib, 13)
    save(far)
    cp[9].wait_recv()
    cp[11].wait_recv()
    save(ring.zp * 2 + ring.oc)
    done(ring.zp)
    yield
    cp[12].wait_recv()
    cp[13].wait_recv()
    save(ring.zz * 2 + ring.oc)
    done(ring.zz)
    for index in range(14):
        cp[index].wait_send()
    for copy in local:
        copy.wait()


def scatter_steps(ring, product, part, sib_in, far_in, end_in, ss, rs, ready, before=None):
    rows = TOK // CHUNKS
    half = rows // 2
    c, oc = ring.c, ring.oc
    up, dn, sib = ring.up, ring.dn, ring.sib
    order = (ring.zz, ring.zp, ring.zm, ring.z)
    step = 512
    cp = {}

    def send(q, index, src, dst, device):
        n = q * 10 + index
        cp[q, index] = remote(src, dst, ss.at[n], rs.at[n], device)

    def multiply(index):
        row = pl.multiple_of(order[index] * (2 * TOK), 2 * TOK)

        def one(n, carry):
            col = pl.ds(pl.multiple_of(n * step, step), step)
            res = product(pl.ds(row, 2 * TOK), col).astype(BF)
            part[index, 0, :, col] = res[:TOK]
            part[index, 1, :, col] = res[TOK:]
            return carry

        lax.fori_loop(0, D // step, one, 0)
        for q in range(CHUNKS):
            at = pl.ds(q * rows, rows)
            send(q, index, part.at[index, oc, at, :], sib_in.at[index, at, :], sib)

    def add(index, first, count, other):
        def one(i, carry):
            at = pl.ds(pl.multiple_of(first + i * 16, 16), 16)
            part[index, c, at, :] = (part[index, c, at, :].astype(F32) + other(at)).astype(BF)
            return carry

        lax.fori_loop(0, count // 16, one, 0)

    def add_sib(q, index):
        cp[q, index].wait_recv()
        add(index, q * rows, rows, lambda at: sib_in[index, at, :].astype(F32))

    def piece(q, which):
        return pl.ds(q * rows + which * half, half)

    def far(q):
        add_sib(q, 0)
        send(q, 4, part.at[0, c, piece(q, 0), :], far_in.at[piece(q, 0), :], up)
        send(q, 5, part.at[0, c, piece(q, 1), :], far_in.at[piece(q, 1), :], dn)

    def near_up(q):
        add_sib(q, 1)
        send(q, 6, part.at[1, c, piece(q, 1), :], end_in.at[0, piece(q, 1), :], up)

    def near_dn(q):
        add_sib(q, 2)
        send(q, 7, part.at[2, c, piece(q, 0), :], end_in.at[1, piece(q, 0), :], dn)

    def passed(q):
        for which, device in ((0, up), (1, dn)):
            cp[q, 4 + which].wait_recv()
            at = piece(q, which)
            add(1 + which, q * rows + which * half, half, lambda at: far_in[at, :].astype(F32))
            send(q, 8 + which, part.at[1 + which, c, at, :], end_in.at[which, at, :], device)

    def make(index, mid):
        if before is not None:
            before(index, order[index], mid)
        else:
            mid()

    def each(one):
        for q in range(CHUNKS):
            one(q)

    make(0, lambda: None)
    multiply(0)
    make(1, lambda: each(far))
    multiply(1)
    make(2, lambda: each(near_up))
    multiply(2)
    make(3, lambda: each(near_dn))
    multiply(3)
    yield
    each(passed)
    yield
    each(lambda q: add_sib(q, 3))
    yield
    for q in range(CHUNKS):
        for index in range(6, 10):
            cp[q, index].wait_recv()
        ready(q)
        yield
    for copy in cp.values():
        copy.wait_send()


def rows_reduce_steps(ring, src_ref, q, part, sib_in, far_in, end_in, ss, rs, ls, ready):
    rows = TOK // CHUNKS
    half = rows // 2
    order = (ring.zz, ring.zp, ring.zm, ring.z)
    up, dn, sib = ring.up, ring.dn, ring.sib
    cp, loads = {}, []

    def send(index, src, dst, device):
        cp[index] = remote(src, dst, ss.at[index], rs.at[index], device)

    def source(index, core):
        start = order[index] * (2 * TOK) + core * TOK + q * rows
        return src_ref.at[pl.ds(pl.multiple_of(start, 16), rows), :]

    def add(index, first, count, other):
        def one(i, carry):
            at = pl.ds(pl.multiple_of(first + i * 16, 16), 16)
            part[index, at, :] = (part[index, at, :].astype(F32) + other(at)).astype(BF)
            return carry

        lax.fori_loop(0, count // 16, one, 0)

    def add_sib(index):
        loads[index].wait()
        cp[index].wait_recv()
        add(index, 0, rows, lambda at: sib_in[index, at, :].astype(F32))

    low, high = pl.ds(0, half), pl.ds(half, half)
    for index in range(4):
        send(index, source(index, ring.oc), sib_in.at[index], sib)
        loads.append(load(source(index, ring.c), part.at[index], ls.at[index]))
    yield
    add_sib(0)
    send(4, part.at[0, low, :], far_in.at[low, :], up)
    send(5, part.at[0, high, :], far_in.at[high, :], dn)
    add_sib(1)
    send(6, part.at[1, high, :], end_in.at[0, high, :], up)
    add_sib(2)
    send(7, part.at[2, low, :], end_in.at[1, low, :], dn)
    add_sib(3)
    yield
    for which, device in ((0, up), (1, dn)):
        cp[4 + which].wait_recv()
        at = (low, high)[which]
        add(1 + which, which * half, half, lambda at: far_in[at, :].astype(F32))
        send(8 + which, part.at[1 + which, at, :], end_in.at[which, at, :], device)
    yield
    for index in range(6, 10):
        cp[index].wait_recv()

    def total(i, carry):
        at = pl.ds(pl.multiple_of(i * 16, 16), 16)
        ready(
            at,
            pl.ds(pl.multiple_of(q * rows + i * 16, 16), 16),
            part[3, at, :].astype(F32)
            + end_in[0, at, :].astype(F32)
            + end_in[1, at, :].astype(F32),
        )
        return carry

    lax.fori_loop(0, rows // 16, total, 0)
    for copy in cp.values():
        copy.wait_send()


ROWS_SCRATCH = {
    "bpart": pltpu.VMEM((4, TOK // CHUNKS, D), BF),
    "bsib": pltpu.VMEM((4, TOK // CHUNKS, D), BF),
    "bfar": pltpu.VMEM((TOK // CHUNKS, D), BF),
    "bend": pltpu.VMEM((2, TOK // CHUNKS, D), BF),
    "bss": pltpu.SemaphoreType.DMA((10,)),
    "brs": pltpu.SemaphoreType.DMA((10,)),
    "bls": pltpu.SemaphoreType.DMA((4,)),
}
SCATTER_SCRATCH = {
    "part": pltpu.VMEM((4, 2, TOK, D), BF),
    "sib_in": pltpu.VMEM((4, TOK, D), BF),
    "far_in": pltpu.VMEM((TOK, D), BF),
    "end_in": pltpu.VMEM((2, TOK, D), BF),
    "sss": pltpu.SemaphoreType.DMA((10 * CHUNKS,)),
    "srs": pltpu.SemaphoreType.DMA((10 * CHUNKS,)),
}
GATHER_SCRATCH = {
    "buf": pltpu.VMEM((8, TOK, D), BF),
    "ss": pltpu.SemaphoreType.DMA((14 * CHUNKS,)),
    "rs": pltpu.SemaphoreType.DMA((14 * CHUNKS,)),
    "ls": pltpu.SemaphoreType.DMA((8,)),
}
HALF_SCRATCH = {
    "cbuf": pltpu.VMEM((8, TOK // 2, D), BF),
    "css": pltpu.SemaphoreType.DMA((14,)),
    "crs": pltpu.SemaphoreType.DMA((14,)),
    "cls": pltpu.SemaphoreType.DMA((8,)),
}


def plane_view(plane, ref, half, stage, place, part):
    cols = pl.ds(half * (D // 2) + (part or 0) * (D // 4), D // 2 if part is None else D // 4)
    if stage == 0:
        return ref.at[place, plane.y, :, cols] if half == 0 else ref.at[plane.x, place, :, cols]
    return ref.at[:, place, :, cols] if half == 0 else ref.at[place, :, :, cols]


def plane_gather_steps(plane, buf, ss, rs):
    copies = []
    quarter = D // 4

    def view(half, first, second, part):
        x, y = (first, second) if half == 0 else (second, first)
        cols = pl.ds(half * 2 * quarter + (part or 0) * quarter, quarter if part is not None else 2 * quarter)
        return buf.at[x, y, :, cols]

    def send(ref, device):
        copies.append(remote(ref, ref, ss.at[len(copies)], rs.at[len(copies)], device))
        return copies[-1]

    firsts = [plane.ring(half == 0) for half in (0, 1)]
    seconds = [plane.ring(half == 1) for half in (0, 1)]
    near, passed, spread = {}, {}, {}

    def go_on(half, place):
        me, plus, minus, far, to_plus, to_minus = seconds[half]
        piece = view(half, place, me, None)
        spread[half, len(spread)] = (place, send(piece, to_plus), send(piece, to_minus))

    def pass_on(entry):
        half, (place, up, dn) = entry
        me, plus, minus, far, to_plus, to_minus = seconds[half]
        up.wait_recv()
        send(view(half, place, minus, 0), to_plus)
        dn.wait_recv()
        send(view(half, place, plus, 1), to_minus)

    for half in (0, 1):
        me, plus, minus, far, to_plus, to_minus = firsts[half]
        piece = view(half, me, seconds[half][0], None)
        near[half] = (send(piece, to_plus), send(piece, to_minus))
    for half in (0, 1):
        go_on(half, firsts[half][0])
    yield
    for half in (0, 1):
        me, plus, minus, far, to_plus, to_minus = firsts[half]
        other = seconds[half][0]
        near[half][0].wait_recv()
        up = send(view(half, minus, other, 0), to_plus)
        near[half][1].wait_recv()
        passed[half] = (up, send(view(half, plus, other, 1), to_minus))
    for half in (0, 1):
        go_on(half, firsts[half][2])
        go_on(half, firsts[half][1])
    yield
    for half in (0, 1):
        passed[half][0].wait_recv()
        passed[half][1].wait_recv()
        go_on(half, firsts[half][3])
    entries = [(key[0], value) for key, value in spread.items()]
    for entry in entries[:2]:
        pass_on(entry)
    yield
    for entry in entries[2:]:
        pass_on(entry)
    yield
    for copy in copies[-2 * len(entries) :]:
        copy.wait_recv()
    for copy in copies:
        copy.wait_send()


GATHER_COPIES = 40


def plane_reduce_scratch(name, rows):
    return {
        name: pltpu.VMEM((4, 4, rows, D), BF),
        name + "_far": pltpu.VMEM((2, 2, 4, rows, D // 4), BF),
        name + "_end": pltpu.VMEM((2, 2, 4, rows, D // 2), BF),
        name + "_far2": pltpu.VMEM((2, 2, rows, D // 4), BF),
        name + "_end2": pltpu.VMEM((2, 2, rows, D // 2), BF),
        name + "_ss": pltpu.SemaphoreType.DMA((24,)),
        name + "_rs": pltpu.SemaphoreType.DMA((24,)),
    }


def plane_reduce(plane, r, name, outs):
    refs = [getattr(r, name + end) for end in ("", "_far", "_end", "_far2", "_end2", "_ss", "_rs")]
    return plane_reduce_steps(plane, *refs, outs)


def plane_reduce_steps(plane, grads, far_a, end_a, far_b, end_b, ss, rs, outs):
    copies = []
    rows = grads.shape[2]

    def send(src, dst, device):
        copies.append(remote(src, dst, ss.at[len(copies)], rs.at[len(copies)], device))
        return copies[-1]

    def add(view, *others):
        def one(i, carry):
            at = pl.ds(pl.multiple_of(i * 16, 16), 16)
            piece = view.at[..., at, :]
            total = piece[...].astype(F32)
            for other in others:
                total = total + other.at[..., at, :][...].astype(F32)
            piece[...] = total.astype(BF)
            return carry

        lax.fori_loop(0, rows // 16, one, 0)

    for stage in (0, 1):
        rings = [plane.ring(half != stage) for half in (0, 1)]
        far_in, end_in = (far_a, end_a) if stage == 0 else (far_b, end_b)

        def view(half, place, part):
            return plane_view(plane, grads, half, 1 - stage, place, part)

        def ends(half, side, part):
            if part is None:
                return end_in.at[half, side]
            return end_in.at[half, side, ..., pl.ds(part * (D // 4), D // 4)]

        first, last = [], []
        for half in (0, 1):
            me, plus, minus, far, to_plus, to_minus = rings[half]
            first.append(
                (
                    send(view(half, far, 0), far_in.at[half, 0], to_plus),
                    send(view(half, far, 1), far_in.at[half, 1], to_minus),
                )
            )
            last.append(send(view(half, plus, 1), ends(half, 0, 1), to_plus))
            last.append(send(view(half, minus, 0), ends(half, 1, 0), to_minus))
        yield
        for half in (0, 1):
            me, plus, minus, far, to_plus, to_minus = rings[half]
            first[half][0].wait_recv()
            add(view(half, plus, 0), far_in.at[half, 0])
            last.append(send(view(half, plus, 0), ends(half, 0, 0), to_plus))
            first[half][1].wait_recv()
            add(view(half, minus, 1), far_in.at[half, 1])
            last.append(send(view(half, minus, 1), ends(half, 1, 1), to_minus))
        yield
        for copy in last:
            copy.wait_recv()
        for half in (0, 1):
            me = rings[half][0]
            if stage == 0:
                add(view(half, me, None), ends(half, 0, None), ends(half, 1, None))
            else:
                cols = pl.ds(half * (D // 2), D // 2)
                total = (
                    view(half, me, None)[...].astype(F32)
                    + end_in[half, 0].astype(F32)
                    + end_in[half, 1].astype(F32)
                )
                for start, out_ref in outs:
                    out_ref[:, cols] = total[start : start + out_ref.shape[0]]
    for copy in copies:
        copy.wait_send()


def load(src, dst, sem):
    copy = pltpu.make_async_copy(src, dst, sem)
    copy.start()
    return copy


def params(collective_id, limit=58):
    return pltpu.CompilerParams(
        collective_id=collective_id, has_side_effects=True, vmem_limit_bytes=limit << 20
    )


def sds(shape, dtype=BF):
    return jax.ShapeDtypeStruct(shape, dtype)


def scale_of(rows):
    return lax.rsqrt(jnp.mean(rows * rows, axis=-1, keepdims=True) + EPSILON)


def by_rows(one, start=0, rows=TOK):
    def step(i, carry):
        one(pl.ds(pl.multiple_of(start + i * 16, 16), 16))
        return carry

    lax.fori_loop(0, rows // 16, step, 0)


def total_rows(part, end_in, c, at):
    return (
        part[3, c, at, :].astype(F32)
        + end_in[0, at, :].astype(F32)
        + end_in[1, at, :].astype(F32)
    )


def chip_rows(chip):
    return pl.ds(pl.multiple_of(chip * (2 * TOK), 2 * TOK), 2 * TOK)


def build(body, inputs, outputs, scratch, collective_id):
    names = list(inputs) + list(outputs)
    early = [name for name, (_, spec) in inputs.items() if spec is VM]
    late = [name for name, (_, spec) in outputs.items() if spec is VM]
    scratch = dict(scratch)
    for name in early:
        scratch["vm_" + name] = pltpu.VMEM(inputs[name][0].shape, inputs[name][0].dtype)
    for name in late:
        scratch["vm_" + name] = pltpu.VMEM(outputs[name][0].shape, outputs[name][0].dtype)
    scratch["in_sems"] = pltpu.SemaphoreType.DMA((max(len(early), 1),))
    scratch["out_sems"] = pltpu.SemaphoreType.DMA((max(len(late), 1),))
    names += list(scratch)

    def kernel(*refs):
        r = types.SimpleNamespace(**dict(zip(names, refs)))
        coming, going = {}, {}
        for n, name in enumerate(early):
            local = getattr(r, "vm_" + name)
            coming[name] = load(getattr(r, name), local, r.in_sems.at[n])
            setattr(r, name, local)
        targets = {name: getattr(r, name) for name in late}
        for name in late:
            setattr(r, name, getattr(r, "vm_" + name))

        def need(*wanted):
            for name in wanted or list(coming):
                if name in coming:
                    coming.pop(name).wait()

        def flush(*wanted):
            for name in wanted or late:
                if name not in going:
                    sem = r.out_sems.at[late.index(name)]
                    going[name] = load(getattr(r, name), targets[name], sem)

        r.need, r.flush = need, flush
        body(r)
        need()
        flush()
        for copy in going.values():
            copy.wait()

    results = pl.pallas_call(
        kernel,
        out_shape=tuple(shape for shape, _ in outputs.values()),
        in_specs=[ANY if spec is VM else spec for _, spec in inputs.values()],
        out_specs=tuple(ANY for _ in outputs),
        scratch_shapes=list(scratch.values()),
        compiler_params=params(collective_id),
    )(*[array for array, _ in inputs.values()])
    return types.SimpleNamespace(**dict(zip(outputs, results)))


def vm(array):
    return (array, VM)


def hbm(array):
    return (array, ANY)


def signal(partners):
    barrier = pltpu.get_barrier_semaphore()
    for device in partners:
        pl.semaphore_signal(barrier, inc=1, device_id=device, device_id_type=MESH)


def arrive(partners):
    pl.semaphore_wait(pltpu.get_barrier_semaphore(), len(partners))


def scatter(ring, r, product, ready, before=None):
    return scatter_steps(
        ring, product, r.part, r.sib_in, r.far_in, r.end_in, r.sss, r.srs, ready, before
    )


def scatter_gather(ring, r, product, one, out_ref, kept, done=None, others=(), before=None):
    rows = TOK // CHUNKS
    gathers = []

    def ready(q):
        by_rows(one, q * rows, rows)
        last = q == CHUNKS - 1
        if last:
            r.flush(*kept)
        steps = gather_steps(
            ring,
            r.buf,
            out_ref,
            r.ss,
            r.rs,
            r.ls,
            rows,
            start=q * rows,
            base=14 * q,
            keep=last,
            ready=done if last else None,
        )
        advance(steps)
        gathers.append(steps)

    weave(scatter(ring, r, product, ready, before), *others)
    for _ in range(5):
        for steps in gathers:
            advance(steps)
        for other in others:
            advance(other)
    for steps in gathers:
        finish(steps)


def sums_of(r, ring, at):
    return total_rows(r.part, r.end_in, ring.c, at)


def half_gather(ring, r, out_ref):
    return gather_steps(ring, r.cbuf, out_ref, r.css, r.crs, r.cls, TOK // 2)


def rows_reduce(ring, r, q, ready):
    return rows_reduce_steps(
        ring, r.down, q, r.bpart, r.bsib, r.bfar, r.bend, r.bss, r.brs, r.bls, ready
    )


def norm_into(r, ring, gain_ref, at, rows):
    r.buf[ring.z * 2 + ring.c, at, :] = (rows * scale_of(rows) * gain_ref[...]).astype(BF)


def first_part(r, ring, plane):
    def one(at):
        norm_into(r, ring, r.gain_a, at, r.x[at, :].astype(F32))

    by_rows(one)
    arrive(r.partners)
    r.need()
    weights = plane_gather_steps(plane, r.wide, r.wss, r.wrs)

    def project(chip):
        h = r.buf[pl.ds(2 * chip, 2)].reshape(2 * TOK, D)
        r.raw[chip_rows(chip), :] = dnt(h, r.wide[...].reshape(16 * BIN_PAD, D)).astype(BF)

    rows = gather_steps(ring, r.buf, r.h, r.fss, r.frs, r.fls, TOK, ready=project)
    outs = plane_gather_steps(plane, r.wout, r.oss, r.ors)
    advance(weights)
    advance(rows)
    advance(weights)
    advance(outs)
    advance(weights)
    advance(outs)
    advance(rows)
    advance(weights)
    advance(rows)
    finish(weights)
    advance(outs)
    keep = load(r.wide, r.w_in, r.wls.at[0])
    finish(rows)
    return outs, keep


def ring_forward(r, ring, y_ref, w_ref, gain_ref, others=(), before=None):
    def product(rows, col):
        return dnn(y_ref[rows, :], w_ref[:, :, :, col].reshape(256, -1))

    def one(at):
        rows = r.x[at, :].astype(F32) + sums_of(r, ring, at)
        r.x_out[at, :] = rows
        norm_into(r, ring, gain_ref, at, rows)

    scatter_gather(ring, r, product, one, r.h_out, ("x_out",), others=others, before=before)


def norm_back_rows(v_ref, gain_ref, grads, at):
    rows = v_ref[at, :].astype(F32)
    scale = scale_of(rows)
    unit = rows * scale
    scaled = grads * gain_ref[...]
    return scale * (scaled - unit * jnp.mean(scaled * unit, axis=-1, keepdims=True))


def ring_backward(r, ring, product, wo_ref, others, before=None, also=None):
    def one(at):
        grad = sums_of(r, ring, at)
        rows = r.res[at, :].astype(F32) + norm_back_rows(r.v, r.gain, grad, at)
        r.d_out[at, :] = rows
        r.buf[ring.z * 2 + ring.c, at, :] = rows.astype(BF)

    def done(chip):
        rows = r.buf[pl.ds(2 * chip, 2)].reshape(2 * TOK, D)
        r.dy_out[chip_rows(chip), :] = dnt(rows, wo_ref[...].reshape(256, D)).astype(BF)
        if also is not None:
            also(chip, rows)

    scatter_gather(ring, r, product, one, r.e_out, ("d_out",), done, others, before)


CHUNK = 8 * UNIT_PAD


def mlp_chip(r, chip, i):
    at = chip_rows(chip)
    tokens = pl.ds(2 * chip, 2)
    count = 2 * CHUNK // 3
    shard = 5 * i
    skip = i * count - shard * UNIT_PAD

    def part(w):
        return w[shard : shard + 6].reshape(6 * UNIT_PAD, D)[skip : skip + count]

    rows = r.hv[tokens].reshape(2 * TOK, D)
    gate = dnt(rows, part(r.wv.at[0]))
    up = dnt(rows, part(r.wv.at[1]))
    d_act = dnt(r.cotv[tokens].reshape(2 * TOK, D), part(r.downv))
    sig = 1.0 / (1.0 + jnp.exp(-gate))
    silu = gate * sig
    first = i * count
    r.act[at, first : first + count] = (silu * up).astype(BF)
    r.d_gu[at, first : first + count] = (
        d_act * up * (sig * (1.0 + gate * (1.0 - sig)))
    ).astype(BF)
    first += 2 * CHUNK
    r.d_gu[at, first : first + count] = (d_act * silu).astype(BF)


def mlp_down_steps(r):
    for n in range(4):
        at = slice(2 * TOK * n, 2 * TOK * (n + 1))
        for col in range(0, D, 512):
            r.outv[at, col : col + 512] = dnn(
                r.act[at, :], r.downv[:, :, col : col + 512].reshape(2 * CHUNK, 512)
            ).astype(BF)
        if n == 1:
            yield
    copy = load(r.outv, r.down, r.msem.at[9])
    yield
    copy.wait()


def mlp_grad_steps(r, jobs):
    copies = []
    for n, (lhs, col, rhs, off, half, w) in enumerate(jobs):
        slot = n % 2
        if n >= 2:
            copies[n - 2].wait()

        res = dtn(lhs[:, col : col + CHUNK], rhs[...].reshape(HALF_TOK, D))
        r.stage[slot] = res.astype(BF).reshape(8, UNIT_PAD, D)
        if w is not None:
            own = w[8 * half : 8 * half + 8].reshape(CHUNK, D).astype(F32)
            r.gacc[...] += jnp.sum(res * own, axis=0, keepdims=True)
        copies.append(
            load(
                r.stage.at[slot],
                r.grads.at[pl.ds(8 * half, 8), pl.ds(off, UNIT_PAD), :],
                r.gsem.at[n],
            )
        )
        yield
    copies[-2].wait()
    copies[-1].wait()


def mlp_body(r):
    ring = Ring()
    partners = (ring.up, ring.dn, ring.sib)
    half = TOK // 2
    weights_in, tokens_in = {}, {}

    def fetch(index, chip):
        at = pl.ds(2 * chip, 2)
        pairs = (
            (r.h.at[at], r.hv.at[at]),
            (r.lo.at[at], r.cotv.at[at, pl.ds(0, half), :]),
            (r.hi.at[at], r.cotv.at[at, pl.ds(half, half), :]),
        )
        tokens_in[index] = [
            load(src, dst, r.tsem.at[3 * index + n]) for n, (src, dst) in enumerate(pairs)
        ]

    fetch(0, ring.zz)
    for i in range(2):
        for n, ref in enumerate((r.wv.at[0], r.wv.at[1], r.downv)):
            weights_in[i, n] = load(
                r.w.at[pl.ds(8 * i, 8), pl.ds(n * UNIT_PAD, UNIT_PAD), :],
                ref.at[pl.ds(8 * i, 8)],
                r.msem.at[3 * i + n],
            )
    for index, chip in ((1, ring.zp), (2, ring.zm), (3, ring.z)):
        fetch(index, chip)
    late = load(r.wo.at[:, :, pl.ds(48, 16), :], r.wov, r.msem.at[10])
    signal(partners)
    r.gacc[...] = jnp.zeros_like(r.gacc)
    arrive(partners)
    r.need()

    def before(index, chip, mid):
        for copy in tokens_in[index]:
            copy.wait()
        for i in range(3):
            if index == 0 and i < 2:
                for n in range(3):
                    weights_in[i, n].wait()
            mlp_chip(r, chip, i)
            if i == 1:
                mid()

    def product(rows, col):
        return dnn(r.d_gu[rows, :], r.wv[:, :, :, col].reshape(4 * CHUNK, -1))

    def weights():
        yield from mlp_down_steps(r)
        jobs = [
            (r.d_gu, n * CHUNK, r.hv, (n // 2) * UNIT_PAD, n % 2, r.wv.at[n // 2])
            for n in range(4)
        ]
        jobs += [(r.act, n * CHUNK, r.cotv, 2 * UNIT_PAD, n, None) for n in range(2)]
        yield from mlp_grad_steps(r, jobs)

    weight_grads = weights()
    late.wait()
    ring_backward(r, ring, product, r.wov, (weight_grads,), before)
    finish(weight_grads)
    r.gain_out[...] = r.gacc[...] / r.gain[...]


def mlp_step(h, lo, hi, w, wo, v, gain, cot):
    return build(
        mlp_body,
        {
            "h": hbm(h),
            "lo": hbm(lo),
            "hi": hbm(hi),
            "w": hbm(w),
            "wo": hbm(wo),
            "v": vm(v),
            "gain": vm(gain),
            "res": vm(cot),
        },
        {
            "down": (sds((HALF_TOK, D)), ANY),
            "d_out": (sds((TOK, D), F32), VM),
            "gain_out": (sds((1, D), F32), VM),
            "e_out": (sds((8, TOK, D)), ANY),
            "dy_out": (sds((HALF_TOK, 256)), VM),
            "grads": (sds((16, 3 * UNIT_PAD, D)), ANY),
        },
        {
            "hv": pltpu.VMEM((8, TOK, D), BF),
            "cotv": pltpu.VMEM((8, TOK, D), BF),
            "wv": pltpu.VMEM((2, 16, UNIT_PAD, D), BF),
            "downv": pltpu.VMEM((16, UNIT_PAD, D), BF),
            "wov": pltpu.VMEM((4, 4, 16, D), BF),
            "act": pltpu.VMEM((HALF_TOK, 2 * CHUNK), BF),
            "d_gu": pltpu.VMEM((HALF_TOK, 4 * CHUNK), BF),
            "outv": pltpu.VMEM((HALF_TOK, D), BF),
            "stage": pltpu.VMEM((2, 8, UNIT_PAD, D), BF),
            "gacc": pltpu.VMEM((1, D), F32),
            "msem": pltpu.SemaphoreType.DMA((11,)),
            "tsem": pltpu.SemaphoreType.DMA((12,)),
            "gsem": pltpu.SemaphoreType.DMA((6,)),
        }
        | SCATTER_SCRATCH
        | GATHER_SCRATCH,
        4,
    )


def state_tables():
    first = np.zeros((128, STATE), np.float32)
    second = np.zeros((128, STATE), np.float32)
    bias = np.zeros((8, STATE), np.float32)
    coef = np.zeros((8, STATE), np.float32)
    bias[0, 0] = bias[1, 0] = 1.0
    coef[0, 0] = 1.0
    at = 1
    for i in range(FEAT):
        first[i, at] = 1.0
        bias[1, at] = 1.0
        coef[0, at] = 1.0 / math.sqrt(FEAT)
        at += 1
    for i in range(FEAT):
        for j in range(i, FEAT):
            first[i, at] = 1.0
            second[j, at] = 1.0
            coef[0, at] = (0.5 if i == j else 1.0) / FEAT
            at += 1
    picks = np.zeros((4, 128, 128), np.float32)
    for which in range(4):
        for i in range(FEAT):
            picks[which, which * FEAT + i, i] = 1.0
    return (
        np.stack([first, second]),
        np.concatenate([bias[:2], coef[:1], np.zeros((5, STATE), np.float32)]),
        picks,
    )


def select_table(width):
    table = np.zeros((16 * BIN_PAD, 3 * HEAD_V), np.float32)
    for shard in range(16):
        for i in range(width):
            head, col = shard // 8, (shard % 8) * width + i
            to = 2 * HEAD_V + 2 * FEAT * head + col if col < 2 * FEAT else head * HEAD_V + col - 2 * FEAT
            table[shard * BIN_PAD + i, to] = 1.0
    return table


BLK = 256
NBLK = HALF_TOK // BLK
INV_ROOT = 1.0 / math.sqrt(FEAT)


def rows_of(b):
    return slice(b * BLK, (b + 1) * BLK)


def head_of(j):
    return slice(j * HEAD_V, (j + 1) * HEAD_V)


def chip_block(b):
    return pl.ds(pl.multiple_of(b * BLK, BLK), BLK) if not isinstance(b, int) else rows_of(b)


def causal_mask(start, edge):
    t = start + lax.broadcasted_iota(jnp.int32, (BLK, BLK), 0)
    u = start + lax.broadcasted_iota(jnp.int32, (BLK, BLK), 1)
    return (u <= t) & ((t >= edge) == (u >= edge))


class Linear:
    def __init__(self, r):
        self.r = r
        self.xh = lax.axis_index("xh")
        self.partner = {"xh": 1 - self.xh}
        self.edge = jnp.where(self.xh == 0, EDGE, HALF_TOK - EDGE)
        self.second = jnp.where(self.xh == 1, 1.0, 0.0)
        self.coef = r.t[2:3, :]

    def vectors(self):
        r = self.r
        small = r.p[:, 2 * HEAD_V :]
        for j in range(2):
            r.qs[j] = dnn(small, r.pick[2 * j]).astype(BF)
            r.ks[j] = dnn(small, r.pick[2 * j + 1]).astype(BF)

    def factors(self, vecs):
        r = self.r
        return dnn(vecs, r.e[0]) + r.t[0:1, :], dnn(vecs, r.e[1]) + r.t[1:2, :]

    def factors_back(self, grad, one, two):
        r = self.r
        return dnt((grad * two).astype(BF), r.e[0]) + dnt((grad * one).astype(BF), r.e[1])

    def key_open(self, width):
        slot = lax.broadcasted_iota(jnp.int32, (BLK, width), 0)
        return (slot >= EDGE) | (self.xh == 1)

    def sees_state(self, b, width):
        slot = b * BLK + lax.broadcasted_iota(jnp.int32, (BLK, width), 0)
        return (slot < HALF_TOK - EDGE) | (self.xh == 0)

    def scores(self, j, b):
        r = self.r
        scores = dnt(r.qs[j, chip_block(b), :], r.ks[j, chip_block(b), :]) * INV_ROOT
        mask = causal_mask(b * BLK, self.edge)
        return scores, mask, jnp.where(mask, 1.0 + scores + 0.5 * scores * scores, 0.0)


def linear_states(r, lin):
    for b in range(NBLK):
        r.p[rows_of(b), :] = dnn(r.raw[rows_of(b), :], r.sel[...]).astype(BF)
    lin.vectors()
    for j in range(2):
        sv = jnp.zeros((HEAD_V, STATE), F32)
        sn = jnp.zeros((1, STATE), F32)
        for b in range(NBLK):
            r.pre_v[j, b] = sv
            r.pre_n[j, b] = jnp.broadcast_to(sn, (8, STATE))
            one, two = lin.factors(r.ks[j, rows_of(b), :])
            phi = one * two
            if b == 0:
                phi = jnp.where(lin.key_open(STATE), phi, 0.0)
            sv = sv + dtn(r.p[rows_of(b), head_of(j)], phi.astype(BF)) * lin.coef
            sn = sn + jnp.sum(phi, axis=0, keepdims=True) * lin.coef
        r.sv_s[j] = sv.astype(BF)
        r.sn_s[j] = jnp.broadcast_to(sn, (8, STATE))
    return (
        remote(r.sv_s, r.sv_r, r.xss.at[0], r.xrs.at[0], lin.partner),
        remote(r.sn_s, r.sn_r, r.xss.at[1], r.xrs.at[1], lin.partner),
    )


def linear_own(r, lin, b):
    rows = chip_block(b)
    for j in range(2):
        _, _, kernel = lin.scores(j, b)
        r.num[j, rows, :] = dnn(kernel.astype(BF), r.p[rows, head_of(j)])
        r.den[j, rows, :] = jnp.broadcast_to(
            jnp.sum(kernel, axis=-1, keepdims=True), (BLK, HEAD_V)
        )


def linear_rest(r, lin, b):
    rows = chip_block(b)
    for j in range(2):
        state_v = (r.pre_v[j, b] + r.sv_r[j].astype(F32) * lin.second).astype(BF)
        state_n = r.pre_n[j, b] + r.sn_r[j] * lin.second
        r.sv[j, b] = state_v
        r.sn[j, b] = state_n
        one, two = lin.factors(r.qs[j, rows, :])
        phi = one * two
        den = jnp.sum(phi * state_n[0:1, :], axis=-1, keepdims=True)
        num = dnt(phi.astype(BF), state_v)
        seen = lin.sees_state(b, HEAD_V)
        top = r.num[j, rows, :] + jnp.where(seen, num, 0.0)
        bottom = r.den[j, rows, :] + jnp.where(seen, den, 0.0)
        r.y[rows, head_of(j)] = (top / bottom).astype(BF)


STATE_SCRATCH = {
    "qs": pltpu.VMEM((2, HALF_TOK, 128), BF),
    "ks": pltpu.VMEM((2, HALF_TOK, 128), BF),
    "sv_s": pltpu.VMEM((2, HEAD_V, STATE), BF),
    "sn_s": pltpu.VMEM((2, 8, STATE), F32),
    "sv_r": pltpu.VMEM((2, HEAD_V, STATE), BF),
    "sn_r": pltpu.VMEM((2, 8, STATE), F32),
    "pre_v": pltpu.VMEM((2, NBLK, HEAD_V, STATE), F32),
    "pre_n": pltpu.VMEM((2, NBLK, 8, STATE), F32),
    "xss": pltpu.SemaphoreType.DMA((2,)),
    "xrs": pltpu.SemaphoreType.DMA((2,)),
}


def mask_cotangent(r, ring):
    first = lax.axis_index("xh") * HALF_TOK + (ring.z * 2 + ring.c) * TOK
    slot = first + lax.broadcasted_iota(jnp.int32, (TOK, 1), 0)
    last = 2 * HALF_TOK - EDGE
    start = jnp.where(slot < EDGE, 0, jnp.where(slot < last, EDGE, last))
    length = jnp.where(
        slot < EDGE, r.lengths[0, 0], jnp.where(slot < last, r.lengths[0, 1], r.lengths[0, 2])
    )
    valid = (slot - start) < length
    rows = r.cot[...].astype(F32)
    r.cot_out[...] = jnp.where(valid, rows, 0.0).astype(BF)


def linear_body(r):
    ring, plane = Ring(), Plane()
    r.partners = (ring.up, ring.dn, ring.sib, {"xh": 1 - lax.axis_index("xh")})
    r.partners += plane.neighbours()
    signal(r.partners)
    r.need("x", "gain_a", "rows_in", "rows_out", "cot")
    mask_cotangent(r, ring)
    own = r.wide.at[plane.x, plane.y]
    own[BIN_PAD // 2 :, :] = jnp.zeros((BIN_PAD // 2, D), BF)
    own[: r.rows_in.shape[0], :] = r.rows_in[...]
    r.wout[plane.x, plane.y] = r.rows_out[...]
    r.cbuf[ring.z * 2 + ring.c] = r.cot_out[: TOK // 2, :]
    r.flush("cot_out")
    outs, keep = first_part(r, ring, plane)
    cots = half_gather(ring, r, r.lo)
    advance(cots)
    lin = Linear(r)
    states = linear_states(r, lin)
    advance(outs)
    linear_own(r, lin, ring.zz)
    advance(outs)
    linear_own(r, lin, ring.zp)
    advance(cots)
    advance(cots)
    finish(outs)
    keep_out = load(r.wout, r.w_out, r.wls.at[1])

    def before(index, chip, mid):
        if index == 0:
            for copy in states:
                copy.wait_recv()
        if index >= 2:
            linear_own(r, lin, chip)
        linear_rest(r, lin, chip)
        mid()
        if index == 3:
            r.flush("y", "p", "sv", "sn")

    ring_forward(r, ring, r.y, r.wout, r.gain_b, (cots,), before)
    finish(cots)
    keep.wait()
    keep_out.wait()
    for copy in states:
        copy.wait_send()


def linear_step(select, tables, cot, lengths, x, gain_a, gain_b, rows_in, rows_out):
    return build(
        linear_body,
        {
            "x": vm(x),
            "gain_a": vm(gain_a),
            "rows_in": vm(rows_in),
            "rows_out": vm(rows_out),
            "cot": vm(cot),
            "gain_b": vm(gain_b),
            "sel": vm(select),
            "e": vm(tables[0]),
            "t": vm(tables[1]),
            "pick": vm(tables[2]),
            "lengths": (lengths, SM),
        },
        {
            "cot_out": (sds((TOK, D)), VM),
            "h": (sds((8, TOK, D)), ANY),
            "w_in": (sds((4, 4, BIN_PAD, D)), ANY),
            "w_out": (sds((4, 4, 16, D)), ANY),
            "y": (sds((HALF_TOK, 2 * HEAD_V)), VM),
            "p": (sds((HALF_TOK, 3 * HEAD_V)), VM),
            "sv": (sds((2, NBLK, HEAD_V, STATE)), VM),
            "sn": (sds((2, NBLK, 8, STATE), F32), VM),
            "lo": (sds((8, TOK // 2, D)), ANY),
            "x_out": (sds((TOK, D), F32), VM),
            "h_out": (sds((8, TOK, D)), ANY),
        },
        {
            "raw": pltpu.VMEM((HALF_TOK, 16 * BIN_PAD), BF),
            "num": pltpu.VMEM((2, HALF_TOK, HEAD_V), F32),
            "den": pltpu.VMEM((2, HALF_TOK, HEAD_V), F32),
            "wide": pltpu.VMEM((4, 4, BIN_PAD, D), BF),
            "wout": pltpu.VMEM((4, 4, 16, D), BF),
            "wss": pltpu.SemaphoreType.DMA((GATHER_COPIES,)),
            "wrs": pltpu.SemaphoreType.DMA((GATHER_COPIES,)),
            "oss": pltpu.SemaphoreType.DMA((GATHER_COPIES,)),
            "ors": pltpu.SemaphoreType.DMA((GATHER_COPIES,)),
            "wls": pltpu.SemaphoreType.DMA((2,)),
            "fss": pltpu.SemaphoreType.DMA((14,)),
            "frs": pltpu.SemaphoreType.DMA((14,)),
            "fls": pltpu.SemaphoreType.DMA((8,)),
        }
        | STATE_SCRATCH
        | HALF_SCRATCH
        | SCATTER_SCRATCH
        | GATHER_SCRATCH,
        2,
    )


def linear_backward_own(r, lin, sums):
    lin.vectors()
    for j in range(2):
        tv = jnp.zeros((HEAD_V, STATE), F32)
        tn = jnp.zeros((1, STATE), F32)
        for b in range(NBLK):
            queries = r.qs[j, rows_of(b), :]
            grads = r.dy[rows_of(b), head_of(j)]
            one, two = lin.factors(queries)
            phi = one * two
            phi_low = phi.astype(BF)
            seen = lin.sees_state(b, 1)
            state_v, state_n = r.sv[j, b], r.sn[j, b, 0:1, :]
            scores, mask, kernel = lin.scores(j, b)
            weight_grad = dnt(grads, r.p[rows_of(b), head_of(j)])
            den = jnp.sum(phi * state_n, axis=-1, keepdims=True)
            num = dnt(phi_low, state_v)
            dot = jnp.sum(num * grads.astype(F32), axis=-1, keepdims=True)
            total = jnp.where(seen, den, 0.0) + jnp.sum(kernel, axis=-1, keepdims=True)
            dot = jnp.where(seen, dot, 0.0) + jnp.sum(kernel * weight_grad, axis=-1, keepdims=True)
            inverse = 1.0 / total
            mean = dot * inverse
            grads_n = (grads.astype(F32) * inverse).astype(BF)
            score_grad = jnp.where(
                mask, (weight_grad - mean) * inverse * (1.0 + scores), 0.0
            ).astype(BF)
            r.dk[j, rows_of(b), :] = dtn(score_grad, queries)
            r.dv[j, rows_of(b), :] = dtn(kernel.astype(BF), grads_n)
            shift = jnp.where(seen, -(mean * inverse), 0.0)
            grads_s = jnp.where(seen, grads_n, jnp.zeros_like(grads_n))
            phi_grad = dnn(grads_s, state_v) + shift * state_n
            r.dq[j, rows_of(b), :] = dnn(
                score_grad, r.ks[j, rows_of(b), :]
            ) * INV_ROOT + lin.factors_back(phi_grad, one, two)
            own_v = dtn(grads_s, phi_low) * lin.coef
            own_n = jnp.sum(shift * phi, axis=0, keepdims=True) * lin.coef
            r.pre_v[j, b] = own_v
            r.pre_n[j, b] = jnp.broadcast_to(own_n, (8, STATE))
            tv, tn = tv + own_v, tn + own_n
            if (j, b) in ((0, 0), (0, 3)):
                advance(sums)
        r.sv_s[j] = tv.astype(BF)
        r.sn_s[j] = jnp.broadcast_to(tn, (8, STATE))
    copies = (
        remote(r.sv_s, r.sv_r, r.xss.at[0], r.xrs.at[0], lin.partner),
        remote(r.sn_s, r.sn_r, r.xss.at[1], r.xrs.at[1], lin.partner),
    )
    for j in range(2):
        tv = jnp.zeros((HEAD_V, STATE), F32)
        tn = jnp.zeros((8, STATE), F32)
        for b in reversed(range(NBLK)):
            own_v, own_n = r.pre_v[j, b], r.pre_n[j, b]
            r.pre_v[j, b] = tv
            r.pre_n[j, b] = tn
            tv, tn = tv + own_v, tn + own_n
    return copies


def linear_backward_rest(r, lin, b):
    rows = chip_block(b)
    first = 1.0 - lin.second
    visible = lin.key_open(STATE) | (b > 0)
    placed = jnp.zeros((BLK, 128), F32)
    for j in range(2):
        one, two = lin.factors(r.ks[j, rows, :])
        phi = jnp.where(visible, one * two, 0.0)
        state = (r.pre_v[j, b] + r.sv_r[j].astype(F32) * first).astype(BF)
        state_n = r.pre_n[j, b, 0:1, :] + r.sn_r[j, 0:1, :] * first
        phi_grad = jnp.where(visible, dnn(r.p[rows, head_of(j)], state) + state_n, 0.0)
        key_grad = r.dk[j, rows, :] * INV_ROOT + lin.factors_back(phi_grad, one, two)
        value_grad = r.dv[j, rows, :] + dnt(phi.astype(BF), state)
        r.dp[rows, head_of(j)] = value_grad.astype(BF)
        placed = placed + dnt(r.dq[j, rows, :].astype(BF), r.pick[2 * j])
        placed = placed + dnt(key_grad.astype(BF), r.pick[2 * j + 1])
    r.dp[rows, 2 * HEAD_V :] = placed.astype(BF)
    r.draw[rows, :] = dnt(r.dp[rows, :], r.sel[...]).astype(BF)


def sum_steps(ring, plane, r):
    copies = []
    stages = (
        (r.ring_in, ring.z * 2 + ring.c, 8, lambda t: {"z": lax.div(t, 2), "c": lax.rem(t, 2)}),
        (r.x_in, plane.x, 4, plane.at_x),
        (r.y_in, plane.y, 4, plane.at_y),
    )
    for dst, own, count, device_of in stages:
        dst[own] = r.pack[...]
        sent = []
        for o in range(1, count):
            n = len(copies) + len(sent)
            device = device_of(lax.rem(own + o, count))
            sent.append(remote(r.pack, dst.at[own], r.pss.at[n], r.prs.at[n], device))
        yield
        for copy in sent:
            copy.wait_recv()
        for copy in sent:
            copy.wait_send()
        copies += sent
        total = dst[0]
        for k in range(1, count):
            total = total + dst[k]
        r.pack[...] = total


def last_body(r):
    ring, plane = Ring(), Plane()
    me = ring.z * 2 + ring.c
    partners = []
    for o in range(1, 8):
        to = lax.rem(me + o, 8)
        partners.append({"z": lax.div(to, 2), "c": lax.rem(to, 2)})
    for o in range(1, 4):
        partners.append(plane.at_x(lax.rem(plane.x + o, 4)))
        partners.append(plane.at_y(lax.rem(plane.y + o, 4)))
    signal(partners)
    loads = [
        load(r.g, r.win, r.lsem.at[0]),
        load(r.w, r.wv, r.lsem.at[1]),
        load(r.h, r.hv, r.lsem.at[2]),
    ]
    def write(at, rows, total):
        r.out[rows, :] = (r.x3[rows, :] + total).astype(BF)

    sums = rows_reduce(ring, r, 1, write)
    win = plane_reduce(plane, r, "win", ((0, r.win_in), (48, r.win_out), (64, r.lin_out)))
    arrive(partners)
    advance(sums)
    loads[0].wait()
    advance(win)
    r.need()
    r.out[: TOK // 2, :] = r.low[...]
    lin = Linear(r)
    states = linear_backward_own(r, lin, sums)
    advance(win)
    finish(sums)
    r.flush("out")
    for copy in loads[1:]:
        copy.wait()

    def before(index, chip, mid):
        if index == 0:
            for copy in states:
                copy.wait_recv()
        linear_backward_rest(r, lin, chip)
        mid()

    wide = D // 8

    def product(rows, col):
        return dnn(r.draw[rows, :], r.wv[:, :, :, col].reshape(16 * BIN_PAD, -1))

    def weights():
        for k in range(4):
            cols = slice(k * 512, (k + 1) * 512)
            res = dtn(r.draw[...], r.hv[:, :, cols].reshape(HALF_TOK, 512))
            own = r.wv[:, :, :, cols].reshape(16 * BIN_PAD, 512).astype(F32)
            r.gacc[:, cols] = jnp.sum(res * own, axis=0, keepdims=True)
            r.lin[:, :, :, cols] = res.astype(BF).reshape(4, 4, BIN_PAD, 512)
        reduce = plane_reduce(plane, r, "lin", ((0, r.lin_in),))
        advance(reduce)
        gains = (r.gacc[...] / r.gain[...], r.gain_b[...], r.gain_c[...])
        for n, gain in enumerate(gains):
            for i in range(8):
                r.pack[i : i + 1, n * wide : (n + 1) * wide] = gain[:, i * wide : (i + 1) * wide]
        gain_sums = sum_steps(ring, plane, r)
        advance(gain_sums)
        yield
        advance(reduce)
        advance(gain_sums)
        yield
        advance(reduce)
        advance(gain_sums)
        advance(win)
        yield
        yield
        advance(reduce)
        finish(gain_sums)
        advance(win)
        yield
        finish(win)
        r.flush("win_in", "win_out", "lin_out", "d_out")
        finish(reduce)

    weight_grads = weights()

    def one(at):
        r.d_out[at, :] = r.res[at, :] + norm_back_rows(r.v, r.gain, sums_of(r, ring, at), at)

    def ready(q):
        by_rows(one, q * (TOK // CHUNKS), TOK // CHUNKS)

    weave(scatter(ring, r, product, ready, before), weight_grads)
    for copy in states:
        copy.wait_send()
    finish(weight_grads)
    for n, out in enumerate((r.ga, r.gb, r.gc)):
        for i in range(8):
            out[:, i * wide : (i + 1) * wide] = r.pack[i : i + 1, n * wide : (n + 1) * wide]


def last_step(lin, dy, select, tables, down, x3, low, g, w, h, v, gain, res, gain_b, gain_c, width):
    small = (8, 3 * D // 8)
    return build(
        last_body,
        {
            "p": vm(lin.p),
            "dy": vm(dy),
            "sv": vm(lin.sv),
            "sn": vm(lin.sn),
            "sel": vm(select),
            "e": vm(tables[0]),
            "t": vm(tables[1]),
            "pick": vm(tables[2]),
            "down": hbm(down),
            "x3": vm(x3),
            "low": vm(low),
            "g": hbm(g),
            "w": hbm(w),
            "h": hbm(h),
            "v": vm(v),
            "gain": vm(gain),
            "res": vm(res),
            "gain_b": vm(gain_b),
            "gain_c": vm(gain_c),
        },
        {
            "out": (sds((TOK, D)), VM),
            "d_out": (sds((TOK, D), F32), VM),
            "ga": (sds((1, D), F32), VM),
            "gb": (sds((1, D), F32), VM),
            "gc": (sds((1, D), F32), VM),
            "win_in": (sds((48, D), F32), VM),
            "win_out": (sds((16, D), F32), VM),
            "lin_in": (sds((width, D), F32), VM),
            "lin_out": (sds((16, D), F32), VM),
        },
        {
            "dp": pltpu.VMEM((HALF_TOK, 3 * HEAD_V), BF),
            "draw": pltpu.VMEM((HALF_TOK, 16 * BIN_PAD), BF),
            "dq": pltpu.VMEM((2, HALF_TOK, 128), F32),
            "dk": pltpu.VMEM((2, HALF_TOK, 128), F32),
            "dv": pltpu.VMEM((2, HALF_TOK, HEAD_V), F32),
            "wv": pltpu.VMEM((4, 4, BIN_PAD, D), BF),
            "hv": pltpu.VMEM((8, TOK, D), BF),
            "gacc": pltpu.VMEM((1, D), F32),
            "pack": pltpu.VMEM(small, F32),
            "ring_in": pltpu.VMEM((8,) + small, F32),
            "x_in": pltpu.VMEM((4,) + small, F32),
            "y_in": pltpu.VMEM((4,) + small, F32),
            "pss": pltpu.SemaphoreType.DMA((13,)),
            "prs": pltpu.SemaphoreType.DMA((13,)),
            "lsem": pltpu.SemaphoreType.DMA((3,)),
        }
        | STATE_SCRATCH
        | ROWS_SCRATCH
        | plane_reduce_scratch("win", 80)
        | plane_reduce_scratch("lin", BIN_PAD)
        | SCATTER_SCRATCH,
        6,
    )


WBLK = 128
WKEYS = WBLK + WINDOW
INV_ROOT_V = 1.0 / math.sqrt(HEAD_V)


def turn_tables():
    slot = np.arange(2 * HALF_TOK)
    last = 2 * HALF_TOK - EDGE
    position = slot - np.where(slot < EDGE, 0, np.where(slot < last, EDGE, last))
    frequency = np.exp(-math.log(10000.0) * np.arange(HEAD_V // 2) * 2.0 / HEAD_V)
    angles = position[:, None] * frequency[None, :]
    cosine, sine = np.cos(angles), np.sin(angles)
    pair = np.stack(
        [np.concatenate([cosine, cosine], axis=1), np.concatenate([-sine, sine], axis=1)]
    )
    return pair.reshape(2, 2, HALF_TOK, HEAD_V).transpose(1, 0, 2, 3).astype(np.float32)


class Window:
    def __init__(self):
        self.xh = lax.axis_index("xh")
        self.partner = {"xh": 1 - self.xh}
        self.edge = jnp.where(self.xh == 0, EDGE, HALF_TOK - EDGE)
        self.lowest = jnp.where(self.xh == 0, 0, -WINDOW)

    def mask(self, b):
        t = b * WBLK + lax.broadcasted_iota(jnp.int32, (WBLK, WKEYS), 0)
        u = b * WBLK - WINDOW + lax.broadcasted_iota(jnp.int32, (WBLK, WKEYS), 1)
        same = (t >= self.edge) == (u >= self.edge)
        return (u <= t) & (t - u < WINDOW) & same & (u >= self.lowest)

    def probs(self, r, b, j):
        rows, keys, head = window_rows(b), window_keys(b), head_of(j)
        scores = dnt(r.q[rows, head], r.kv[keys, head]) * INV_ROOT_V
        scores = jnp.where(self.mask(b), scores, -1e30)
        exps = jnp.exp(scores - jnp.max(scores, axis=-1, keepdims=True))
        return exps / jnp.sum(exps, axis=-1, keepdims=True)


def window_rows(b):
    return pl.ds(b * WBLK if isinstance(b, int) else pl.multiple_of(b * WBLK, WBLK), WBLK)


def window_keys(b):
    return pl.ds(b * WBLK if isinstance(b, int) else pl.multiple_of(b * WBLK, WBLK), WKEYS)


def window_vectors(r, win, cots):
    size = 2 * TOK
    blocks = HALF_TOK // size

    def turned(vecs, rows):
        return (
            vecs * r.turn[0, rows, :] + pltpu.roll(vecs, HEAD_V // 2, 1) * r.turn[1, rows, :]
        ).astype(BF)

    for b in (blocks - 1,) + tuple(range(blocks - 1)):
        rows = slice(b * size, (b + 1) * size)
        shifted = slice(WINDOW + b * size, WINDOW + (b + 1) * size)
        tokens = r.hv[2 * b : 2 * b + 2].reshape(size, D)
        for j in range(2):
            proj = dnt(tokens, r.wiv[2 * j : 2 * j + 2].reshape(384, D))
            r.q[rows, head_of(j)] = turned(proj[:, :128], rows)
            r.kv[shifted, head_of(j)] = turned(proj[:, 128:256], rows)
            r.kv[shifted, head_of(2 + j)] = proj[:, 256:].astype(BF)
        if b == blocks - 1:
            copy = remote(
                r.kv.at[pl.ds(HALF_TOK, WINDOW), :],
                r.kv.at[pl.ds(0, WINDOW), :],
                r.xss,
                r.xrs,
                win.partner,
            )
    advance(cots)
    return copy


def window_chip(r, win, chip):
    for i in range(2 * TOK // WBLK):
        b = chip * (2 * TOK // WBLK) + i
        for j in range(2):
            r.y[window_rows(b), head_of(j)] = dnn(
                win.probs(r, b, j).astype(BF), r.kv[window_keys(b), head_of(2 + j)]
            ).astype(BF)


def window_body(r):
    ring = Ring()
    partners = (ring.up, ring.dn, ring.sib, {"xh": 1 - lax.axis_index("xh")})
    signal(partners)
    loads = (
        load(r.w.at[:, :, pl.ds(0, 48), :], r.wiv, r.lsem.at[0]),
        load(r.h, r.hv, r.lsem.at[1]),
        load(r.turns.at[lax.axis_index("xh")], r.turn, r.lsem.at[2]),
        load(r.w.at[:, :, pl.ds(48, 16), :], r.wov, r.lsem.at[3]),
    )
    r.need("cot")
    r.cbuf[ring.z * 2 + ring.c] = r.cot[TOK // 2 :, :]
    arrive(partners)
    cots = half_gather(ring, r, r.hi)
    advance(cots)
    r.need()
    for copy in loads:
        copy.wait()
    win = Window()
    halo = window_vectors(r, win, cots)

    def before(index, chip, mid):
        if index == 0:
            halo.wait_recv()
        window_chip(r, win, chip)
        mid()
        if index == 3:
            r.flush("y", "q", "kv")

    ring_forward(r, ring, r.y, r.wov, r.gain, (cots,), before)
    finish(cots)
    halo.wait_send()


def window_step(h, w, turns, cot, x, gain):
    return build(
        window_body,
        {
            "h": hbm(h),
            "w": hbm(w),
            "turns": hbm(turns),
            "cot": vm(cot),
            "x": vm(x),
            "gain": vm(gain),
        },
        {
            "y": (sds((HALF_TOK, 256)), VM),
            "q": (sds((HALF_TOK, 256)), VM),
            "kv": (sds((HALF_TOK + WINDOW, 512)), VM),
            "hi": (sds((8, TOK // 2, D)), ANY),
            "x_out": (sds((TOK, D), F32), VM),
            "h_out": (sds((8, TOK, D)), ANY),
        },
        {
            "hv": pltpu.VMEM((8, TOK, D), BF),
            "wiv": pltpu.VMEM((4, 4, 48, D), BF),
            "wov": pltpu.VMEM((4, 4, 16, D), BF),
            "turn": pltpu.VMEM((2, HALF_TOK, HEAD_V), F32),
            "lsem": pltpu.SemaphoreType.DMA((4,)),
            "xss": pltpu.SemaphoreType.DMA,
            "xrs": pltpu.SemaphoreType.DMA,
        }
        | HALF_SCRATCH
        | SCATTER_SCRATCH
        | GATHER_SCRATCH,
        3,
    )


def window_back_halo(r, win):
    rows, keys = window_rows(0), window_keys(0)
    for j in range(2):
        head, vals = head_of(j), head_of(2 + j)
        probs = win.probs(r, 0, j)
        prob_grad = dnt(r.dy[rows, head], r.kv[keys, vals])
        score_grad = (
            probs * (prob_grad - jnp.sum(prob_grad * probs, axis=-1, keepdims=True))
        ).astype(BF)
        r.halo_s[:, head] = dtn(score_grad, r.q[rows, head])[:WINDOW] * INV_ROOT_V
        r.halo_s[:, vals] = dtn(probs.astype(BF), r.dy[rows, head])[:WINDOW]
    return remote(r.halo_s, r.halo, r.xss, r.xrs, win.partner)


def turned_back(r, rows, grads):
    return (
        grads * r.turn[0, rows, :] + pltpu.roll(grads * r.turn[1, rows, :], HEAD_V // 2, 1)
    ).astype(BF)


def window_back_block(r, win, b):
    rows, keys = window_rows(b), window_keys(b)
    for j in range(2):
        head, vals = head_of(j), head_of(2 + j)
        queries, grads = r.q[rows, head], r.dy[rows, head]
        probs = win.probs(r, b, j)
        prob_grad = dnt(grads, r.kv[keys, vals])
        score_grad = (
            probs * (prob_grad - jnp.sum(prob_grad * probs, axis=-1, keepdims=True))
        ).astype(BF)
        r.dp[rows, head_of(3 * j)] = turned_back(
            r, rows, dnn(score_grad, r.kv[keys, head]) * INV_ROOT_V
        )
        r.dkv[keys, head] += dtn(score_grad, queries) * INV_ROOT_V
        r.dkv[keys, vals] += dtn(probs.astype(BF), grads)


def window_back_chip(r, chip):
    last = pl.ds(pl.multiple_of((chip + 1) * (2 * TOK), WINDOW), WINDOW)
    r.dkv[last, :] += jnp.where(chip == HALF_TOK // (2 * TOK) - 1, r.halo[...], 0.0)
    shifted = pl.ds(pl.multiple_of(chip * (2 * TOK) + WINDOW, WINDOW), 2 * TOK)
    rows = chip_rows(chip)
    for j in range(2):
        r.dp[rows, head_of(3 * j + 1)] = turned_back(r, rows, r.dkv[shifted, head_of(j)])
        r.dp[rows, head_of(3 * j + 2)] = r.dkv[shifted, head_of(2 + j)].astype(BF)


def window_back_body(r):
    ring = Ring()
    partners = (ring.up, ring.dn, ring.sib, {"xh": 1 - lax.axis_index("xh")})
    signal(partners)
    turning = load(r.turns.at[lax.axis_index("xh")], r.turn, r.lsem.at[0])
    loads = [
        load(r.w.at[:, :, pl.ds(0, 48), :], r.wiv, r.lsem.at[1]),
        load(r.h, r.hv, r.lsem.at[2]),
        load(r.e, r.ev, r.lsem.at[3]),
        load(r.wo, r.wov, r.lsem.at[4]),
    ]
    r.dkv[...] = jnp.zeros_like(r.dkv)
    r.oacc[...] = jnp.zeros_like(r.oacc)
    r.gacc[...] = jnp.zeros_like(r.gacc)

    def write(at, rows, total):
        r.low[at, :] = (r.x3[rows, :] + total).astype(BF)

    sums = rows_reduce(ring, r, 0, write)
    arrive(partners)
    advance(sums)
    r.need()
    turning.wait()
    win = Window()
    halo = window_back_halo(r, win)
    for copy in loads:
        copy.wait()
    blocks = HALF_TOK // WBLK

    def before(index, chip, mid):
        turns = ((0, 1, 2), (0, 1), (1, 2), (1,))[index]
        for n in turns:
            window_back_block(r, win, lax.rem(2 * chip + n, blocks))
            if n == turns[0]:
                mid()
        if index == 0:
            advance(sums)
            halo.wait_recv()
        window_back_chip(r, chip)
        if index in (1, 3):
            advance(sums)

    def product(rows, col):
        return dnn(r.dp[rows, :], r.wiv[:, :, :, col].reshape(768, -1))

    def weights():
        for k in range(4):
            cols = slice(k * 512, (k + 1) * 512)
            rows = r.hv[:, :, cols].reshape(HALF_TOK, 512)
            for i in range(2):
                res = dtn(r.dp[:, i * 384 : (i + 1) * 384], rows)
                own = r.wiv[2 * i : 2 * i + 2, :, :, cols].reshape(384, 512).astype(F32)
                r.gacc[:, cols] += jnp.sum(res * own, axis=0, keepdims=True)
                r.gstage[2 * i : 2 * i + 2, :, :48, cols] = res.astype(BF).reshape(2, 4, 48, 512)
            res = dtn(r.y[...], r.ev[:, :, cols].reshape(HALF_TOK, 512)).astype(BF)
            r.gstage[:, :, 48:, cols] = res.reshape(4, 4, 16, 512)
            yield
        copy = load(r.gstage, r.grads.at[:, :, pl.ds(0, 64), :], r.lsem.at[5])
        yield
        copy.wait()

    def also(chip, rows):
        r.oacc[...] += dtn(r.y1[chip_rows(chip), :], rows)

    weight_grads = weights()
    ring_backward(r, ring, product, r.wov, (weight_grads,), before, also)
    finish(sums)
    halo.wait_send()
    r.ostage[...] = r.oacc[...].astype(BF).reshape(4, 4, 16, D)
    copy = load(r.ostage, r.grads.at[:, :, pl.ds(64, 16), :], r.lsem.at[6])
    finish(weight_grads)
    copy.wait()
    r.gain_out[...] = r.gacc[...] / r.gain[...]


def window_back_step(win, y1, dy, turns, down, x3, w, wo, h, e, v, gain, res):
    return build(
        window_back_body,
        {
            "q": vm(win.q),
            "kv": vm(win.kv),
            "dy": vm(dy),
            "turns": hbm(turns),
            "down": hbm(down),
            "x3": vm(x3),
            "w": hbm(w),
            "wo": hbm(wo),
            "h": hbm(h),
            "e": hbm(e),
            "y": vm(win.y),
            "y1": vm(y1),
            "v": vm(v),
            "gain": vm(gain),
            "res": vm(res),
        },
        {
            "low": (sds((TOK // 2, D)), VM),
            "d_out": (sds((TOK, D), F32), VM),
            "gain_out": (sds((1, D), F32), VM),
            "e_out": (sds((8, TOK, D)), ANY),
            "dy_out": (sds((HALF_TOK, 256)), VM),
            "grads": (sds((4, 4, 80, D)), ANY),
        },
        {
            "dkv": pltpu.VMEM((HALF_TOK + WINDOW, 512), F32),
            "halo": pltpu.VMEM((WINDOW, 512), F32),
            "halo_s": pltpu.VMEM((WINDOW, 512), F32),
            "turn": pltpu.VMEM((2, HALF_TOK, HEAD_V), F32),
            "dp": pltpu.VMEM((HALF_TOK, 768), BF),
            "wiv": pltpu.VMEM((4, 4, 48, D), BF),
            "wov": pltpu.VMEM((4, 4, 16, D), BF),
            "hv": pltpu.VMEM((8, TOK, D), BF),
            "ev": pltpu.VMEM((8, TOK, D), BF),
            "gstage": pltpu.VMEM((4, 4, 64, D), BF),
            "oacc": pltpu.VMEM((256, D), F32),
            "ostage": pltpu.VMEM((4, 4, 16, D), BF),
            "gacc": pltpu.VMEM((1, D), F32),
            "lsem": pltpu.SemaphoreType.DMA((7,)),
            "xss": pltpu.SemaphoreType.DMA,
            "xrs": pltpu.SemaphoreType.DMA,
        }
        | ROWS_SCRATCH
        | SCATTER_SCRATCH
        | GATHER_SCRATCH,
        5,
    )


def padded(rows, count):
    return jnp.pad(rows, ((0, count - rows.shape[0]), (0, 0)))


def end_kernel(*refs):
    ff, copied, gate_up, down = refs[0], refs[1:-2], refs[-2], refs[-1]
    count = len(copied) // 2
    for n in range(count):
        copied[count + n][...] = copied[n][...]
    units = down.shape[0]
    gate_up[:, 0, :] = ff[:units].astype(F32)
    gate_up[:, 1, :] = ff[UNIT_PAD : UNIT_PAD + units].astype(F32)
    down[...] = ff[2 * UNIT_PAD : 2 * UNIT_PAD + units].astype(F32)


def end_step(ff, arrays, units):
    results = pl.pallas_call(
        end_kernel,
        out_shape=tuple(sds(array.shape, array.dtype) for array in arrays)
        + (sds((units, 2, D), F32), sds((units, D), F32)),
        in_specs=[VM] * (1 + len(arrays)),
        out_specs=(VM,) * (len(arrays) + 2),
        compiler_params=pltpu.CompilerParams(vmem_limit_bytes=60 << 20),
    )(ff, *arrays)
    return results


def body(
    block_input,
    cotangent,
    lengths,
    gain_a,
    based_in,
    based_out,
    gain_b,
    swa_in,
    swa_out,
    gain_c,
    mlp_in,
    mlp_down,
):
    gains = [gain.reshape(1, D) for gain in (gain_a, gain_b, gain_c)]
    units = mlp_down.shape[0]
    wide = based_in.shape[1]
    win_all = lax.all_gather(
        jnp.concatenate([swa_in.T, swa_out], axis=0), PLANE, axis=0, tiled=True
    ).reshape(4, 4, 64, D)
    ff_all = lax.all_gather(
        jnp.concatenate(
            [padded(part, UNIT_PAD) for part in (mlp_in[:, 0, :].T, mlp_in[:, 1, :].T, mlp_down)],
            axis=0,
        ),
        PLANE,
        axis=0,
        tiled=True,
    ).reshape(16, 3 * UNIT_PAD, D)
    tables = tuple(
        jnp.asarray(table, kind) for table, kind in zip(state_tables(), (BF, F32, BF))
    )
    select = jnp.asarray(select_table(wide), BF)

    turns = jnp.asarray(turn_tables())

    lin = linear_step(
        select,
        tables,
        cotangent,
        lengths,
        block_input,
        gains[0],
        gains[1],
        based_in.T,
        based_out,
    )
    win = window_step(lin.h_out, win_all, turns, lin.cot_out, lin.x_out, gains[2])
    mlp = mlp_step(win.h_out, lin.lo, win.hi, ff_all, win_all, win.x_out, gains[2], lin.cot_out)
    ff_grads = lax.psum_scatter(
        mlp.grads.reshape(-1, D), PLANE, scatter_dimension=0, tiled=True
    )
    back = window_back_step(
        win,
        lin.y,
        mlp.dy_out,
        turns,
        mlp.down,
        win.x_out,
        win_all,
        lin.w_out,
        lin.h_out,
        mlp.e_out,
        lin.x_out,
        gains[1],
        mlp.d_out,
    )
    end = last_step(
        lin,
        back.dy_out,
        select,
        tables,
        mlp.down,
        win.x_out,
        back.low,
        back.grads,
        lin.w_in,
        lin.h,
        block_input,
        gains[0],
        back.d_out,
        back.gain_out,
        mlp.gain_out,
        wide,
    )
    names = ("out", "d_out", "ga", "lin_in", "lin_out", "gb", "win_in", "win_out", "gc")
    results = end_step(ff_grads, [getattr(end, name) for name in names], units)
    out, d_out, ga, lin_in, lin_out, gb, win_in, win_out, gc, gate_up, down = results
    return (
        out,
        d_out,
        ga.reshape(D),
        lin_in.T,
        lin_out,
        gb.reshape(D),
        win_in.T,
        win_out,
        gc.reshape(D),
        jnp.transpose(gate_up, (2, 1, 0)),
        down,
    )


def solution(mesh):
    grid = Mesh(mesh.devices.reshape(2, 4, 2, 4, 2), ALL)
    tokens = P(ALL, None)
    weight = ("xh", "z", "c", "xl", "y")
    rows, cols = P(weight, None), P(None, weight)
    return jax.shard_map(
        body,
        mesh=grid,
        in_specs=(
            tokens,
            tokens,
            P(("xl", "y"), None),
            P(),
            cols,
            rows,
            P(),
            cols,
            rows,
            P(),
            P(None, None, weight),
            rows,
        ),
        out_specs=(
            tokens,
            tokens,
            P(),
            cols,
            rows,
            P(),
            cols,
            rows,
            P(),
            P(None, None, weight),
            rows,
        ),
        check_vma=False,
    )
```

```python
import functools
import math
import types

import jax
import jax.numpy as jnp
import numpy as np
from jax import lax
from jax.experimental import pallas as pl
from jax.experimental.pallas import tpu as pltpu
from jax.sharding import Mesh
from jax.sharding import PartitionSpec as P

FEAT = 16
HEAD_V = 128
WINDOW = 64
EPSILON = 1e-05
D = 2048
TOK = 128
HALF_TOK = 1024
EDGE = 64
UNIT_PAD = 48
BIN_PAD = 32
STATE = 256
PLANE = ("xh", "xl", "y")
RING = ("z", "c")
ALL = ("xl", "y", "xh", "z", "c")
MESH = pl.DeviceIdType.MESH
BF = jnp.bfloat16
F32 = jnp.float32
VM = pl.BlockSpec(memory_space=pltpu.VMEM)
ANY = pl.BlockSpec(memory_space=pl.ANY)
SM = pl.BlockSpec(memory_space=pltpu.SMEM)


def dnn(a, b):
    return lax.dot_general(a, b, (((1,), (0,)), ((), ())), preferred_element_type=F32)


def dnt(a, b):
    return lax.dot_general(a, b, (((1,), (1,)), ((), ())), preferred_element_type=F32)


def dtn(a, b):
    return lax.dot_general(a, b, (((0,), (0,)), ((), ())), preferred_element_type=F32)


def remote(src, dst, send_sem, recv_sem, device):
    copy = pltpu.make_async_remote_copy(
        src_ref=src,
        dst_ref=dst,
        send_sem=send_sem,
        recv_sem=recv_sem,
        device_id=device,
        device_id_type=MESH,
    )
    copy.start()
    return copy


def greet(devices):
    barrier = pltpu.get_barrier_semaphore()
    for device in devices:
        pl.semaphore_signal(barrier, inc=1, device_id=device, device_id_type=MESH)
    pl.semaphore_wait(barrier, len(devices))


class Ring:
    def __init__(self):
        self.z = lax.axis_index("z")
        self.c = lax.axis_index("c")
        self.oc = 1 - self.c
        self.zp = lax.rem(self.z + 1, 4)
        self.zm = lax.rem(self.z + 3, 4)
        self.zz = lax.rem(self.z + 2, 4)
        self.up = {"z": self.zp}
        self.dn = {"z": self.zm}
        self.sib = {"c": self.oc}

    def greet(self):
        greet((self.up, self.dn, self.sib))


class Plane:
    def __init__(self):
        self.x = lax.axis_index("xh") * 2 + lax.axis_index("xl")
        self.y = lax.axis_index("y")

    def at_x(self, x):
        return {"xh": lax.div(x, 2), "xl": lax.rem(x, 2)}

    def at_y(self, y):
        return {"y": y}

    def ring(self, along_x):
        me = self.x if along_x else self.y
        plus, minus, far = lax.rem(me + 1, 4), lax.rem(me + 3, 4), lax.rem(me + 2, 4)
        to = self.at_x if along_x else self.at_y
        return me, plus, minus, far, to(plus), to(minus)

    def neighbours(self):
        xs, ys = self.ring(True), self.ring(False)
        return (xs[4], xs[5], ys[4], ys[5])


def finish(steps):
    for _ in steps:
        pass


def advance(steps):
    next(steps, None)


def weave(main, *others):
    for _ in main:
        for other in others:
            advance(other)


CHUNKS = 2


def gather_steps(ring, buf, out_ref, ss, rs, ls, rows, start=0, base=0, keep=True, ready=None):
    half = rows // 2
    me = ring.z * 2 + ring.c
    below, above, far = ring.zm * 2 + ring.c, ring.zp * 2 + ring.c, ring.zz * 2 + ring.c

    def send(slot, part, device, index):
        piece = buf.at[slot, pl.ds(start + part * half, half), :]
        return remote(piece, piece, ss.at[base + index], rs.at[base + index], device)

    local = []

    def save(slot):
        if keep:
            copy = pltpu.make_async_copy(buf.at[slot], out_ref.at[slot], ls.at[len(local)])
            copy.start()
            local.append(copy)

    def done(chip):
        if ready is not None:
            ready(chip)

    up, dn, sib = ring.up, ring.dn, ring.sib
    cp = {}
    cp[0] = send(me, 0, up, 0)
    cp[1] = send(me, 1, dn, 1)
    cp[2] = send(me, 1, up, 2)
    cp[3] = send(me, 0, dn, 3)
    cp[4] = send(me, 0, sib, 4)
    cp[5] = send(me, 1, sib, 5)
    save(me)
    yield
    cp[0].wait_recv()
    cp[6] = send(below, 0, up, 6)
    cp[8] = send(below, 0, sib, 8)
    cp[1].wait_recv()
    cp[7] = send(above, 1, dn, 7)
    cp[9] = send(above, 1, sib, 9)
    yield
    cp[2].wait_recv()
    cp[10] = send(below, 1, sib, 10)
    save(below)
    cp[3].wait_recv()
    cp[11] = send(above, 0, sib, 11)
    save(above)
    yield
    cp[4].wait_recv()
    cp[5].wait_recv()
    save(ring.z * 2 + ring.oc)
    done(ring.z)
    cp[8].wait_recv()
    cp[10].wait_recv()
    save(ring.zm * 2 + ring.oc)
    done(ring.zm)
    yield
    cp[6].wait_recv()
    cp[12] = send(far, 0, sib, 12)
    cp[7].wait_recv()
    cp[13] = send(far, 1, sib, 13)
    save(far)
    cp[9].wait_recv()
    cp[11].wait_recv()
    save(ring.zp * 2 + ring.oc)
    done(ring.zp)
    yield
    cp[12].wait_recv()
    cp[13].wait_recv()
    save(ring.zz * 2 + ring.oc)
    done(ring.zz)
    for index in range(14):
        cp[index].wait_send()
    for copy in local:
        copy.wait()


def scatter_steps(ring, product, part, sib_in, far_in, end_in, ss, rs, ready, before=None):
    rows = TOK // CHUNKS
    half = rows // 2
    c, oc = ring.c, ring.oc
    up, dn, sib = ring.up, ring.dn, ring.sib
    order = (ring.zz, ring.zp, ring.zm, ring.z)
    step = 512
    cp = {}

    def send(q, index, src, dst, device):
        n = q * 10 + index
        cp[q, index] = remote(src, dst, ss.at[n], rs.at[n], device)

    def multiply(index):
        row = pl.multiple_of(order[index] * (2 * TOK), 2 * TOK)

        def one(n, carry):
            col = pl.ds(pl.multiple_of(n * step, step), step)
            res = product(pl.ds(row, 2 * TOK), col).astype(BF)
            part[index, 0, :, col] = res[:TOK]
            part[index, 1, :, col] = res[TOK:]
            return carry

        lax.fori_loop(0, D // step, one, 0)
        for q in range(CHUNKS):
            at = pl.ds(q * rows, rows)
            send(q, index, part.at[index, oc, at, :], sib_in.at[index, at, :], sib)

    def add(index, first, count, other):
        def one(i, carry):
            at = pl.ds(pl.multiple_of(first + i * 16, 16), 16)
            part[index, c, at, :] = (part[index, c, at, :].astype(F32) + other(at)).astype(BF)
            return carry

        lax.fori_loop(0, count // 16, one, 0)

    def add_sib(q, index):
        cp[q, index].wait_recv()
        add(index, q * rows, rows, lambda at: sib_in[index, at, :].astype(F32))

    def piece(q, which):
        return pl.ds(q * rows + which * half, half)

    def far(q):
        add_sib(q, 0)
        send(q, 4, part.at[0, c, piece(q, 0), :], far_in.at[piece(q, 0), :], up)
        send(q, 5, part.at[0, c, piece(q, 1), :], far_in.at[piece(q, 1), :], dn)

    def near_up(q):
        add_sib(q, 1)
        send(q, 6, part.at[1, c, piece(q, 1), :], end_in.at[0, piece(q, 1), :], up)

    def near_dn(q):
        add_sib(q, 2)
        send(q, 7, part.at[2, c, piece(q, 0), :], end_in.at[1, piece(q, 0), :], dn)

    def passed(q):
        for which, device in ((0, up), (1, dn)):
            cp[q, 4 + which].wait_recv()
            at = piece(q, which)
            add(1 + which, q * rows + which * half, half, lambda at: far_in[at, :].astype(F32))
            send(q, 8 + which, part.at[1 + which, c, at, :], end_in.at[which, at, :], device)

    def make(index, mid):
        if before is not None:
            before(index, order[index], mid)
        else:
            mid()

    def each(one):
        for q in range(CHUNKS):
            one(q)

    make(0, lambda: None)
    multiply(0)
    make(1, lambda: each(far))
    multiply(1)
    make(2, lambda: each(near_up))
    multiply(2)
    make(3, lambda: each(near_dn))
    multiply(3)
    yield
    each(passed)
    yield
    each(lambda q: add_sib(q, 3))
    yield
    for q in range(CHUNKS):
        for index in range(6, 10):
            cp[q, index].wait_recv()
        ready(q)
        yield
    for copy in cp.values():
        copy.wait_send()


def rows_reduce_steps(ring, src_ref, q, part, sib_in, far_in, end_in, ss, rs, ls, ready):
    rows = TOK // CHUNKS
    half = rows // 2
    order = (ring.zz, ring.zp, ring.zm, ring.z)
    up, dn, sib = ring.up, ring.dn, ring.sib
    cp, loads = {}, []

    def send(index, src, dst, device):
        cp[index] = remote(src, dst, ss.at[index], rs.at[index], device)

    def source(index, core):
        start = order[index] * (2 * TOK) + core * TOK + q * rows
        return src_ref.at[pl.ds(pl.multiple_of(start, 16), rows), :]

    def add(index, first, count, other):
        def one(i, carry):
            at = pl.ds(pl.multiple_of(first + i * 16, 16), 16)
            part[index, at, :] = (part[index, at, :].astype(F32) + other(at)).astype(BF)
            return carry

        lax.fori_loop(0, count // 16, one, 0)

    def add_sib(index):
        loads[index].wait()
        cp[index].wait_recv()
        add(index, 0, rows, lambda at: sib_in[index, at, :].astype(F32))

    low, high = pl.ds(0, half), pl.ds(half, half)
    for index in range(4):
        send(index, source(index, ring.oc), sib_in.at[index], sib)
        loads.append(load(source(index, ring.c), part.at[index], ls.at[index]))
    yield
    add_sib(0)
    send(4, part.at[0, low, :], far_in.at[low, :], up)
    send(5, part.at[0, high, :], far_in.at[high, :], dn)
    add_sib(1)
    send(6, part.at[1, high, :], end_in.at[0, high, :], up)
    add_sib(2)
    send(7, part.at[2, low, :], end_in.at[1, low, :], dn)
    add_sib(3)
    yield
    for which, device in ((0, up), (1, dn)):
        cp[4 + which].wait_recv()
        at = (low, high)[which]
        add(1 + which, which * half, half, lambda at: far_in[at, :].astype(F32))
        send(8 + which, part.at[1 + which, at, :], end_in.at[which, at, :], device)
    yield
    for index in range(6, 10):
        cp[index].wait_recv()

    def total(i, carry):
        at = pl.ds(pl.multiple_of(i * 16, 16), 16)
        ready(
            at,
            pl.ds(pl.multiple_of(q * rows + i * 16, 16), 16),
            part[3, at, :].astype(F32)
            + end_in[0, at, :].astype(F32)
            + end_in[1, at, :].astype(F32),
        )
        return carry

    lax.fori_loop(0, rows // 16, total, 0)
    for copy in cp.values():
        copy.wait_send()


ROWS_SCRATCH = {
    "bpart": pltpu.VMEM((4, TOK // CHUNKS, D), BF),
    "bsib": pltpu.VMEM((4, TOK // CHUNKS, D), BF),
    "bfar": pltpu.VMEM((TOK // CHUNKS, D), BF),
    "bend": pltpu.VMEM((2, TOK // CHUNKS, D), BF),
    "bss": pltpu.SemaphoreType.DMA((10,)),
    "brs": pltpu.SemaphoreType.DMA((10,)),
    "bls": pltpu.SemaphoreType.DMA((4,)),
}
SCATTER_SCRATCH = {
    "part": pltpu.VMEM((4, 2, TOK, D), BF),
    "sib_in": pltpu.VMEM((4, TOK, D), BF),
    "far_in": pltpu.VMEM((TOK, D), BF),
    "end_in": pltpu.VMEM((2, TOK, D), BF),
    "sss": pltpu.SemaphoreType.DMA((10 * CHUNKS,)),
    "srs": pltpu.SemaphoreType.DMA((10 * CHUNKS,)),
}
GATHER_SCRATCH = {
    "buf": pltpu.VMEM((8, TOK, D), BF),
    "ss": pltpu.SemaphoreType.DMA((14 * CHUNKS,)),
    "rs": pltpu.SemaphoreType.DMA((14 * CHUNKS,)),
    "ls": pltpu.SemaphoreType.DMA((8,)),
}
HALF_SCRATCH = {
    "cbuf": pltpu.VMEM((8, TOK // 2, D), BF),
    "css": pltpu.SemaphoreType.DMA((14,)),
    "crs": pltpu.SemaphoreType.DMA((14,)),
    "cls": pltpu.SemaphoreType.DMA((8,)),
}


def plane_view(plane, ref, half, stage, place, part):
    cols = pl.ds(half * (D // 2) + (part or 0) * (D // 4), D // 2 if part is None else D // 4)
    if stage == 0:
        return ref.at[place, plane.y, :, cols] if half == 0 else ref.at[plane.x, place, :, cols]
    return ref.at[:, place, :, cols] if half == 0 else ref.at[place, :, :, cols]


def plane_gather_steps(plane, buf, ss, rs):
    copies = []
    quarter = D // 4

    def view(half, first, second, part):
        x, y = (first, second) if half == 0 else (second, first)
        cols = pl.ds(half * 2 * quarter + (part or 0) * quarter, quarter if part is not None else 2 * quarter)
        return buf.at[x, y, :, cols]

    def send(ref, device):
        copies.append(remote(ref, ref, ss.at[len(copies)], rs.at[len(copies)], device))
        return copies[-1]

    firsts = [plane.ring(half == 0) for half in (0, 1)]
    seconds = [plane.ring(half == 1) for half in (0, 1)]
    near, passed, spread = {}, {}, {}

    def go_on(half, place):
        me, plus, minus, far, to_plus, to_minus = seconds[half]
        piece = view(half, place, me, None)
        spread[half, len(spread)] = (place, send(piece, to_plus), send(piece, to_minus))

    def pass_on(entry):
        half, (place, up, dn) = entry
        me, plus, minus, far, to_plus, to_minus = seconds[half]
        up.wait_recv()
        send(view(half, place, minus, 0), to_plus)
        dn.wait_recv()
        send(view(half, place, plus, 1), to_minus)

    for half in (0, 1):
        me, plus, minus, far, to_plus, to_minus = firsts[half]
        piece = view(half, me, seconds[half][0], None)
        near[half] = (send(piece, to_plus), send(piece, to_minus))
    for half in (0, 1):
        go_on(half, firsts[half][0])
    yield
    for half in (0, 1):
        me, plus, minus, far, to_plus, to_minus = firsts[half]
        other = seconds[half][0]
        near[half][0].wait_recv()
        up = send(view(half, minus, other, 0), to_plus)
        near[half][1].wait_recv()
        passed[half] = (up, send(view(half, plus, other, 1), to_minus))
    for half in (0, 1):
        go_on(half, firsts[half][2])
        go_on(half, firsts[half][1])
    yield
    for half in (0, 1):
        passed[half][0].wait_recv()
        passed[half][1].wait_recv()
        go_on(half, firsts[half][3])
    entries = [(key[0], value) for key, value in spread.items()]
    for entry in entries[:2]:
        pass_on(entry)
    yield
    for entry in entries[2:]:
        pass_on(entry)
    yield
    for copy in copies[-2 * len(entries) :]:
        copy.wait_recv()
    for copy in copies:
        copy.wait_send()


GATHER_COPIES = 40


def plane_reduce_scratch(name, rows):
    return {
        name: pltpu.VMEM((4, 4, rows, D), BF),
        name + "_far": pltpu.VMEM((2, 2, 4, rows, D // 4), BF),
        name + "_end": pltpu.VMEM((2, 2, 4, rows, D // 2), BF),
        name + "_far2": pltpu.VMEM((2, 2, rows, D // 4), BF),
        name + "_end2": pltpu.VMEM((2, 2, rows, D // 2), BF),
        name + "_ss": pltpu.SemaphoreType.DMA((24,)),
        name + "_rs": pltpu.SemaphoreType.DMA((24,)),
    }


def plane_reduce(plane, r, name, outs):
    refs = [getattr(r, name + end) for end in ("", "_far", "_end", "_far2", "_end2", "_ss", "_rs")]
    return plane_reduce_steps(plane, *refs, outs)


def plane_reduce_steps(plane, grads, far_a, end_a, far_b, end_b, ss, rs, outs):
    copies = []
    rows = grads.shape[2]

    def send(src, dst, device):
        copies.append(remote(src, dst, ss.at[len(copies)], rs.at[len(copies)], device))
        return copies[-1]

    def add(view, *others):
        def one(i, carry):
            at = pl.ds(pl.multiple_of(i * 16, 16), 16)
            piece = view.at[..., at, :]
            total = piece[...].astype(F32)
            for other in others:
                total = total + other.at[..., at, :][...].astype(F32)
            piece[...] = total.astype(BF)
            return carry

        lax.fori_loop(0, rows // 16, one, 0)

    for stage in (0, 1):
        rings = [plane.ring(half != stage) for half in (0, 1)]
        far_in, end_in = (far_a, end_a) if stage == 0 else (far_b, end_b)

        def view(half, place, part):
            return plane_view(plane, grads, half, 1 - stage, place, part)

        def ends(half, side, part):
            if part is None:
                return end_in.at[half, side]
            return end_in.at[half, side, ..., pl.ds(part * (D // 4), D // 4)]

        first, last = [], []
        for half in (0, 1):
            me, plus, minus, far, to_plus, to_minus = rings[half]
            first.append(
                (
                    send(view(half, far, 0), far_in.at[half, 0], to_plus),
                    send(view(half, far, 1), far_in.at[half, 1], to_minus),
                )
            )
            last.append(send(view(half, plus, 1), ends(half, 0, 1), to_plus))
            last.append(send(view(half, minus, 0), ends(half, 1, 0), to_minus))
        yield
        for half in (0, 1):
            me, plus, minus, far, to_plus, to_minus = rings[half]
            first[half][0].wait_recv()
            add(view(half, plus, 0), far_in.at[half, 0])
            last.append(send(view(half, plus, 0), ends(half, 0, 0), to_plus))
            first[half][1].wait_recv()
            add(view(half, minus, 1), far_in.at[half, 1])
            last.append(send(view(half, minus, 1), ends(half, 1, 1), to_minus))
        yield
        for copy in last:
            copy.wait_recv()
        for half in (0, 1):
            me = rings[half][0]
            if stage == 0:
                add(view(half, me, None), ends(half, 0, None), ends(half, 1, None))
            else:
                cols = pl.ds(half * (D // 2), D // 2)
                total = (
                    view(half, me, None)[...].astype(F32)
                    + end_in[half, 0].astype(F32)
                    + end_in[half, 1].astype(F32)
                )
                for start, out_ref in outs:
                    out_ref[:, cols] = total[start : start + out_ref.shape[0]]
    for copy in copies:
        copy.wait_send()


def load(src, dst, sem):
    copy = pltpu.make_async_copy(src, dst, sem)
    copy.start()
    return copy


def params(collective_id, limit=58):
    return pltpu.CompilerParams(
        collective_id=collective_id, has_side_effects=True, vmem_limit_bytes=limit << 20
    )


def sds(shape, dtype=BF):
    return jax.ShapeDtypeStruct(shape, dtype)


def scale_of(rows):
    return lax.rsqrt(jnp.mean(rows * rows, axis=-1, keepdims=True) + EPSILON)


def by_rows(one, start=0, rows=TOK):
    def step(i, carry):
        one(pl.ds(pl.multiple_of(start + i * 16, 16), 16))
        return carry

    lax.fori_loop(0, rows // 16, step, 0)


def total_rows(part, end_in, c, at):
    return (
        part[3, c, at, :].astype(F32)
        + end_in[0, at, :].astype(F32)
        + end_in[1, at, :].astype(F32)
    )


def chip_rows(chip):
    return pl.ds(pl.multiple_of(chip * (2 * TOK), 2 * TOK), 2 * TOK)


def build(body, inputs, outputs, scratch, collective_id):
    names = list(inputs) + list(outputs)
    early = [name for name, (_, spec) in inputs.items() if spec is VM]
    late = [name for name, (_, spec) in outputs.items() if spec is VM]
    scratch = dict(scratch)
    for name in early:
        scratch["vm_" + name] = pltpu.VMEM(inputs[name][0].shape, inputs[name][0].dtype)
    for name in late:
        scratch["vm_" + name] = pltpu.VMEM(outputs[name][0].shape, outputs[name][0].dtype)
    scratch["in_sems"] = pltpu.SemaphoreType.DMA((max(len(early), 1),))
    scratch["out_sems"] = pltpu.SemaphoreType.DMA((max(len(late), 1),))
    names += list(scratch)

    def kernel(*refs):
        r = types.SimpleNamespace(**dict(zip(names, refs)))
        coming, going = {}, {}
        for n, name in enumerate(early):
            local = getattr(r, "vm_" + name)
            coming[name] = load(getattr(r, name), local, r.in_sems.at[n])
            setattr(r, name, local)
        targets = {name: getattr(r, name) for name in late}
        for name in late:
            setattr(r, name, getattr(r, "vm_" + name))

        def need(*wanted):
            for name in wanted or list(coming):
                if name in coming:
                    coming.pop(name).wait()

        def flush(*wanted):
            for name in wanted or late:
                if name not in going:
                    sem = r.out_sems.at[late.index(name)]
                    going[name] = load(getattr(r, name), targets[name], sem)

        r.need, r.flush = need, flush
        body(r)
        need()
        flush()
        for copy in going.values():
            copy.wait()

    results = pl.pallas_call(
        kernel,
        out_shape=tuple(shape for shape, _ in outputs.values()),
        in_specs=[ANY if spec is VM else spec for _, spec in inputs.values()],
        out_specs=tuple(ANY for _ in outputs),
        scratch_shapes=list(scratch.values()),
        compiler_params=params(collective_id),
    )(*[array for array, _ in inputs.values()])
    return types.SimpleNamespace(**dict(zip(outputs, results)))


def vm(array):
    return (array, VM)


def hbm(array):
    return (array, ANY)


def signal(partners):
    barrier = pltpu.get_barrier_semaphore()
    for device in partners:
        pl.semaphore_signal(barrier, inc=1, device_id=device, device_id_type=MESH)


def arrive(partners):
    pl.semaphore_wait(pltpu.get_barrier_semaphore(), len(partners))


def scatter(ring, r, product, ready, before=None):
    return scatter_steps(
        ring, product, r.part, r.sib_in, r.far_in, r.end_in, r.sss, r.srs, ready, before
    )


def scatter_gather(ring, r, product, one, out_ref, kept, done=None, others=(), before=None):
    rows = TOK // CHUNKS
    gathers = []

    def ready(q):
        by_rows(one, q * rows, rows)
        last = q == CHUNKS - 1
        if last:
            r.flush(*kept)
        steps = gather_steps(
            ring,
            r.buf,
            out_ref,
            r.ss,
            r.rs,
            r.ls,
            rows,
            start=q * rows,
            base=14 * q,
            keep=last,
            ready=done if last else None,
        )
        advance(steps)
        gathers.append(steps)

    weave(scatter(ring, r, product, ready, before), *others)
    for _ in range(5):
        for steps in gathers:
            advance(steps)
        for other in others:
            advance(other)
    for steps in gathers:
        finish(steps)


def sums_of(r, ring, at):
    return total_rows(r.part, r.end_in, ring.c, at)


def half_gather(ring, r, out_ref):
    return gather_steps(ring, r.cbuf, out_ref, r.css, r.crs, r.cls, TOK // 2)


def rows_reduce(ring, r, q, ready):
    return rows_reduce_steps(
        ring, r.down, q, r.bpart, r.bsib, r.bfar, r.bend, r.bss, r.brs, r.bls, ready
    )


def norm_into(r, ring, gain_ref, at, rows):
    r.buf[ring.z * 2 + ring.c, at, :] = (rows * scale_of(rows) * gain_ref[...]).astype(BF)


def first_part(r, ring, plane):
    def one(at):
        norm_into(r, ring, r.gain_a, at, r.x[at, :].astype(F32))

    by_rows(one)
    arrive(r.partners)
    r.need()
    weights = plane_gather_steps(plane, r.wide, r.wss, r.wrs)

    def project(chip):
        h = r.buf[pl.ds(2 * chip, 2)].reshape(2 * TOK, D)
        r.raw[chip_rows(chip), :] = dnt(h, r.wide[...].reshape(16 * BIN_PAD, D)).astype(BF)

    rows = gather_steps(ring, r.buf, r.h, r.fss, r.frs, r.fls, TOK, ready=project)
    outs = plane_gather_steps(plane, r.wout, r.oss, r.ors)
    advance(weights)
    advance(rows)
    advance(weights)
    advance(outs)
    advance(weights)
    advance(outs)
    advance(rows)
    advance(weights)
    advance(rows)
    finish(weights)
    advance(outs)
    keep = load(r.wide, r.w_in, r.wls.at[0])
    finish(rows)
    return outs, keep


def ring_forward(r, ring, y_ref, w_ref, gain_ref, others=(), before=None):
    def product(rows, col):
        return dnn(y_ref[rows, :], w_ref[:, :, :, col].reshape(256, -1))

    def one(at):
        rows = r.x[at, :].astype(F32) + sums_of(r, ring, at)
        r.x_out[at, :] = rows
        norm_into(r, ring, gain_ref, at, rows)

    scatter_gather(ring, r, product, one, r.h_out, ("x_out",), others=others, before=before)


def norm_back_rows(v_ref, gain_ref, grads, at):
    rows = v_ref[at, :].astype(F32)
    scale = scale_of(rows)
    unit = rows * scale
    scaled = grads * gain_ref[...]
    return scale * (scaled - unit * jnp.mean(scaled * unit, axis=-1, keepdims=True))


def ring_backward(r, ring, product, wo_ref, others, before=None, also=None):
    def one(at):
        grad = sums_of(r, ring, at)
        rows = r.res[at, :].astype(F32) + norm_back_rows(r.v, r.gain, grad, at)
        r.d_out[at, :] = rows
        r.buf[ring.z * 2 + ring.c, at, :] = rows.astype(BF)

    def done(chip):
        rows = r.buf[pl.ds(2 * chip, 2)].reshape(2 * TOK, D)
        r.dy_out[chip_rows(chip), :] = dnt(rows, wo_ref[...].reshape(256, D)).astype(BF)
        if also is not None:
            also(chip, rows)

    scatter_gather(ring, r, product, one, r.e_out, ("d_out",), done, others, before)


CHUNK = 8 * UNIT_PAD


def mlp_chip(r, chip, i):
    at = chip_rows(chip)
    tokens = pl.ds(2 * chip, 2)
    count = 2 * CHUNK // 3
    shard = 5 * i
    skip = i * count - shard * UNIT_PAD

    def part(w):
        return w[shard : shard + 6].reshape(6 * UNIT_PAD, D)[skip : skip + count]

    rows = r.hv[tokens].reshape(2 * TOK, D)
    gate = dnt(rows, part(r.wv.at[0]))
    up = dnt(rows, part(r.wv.at[1]))
    d_act = dnt(r.cotv[tokens].reshape(2 * TOK, D), part(r.downv))
    sig = 1.0 / (1.0 + jnp.exp(-gate))
    silu = gate * sig
    first = i * count
    r.act[at, first : first + count] = (silu * up).astype(BF)
    r.d_gu[at, first : first + count] = (
        d_act * up * (sig * (1.0 + gate * (1.0 - sig)))
    ).astype(BF)
    first += 2 * CHUNK
    r.d_gu[at, first : first + count] = (d_act * silu).astype(BF)


def mlp_down_steps(r):
    for n in range(4):
        at = slice(2 * TOK * n, 2 * TOK * (n + 1))
        for col in range(0, D, 512):
            r.outv[at, col : col + 512] = dnn(
                r.act[at, :], r.downv[:, :, col : col + 512].reshape(2 * CHUNK, 512)
            ).astype(BF)
        if n == 1:
            yield
    copy = load(r.outv, r.down, r.msem.at[9])
    yield
    copy.wait()


def mlp_grad_steps(r, jobs):
    copies = []
    for n, (lhs, col, rhs, off, half, w) in enumerate(jobs):
        slot = n % 2
        if n >= 2:
            copies[n - 2].wait()

        res = dtn(lhs[:, col : col + CHUNK], rhs[...].reshape(HALF_TOK, D))
        r.stage[slot] = res.astype(BF).reshape(8, UNIT_PAD, D)
        if w is not None:
            own = w[8 * half : 8 * half + 8].reshape(CHUNK, D).astype(F32)
            r.gacc[...] += jnp.sum(res * own, axis=0, keepdims=True)
        copies.append(
            load(
                r.stage.at[slot],
                r.grads.at[pl.ds(8 * half, 8), pl.ds(off, UNIT_PAD), :],
                r.gsem.at[n],
            )
        )
        yield
    copies[-2].wait()
    copies[-1].wait()


def mlp_body(r):
    ring = Ring()
    partners = (ring.up, ring.dn, ring.sib)
    half = TOK // 2
    weights_in, tokens_in = {}, {}

    def fetch(index, chip):
        at = pl.ds(2 * chip, 2)
        pairs = (
            (r.h.at[at], r.hv.at[at]),
            (r.lo.at[at], r.cotv.at[at, pl.ds(0, half), :]),
            (r.hi.at[at], r.cotv.at[at, pl.ds(half, half), :]),
        )
        tokens_in[index] = [
            load(src, dst, r.tsem.at[3 * index + n]) for n, (src, dst) in enumerate(pairs)
        ]

    fetch(0, ring.zz)
    for i in range(2):
        for n, ref in enumerate((r.wv.at[0], r.wv.at[1], r.downv)):
            weights_in[i, n] = load(
                r.w.at[pl.ds(8 * i, 8), pl.ds(n * UNIT_PAD, UNIT_PAD), :],
                ref.at[pl.ds(8 * i, 8)],
                r.msem.at[3 * i + n],
            )
    for index, chip in ((1, ring.zp), (2, ring.zm), (3, ring.z)):
        fetch(index, chip)
    late = load(r.wo.at[:, :, pl.ds(48, 16), :], r.wov, r.msem.at[10])
    signal(partners)
    r.gacc[...] = jnp.zeros_like(r.gacc)
    r.oacc[...] = jnp.zeros_like(r.oacc)
    arrive(partners)
    r.need()

    def before(index, chip, mid):
        for copy in tokens_in[index]:
            copy.wait()
        for i in range(3):
            if index == 0 and i < 2:
                for n in range(3):
                    weights_in[i, n].wait()
            mlp_chip(r, chip, i)
            if i == 1:
                mid()

    def product(rows, col):
        return dnn(r.d_gu[rows, :], r.wv[:, :, :, col].reshape(4 * CHUNK, -1))

    def weights():
        yield from mlp_down_steps(r)
        jobs = [
            (r.d_gu, n * CHUNK, r.hv, (n // 2) * UNIT_PAD, n % 2, r.wv.at[n // 2])
            for n in range(4)
        ]
        jobs += [(r.act, n * CHUNK, r.cotv, 2 * UNIT_PAD, n, None) for n in range(2)]
        yield from mlp_grad_steps(r, jobs)

    weight_grads = weights()
    def also(chip, rows):
        r.oacc[...] += dtn(r.y[chip_rows(chip), :], rows)

    late.wait()
    ring_backward(r, ring, product, r.wov, (weight_grads,), before, also)
    r.ostage[...] = r.oacc[...].astype(BF).reshape(16, 16, D)
    copy = load(r.ostage, r.grads.at[:, pl.ds(3 * UNIT_PAD, 16), :], r.msem.at[6])
    finish(weight_grads)
    copy.wait()
    r.gain_out[...] = r.gacc[...] / r.gain[...]


def mlp_step(h, lo, hi, w, wo, y, v, gain, cot):
    return build(
        mlp_body,
        {
            "h": hbm(h),
            "lo": hbm(lo),
            "hi": hbm(hi),
            "w": hbm(w),
            "wo": hbm(wo),
            "y": vm(y),
            "v": vm(v),
            "gain": vm(gain),
            "res": vm(cot),
        },
        {
            "down": (sds((HALF_TOK, D)), ANY),
            "d_out": (sds((TOK, D), F32), VM),
            "gain_out": (sds((1, D), F32), VM),
            "e_out": (sds((8, TOK, D)), ANY),
            "dy_out": (sds((HALF_TOK, 256)), VM),
            "grads": (sds((16, 3 * UNIT_PAD + 16, D)), ANY),
        },
        {
            "hv": pltpu.VMEM((8, TOK, D), BF),
            "cotv": pltpu.VMEM((8, TOK, D), BF),
            "wv": pltpu.VMEM((2, 16, UNIT_PAD, D), BF),
            "downv": pltpu.VMEM((16, UNIT_PAD, D), BF),
            "wov": pltpu.VMEM((4, 4, 16, D), BF),
            "act": pltpu.VMEM((HALF_TOK, 2 * CHUNK), BF),
            "d_gu": pltpu.VMEM((HALF_TOK, 4 * CHUNK), BF),
            "outv": pltpu.VMEM((HALF_TOK, D), BF),
            "oacc": pltpu.VMEM((256, D), F32),
            "ostage": pltpu.VMEM((16, 16, D), BF),
            "stage": pltpu.VMEM((2, 8, UNIT_PAD, D), BF),
            "gacc": pltpu.VMEM((1, D), F32),
            "msem": pltpu.SemaphoreType.DMA((11,)),
            "tsem": pltpu.SemaphoreType.DMA((12,)),
            "gsem": pltpu.SemaphoreType.DMA((6,)),
        }
        | SCATTER_SCRATCH
        | GATHER_SCRATCH,
        4,
    )


def state_tables():
    first = np.zeros((128, STATE), np.float32)
    second = np.zeros((128, STATE), np.float32)
    bias = np.zeros((8, STATE), np.float32)
    coef = np.zeros((8, STATE), np.float32)
    bias[0, 0] = bias[1, 0] = 1.0
    coef[0, 0] = 1.0
    at = 1
    for i in range(FEAT):
        first[i, at] = 1.0
        bias[1, at] = 1.0
        coef[0, at] = 1.0 / math.sqrt(FEAT)
        at += 1
    for i in range(FEAT):
        for j in range(i, FEAT):
            first[i, at] = 1.0
            second[j, at] = 1.0
            coef[0, at] = (0.5 if i == j else 1.0) / FEAT
            at += 1
    picks = np.zeros((4, 128, 128), np.float32)
    for which in range(4):
        for i in range(FEAT):
            picks[which, which * FEAT + i, i] = 1.0
    return (
        np.stack([first, second]),
        np.concatenate([bias[:2], coef[:1], np.zeros((5, STATE), np.float32)]),
        picks,
    )


def select_table(width):
    table = np.zeros((16 * BIN_PAD, 3 * HEAD_V), np.float32)
    for shard in range(16):
        for i in range(width):
            head, col = shard // 8, (shard % 8) * width + i
            to = 2 * HEAD_V + 2 * FEAT * head + col if col < 2 * FEAT else head * HEAD_V + col - 2 * FEAT
            table[shard * BIN_PAD + i, to] = 1.0
    return table


BLK = 256
NBLK = HALF_TOK // BLK
INV_ROOT = 1.0 / math.sqrt(FEAT)


def rows_of(b):
    return slice(b * BLK, (b + 1) * BLK)


def head_of(j):
    return slice(j * HEAD_V, (j + 1) * HEAD_V)


def chip_block(b):
    return pl.ds(pl.multiple_of(b * BLK, BLK), BLK) if not isinstance(b, int) else rows_of(b)


def causal_mask(start, edge):
    t = start + lax.broadcasted_iota(jnp.int32, (BLK, BLK), 0)
    u = start + lax.broadcasted_iota(jnp.int32, (BLK, BLK), 1)
    return (u <= t) & ((t >= edge) == (u >= edge))


class Linear:
    def __init__(self, r):
        self.r = r
        self.xh = lax.axis_index("xh")
        self.partner = {"xh": 1 - self.xh}
        self.edge = jnp.where(self.xh == 0, EDGE, HALF_TOK - EDGE)
        self.second = jnp.where(self.xh == 1, 1.0, 0.0)
        self.coef = r.t[2:3, :]

    def vectors(self):
        r = self.r
        small = r.p[:, 2 * HEAD_V :]
        for j in range(2):
            r.qs[j] = dnn(small, r.pick[2 * j]).astype(BF)
            r.ks[j] = dnn(small, r.pick[2 * j + 1]).astype(BF)

    def factors(self, vecs):
        r = self.r
        return dnn(vecs, r.e[0]) + r.t[0:1, :], dnn(vecs, r.e[1]) + r.t[1:2, :]

    def factors_back(self, grad, one, two):
        r = self.r
        return dnt((grad * two).astype(BF), r.e[0]) + dnt((grad * one).astype(BF), r.e[1])

    def key_open(self, width):
        slot = lax.broadcasted_iota(jnp.int32, (BLK, width), 0)
        return (slot >= EDGE) | (self.xh == 1)

    def sees_state(self, b, width):
        slot = b * BLK + lax.broadcasted_iota(jnp.int32, (BLK, width), 0)
        return (slot < HALF_TOK - EDGE) | (self.xh == 0)

    def scores(self, j, b):
        r = self.r
        scores = dnt(r.qs[j, chip_block(b), :], r.ks[j, chip_block(b), :]) * INV_ROOT
        mask = causal_mask(b * BLK, self.edge)
        return scores, mask, jnp.where(mask, 1.0 + scores + 0.5 * scores * scores, 0.0)


def linear_states(r, lin):
    for b in range(NBLK):
        r.p[rows_of(b), :] = dnn(r.raw[rows_of(b), :], r.sel[...]).astype(BF)
    lin.vectors()
    for j in range(2):
        sv = jnp.zeros((HEAD_V, STATE), F32)
        sn = jnp.zeros((1, STATE), F32)
        for b in range(NBLK):
            r.pre_v[j, b] = sv
            r.pre_n[j, b] = jnp.broadcast_to(sn, (8, STATE))
            one, two = lin.factors(r.ks[j, rows_of(b), :])
            phi = one * two
            if b == 0:
                phi = jnp.where(lin.key_open(STATE), phi, 0.0)
            sv = sv + dtn(r.p[rows_of(b), head_of(j)], phi.astype(BF)) * lin.coef
            sn = sn + jnp.sum(phi, axis=0, keepdims=True) * lin.coef
        r.sv_s[j] = sv.astype(BF)
        r.sn_s[j] = jnp.broadcast_to(sn, (8, STATE))
    return (
        remote(r.sv_s, r.sv_r, r.xss.at[0], r.xrs.at[0], lin.partner),
        remote(r.sn_s, r.sn_r, r.xss.at[1], r.xrs.at[1], lin.partner),
    )


def linear_own(r, lin, b):
    rows = chip_block(b)
    for j in range(2):
        _, _, kernel = lin.scores(j, b)
        r.num[j, rows, :] = dnn(kernel.astype(BF), r.p[rows, head_of(j)])
        r.den[j, rows, :] = jnp.broadcast_to(
            jnp.sum(kernel, axis=-1, keepdims=True), (BLK, HEAD_V)
        )


def linear_rest(r, lin, b):
    rows = chip_block(b)
    for j in range(2):
        state_v = (r.pre_v[j, b] + r.sv_r[j].astype(F32) * lin.second).astype(BF)
        state_n = r.pre_n[j, b] + r.sn_r[j] * lin.second
        r.sv[j, b] = state_v
        r.sn[j, b] = state_n
        one, two = lin.factors(r.qs[j, rows, :])
        phi = one * two
        den = jnp.sum(phi * state_n[0:1, :], axis=-1, keepdims=True)
        num = dnt(phi.astype(BF), state_v)
        seen = lin.sees_state(b, HEAD_V)
        top = r.num[j, rows, :] + jnp.where(seen, num, 0.0)
        bottom = r.den[j, rows, :] + jnp.where(seen, den, 0.0)
        r.y[rows, head_of(j)] = (top / bottom).astype(BF)


STATE_SCRATCH = {
    "qs": pltpu.VMEM((2, HALF_TOK, 128), BF),
    "ks": pltpu.VMEM((2, HALF_TOK, 128), BF),
    "sv_s": pltpu.VMEM((2, HEAD_V, STATE), BF),
    "sn_s": pltpu.VMEM((2, 8, STATE), F32),
    "sv_r": pltpu.VMEM((2, HEAD_V, STATE), BF),
    "sn_r": pltpu.VMEM((2, 8, STATE), F32),
    "pre_v": pltpu.VMEM((2, NBLK, HEAD_V, STATE), F32),
    "pre_n": pltpu.VMEM((2, NBLK, 8, STATE), F32),
    "xss": pltpu.SemaphoreType.DMA((2,)),
    "xrs": pltpu.SemaphoreType.DMA((2,)),
}


def mask_cotangent(r, ring):
    first = lax.axis_index("xh") * HALF_TOK + (ring.z * 2 + ring.c) * TOK
    slot = first + lax.broadcasted_iota(jnp.int32, (TOK, 1), 0)
    last = 2 * HALF_TOK - EDGE
    start = jnp.where(slot < EDGE, 0, jnp.where(slot < last, EDGE, last))
    length = jnp.where(
        slot < EDGE, r.lengths[0, 0], jnp.where(slot < last, r.lengths[0, 1], r.lengths[0, 2])
    )
    valid = (slot - start) < length
    rows = r.cot[...].astype(F32)
    r.cot_out[...] = jnp.where(valid, rows, 0.0).astype(BF)


def linear_body(r):
    ring, plane = Ring(), Plane()
    r.partners = (ring.up, ring.dn, ring.sib, {"xh": 1 - lax.axis_index("xh")})
    r.partners += plane.neighbours()
    signal(r.partners)
    r.need("x", "gain_a", "rows_in", "rows_out", "cot")
    mask_cotangent(r, ring)
    own = r.wide.at[plane.x, plane.y]
    own[BIN_PAD // 2 :, :] = jnp.zeros((BIN_PAD // 2, D), BF)
    own[: r.rows_in.shape[0], :] = r.rows_in[...]
    r.wout[plane.x, plane.y] = r.rows_out[...]
    r.cbuf[ring.z * 2 + ring.c] = r.cot_out[: TOK // 2, :]
    r.flush("cot_out")
    outs, keep = first_part(r, ring, plane)
    cots = half_gather(ring, r, r.lo)
    advance(cots)
    lin = Linear(r)
    states = linear_states(r, lin)
    advance(outs)
    linear_own(r, lin, ring.zz)
    advance(outs)
    linear_own(r, lin, ring.zp)
    advance(cots)
    advance(cots)
    finish(outs)
    keep_out = load(r.wout, r.w_out, r.wls.at[1])

    def before(index, chip, mid):
        if index == 0:
            for copy in states:
                copy.wait_recv()
        if index >= 2:
            linear_own(r, lin, chip)
        linear_rest(r, lin, chip)
        mid()
        if index == 3:
            r.flush("y", "p", "sv", "sn")

    ring_forward(r, ring, r.y, r.wout, r.gain_b, (cots,), before)
    finish(cots)
    keep.wait()
    keep_out.wait()
    for copy in states:
        copy.wait_send()


def linear_step(select, tables, cot, lengths, x, gain_a, gain_b, rows_in, rows_out):
    return build(
        linear_body,
        {
            "x": vm(x),
            "gain_a": vm(gain_a),
            "rows_in": vm(rows_in),
            "rows_out": vm(rows_out),
            "cot": vm(cot),
            "gain_b": vm(gain_b),
            "sel": vm(select),
            "e": vm(tables[0]),
            "t": vm(tables[1]),
            "pick": vm(tables[2]),
            "lengths": (lengths, SM),
        },
        {
            "cot_out": (sds((TOK, D)), VM),
            "h": (sds((8, TOK, D)), ANY),
            "w_in": (sds((4, 4, BIN_PAD, D)), ANY),
            "w_out": (sds((4, 4, 16, D)), ANY),
            "y": (sds((HALF_TOK, 2 * HEAD_V)), VM),
            "p": (sds((HALF_TOK, 3 * HEAD_V)), VM),
            "sv": (sds((2, NBLK, HEAD_V, STATE)), VM),
            "sn": (sds((2, NBLK, 8, STATE), F32), VM),
            "lo": (sds((8, TOK // 2, D)), ANY),
            "x_out": (sds((TOK, D), F32), VM),
            "h_out": (sds((8, TOK, D)), ANY),
        },
        {
            "raw": pltpu.VMEM((HALF_TOK, 16 * BIN_PAD), BF),
            "num": pltpu.VMEM((2, HALF_TOK, HEAD_V), F32),
            "den": pltpu.VMEM((2, HALF_TOK, HEAD_V), F32),
            "wide": pltpu.VMEM((4, 4, BIN_PAD, D), BF),
            "wout": pltpu.VMEM((4, 4, 16, D), BF),
            "wss": pltpu.SemaphoreType.DMA((GATHER_COPIES,)),
            "wrs": pltpu.SemaphoreType.DMA((GATHER_COPIES,)),
            "oss": pltpu.SemaphoreType.DMA((GATHER_COPIES,)),
            "ors": pltpu.SemaphoreType.DMA((GATHER_COPIES,)),
            "wls": pltpu.SemaphoreType.DMA((2,)),
            "fss": pltpu.SemaphoreType.DMA((14,)),
            "frs": pltpu.SemaphoreType.DMA((14,)),
            "fls": pltpu.SemaphoreType.DMA((8,)),
        }
        | STATE_SCRATCH
        | HALF_SCRATCH
        | SCATTER_SCRATCH
        | GATHER_SCRATCH,
        2,
    )


def linear_backward_own(r, lin, sums):
    lin.vectors()
    for j in range(2):
        tv = jnp.zeros((HEAD_V, STATE), F32)
        tn = jnp.zeros((1, STATE), F32)
        for b in range(NBLK):
            queries = r.qs[j, rows_of(b), :]
            grads = r.dy[rows_of(b), head_of(j)]
            one, two = lin.factors(queries)
            phi = one * two
            phi_low = phi.astype(BF)
            seen = lin.sees_state(b, 1)
            state_v, state_n = r.sv[j, b], r.sn[j, b, 0:1, :]
            scores, mask, kernel = lin.scores(j, b)
            weight_grad = dnt(grads, r.p[rows_of(b), head_of(j)])
            den = jnp.sum(phi * state_n, axis=-1, keepdims=True)
            num = dnt(phi_low, state_v)
            dot = jnp.sum(num * grads.astype(F32), axis=-1, keepdims=True)
            total = jnp.where(seen, den, 0.0) + jnp.sum(kernel, axis=-1, keepdims=True)
            dot = jnp.where(seen, dot, 0.0) + jnp.sum(kernel * weight_grad, axis=-1, keepdims=True)
            inverse = 1.0 / total
            mean = dot * inverse
            grads_n = (grads.astype(F32) * inverse).astype(BF)
            score_grad = jnp.where(
                mask, (weight_grad - mean) * inverse * (1.0 + scores), 0.0
            ).astype(BF)
            r.dk[j, rows_of(b), :] = dtn(score_grad, queries)
            r.dv[j, rows_of(b), :] = dtn(kernel.astype(BF), grads_n)
            shift = jnp.where(seen, -(mean * inverse), 0.0)
            grads_s = jnp.where(seen, grads_n, jnp.zeros_like(grads_n))
            phi_grad = dnn(grads_s, state_v) + shift * state_n
            r.dq[j, rows_of(b), :] = dnn(
                score_grad, r.ks[j, rows_of(b), :]
            ) * INV_ROOT + lin.factors_back(phi_grad, one, two)
            own_v = dtn(grads_s, phi_low) * lin.coef
            own_n = jnp.sum(shift * phi, axis=0, keepdims=True) * lin.coef
            r.pre_v[j, b] = own_v
            r.pre_n[j, b] = jnp.broadcast_to(own_n, (8, STATE))
            tv, tn = tv + own_v, tn + own_n
            if (j, b) in ((0, 0), (0, 3)):
                advance(sums)
        r.sv_s[j] = tv.astype(BF)
        r.sn_s[j] = jnp.broadcast_to(tn, (8, STATE))
    copies = (
        remote(r.sv_s, r.sv_r, r.xss.at[0], r.xrs.at[0], lin.partner),
        remote(r.sn_s, r.sn_r, r.xss.at[1], r.xrs.at[1], lin.partner),
    )
    for j in range(2):
        tv = jnp.zeros((HEAD_V, STATE), F32)
        tn = jnp.zeros((8, STATE), F32)
        for b in reversed(range(NBLK)):
            own_v, own_n = r.pre_v[j, b], r.pre_n[j, b]
            r.pre_v[j, b] = tv
            r.pre_n[j, b] = tn
            tv, tn = tv + own_v, tn + own_n
    return copies


def linear_backward_rest(r, lin, b):
    rows = chip_block(b)
    first = 1.0 - lin.second
    visible = lin.key_open(STATE) | (b > 0)
    placed = jnp.zeros((BLK, 128), F32)
    for j in range(2):
        one, two = lin.factors(r.ks[j, rows, :])
        phi = jnp.where(visible, one * two, 0.0)
        state = (r.pre_v[j, b] + r.sv_r[j].astype(F32) * first).astype(BF)
        state_n = r.pre_n[j, b, 0:1, :] + r.sn_r[j, 0:1, :] * first
        phi_grad = jnp.where(visible, dnn(r.p[rows, head_of(j)], state) + state_n, 0.0)
        key_grad = r.dk[j, rows, :] * INV_ROOT + lin.factors_back(phi_grad, one, two)
        value_grad = r.dv[j, rows, :] + dnt(phi.astype(BF), state)
        r.dp[rows, head_of(j)] = value_grad.astype(BF)
        placed = placed + dnt(r.dq[j, rows, :].astype(BF), r.pick[2 * j])
        placed = placed + dnt(key_grad.astype(BF), r.pick[2 * j + 1])
    r.dp[rows, 2 * HEAD_V :] = placed.astype(BF)
    r.draw[rows, :] = dnt(r.dp[rows, :], r.sel[...]).astype(BF)


def sum_steps(ring, plane, r):
    copies = []
    stages = (
        (r.ring_in, ring.z * 2 + ring.c, 8, lambda t: {"z": lax.div(t, 2), "c": lax.rem(t, 2)}),
        (r.x_in, plane.x, 4, plane.at_x),
        (r.y_in, plane.y, 4, plane.at_y),
    )
    for dst, own, count, device_of in stages:
        dst[own] = r.pack[...]
        sent = []
        for o in range(1, count):
            n = len(copies) + len(sent)
            device = device_of(lax.rem(own + o, count))
            sent.append(remote(r.pack, dst.at[own], r.pss.at[n], r.prs.at[n], device))
        yield
        for copy in sent:
            copy.wait_recv()
        for copy in sent:
            copy.wait_send()
        copies += sent
        total = dst[0]
        for k in range(1, count):
            total = total + dst[k]
        r.pack[...] = total


def last_body(r):
    ring, plane = Ring(), Plane()
    me = ring.z * 2 + ring.c
    partners = []
    for o in range(1, 8):
        to = lax.rem(me + o, 8)
        partners.append({"z": lax.div(to, 2), "c": lax.rem(to, 2)})
    for o in range(1, 4):
        partners.append(plane.at_x(lax.rem(plane.x + o, 4)))
        partners.append(plane.at_y(lax.rem(plane.y + o, 4)))
    signal(partners)
    loads = [
        load(r.g, r.win, r.lsem.at[0]),
        load(r.w, r.wv, r.lsem.at[1]),
        load(r.h, r.hv, r.lsem.at[2]),
    ]
    def write(at, rows, total):
        r.out[rows, :] = (r.x3[rows, :] + total).astype(BF)

    sums = rows_reduce(ring, r, 1, write)
    win = plane_reduce(plane, r, "win", ((0, r.win_in), (48, r.lin_out)))
    arrive(partners)
    advance(sums)
    loads[0].wait()
    advance(win)
    r.need()
    r.out[: TOK // 2, :] = r.low[...]
    lin = Linear(r)
    states = linear_backward_own(r, lin, sums)
    advance(win)
    finish(sums)
    r.flush("out")
    for copy in loads[1:]:
        copy.wait()

    def before(index, chip, mid):
        if index == 0:
            for copy in states:
                copy.wait_recv()
        linear_backward_rest(r, lin, chip)
        mid()

    wide = D // 8

    def product(rows, col):
        return dnn(r.draw[rows, :], r.wv[:, :, :, col].reshape(16 * BIN_PAD, -1))

    def weights():
        for k in range(4):
            cols = slice(k * 512, (k + 1) * 512)
            res = dtn(r.draw[...], r.hv[:, :, cols].reshape(HALF_TOK, 512))
            own = r.wv[:, :, :, cols].reshape(16 * BIN_PAD, 512).astype(F32)
            r.gacc[:, cols] = jnp.sum(res * own, axis=0, keepdims=True)
            r.lin[:, :, :, cols] = res.astype(BF).reshape(4, 4, BIN_PAD, 512)
        reduce = plane_reduce(plane, r, "lin", ((0, r.lin_in),))
        advance(reduce)
        gains = (r.gacc[...] / r.gain[...], r.gain_b[...], r.gain_c[...])
        for n, gain in enumerate(gains):
            for i in range(8):
                r.pack[i : i + 1, n * wide : (n + 1) * wide] = gain[:, i * wide : (i + 1) * wide]
        gain_sums = sum_steps(ring, plane, r)
        advance(gain_sums)
        yield
        advance(reduce)
        advance(gain_sums)
        yield
        advance(reduce)
        advance(gain_sums)
        advance(win)
        yield
        yield
        advance(reduce)
        finish(gain_sums)
        advance(win)
        yield
        finish(win)
        r.flush("win_in", "lin_out", "d_out")
        finish(reduce)

    weight_grads = weights()

    def one(at):
        r.d_out[at, :] = r.res[at, :] + norm_back_rows(r.v, r.gain, sums_of(r, ring, at), at)

    def ready(q):
        by_rows(one, q * (TOK // CHUNKS), TOK // CHUNKS)

    weave(scatter(ring, r, product, ready, before), weight_grads)
    for copy in states:
        copy.wait_send()
    finish(weight_grads)
    for n, out in enumerate((r.ga, r.gb, r.gc)):
        for i in range(8):
            out[:, i * wide : (i + 1) * wide] = r.pack[i : i + 1, n * wide : (n + 1) * wide]


def last_step(lin, dy, select, tables, down, x3, low, g, w, h, v, gain, res, gain_b, gain_c, width):
    small = (8, 3 * D // 8)
    return build(
        last_body,
        {
            "p": vm(lin.p),
            "dy": vm(dy),
            "sv": vm(lin.sv),
            "sn": vm(lin.sn),
            "sel": vm(select),
            "e": vm(tables[0]),
            "t": vm(tables[1]),
            "pick": vm(tables[2]),
            "down": hbm(down),
            "x3": vm(x3),
            "low": vm(low),
            "g": hbm(g),
            "w": hbm(w),
            "h": hbm(h),
            "v": vm(v),
            "gain": vm(gain),
            "res": vm(res),
            "gain_b": vm(gain_b),
            "gain_c": vm(gain_c),
        },
        {
            "out": (sds((TOK, D)), VM),
            "d_out": (sds((TOK, D), F32), VM),
            "ga": (sds((1, D), F32), VM),
            "gb": (sds((1, D), F32), VM),
            "gc": (sds((1, D), F32), VM),
            "win_in": (sds((48, D), F32), VM),
            "lin_in": (sds((width, D), F32), VM),
            "lin_out": (sds((16, D), F32), VM),
        },
        {
            "dp": pltpu.VMEM((HALF_TOK, 3 * HEAD_V), BF),
            "draw": pltpu.VMEM((HALF_TOK, 16 * BIN_PAD), BF),
            "dq": pltpu.VMEM((2, HALF_TOK, 128), F32),
            "dk": pltpu.VMEM((2, HALF_TOK, 128), F32),
            "dv": pltpu.VMEM((2, HALF_TOK, HEAD_V), F32),
            "wv": pltpu.VMEM((4, 4, BIN_PAD, D), BF),
            "hv": pltpu.VMEM((8, TOK, D), BF),
            "gacc": pltpu.VMEM((1, D), F32),
            "pack": pltpu.VMEM(small, F32),
            "ring_in": pltpu.VMEM((8,) + small, F32),
            "x_in": pltpu.VMEM((4,) + small, F32),
            "y_in": pltpu.VMEM((4,) + small, F32),
            "pss": pltpu.SemaphoreType.DMA((13,)),
            "prs": pltpu.SemaphoreType.DMA((13,)),
            "lsem": pltpu.SemaphoreType.DMA((3,)),
        }
        | STATE_SCRATCH
        | ROWS_SCRATCH
        | plane_reduce_scratch("win", 64)
        | plane_reduce_scratch("lin", BIN_PAD)
        | SCATTER_SCRATCH,
        6,
    )


WBLK = 128
WKEYS = WBLK + WINDOW
INV_ROOT_V = 1.0 / math.sqrt(HEAD_V)


def turn_tables():
    slot = np.arange(2 * HALF_TOK)
    last = 2 * HALF_TOK - EDGE
    position = slot - np.where(slot < EDGE, 0, np.where(slot < last, EDGE, last))
    frequency = np.exp(-math.log(10000.0) * np.arange(HEAD_V // 2) * 2.0 / HEAD_V)
    angles = position[:, None] * frequency[None, :]
    cosine, sine = np.cos(angles), np.sin(angles)
    pair = np.stack(
        [np.concatenate([cosine, cosine], axis=1), np.concatenate([-sine, sine], axis=1)]
    )
    return pair.reshape(2, 2, HALF_TOK, HEAD_V).transpose(1, 0, 2, 3).astype(np.float32)


class Window:
    def __init__(self):
        self.xh = lax.axis_index("xh")
        self.partner = {"xh": 1 - self.xh}
        self.edge = jnp.where(self.xh == 0, EDGE, HALF_TOK - EDGE)
        self.lowest = jnp.where(self.xh == 0, 0, -WINDOW)

    def mask(self, b):
        t = b * WBLK + lax.broadcasted_iota(jnp.int32, (WBLK, WKEYS), 0)
        u = b * WBLK - WINDOW + lax.broadcasted_iota(jnp.int32, (WBLK, WKEYS), 1)
        same = (t >= self.edge) == (u >= self.edge)
        return (u <= t) & (t - u < WINDOW) & same & (u >= self.lowest)

    def probs(self, r, b, j):
        rows, keys, head = window_rows(b), window_keys(b), head_of(j)
        scores = dnt(r.q[rows, head], r.kv[keys, head]) * INV_ROOT_V
        scores = jnp.where(self.mask(b), scores, -1e30)
        exps = jnp.exp(scores - jnp.max(scores, axis=-1, keepdims=True))
        return exps / jnp.sum(exps, axis=-1, keepdims=True)


def window_rows(b):
    return pl.ds(b * WBLK if isinstance(b, int) else pl.multiple_of(b * WBLK, WBLK), WBLK)


def window_keys(b):
    return pl.ds(b * WBLK if isinstance(b, int) else pl.multiple_of(b * WBLK, WBLK), WKEYS)


def window_vectors(r, win, cots):
    size = 2 * TOK
    blocks = HALF_TOK // size

    def turned(vecs, rows):
        return (
            vecs * r.turn[0, rows, :] + pltpu.roll(vecs, HEAD_V // 2, 1) * r.turn[1, rows, :]
        ).astype(BF)

    for b in (blocks - 1,) + tuple(range(blocks - 1)):
        rows = slice(b * size, (b + 1) * size)
        shifted = slice(WINDOW + b * size, WINDOW + (b + 1) * size)
        tokens = r.hv[2 * b : 2 * b + 2].reshape(size, D)
        for j in range(2):
            proj = dnt(tokens, r.wiv[2 * j : 2 * j + 2].reshape(384, D))
            r.q[rows, head_of(j)] = turned(proj[:, :128], rows)
            r.kv[shifted, head_of(j)] = turned(proj[:, 128:256], rows)
            r.kv[shifted, head_of(2 + j)] = proj[:, 256:].astype(BF)
        if b == blocks - 1:
            copy = remote(
                r.kv.at[pl.ds(HALF_TOK, WINDOW), :],
                r.kv.at[pl.ds(0, WINDOW), :],
                r.xss,
                r.xrs,
                win.partner,
            )
    advance(cots)
    return copy


def window_chip(r, win, chip):
    for i in range(2 * TOK // WBLK):
        b = chip * (2 * TOK // WBLK) + i
        for j in range(2):
            r.y[window_rows(b), head_of(j)] = dnn(
                win.probs(r, b, j).astype(BF), r.kv[window_keys(b), head_of(2 + j)]
            ).astype(BF)


def window_body(r):
    ring = Ring()
    partners = (ring.up, ring.dn, ring.sib, {"xh": 1 - lax.axis_index("xh")})
    signal(partners)
    loads = (
        load(r.w.at[:, :, pl.ds(0, 48), :], r.wiv, r.lsem.at[0]),
        load(r.h, r.hv, r.lsem.at[1]),
        load(r.turns.at[lax.axis_index("xh")], r.turn, r.lsem.at[2]),
        load(r.w.at[:, :, pl.ds(48, 16), :], r.wov, r.lsem.at[3]),
    )
    r.need("cot")
    r.cbuf[ring.z * 2 + ring.c] = r.cot[TOK // 2 :, :]
    arrive(partners)
    cots = half_gather(ring, r, r.hi)
    advance(cots)
    r.need()
    for copy in loads:
        copy.wait()
    win = Window()
    halo = window_vectors(r, win, cots)

    def before(index, chip, mid):
        if index == 0:
            halo.wait_recv()
        window_chip(r, win, chip)
        mid()
        if index == 3:
            r.flush("y", "q", "kv")

    ring_forward(r, ring, r.y, r.wov, r.gain, (cots,), before)
    finish(cots)
    halo.wait_send()


def window_step(h, w, turns, cot, x, gain):
    return build(
        window_body,
        {
            "h": hbm(h),
            "w": hbm(w),
            "turns": hbm(turns),
            "cot": vm(cot),
            "x": vm(x),
            "gain": vm(gain),
        },
        {
            "y": (sds((HALF_TOK, 256)), VM),
            "q": (sds((HALF_TOK, 256)), VM),
            "kv": (sds((HALF_TOK + WINDOW, 512)), VM),
            "hi": (sds((8, TOK // 2, D)), ANY),
            "x_out": (sds((TOK, D), F32), VM),
            "h_out": (sds((8, TOK, D)), ANY),
        },
        {
            "hv": pltpu.VMEM((8, TOK, D), BF),
            "wiv": pltpu.VMEM((4, 4, 48, D), BF),
            "wov": pltpu.VMEM((4, 4, 16, D), BF),
            "turn": pltpu.VMEM((2, HALF_TOK, HEAD_V), F32),
            "lsem": pltpu.SemaphoreType.DMA((4,)),
            "xss": pltpu.SemaphoreType.DMA,
            "xrs": pltpu.SemaphoreType.DMA,
        }
        | HALF_SCRATCH
        | SCATTER_SCRATCH
        | GATHER_SCRATCH,
        3,
    )


def window_back_halo(r, win):
    rows, keys = window_rows(0), window_keys(0)
    for j in range(2):
        head, vals = head_of(j), head_of(2 + j)
        probs = win.probs(r, 0, j)
        prob_grad = dnt(r.dy[rows, head], r.kv[keys, vals])
        score_grad = (
            probs * (prob_grad - jnp.sum(prob_grad * probs, axis=-1, keepdims=True))
        ).astype(BF)
        r.halo_s[:, head] = dtn(score_grad, r.q[rows, head])[:WINDOW] * INV_ROOT_V
        r.halo_s[:, vals] = dtn(probs.astype(BF), r.dy[rows, head])[:WINDOW]
    return remote(r.halo_s, r.halo, r.xss, r.xrs, win.partner)


def turned_back(r, rows, grads):
    return (
        grads * r.turn[0, rows, :] + pltpu.roll(grads * r.turn[1, rows, :], HEAD_V // 2, 1)
    ).astype(BF)


def window_back_block(r, win, b):
    rows, keys = window_rows(b), window_keys(b)
    for j in range(2):
        head, vals = head_of(j), head_of(2 + j)
        queries, grads = r.q[rows, head], r.dy[rows, head]
        probs = win.probs(r, b, j)
        prob_grad = dnt(grads, r.kv[keys, vals])
        score_grad = (
            probs * (prob_grad - jnp.sum(prob_grad * probs, axis=-1, keepdims=True))
        ).astype(BF)
        r.dp[rows, head_of(3 * j)] = turned_back(
            r, rows, dnn(score_grad, r.kv[keys, head]) * INV_ROOT_V
        )
        r.dkv[keys, head] += dtn(score_grad, queries) * INV_ROOT_V
        r.dkv[keys, vals] += dtn(probs.astype(BF), grads)


def window_back_chip(r, chip):
    last = pl.ds(pl.multiple_of((chip + 1) * (2 * TOK), WINDOW), WINDOW)
    r.dkv[last, :] += jnp.where(chip == HALF_TOK // (2 * TOK) - 1, r.halo[...], 0.0)
    shifted = pl.ds(pl.multiple_of(chip * (2 * TOK) + WINDOW, WINDOW), 2 * TOK)
    rows = chip_rows(chip)
    for j in range(2):
        r.dp[rows, head_of(3 * j + 1)] = turned_back(r, rows, r.dkv[shifted, head_of(j)])
        r.dp[rows, head_of(3 * j + 2)] = r.dkv[shifted, head_of(2 + j)].astype(BF)


def window_back_body(r):
    ring = Ring()
    partners = (ring.up, ring.dn, ring.sib, {"xh": 1 - lax.axis_index("xh")})
    signal(partners)
    turning = load(r.turns.at[lax.axis_index("xh")], r.turn, r.lsem.at[0])
    loads = [
        load(r.w.at[:, :, pl.ds(0, 48), :], r.wiv, r.lsem.at[1]),
        load(r.h, r.hv, r.lsem.at[2]),
        load(r.wo, r.wov, r.lsem.at[4]),
    ]
    r.dkv[...] = jnp.zeros_like(r.dkv)
    r.oacc[...] = jnp.zeros_like(r.oacc)
    r.gacc[...] = jnp.zeros_like(r.gacc)

    def write(at, rows, total):
        r.low[at, :] = (r.x3[rows, :] + total).astype(BF)

    sums = rows_reduce(ring, r, 0, write)
    arrive(partners)
    advance(sums)
    r.need()
    turning.wait()
    win = Window()
    halo = window_back_halo(r, win)
    for copy in loads:
        copy.wait()
    blocks = HALF_TOK // WBLK

    def before(index, chip, mid):
        turns = ((0, 1, 2), (0, 1), (1, 2), (1,))[index]
        for n in turns:
            window_back_block(r, win, lax.rem(2 * chip + n, blocks))
            if n == turns[0]:
                mid()
        if index == 0:
            advance(sums)
            halo.wait_recv()
        window_back_chip(r, chip)
        if index in (1, 3):
            advance(sums)

    def product(rows, col):
        return dnn(r.dp[rows, :], r.wiv[:, :, :, col].reshape(768, -1))

    def weights():
        for k in range(4):
            cols = slice(k * 512, (k + 1) * 512)
            rows = r.hv[:, :, cols].reshape(HALF_TOK, 512)
            for i in range(2):
                res = dtn(r.dp[:, i * 384 : (i + 1) * 384], rows)
                own = r.wiv[2 * i : 2 * i + 2, :, :, cols].reshape(384, 512).astype(F32)
                r.gacc[:, cols] += jnp.sum(res * own, axis=0, keepdims=True)
                r.gstage[2 * i : 2 * i + 2, :, :, cols] = res.astype(BF).reshape(2, 4, 48, 512)
            yield
        copy = load(r.gstage, r.grads.at[:, :, pl.ds(0, 48), :], r.lsem.at[5])
        yield
        copy.wait()

    def also(chip, rows):
        r.oacc[...] += dtn(r.y1[chip_rows(chip), :], rows)

    weight_grads = weights()
    ring_backward(r, ring, product, r.wov, (weight_grads,), before, also)
    finish(sums)
    halo.wait_send()
    r.ostage[...] = r.oacc[...].astype(BF).reshape(4, 4, 16, D)
    copy = load(r.ostage, r.grads.at[:, :, pl.ds(48, 16), :], r.lsem.at[6])
    finish(weight_grads)
    copy.wait()
    r.gain_out[...] = r.gacc[...] / r.gain[...]


def window_back_step(win, y1, dy, turns, down, x3, w, wo, h, v, gain, res):
    return build(
        window_back_body,
        {
            "q": vm(win.q),
            "kv": vm(win.kv),
            "dy": vm(dy),
            "turns": hbm(turns),
            "down": hbm(down),
            "x3": vm(x3),
            "w": hbm(w),
            "wo": hbm(wo),
            "h": hbm(h),
            "y1": vm(y1),
            "v": vm(v),
            "gain": vm(gain),
            "res": vm(res),
        },
        {
            "low": (sds((TOK // 2, D)), VM),
            "d_out": (sds((TOK, D), F32), VM),
            "gain_out": (sds((1, D), F32), VM),
            "e_out": (sds((8, TOK, D)), ANY),
            "dy_out": (sds((HALF_TOK, 256)), VM),
            "grads": (sds((4, 4, 64, D)), ANY),
        },
        {
            "dkv": pltpu.VMEM((HALF_TOK + WINDOW, 512), F32),
            "halo": pltpu.VMEM((WINDOW, 512), F32),
            "halo_s": pltpu.VMEM((WINDOW, 512), F32),
            "turn": pltpu.VMEM((2, HALF_TOK, HEAD_V), F32),
            "dp": pltpu.VMEM((HALF_TOK, 768), BF),
            "wiv": pltpu.VMEM((4, 4, 48, D), BF),
            "wov": pltpu.VMEM((4, 4, 16, D), BF),
            "hv": pltpu.VMEM((8, TOK, D), BF),
            "gstage": pltpu.VMEM((4, 4, 48, D), BF),
            "oacc": pltpu.VMEM((256, D), F32),
            "ostage": pltpu.VMEM((4, 4, 16, D), BF),
            "gacc": pltpu.VMEM((1, D), F32),
            "lsem": pltpu.SemaphoreType.DMA((7,)),
            "xss": pltpu.SemaphoreType.DMA,
            "xrs": pltpu.SemaphoreType.DMA,
        }
        | ROWS_SCRATCH
        | SCATTER_SCRATCH
        | GATHER_SCRATCH,
        5,
    )


def padded(rows, count):
    return jnp.pad(rows, ((0, count - rows.shape[0]), (0, 0)))


def end_kernel(*refs):
    ff, copied, (gate_up, down, win_out) = refs[0], refs[1:-3], refs[-3:]
    count = len(copied) // 2
    for n in range(count):
        copied[count + n][...] = copied[n][...]
    units = down.shape[0]
    gate_up[:, 0, :] = ff[:units].astype(F32)
    gate_up[:, 1, :] = ff[UNIT_PAD : UNIT_PAD + units].astype(F32)
    down[...] = ff[2 * UNIT_PAD : 2 * UNIT_PAD + units].astype(F32)
    win_out[...] = ff[3 * UNIT_PAD :].astype(F32)


def end_step(ff, arrays, units):
    results = pl.pallas_call(
        end_kernel,
        out_shape=tuple(sds(array.shape, array.dtype) for array in arrays)
        + (sds((units, 2, D), F32), sds((units, D), F32), sds((16, D), F32)),
        in_specs=[VM] * (1 + len(arrays)),
        out_specs=(VM,) * (len(arrays) + 3),
        compiler_params=pltpu.CompilerParams(vmem_limit_bytes=60 << 20),
    )(ff, *arrays)
    return results


def body(
    block_input,
    cotangent,
    lengths,
    gain_a,
    based_in,
    based_out,
    gain_b,
    swa_in,
    swa_out,
    gain_c,
    mlp_in,
    mlp_down,
):
    gains = [gain.reshape(1, D) for gain in (gain_a, gain_b, gain_c)]
    units = mlp_down.shape[0]
    wide = based_in.shape[1]
    win_all = lax.all_gather(
        jnp.concatenate([swa_in.T, swa_out], axis=0), PLANE, axis=0, tiled=True
    ).reshape(4, 4, 64, D)
    ff_all = lax.all_gather(
        jnp.concatenate(
            [padded(part, UNIT_PAD) for part in (mlp_in[:, 0, :].T, mlp_in[:, 1, :].T, mlp_down)],
            axis=0,
        ),
        PLANE,
        axis=0,
        tiled=True,
    ).reshape(16, 3 * UNIT_PAD, D)
    tables = tuple(
        jnp.asarray(table, kind) for table, kind in zip(state_tables(), (BF, F32, BF))
    )
    select = jnp.asarray(select_table(wide), BF)

    turns = jnp.asarray(turn_tables())

    lin = linear_step(
        select,
        tables,
        cotangent,
        lengths,
        block_input,
        gains[0],
        gains[1],
        based_in.T,
        based_out,
    )
    win = window_step(lin.h_out, win_all, turns, lin.cot_out, lin.x_out, gains[2])
    mlp = mlp_step(win.h_out, lin.lo, win.hi, ff_all, win_all, win.y, win.x_out, gains[2], lin.cot_out)
    ff_grads = lax.psum_scatter(
        mlp.grads.reshape(-1, D), PLANE, scatter_dimension=0, tiled=True
    )
    back = window_back_step(
        win,
        lin.y,
        mlp.dy_out,
        turns,
        mlp.down,
        win.x_out,
        win_all,
        lin.w_out,
        lin.h_out,
        lin.x_out,
        gains[1],
        mlp.d_out,
    )
    end = last_step(
        lin,
        back.dy_out,
        select,
        tables,
        mlp.down,
        win.x_out,
        back.low,
        back.grads,
        lin.w_in,
        lin.h,
        block_input,
        gains[0],
        back.d_out,
        back.gain_out,
        mlp.gain_out,
        wide,
    )
    names = ("out", "d_out", "ga", "lin_in", "lin_out", "gb", "win_in", "gc")
    results = end_step(ff_grads, [getattr(end, name) for name in names], units)
    out, d_out, ga, lin_in, lin_out, gb, win_in, gc, gate_up, down, win_out = results
    return (
        out,
        d_out,
        ga.reshape(D),
        lin_in.T,
        lin_out,
        gb.reshape(D),
        win_in.T,
        win_out,
        gc.reshape(D),
        jnp.transpose(gate_up, (2, 1, 0)),
        down,
    )


def solution(mesh):
    grid = Mesh(mesh.devices.reshape(2, 4, 2, 4, 2), ALL)
    tokens = P(ALL, None)
    weight = ("xh", "z", "c", "xl", "y")
    rows, cols = P(weight, None), P(None, weight)
    return jax.shard_map(
        body,
        mesh=grid,
        in_specs=(
            tokens,
            tokens,
            P(("xl", "y"), None),
            P(),
            cols,
            rows,
            P(),
            cols,
            rows,
            P(),
            P(None, None, weight),
            rows,
        ),
        out_specs=(
            tokens,
            tokens,
            P(),
            cols,
            rows,
            P(),
            cols,
            rows,
            P(),
            P(None, None, weight),
            rows,
        ),
        check_vma=False,
    )
```
